32 devices in a mesh: lat: 4 (over x, core), lon: 8 (over z, y).
Axes of the slice: x: 2, y: 2, z: 4, core: 2. Of those that a mesh axis runs over, the one named last changes fastest.
Arguments:
- tokens: bfloat16 [4, 96, 96, 512], P(None, 'lat', 'lon'), may hold values from -6 to 6
- cotangent: bfloat16 [4, 96, 96, 512], P(None, 'lat', 'lon'), may hold values from -6 to 6
- w_qkv: bfloat16 [512, 1536], replicated, may hold values from -2 to 2
- w_proj: bfloat16 [512, 512], replicated, may hold values from -0.25 to 0.25
- shifts: int32 [4, 2], replicated, may hold values from 0 to 11, as said below
- region_ids: int32 [96], replicated, may hold values from 0 to 1999, as said below
Outputs:
- mixed: bfloat16 [4, 96, 96, 512], P(None, 'lat', 'lon')
- grad_tokens: bfloat16 [4, 96, 96, 512], P(None, 'lat', 'lon')
- grad_qkv: float32 [512, 1536], replicated
- grad_proj: float32 [512, 512], replicated
The draws below stay inside these ranges and needn't reach their ends.
Inputs may be any that keep to these rules, and one draw needn't show every extreme that they name: For each level l, shifts[l, 0] is below 6 and shifts[l, 1] below 12; some level has shifts[l, 0] = 5 and some level has shifts[l, 1] = 11. region_ids is one positive label on the first 1 to 5 rows, another, larger positive label on the last 1 to 5 rows, and 0 on all others.
All inputs are finite; a program needn't handle non-finite values.
Results may differ from the reference program's by a relative error of at most 0.006.
The reference program's roundings to bfloat16 on the way count: a program that leaves them out, or rounds other values in their place, can miss the bound.
Values may be sent and summed in bfloat16 or wider, within the bound.
No kernel may reach another device: no remote copies, remote signals or barrier semaphores. Data moves between devices by JAX's collectives and lax.ppermute only.
A program may use at most 128 MiB of HBM per device.

```python
import math
import jax
import jax.numpy as jnp
from jax import lax

D = 512
HEADS = 16
LEV = 4
WLAT = 6
WLON = 12
NLAT = 96
NLON = 96
TOKENS = 36864


def draw_w_qkv(key, part):
    key = jax.random.fold_in(key, 2)
    first = jax.random.fold_in(key, 0)
    result = jax.random.truncated_normal(first, -4.0, 4.0, (D, 3 * D), jnp.float32) / math.sqrt(D)
    return result.astype(jnp.bfloat16)


def draw_shifts(key, part):
    key = jax.random.fold_in(key, 3)
    first, second, third, fourth = jax.random.split(key, 4)
    lat_part = jnp.concatenate([jax.random.permutation(first, WLAT - 1)[:LEV - 1].astype(jnp.int32), jnp.array([WLAT - 1], jnp.int32)])
    lon_part = jnp.concatenate([jax.random.permutation(second, WLON - 1)[:LEV - 1].astype(jnp.int32), jnp.array([WLON - 1], jnp.int32)])
    lat_part = lat_part[jax.random.permutation(third, LEV)]
    lon_part = lon_part[jax.random.permutation(fourth, LEV)]
    return jnp.stack([lat_part, lon_part], axis=1).astype(jnp.int32)


def draw_region_ids(key, part):
    key = jax.random.fold_in(key, 5)
    first, second, third = jax.random.split(key, 3)
    top_rows = jax.random.randint(first, (), 1, WLAT)
    bottom_rows = jax.random.randint(second, (), 1, WLAT)
    top_label = jax.random.randint(third, (), 1, 999)
    bottom_label = 1999
    row_index = jnp.arange(NLAT, dtype=jnp.int32)
    labels = jnp.where(row_index < top_rows, top_label, jnp.where(row_index >= NLAT - bottom_rows, bottom_label, 0))
    return labels.astype(jnp.int32)


def levels(own_key, extent, pieces, low, high):
    level = 1.0
    for position, shards_of in pieces:
        steps = jax.random.uniform(jax.random.fold_in(jax.random.fold_in(own_key, 6), position), (shards_of,), jnp.float32, low / len(pieces), high / len(pieces))
        level = level * jnp.repeat(jnp.exp(steps), extent[position] // shards_of).reshape((-1,) + (1,) * (len(extent) - 1 - position))
    return level


def scatter_about(own_key, dims, spread, most, cuts=(), kind=jnp.bfloat16):
    values = spread * jax.random.normal(own_key, dims, jnp.float32)
    if cuts:
        values = values * levels(own_key, dims, cuts, -0.22, 0.18)
    return jnp.clip(values, -most, most).astype(kind)


def setup_inputs(seed: int = 0) -> dict:
    seeds = jax.random.split(jax.random.key(seed), 7)
    tokens = scatter_about(seeds[0], (LEV, NLAT, NLON, D), 1.0, 6.0, ((1, 4), (2, 8)))
    cotangent = scatter_about(seeds[1], (LEV, NLAT, NLON, D), 1.0, 6.0, ((1, 4), (2, 8)))
    w_qkv = draw_w_qkv(jax.random.fold_in(seeds[6], 71), 0)
    w_proj = scatter_about(seeds[3], (D, D), D ** -0.5, 0.25)
    shifts = draw_shifts(jax.random.fold_in(seeds[6], 71), 0)
    region_ids = draw_region_ids(jax.random.fold_in(seeds[6], 71), 0)
    return dict(tokens=tokens, cotangent=cotangent, w_qkv=w_qkv, w_proj=w_proj, shifts=shifts, region_ids=region_ids)


NORM_EPS = 1e-05
FULL_PRECISION = lax.Precision.HIGHEST

def roll_field(grid_field, shifts, direction):

    def per_level(level_plane, offsets):
        return jnp.roll(level_plane, (direction * offsets[0], direction * offsets[1]), axis=(0, 1))
    return jax.vmap(per_level)(grid_field, shifts)

def make_windows(grid_field):
    lev_count, grid_rows, grid_cols, model_width = grid_field.shape
    shaped = grid_field.reshape(lev_count, grid_rows // WLAT, WLAT, grid_cols // WLON, WLON, model_width)
    shaped = shaped.transpose(1, 3, 0, 2, 4, 5)
    return shaped.reshape(-1, 2, lev_count * WLAT * WLON, model_width)

def undo_windows(blocks, lev_count, grid_rows, grid_cols):
    model_width = blocks.shape[-1]
    shaped = blocks.reshape(grid_rows // WLAT, grid_cols // WLON, lev_count, WLAT, WLON, model_width)
    return shaped.transpose(2, 0, 3, 1, 4, 5).reshape(lev_count, grid_rows, grid_cols, model_width)

def window_labels(rolled_ids, grid_cols):
    lev_count, grid_rows = rolled_ids.shape
    shaped = rolled_ids.reshape(lev_count, grid_rows // WLAT, WLAT)
    full = jnp.broadcast_to(shaped[:, :, :, None, None], (lev_count, grid_rows // WLAT, WLAT, grid_cols // WLON, WLON))
    return full.transpose(1, 3, 0, 2, 4).reshape(-1, 2, lev_count * WLAT * WLON)

def window_forward(tile, labels, w_qkv, w_proj):
    tile_len, model_width = tile.shape
    head_size = model_width // HEADS
    values_full = tile.astype(jnp.float32)
    center = values_full - lax.optimization_barrier(jnp.mean(values_full, axis=1, keepdims=True))
    variance = lax.optimization_barrier(jnp.mean(center * center, axis=1, keepdims=True))
    inv_scale = lax.rsqrt(variance + NORM_EPS)
    standard = center * inv_scale
    normed = standard.astype(jnp.bfloat16)
    projected = jnp.dot(normed, w_qkv, preferred_element_type=jnp.float32)
    queries = projected[:, :model_width].reshape(tile_len, HEADS, head_size)
    key_rows = projected[:, model_width:2 * model_width].reshape(tile_len, HEADS, head_size)
    value_rows = projected[:, 2 * model_width:].astype(jnp.bfloat16).reshape(tile_len, HEADS, head_size)
    scores = jnp.einsum('nhe,mhe->hnm', queries, key_rows, precision=FULL_PRECISION) / math.sqrt(head_size)
    allowed = labels[:, None] == labels[None, :]
    scores = jnp.where(allowed[None, :, :], scores, -jnp.inf)
    weights = jax.nn.softmax(scores, axis=-1)
    rounded_weights = weights.astype(jnp.bfloat16)
    context = jnp.einsum('hnm,mhe->nhe', rounded_weights.astype(jnp.float32), value_rows.astype(jnp.float32))
    context = context.reshape(tile_len, model_width).astype(jnp.bfloat16)
    update = jnp.dot(context, w_proj, preferred_element_type=jnp.float32).astype(jnp.bfloat16)
    stored = (standard, inv_scale, normed, queries, key_rows, value_rows, weights, rounded_weights, context)
    return (update, stored)

def window_backward(stored, grad_tile, w_qkv, w_proj):
    standard, inv_scale, normed, queries, key_rows, value_rows, weights, rounded_weights, context = stored
    tile_len, model_width = grad_tile.shape
    head_size = model_width // HEADS
    grad_context = jnp.dot(grad_tile, w_proj.T, preferred_element_type=jnp.float32).astype(jnp.bfloat16)
    grad_context = grad_context.reshape(tile_len, HEADS, head_size)
    proj_term = jnp.dot(context.T, grad_tile, preferred_element_type=jnp.float32)
    grad_weights = jnp.einsum('nhe,mhe->hnm', grad_context.astype(jnp.float32), value_rows.astype(jnp.float32))
    grad_values = jnp.einsum('hnm,nhe->mhe', rounded_weights.astype(jnp.float32), grad_context.astype(jnp.float32))
    grad_scores = weights * (grad_weights - lax.optimization_barrier(jnp.sum(weights * grad_weights, axis=-1, keepdims=True))) / math.sqrt(head_size)
    grad_queries = jnp.einsum('hnm,mhe->nhe', grad_scores, key_rows, precision=FULL_PRECISION)
    grad_keys = jnp.einsum('hnm,nhe->mhe', grad_scores, queries, precision=FULL_PRECISION)
    grad_projected = jnp.concatenate([grad_queries.reshape(tile_len, model_width), grad_keys.reshape(tile_len, model_width), grad_values.reshape(tile_len, model_width)], axis=1).astype(jnp.bfloat16)
    qkv_term = jnp.dot(normed.T, grad_projected, preferred_element_type=jnp.float32)
    grad_normed = jnp.dot(grad_projected, w_qkv.T, preferred_element_type=jnp.float32)
    grad_input = inv_scale * (grad_normed - lax.optimization_barrier(jnp.mean(grad_normed, axis=1, keepdims=True)) - standard * lax.optimization_barrier(jnp.mean(grad_normed * standard, axis=1, keepdims=True)))
    return (grad_input.astype(jnp.bfloat16), qkv_term, proj_term)

def reference(tokens, cotangent, w_qkv, w_proj, shifts, region_ids):
    lev_count, grid_rows, grid_cols, model_width = tokens.shape
    rolled = roll_field(tokens, shifts, -1)
    rolled_cot = roll_field(cotangent, shifts, -1)
    rolled_ids = jax.vmap(lambda offsets: jnp.roll(region_ids, -offsets[0]))(shifts)
    blocks = make_windows(rolled)
    cot_blocks = make_windows(rolled_cot)
    labels = window_labels(rolled_ids, grid_cols)

    def single(tile, grad_tile, label_row):
        update, stored = window_forward(tile, label_row, w_qkv, w_proj)
        grad_input, qkv_term, proj_term = window_backward(stored, grad_tile, w_qkv, w_proj)
        return (update, grad_input, qkv_term, proj_term)

    def group_step(totals, inputs):
        tile_set, grad_set, label_set = inputs
        update, grad_input, qkv_terms, proj_terms = jax.vmap(single)(tile_set, grad_set, label_set)
        return ((totals[0] + lax.optimization_barrier(jnp.sum(qkv_terms, axis=0)), totals[1] + lax.optimization_barrier(jnp.sum(proj_terms, axis=0))), (update, grad_input))
    zero_totals = (jnp.zeros((model_width, 3 * model_width), jnp.float32), jnp.zeros((model_width, model_width), jnp.float32))
    (qkv_total, proj_total), (updates, grads_back) = lax.scan(group_step, zero_totals, (blocks, cot_blocks, labels))
    update_field = roll_field(undo_windows(updates, lev_count, grid_rows, grid_cols), shifts, 1)
    grad_field = roll_field(undo_windows(grads_back, lev_count, grid_rows, grid_cols), shifts, 1)
    mixed = (tokens.astype(jnp.float32) + update_field.astype(jnp.float32)).astype(jnp.bfloat16)
    grad_tokens = (cotangent.astype(jnp.float32) + grad_field.astype(jnp.float32)).astype(jnp.bfloat16)
    grad_scale = 1.0 / math.sqrt(TOKENS)
    return (mixed, grad_tokens, qkv_total * grad_scale, proj_total * grad_scale)
```

```python
import functools
import math

import jax
import jax.numpy as jnp
from jax import lax
from jax.experimental import pallas as pl
from jax.experimental.pallas import tpu as pltpu
from jax.sharding import PartitionSpec as P

HEADS = 16
WLAT = 6
WLON = 12
NORM_EPS = 1e-05
LANES = 384
BARRED = 2.0**100
BF = jnp.bfloat16
F32 = jnp.float32

NN = (((1,), (0,)), ((), ()))
NT = (((1,), (1,)), ((), ()))
TN = (((0,), (0,)), ((), ()))


def dot(a, b, dims):
    return lax.dot_general(a, b, dims, preferred_element_type=F32)


def split_bf16(value):
    high = value.astype(BF)
    low = (value - high.astype(F32)).astype(BF)
    return high, low


def standardize(tile):
    values_full = tile.astype(F32)
    center = values_full - jnp.mean(values_full, axis=1, keepdims=True)
    variance = jnp.mean(center * center, axis=1, keepdims=True)
    inv_scale = lax.rsqrt(variance + NORM_EPS)
    return center * inv_scale, inv_scale


def window_kernel(
    x_ref, cot_ref, bar_q_ref, bar_k_ref, w_ref, wp_ref,
    update_ref, grad_ref, qkv_ref, proj_ref,
    norm_s, cot_s, q_s, k_s, v_s, g_s, ctx_s, gp_s,
):
    count, width = x_ref.shape
    size = width // HEADS

    @pl.when(pl.program_id(0) == 0)
    def _():
        qkv_ref[...] = jnp.zeros_like(qkv_ref)
        proj_ref[...] = jnp.zeros_like(proj_ref)
        norm_s[...] = jnp.zeros_like(norm_s)
        cot_s[...] = jnp.zeros_like(cot_s)

    standard, _ = standardize(x_ref[...])
    norm_s[:count] = standard.astype(BF)
    cot_s[:count] = cot_ref[...]
    scale = 1.0 / math.sqrt(size)
    q_s[...] = dot(w_ref[:width], norm_s[...], NT)
    k_s[...] = dot(w_ref[width : 2 * width], norm_s[...], NT)
    v_s[...] = dot(w_ref[2 * width :], norm_s[...], NT).astype(BF)
    g_s[...] = dot(wp_ref[...], cot_s[...], NT).astype(BF)

    def head(h, carry):
        rows = pl.ds(pl.multiple_of(h * size, size), size)
        q_high, q_low = split_bf16(q_s[rows] * (scale * math.log2(math.e)))
        k_high, k_low = split_bf16(k_s[rows])
        value = v_s[rows]
        grad_ctx = g_s[rows]
        q_all = jnp.concatenate([q_high, q_low, q_high, bar_q_ref[...]], axis=0)
        k_all = jnp.concatenate([k_high, k_high, k_low, bar_k_ref[...]], axis=0)
        k_tok = k_all.T[:count]
        v_tok = value.T[:count]
        scores = dot(k_tok, q_all, NN)
        expo = jnp.exp2(scores - jnp.max(scores, axis=0, keepdims=True))
        weights = expo * (1.0 / jnp.sum(expo, axis=0, keepdims=True))
        rounded = weights.astype(BF)
        ctx_s[rows] = dot(value[:, :count], rounded, NN)[:, :count].astype(BF)
        grad_w = dot(v_tok, grad_ctx, NN)
        grad_sc = weights * (grad_w - jnp.sum(weights * grad_w, axis=0, keepdims=True))
        high, low = split_bf16(grad_sc)
        k_pair = jnp.concatenate([k_high[:, :count], k_low[:, :count]], axis=0)
        q_pair = jnp.concatenate([q_high, q_low], axis=0)
        gq = dot(k_pair, high, NN)
        gq = gq[:size] + gq[size:] + dot(k_high[:, :count], low, NN)
        gk = dot(q_pair, high, NT)
        gk = gk[:size] + gk[size:] + dot(q_high, low, NT)
        gv = dot(grad_ctx, rounded, NT)
        base = pl.multiple_of(h * size, size)
        gp_s[pl.ds(base, size)] = (gq[:, :count] * scale).astype(BF)
        gp_s[pl.ds(width + base, size)] = (gk * math.log(2.0)).astype(BF)
        gp_s[pl.ds(2 * width + base, size)] = gv.astype(BF)
        return carry

    lax.fori_loop(0, HEADS, head, 0, unroll=2)

    proj_ref[...] += dot(ctx_s[...], cot_ref[...], NN)
    update_ref[...] = dot(ctx_s[...], wp_ref[...], TN).astype(BF)
    qkv_ref[...] += dot(gp_s[...], norm_s[:count], NN)
    grad_normed = dot(gp_s[...], w_ref[...], TN)
    standard, inv_scale = standardize(x_ref[...])
    grad_ref[...] = (
        inv_scale
        * (
            grad_normed
            - jnp.mean(grad_normed, axis=1, keepdims=True)
            - standard * jnp.mean(grad_normed * standard, axis=1, keepdims=True)
        )
    ).astype(BF)


def run_windows(tiles, cots, bar_q, bar_k, w_t, w_proj):
    groups, count, width = tiles.shape
    tile_spec = pl.BlockSpec((None, count, width), lambda i: (i, 0, 0))
    bar_spec = pl.BlockSpec((None, 32, LANES), lambda i: (i, 0, 0))
    whole = lambda shape: pl.BlockSpec(shape, lambda i: (0, 0))
    return pl.pallas_call(
        window_kernel,
        grid=(groups,),
        in_specs=[tile_spec, tile_spec, bar_spec, bar_spec, whole(w_t.shape), whole(w_proj.shape)],
        out_specs=[tile_spec, tile_spec, whole((3 * width, width)), whole((width, width))],
        out_shape=[
            jax.ShapeDtypeStruct(tiles.shape, BF),
            jax.ShapeDtypeStruct(tiles.shape, BF),
            jax.ShapeDtypeStruct((3 * width, width), F32),
            jax.ShapeDtypeStruct((width, width), F32),
        ],
        scratch_shapes=[
            pltpu.VMEM((LANES, width), BF),
            pltpu.VMEM((LANES, width), BF),
            pltpu.VMEM((width, LANES), F32),
            pltpu.VMEM((width, LANES), F32),
            pltpu.VMEM((width, LANES), BF),
            pltpu.VMEM((width, LANES), BF),
            pltpu.VMEM((width, count), BF),
            pltpu.VMEM((3 * width, count), BF),
        ],
        compiler_params=pltpu.CompilerParams(vmem_limit_bytes=48 * 1024 * 1024),
        cost_estimate=pl.CostEstimate(
            flops=20_000_000_000, bytes_accessed=12_000_000, transcendentals=6_000_000
        ),
    )(tiles, cots, bar_q, bar_k, w_t, w_proj)


def bar_features(labels, top, bottom):
    groups, count = labels.shape
    kinds = jnp.stack([jnp.zeros_like(top), top, bottom])
    same = (labels[:, None, :] == kinds[None, :, None]).astype(F32)
    pad = ((0, 0), (0, 29), (0, LANES - count))
    bar_q = jnp.pad(same * -BARRED, pad).astype(BF)
    bar_k = jnp.pad(1.0 - same, pad).astype(BF)
    return bar_q, bar_k


def shifted(block, axis, distance):
    devices = range(lax.axis_size(axis))
    route = [((i - distance) % len(devices), i) for i in devices]
    return lax.ppermute(block, axis, route)


def slice_levels(grid_field, starts, length, axis):

    def per_level(level_plane, offset):
        return lax.dynamic_slice_in_dim(level_plane, offset, length, axis - 1)

    return jax.vmap(per_level)(grid_field, starts)


def make_windows(grid_field):
    lev_count, grid_rows, grid_cols, model_width = grid_field.shape
    shaped = grid_field.reshape(
        lev_count, grid_rows // WLAT, WLAT, grid_cols // WLON, WLON, model_width
    )
    shaped = shaped.transpose(1, 3, 0, 2, 4, 5)
    return shaped.reshape(-1, lev_count * WLAT * WLON, model_width)


def undo_windows(blocks, lev_count, grid_rows, grid_cols):
    model_width = blocks.shape[-1]
    shaped = blocks.reshape(
        grid_rows // WLAT, grid_cols // WLON, lev_count, WLAT, WLON, model_width
    )
    return shaped.transpose(2, 0, 3, 1, 4, 5).reshape(lev_count, grid_rows, grid_cols, model_width)


def window_labels(rolled_ids, grid_cols):
    lev_count, grid_rows = rolled_ids.shape
    shaped = rolled_ids.reshape(lev_count, grid_rows // WLAT, WLAT)
    full = jnp.broadcast_to(
        shaped[:, :, :, None, None], (lev_count, grid_rows // WLAT, WLAT, grid_cols // WLON, WLON)
    )
    return full.transpose(1, 3, 0, 2, 4).reshape(-1, lev_count * WLAT * WLON)


def join_ahead_cols(grid_field, ahead_block, lon_offsets):
    lon_cols = grid_field.shape[2]
    return slice_levels(
        jnp.concatenate([grid_field, ahead_block], axis=2), lon_offsets, lon_cols, 2
    )


def join_ahead_rows(grid_field, below_rows, lat_offsets):
    lat_rows = grid_field.shape[1]
    return slice_levels(jnp.concatenate([grid_field, below_rows], axis=1), lat_offsets, lat_rows, 1)


def join_behind_rows(grid_field, above_rows, lat_offsets):
    lat_rows = grid_field.shape[1]
    return slice_levels(
        jnp.concatenate([above_rows, grid_field], axis=1), WLAT - lat_offsets, lat_rows, 1
    )


def join_behind_cols(grid_field, left_block, lon_offsets):
    lon_cols = grid_field.shape[2]
    return slice_levels(
        jnp.concatenate([left_block, grid_field], axis=2), lon_cols - lon_offsets, lon_cols, 2
    )


def local(tokens, cotangent, w_qkv, w_proj, shifts, region_ids):
    lev_count, lat_rows, lon_cols, model_width = tokens.shape
    lat_offsets = shifts[:, 0]
    lon_offsets = shifts[:, 1]
    grid_rows = lat_rows * lax.axis_size("lat")
    first_row = lax.axis_index("lat") * lat_rows
    rows_wanted = (
        first_row + lat_offsets[:, None] + jnp.arange(lat_rows, dtype=jnp.int32)[None, :]
    ) % grid_rows
    table_rows = jnp.arange(grid_rows, dtype=jnp.int32)
    rolled_ids = jnp.sum(
        jnp.where(
            rows_wanted[:, :, None] == table_rows[None, None, :], region_ids[None, None, :], 0
        ),
        axis=2,
    )
    labels = window_labels(rolled_ids, lon_cols)
    bar_q, bar_k = bar_features(labels, region_ids[0], region_ids[-1])
    ahead_tokens, ahead_cot = shifted((tokens, cotangent), "lon", -1)
    cols_tokens = join_ahead_cols(tokens, ahead_tokens, lon_offsets)
    cols_cot = join_ahead_cols(cotangent, ahead_cot, lon_offsets)
    below_tokens, below_cot = shifted((cols_tokens[:, :WLAT], cols_cot[:, :WLAT]), "lat", -1)
    rolled = join_ahead_rows(cols_tokens, below_tokens, lat_offsets)
    rolled_cot = join_ahead_rows(cols_cot, below_cot, lat_offsets)
    updates, grads_back, qkv_total, proj_total = run_windows(
        make_windows(rolled), make_windows(rolled_cot), bar_q, bar_k, w_qkv.T, w_proj
    )
    update_field = undo_windows(updates, lev_count, lat_rows, lon_cols)
    grad_field = undo_windows(grads_back, lev_count, lat_rows, lon_cols)
    above_update, above_grad = shifted(
        (update_field[:, lat_rows - WLAT :], grad_field[:, lat_rows - WLAT :]), "lat", 1
    )
    update_field = join_behind_rows(update_field, above_update, lat_offsets)
    grad_field = join_behind_rows(grad_field, above_grad, lat_offsets)
    left_update, left_grad = shifted((update_field, grad_field), "lon", 1)
    update_field = join_behind_cols(update_field, left_update, lon_offsets)
    grad_field = join_behind_cols(grad_field, left_grad, lon_offsets)
    mixed = (tokens.astype(F32) + update_field.astype(F32)).astype(BF)
    grad_tokens = (cotangent.astype(F32) + grad_field.astype(F32)).astype(BF)
    qkv_sum, proj_sum = lax.psum((qkv_total, proj_total), ("lat", "lon"))
    total_tokens = lev_count * grid_rows * lon_cols * lax.axis_size("lon")
    grad_scale = 1.0 / math.sqrt(total_tokens)
    return (mixed, grad_tokens, qkv_sum.T * grad_scale, proj_sum * grad_scale)


def solution(mesh):
    return jax.shard_map(
        local,
        mesh=mesh,
        in_specs=(P(None, "lat", "lon", None), P(None, "lat", "lon", None), P(), P(), P(), P()),
        out_specs=(P(None, "lat", "lon", None), P(None, "lat", "lon", None), P(), P()),
        check_vma=False,
    )
```

```python
import functools
import math

import jax
import jax.numpy as jnp
from jax import lax
from jax.experimental import pallas as pl
from jax.experimental.pallas import tpu as pltpu
from jax.sharding import PartitionSpec as P

HEADS = 16
WLAT = 6
WLON = 12
LEV = 4
COUNT = LEV * WLAT * WLON
LANES = 384
ENTRIES = LEV * WLON // 2
PACKED = ENTRIES * WLAT
PHASES = ((0, 8), (8, 8))
NORM_EPS = 1e-05
BARRED = 2.0**100
BF = jnp.bfloat16
F32 = jnp.float32
I32 = jnp.int32

NN = (((1,), (0,)), ((), ()))
NT = (((1,), (1,)), ((), ()))
TN = (((0,), (0,)), ((), ()))
TT = (((0,), (1,)), ((), ()))

SMEM = pl.BlockSpec(memory_space=pltpu.SMEM)
VMEM = pl.BlockSpec(memory_space=pltpu.VMEM)
ANY = pl.BlockSpec(memory_space=pl.ANY)


def dot(a, b, dims):
    return lax.dot_general(a, b, dims, preferred_element_type=F32)


def split_bf16(value):
    high = value.astype(BF)
    low = (value - high.astype(F32)).astype(BF)
    return high, low


def call(kernel, ins, outs, scratch=(), scalars=0, flops=0, transcendentals=0, after=()):
    size = sum(math.prod(a.shape) * a.dtype.itemsize for a in (*ins, *outs))

    def ordered(*refs):
        kernel(*refs[: len(ins)], *refs[len(ins) + len(after) :])

    return pl.pallas_call(
        ordered,
        in_specs=[SMEM] * scalars + [VMEM] * (len(ins) - scalars) + [ANY] * len(after),
        out_specs=[VMEM] * len(outs),
        out_shape=list(outs),
        scratch_shapes=list(scratch),
        compiler_params=pltpu.CompilerParams(vmem_limit_bytes=40 * 1024 * 1024),
        cost_estimate=pl.CostEstimate(
            flops=flops, bytes_accessed=size, transcendentals=transcendentals
        ),
    )(*ins, *after)


def shape_of(dtype, *dims):
    return jax.ShapeDtypeStruct(dims, dtype)


def place(axis):
    dims = (COUNT, 1) if axis == 0 else (1, COUNT)
    token = lax.broadcasted_iota(I32, dims, axis)
    level = sum((token >= n * WLAT * WLON).astype(I32) for n in range(1, LEV))
    rest = token - level * (WLAT * WLON)
    row = sum((rest >= n * WLON).astype(I32) for n in range(1, WLAT))
    return level, row, rest - row * WLON


def by_level(level, values):
    result = jnp.full(level.shape, values[0], I32)
    for n in range(1, LEV):
        result = jnp.where(level == n, values[n], result)
    return result


def from_next_row(shifts, axis):
    level, row, _ = place(axis)
    return row < by_level(level, [shifts[n, 0] for n in range(LEV)])


def from_other_side(shifts, ahead, axis):
    level, row, column = place(axis)
    cut = [shifts[n, 1] for n in range(LEV)]
    counts = cut if ahead else [WLON - c for c in cut]
    starts = [0] * LEV if ahead else cut
    offsets = [0]
    for n in range(LEV - 1):
        offsets.append(offsets[-1] + counts[n])
    at = by_level(level, cut)
    taken = (column < at) if ahead else (column >= at)
    entry = by_level(level, [o - s for o, s in zip(offsets, starts)]) + column
    return taken, jnp.where(taken, entry * WLAT + row, -1)


def pack_matrix(shifts, ahead):
    _, slot = from_other_side(shifts, ahead, 1)
    rows = lax.broadcasted_iota(I32, (PACKED, COUNT), 0)
    return (rows == slot).astype(F32).astype(BF)


def unpack_matrix(shifts, ahead):
    taken, slot = from_other_side(shifts, ahead, 0)
    columns = lax.broadcasted_iota(I32, (COUNT, PACKED), 1)
    return taken, (columns == slot).astype(F32).astype(BF)


def select_other(taken, spread, packed, own):
    return jnp.where(taken, dot(spread, packed, NN), own.astype(F32))


def pack_kernel(ahead, windows, shifts, x_ref, cot_ref, halo_ref, last_ref, *rest):
    tile_refs, send_refs, dense = rest[: windows - 1], rest[windows - 1 : -1], rest[-1]
    lower = from_next_row(shifts, 0)
    chooser = pack_matrix(shifts, ahead)
    for field, ref in enumerate((x_ref, cot_ref)):
        for w in range(windows):
            for level in range(LEV):
                for row in range(WLAT):
                    start = (level * WLAT + row) * WLON
                    dense[w, start : start + WLON] = ref[level, w * WLAT + row].astype(F32)
        halo_ref[field] = dense[0].astype(BF)
        last_ref[field] = dense[windows - 1].astype(BF)
        for w in range(windows - 1):
            tile = jnp.where(lower, dense[w + 1], dense[w]).astype(BF)
            tile_refs[w][field] = tile
            send_refs[w][field] = dot(chooser, tile, NN).astype(BF)


def pack_last_kernel(ahead, shifts, last_ref, halo_ref, tile_ref, send_ref):
    lower = from_next_row(shifts, 0)
    chooser = pack_matrix(shifts, ahead)
    for field in range(2):
        tile = jnp.where(lower, halo_ref[field].astype(F32), last_ref[field].astype(F32))
        tile_ref[field] = tile.astype(BF)
        send_ref[field] = dot(chooser, tile.astype(BF), NN).astype(BF)


def standardize(values_full):
    center = values_full - jnp.mean(values_full, axis=1, keepdims=True)
    variance = jnp.mean(center * center, axis=1, keepdims=True)
    inv_scale = lax.rsqrt(variance + NORM_EPS)
    return center * inv_scale, inv_scale


def bars(shifts, ids, first_row, grid_rows, bar_q, bar_k):
    level, row, _ = place(1)
    wrapped = jnp.where(row < by_level(level, [shifts[n, 0] for n in range(LEV)]), WLAT, 0)
    at = first_row + row + wrapped
    at = jnp.where(at >= grid_rows, at - grid_rows, at)
    top = sum((ids[n] == ids[0]).astype(I32) for n in range(WLAT - 1))
    bottom = sum((ids[grid_rows - 1 - n] == ids[grid_rows - 1]).astype(I32) for n in range(WLAT - 1))
    kind = jnp.where(at < top, 1, jnp.where(at >= grid_rows - bottom, 2, 0))
    features = lax.broadcasted_iota(I32, (32, COUNT), 0)
    same = (features == kind).astype(F32)
    bar_q[...] = jnp.zeros_like(bar_q)
    bar_q[:, :COUNT] = (same * -BARRED).astype(BF)
    bar_k[...] = jnp.zeros_like(bar_k)
    bar_k[:, :COUNT] = jnp.where(features < 3, 1.0 - same, 0.0).astype(BF)


def attend(heads, size, bar_q, bar_k, q_s, k_s, v_s, g_s, ctx_ref, gp_ref):
    scale = 1.0 / math.sqrt(size)
    part = heads * size

    def head(h, carry):
        base = pl.multiple_of(h * size, size)
        rows = pl.ds(base, size)
        q_high, q_low = split_bf16(q_s[rows] * (scale * math.log2(math.e)))
        k_high, k_low = split_bf16(k_s[rows])
        value = v_s[rows]
        grad_ctx = g_s[rows]
        q_all = jnp.concatenate([q_high, q_low, q_high, bar_q[...]], axis=0)
        k_all = jnp.concatenate([k_high, k_high, k_low, bar_k[...]], axis=0)
        k_tok = k_all.T[:COUNT]
        v_tok = value.T[:COUNT]
        scores = dot(k_tok, q_all, NN)
        expo = jnp.exp2(scores - jnp.max(scores, axis=0, keepdims=True))
        weights = expo * (1.0 / jnp.sum(expo, axis=0, keepdims=True))
        rounded = weights.astype(BF)
        ctx_ref[rows] = dot(value[:, :COUNT], rounded, NN)[:, :COUNT].astype(BF)
        grad_w = dot(v_tok, grad_ctx, NN)
        grad_sc = weights * (grad_w - jnp.sum(weights * grad_w, axis=0, keepdims=True))
        high, low = split_bf16(grad_sc)
        k_pair = jnp.concatenate([k_high[:, :COUNT], k_low[:, :COUNT]], axis=0)
        q_pair = jnp.concatenate([q_high, q_low], axis=0)
        gq = dot(k_pair, high, NN)
        gq = gq[:size] + gq[size:] + dot(k_high[:, :COUNT], low, NN)
        gk = dot(q_pair, high, NT)
        gk = gk[:size] + gk[size:] + dot(q_high, low, NT)
        gv = dot(grad_ctx, rounded, NT)
        gp_ref[pl.ds(base, size)] = (gq[:, :COUNT] * scale).astype(BF)
        gp_ref[pl.ds(part + base, size)] = (gk * math.log(2.0)).astype(BF)
        gp_ref[pl.ds(2 * part + base, size)] = gv.astype(BF)
        return carry

    lax.fori_loop(0, heads, head, 0, unroll=2)


def project(first, part, width, w_ref, wp_ref, norm_s, cot_s, q_s, k_s, v_s, g_s):
    norm = norm_s[...]
    q_s[...] = dot(w_ref[first : first + part], norm, NT)
    k_s[...] = dot(w_ref[width + first : width + first + part], norm, NT)
    v_s[...] = dot(w_ref[2 * width + first : 2 * width + first + part], norm, NT).astype(BF)
    g_s[...] = dot(wp_ref[first : first + part], cot_s[...], NT).astype(BF)


def head_scratch(part, width):
    return [
        pltpu.VMEM((LANES, width), BF),
        pltpu.VMEM((LANES, width), BF),
        pltpu.VMEM((32, LANES), BF),
        pltpu.VMEM((32, LANES), BF),
        pltpu.VMEM((part, LANES), F32),
        pltpu.VMEM((part, LANES), F32),
        pltpu.VMEM((part, LANES), BF),
        pltpu.VMEM((part, LANES), BF),
    ]


def first_kernel(
    ahead, window, shifts, ids, spot, own_ref, got_ref, w_ref, wp_ref,
    tile_ref, norm_ref, ctx_ref, gp_ref,
    norm_s, cot_s, bar_q, bar_k, q_s, k_s, v_s, g_s,
):
    width = own_ref.shape[-1]
    size = width // HEADS
    start, heads = PHASES[0]
    taken, spread = unpack_matrix(shifts, ahead)
    x = select_other(taken, spread, got_ref[0], own_ref[0])
    cot = select_other(taken, spread, got_ref[1], own_ref[1]).astype(BF)
    tile_ref[0] = x.astype(BF)
    tile_ref[1] = cot
    normed = standardize(x)[0].astype(BF)
    norm_ref[...] = normed
    norm_s[:COUNT] = normed
    norm_s[COUNT:] = jnp.zeros((LANES - COUNT, width), BF)
    cot_s[:COUNT] = cot
    cot_s[COUNT:] = jnp.zeros((LANES - COUNT, width), BF)
    bars(shifts, ids, spot[0] + window * WLAT, ids.shape[0], bar_q, bar_k)
    project(start * size, heads * size, width, w_ref, wp_ref, norm_s, cot_s, q_s, k_s, v_s, g_s)
    attend(heads, size, bar_q, bar_k, q_s, k_s, v_s, g_s, ctx_ref, gp_ref)


def second_kernel(
    ahead, window, shifts, ids, spot, tile_ref, norm_ref, ctx_a, gp_a, w_ref, wp_ref,
    out_ref, send_ref, ctx_ref, gp_ref,
    norm_s, cot_s, bar_q, bar_k, q_s, k_s, v_s, g_s,
):
    width = norm_ref.shape[-1]
    size = width // HEADS
    start, heads = PHASES[1]
    norm_s[:COUNT] = norm_ref[...]
    norm_s[COUNT:] = jnp.zeros((LANES - COUNT, width), BF)
    cot_s[:COUNT] = tile_ref[1]
    cot_s[COUNT:] = jnp.zeros((LANES - COUNT, width), BF)
    bars(shifts, ids, spot[0] + window * WLAT, ids.shape[0], bar_q, bar_k)
    project(start * size, heads * size, width, w_ref, wp_ref, norm_s, cot_s, q_s, k_s, v_s, g_s)
    attend(heads, size, bar_q, bar_k, q_s, k_s, v_s, g_s, ctx_ref, gp_ref)
    context = jnp.concatenate([ctx_a[...], ctx_ref[...]], axis=0)
    update = dot(context, wp_ref[...], TN).astype(BF)
    parts = []
    for n in range(3):
        for ref in (gp_a, gp_ref):
            part = ref.shape[0] // 3
            parts.append(ref[n * part : (n + 1) * part])
    grad_normed = dot(jnp.concatenate(parts, axis=0), w_ref[...], TN)
    standard, inv_scale = standardize(tile_ref[0].astype(F32))
    grad = inv_scale * (
        grad_normed
        - jnp.mean(grad_normed, axis=1, keepdims=True)
        - standard * jnp.mean(grad_normed * standard, axis=1, keepdims=True)
    )
    grad = grad.astype(BF)
    chooser = pack_matrix(shifts, ahead)
    for field, value in enumerate((update, grad)):
        out_ref[field] = value
        send_ref[field] = dot(chooser, value, NN).astype(BF)


def weight_kernel(windows, kept, spot, *refs):
    norms, tiles, ctxs, gps = (refs[n * windows : (n + 1) * windows] for n in range(4))
    out_ref = refs[-1]
    part = ctxs[0].shape[0]
    width = norms[0].shape[-1]

    def total(left, right, dims):
        return functools.reduce(jnp.add, (dot(a, b, dims) for a, b in zip(left, right)))

    side = spot[1] if kept else 1 - spot[1]

    @pl.when(side == 0)
    def _():
        out_ref[...] = total([n[...] for n in norms], [g[: 2 * part] for g in gps], TT)

    @pl.when(side == 1)
    def _():
        out_ref[:, :part] = total([n[...] for n in norms], [g[2 * part :] for g in gps], TT)
        proj = total([c[...] for c in ctxs], [t[1] for t in tiles], NN)
        half = width // 2
        out_ref[:part, part:] = proj[:, :half]
        out_ref[part:, part:] = proj[:, half:]


def halve_kernel(bit, spot, mine_ref, got_ref, keep_ref, send_ref):
    rows = keep_ref.shape[0]
    for side, ref in ((spot[bit], keep_ref), (1 - spot[bit], send_ref)):
        at = pl.ds(pl.multiple_of(side * rows, rows), rows)
        ref[...] = mine_ref[at] + got_ref[at]


def spread_kernel(spot, mine_ref, got_ref, *out_refs):
    rows = out_refs[0].shape[0]
    for d, ref in enumerate(out_refs):
        at = pl.ds(pl.multiple_of((spot[4] ^ d) * rows, rows), rows)
        ref[...] = mine_ref[at] + got_ref[at]


def gather_sum_kernel(*refs):
    refs[-1][...] = functools.reduce(jnp.add, (r[...] for r in refs[:-1])).astype(BF)


def last_back_kernel(ahead, shifts, own_ref, got_ref, out_ref):
    taken, spread = unpack_matrix(shifts, ahead)
    for field in range(2):
        out_ref[field] = select_other(taken, spread, got_ref[field], own_ref[field]).astype(BF)


def finish_kernel(ahead, windows, shifts, x_ref, cot_ref, above_ref, final_ref, *refs):
    owns, gots = refs[: windows - 1], refs[windows - 1 : 2 * windows - 2]
    outs, dense = refs[2 * windows - 2 : -1], refs[-1]
    lower = from_next_row(shifts, 0)
    taken, spread = unpack_matrix(shifts, ahead)
    for field, ref in enumerate((x_ref, cot_ref)):
        before = above_ref[field].astype(F32)
        for w in range(windows):
            if w < windows - 1:
                here = select_other(taken, spread, gots[w][field], owns[w][field])
            else:
                here = final_ref[field].astype(F32)
            dense[...] = jnp.where(lower, before, here)
            before = here
            for level in range(LEV):
                for row in range(WLAT):
                    start = (level * WLAT + row) * WLON
                    at = w * WLAT + row
                    value = ref[level, at].astype(F32) + dense[start : start + WLON]
                    outs[field][level, at] = value.astype(BF)


def route(pairs_of, lat, lon):
    return [
        (a * lon + o, pairs_of(a, o)[0] * lon + pairs_of(a, o)[1])
        for a in range(lat)
        for o in range(lon)
    ]


def all_sum(weights, operands, spot, beside):
    lat, lon = lax.axis_size("lat"), lax.axis_size("lon")
    core, bit_one, bit_two, far = (spot[n] for n in range(1, 5))
    reach = lon // 2
    width = operands[0].shape[-1]

    def swap(value, pairs_of):
        return lax.ppermute(value, ("lat", "lon"), route(pairs_of, lat, lon))

    def across_core(a, o):
        return a ^ 1, o

    def step_one(a, o):
        return (a, o ^ 1) if a % 2 else (a ^ 2, o)

    def step_two(a, o):
        return (a ^ 2, o) if a % 2 else (a, o ^ 1)

    def along(d):
        return lambda a, o: (a, o ^ (2 * d))

    sent = weights(False, operands, ())
    got = swap(sent, across_core)
    held = weights(True, operands, (sent,))
    after = ()
    for bit, pairs_of in ((2, step_one), (3, step_two)):
        rows = held.shape[0] // 2
        held, sent = call(
            functools.partial(halve_kernel, bit),
            (spot, held, got),
            [shape_of(F32, rows, width)] * 2,
            scalars=1,
            after=after,
        )
        got = swap(sent, pairs_of)
        after = beside(held)
    rows = held.shape[0] // reach
    pieces = call(
        spread_kernel, (spot, held, got), [shape_of(F32, rows, width)] * reach, scalars=1, after=after
    )
    gots = [swap(pieces[d], along(d)) for d in range(1, reach)]
    after = beside(pieces[0])
    sums = call(gather_sum_kernel, (pieces[0], *gots), [shape_of(BF, rows, width)], after=after)[0]
    stack = jnp.stack([sums] + [swap(sums, along(d)) for d in range(1, reach)])
    beside(sums)
    bit = 1
    while bit < reach:
        order = [n ^ bit for n in range(reach)]
        turned = jnp.concatenate([stack[n : n + 1] for n in order], axis=0)
        stack = jnp.where((far & bit) != 0, turned, stack)
        bit *= 2
    held = stack.reshape(-1, width)
    for bit, pairs_of in ((bit_two, step_two), (bit_one, step_one), (core, across_core)):
        got = swap(held, pairs_of)
        held = jnp.where(
            bit == 1, jnp.concatenate([got, held], axis=0), jnp.concatenate([held, got], axis=0)
        )
    return held


def body(ahead, tokens, cotangent, w_t, w_proj, shifts, region_ids):
    levels, lat_rows, lon_cols, width = tokens.shape
    windows = lat_rows // WLAT
    size = width // HEADS
    my_lat, my_lon = lax.axis_index("lat"), lax.axis_index("lon")
    core, high, low = my_lat & 1, my_lat >> 1, my_lon & 1
    spot = jnp.stack(
        [
            my_lat * lat_rows,
            core,
            jnp.where(core == 1, low, high),
            jnp.where(core == 1, high, low),
            my_lon >> 1,
        ]
    ).astype(I32)

    def ring(value, axis, step):
        count = lax.axis_size(axis)
        return lax.ppermute(value, axis, [(i, (i + step) % count) for i in range(count)])

    out_step = -1 if ahead else 1
    pair = shape_of(BF, 2, COUNT, width)
    packed = shape_of(BF, 2, PACKED, width)
    made = call(
        functools.partial(pack_kernel, ahead, windows),
        (shifts, tokens, cotangent),
        [pair, pair] + [pair] * (windows - 1) + [packed] * (windows - 1),
        [pltpu.VMEM((windows, COUNT, width), F32)],
        1,
    )
    halo, last, tiles, sends = made[0], made[1], made[2 : windows + 1], made[windows + 1 :]
    below = ring(halo, "lat", -1)
    gots = [ring(s, "lon", out_step) for s in sends]
    def parts(phase):
        part = PHASES[phase][1] * size
        return part, [shape_of(BF, part, COUNT), shape_of(BF, 3 * part, COUNT)]

    part, shapes = parts(0)
    firsts = []
    tiles = list(tiles)
    for w in range(windows):
        if w == windows - 2:
            last_tile, last_send = call(
                functools.partial(pack_last_kernel, ahead),
                (shifts, last, below),
                [pair, packed],
                scalars=1,
                after=firsts[0][1:2],
            )
            gots.append(ring(last_send, "lon", out_step))
            tiles.append(last_tile)
            after_last = [last_send]
        firsts.append(
            call(
                functools.partial(first_kernel, ahead, w),
                (shifts, region_ids, spot, tiles[w], gots[w], w_t, w_proj),
                [pair, shape_of(BF, COUNT, width), *shapes],
                head_scratch(part, width),
                3,
                9_000_000_000,
                700_000,
                [f[1] for f in firsts[-1:]] + (after_last if w == windows - 2 else []),
            )
        )
    norms = [f[1] for f in firsts]
    whole_tiles = [f[0] for f in firsts]

    def weights(kept, operands, after):
        return call(
            functools.partial(weight_kernel, windows, kept),
            (spot, *operands),
            [shape_of(F32, width, width)],
            scalars=1,
            flops=1_000_000_000,
            after=after,
        )[0]

    part, shapes = parts(1)
    order = [windows - 1, *range(windows - 1)]
    seconds, backs = {}, {}

    def next_second(value):
        if len(seconds) == windows:
            return ()
        w = order[len(seconds)]
        earlier = [backs[order[n]] for n in range(len(seconds) - 1)][-1:]
        seconds[w] = call(
            functools.partial(second_kernel, ahead, w),
            (shifts, region_ids, spot, *firsts[w], w_t, w_proj),
            [pair, packed, *shapes],
            head_scratch(part, width),
            3,
            10_000_000_000,
            700_000,
            (value, *earlier),
        )
        backs[w] = ring(seconds[w][1], "lon", -out_step)
        return (seconds[w][2],)

    def nothing(value):
        return ()

    sum_a = all_sum(
        weights,
        (*norms, *whole_tiles, *[f[2] for f in firsts], *[f[3] for f in firsts]),
        spot,
        next_second,
    )
    while len(seconds) < windows:
        next_second(seconds[order[len(seconds) - 1]][2])
    seconds = [seconds[w] for w in range(windows)]
    backs = [backs[w] for w in range(windows)]
    final = call(
        functools.partial(last_back_kernel, ahead),
        (shifts, seconds[-1][0], backs[-1]),
        [pair],
        scalars=1,
    )[0]
    above = ring(final, "lat", 1)
    sum_b = all_sum(
        weights,
        (*norms, *whole_tiles, *[s[2] for s in seconds], *[s[3] for s in seconds]),
        spot,
        nothing,
    )
    mixed, grad_tokens = call(
        functools.partial(finish_kernel, ahead, windows),
        (
            shifts, tokens, cotangent, above, final,
            *[s[0] for s in seconds[:-1]], *backs[:-1],
        ),
        [shape_of(BF, *tokens.shape)] * 2,
        [pltpu.VMEM((COUNT, width), F32)],
        1,
    )

    total_tokens = levels * lat_rows * lax.axis_size("lat") * lon_cols * lax.axis_size("lon")
    grad_scale = 1.0 / math.sqrt(total_tokens)
    sums = (sum_a, sum_b)
    half = width // 2
    columns = (
        [s[:width, :half] for s in sums]
        + [s[:width, half:] for s in sums]
        + [s[width:, :half] for s in sums]
    )
    grad_qkv = jnp.concatenate(columns, axis=1).astype(F32) * grad_scale
    rows = [
        jnp.concatenate([s[width : width + half, half:], s[width + half :, half:]], axis=1)
        for s in sums
    ]
    grad_proj = jnp.concatenate(rows, axis=0).astype(F32) * grad_scale
    return mixed, grad_tokens, grad_qkv, grad_proj


def local(tokens, cotangent, w_qkv, w_proj, shifts, region_ids):
    return lax.cond(
        jnp.sum(shifts[:, 1]) <= ENTRIES,
        functools.partial(body, True),
        functools.partial(body, False),
        tokens, cotangent, w_qkv.T, w_proj, shifts, region_ids,
    )


def solution(mesh):
    return jax.shard_map(
        local,
        mesh=mesh,
        in_specs=(P(None, "lat", "lon", None), P(None, "lat", "lon", None), P(), P(), P(), P()),
        out_specs=(P(None, "lat", "lon", None), P(None, "lat", "lon", None), P(), P()),
        check_vma=False,
    )
```

```python
import functools
import math

import jax
import jax.numpy as jnp
from jax import lax
from jax.experimental import pallas as pl
from jax.experimental.pallas import tpu as pltpu
from jax.sharding import PartitionSpec as P

HEADS = 16
WLAT = 6
WLON = 12
LEV = 4
COUNT = LEV * WLAT * WLON
LANES = 384
ENTRIES = LEV * WLON // 2
PACKED = ENTRIES * WLAT
PHASES = ((0, 8), (8, 8))
NORM_EPS = 1e-05
BARRED = 2.0**100
BF = jnp.bfloat16
F32 = jnp.float32
I32 = jnp.int32

NN = (((1,), (0,)), ((), ()))
NT = (((1,), (1,)), ((), ()))
TN = (((0,), (0,)), ((), ()))
TT = (((0,), (1,)), ((), ()))

SMEM = pl.BlockSpec(memory_space=pltpu.SMEM)
VMEM = pl.BlockSpec(memory_space=pltpu.VMEM)
ANY = pl.BlockSpec(memory_space=pl.ANY)


def dot(a, b, dims):
    return lax.dot_general(a, b, dims, preferred_element_type=F32)


def split_bf16(value):
    high = value.astype(BF)
    low = (value - high.astype(F32)).astype(BF)
    return high, low


def call(kernel, ins, outs, scratch=(), scalars=0, flops=0, transcendentals=0, after=()):
    size = sum(math.prod(a.shape) * a.dtype.itemsize for a in (*ins, *outs))

    def ordered(*refs):
        kernel(*refs[: len(ins)], *refs[len(ins) + len(after) :])

    return pl.pallas_call(
        ordered,
        in_specs=[SMEM] * scalars + [VMEM] * (len(ins) - scalars) + [ANY] * len(after),
        out_specs=[VMEM] * len(outs),
        out_shape=list(outs),
        scratch_shapes=list(scratch),
        compiler_params=pltpu.CompilerParams(vmem_limit_bytes=24 * 1024 * 1024),
        cost_estimate=pl.CostEstimate(
            flops=flops, bytes_accessed=size, transcendentals=transcendentals
        ),
    )(*ins, *after)


def shape_of(dtype, *dims):
    return jax.ShapeDtypeStruct(dims, dtype)


def place(axis):
    dims = (COUNT, 1) if axis == 0 else (1, COUNT)
    token = lax.broadcasted_iota(I32, dims, axis)
    level = sum((token >= n * WLAT * WLON).astype(I32) for n in range(1, LEV))
    column, row = column_and_row(token - level * (WLAT * WLON))
    return level, row, column


def column_and_row(rest):
    column = sum((rest >= n * WLAT).astype(I32) for n in range(1, WLON))
    return column, rest - column * WLAT


def level_slots(windows, cut, axis):
    part = WLAT * WLON
    size = (windows + 1) * part
    dims = (size, 1) if axis == 0 else (1, size)
    token = lax.broadcasted_iota(I32, dims, axis)
    window = sum((token >= n * part).astype(I32) for n in range(1, windows + 1))
    column, row = column_and_row(token - window * part)
    at = window * WLAT + row + jnp.where(row < cut, WLAT, 0)
    slot = jnp.where(at < windows * WLAT, column * (windows * WLAT) + at, -1)
    first = window == windows
    return jnp.where(first, column * (windows * WLAT) + row, slot), first, row


def by_level(level, values):
    result = jnp.full(level.shape, values[0], I32)
    for n in range(1, LEV):
        result = jnp.where(level == n, values[n], result)
    return result


def from_next_row(shifts, axis):
    level, row, _ = place(axis)
    return row < by_level(level, [shifts[n, 0] for n in range(LEV)])


def from_other_side(shifts, ahead, axis):
    level, row, column = place(axis)
    cut = [shifts[n, 1] for n in range(LEV)]
    counts = cut if ahead else [WLON - c for c in cut]
    starts = [0] * LEV if ahead else cut
    offsets = [0]
    for n in range(LEV - 1):
        offsets.append(offsets[-1] + counts[n])
    at = by_level(level, cut)
    taken = (column < at) if ahead else (column >= at)
    entry = by_level(level, [o - s for o, s in zip(offsets, starts)]) + column
    return taken, jnp.where(taken, entry * WLAT + row, -1)


def pack_matrix(shifts, ahead):
    _, slot = from_other_side(shifts, ahead, 1)
    rows = lax.broadcasted_iota(I32, (PACKED, COUNT), 0)
    return (rows == slot).astype(F32).astype(BF)


def unpack_matrix(shifts, ahead):
    taken, slot = from_other_side(shifts, ahead, 0)
    columns = lax.broadcasted_iota(I32, (COUNT, PACKED), 1)
    return taken, (columns == slot).astype(F32).astype(BF)


def select_other(taken, spread, packed, own):
    return jnp.where(taken, dot(spread, packed, NN), own.astype(F32))


def pack_kernel(ahead, windows, shifts, x_ref, cot_ref, halo_ref, last_ref, *rest):
    tile_refs, send_refs = rest[: windows - 1], rest[windows - 1 :]
    part = WLAT * WLON
    grid = x_ref.shape[1]
    chooser = pack_matrix(shifts, ahead)
    parts = [[[None] * LEV for _ in range(windows + 1)] for _ in range(2)]
    for level in range(LEV):
        slot, _, _ = level_slots(windows, shifts[level, 0], 0)
        cells = lax.broadcasted_iota(I32, ((windows + 1) * part, grid), 1)
        mover = (cells == slot).astype(F32).astype(BF)
        for field, ref in enumerate((x_ref, cot_ref)):
            moved = dot(mover, ref[level], NN)
            for w in range(windows + 1):
                parts[field][w][level] = moved[w * part : (w + 1) * part]
    for field in range(2):
        whole = [jnp.concatenate(p, axis=0).astype(BF) for p in parts[field]]
        for w in range(windows - 1):
            tile_refs[w][field] = whole[w]
            send_refs[w][field] = dot(chooser, whole[w], NN).astype(BF)
        last_ref[field] = whole[windows - 1]
        halo_ref[field] = whole[windows]


def pack_last_kernel(ahead, shifts, last_ref, halo_ref, tile_ref, send_ref):
    lower = from_next_row(shifts, 0)
    chooser = pack_matrix(shifts, ahead)
    for field in range(2):
        tile = jnp.where(lower, halo_ref[field].astype(F32), last_ref[field].astype(F32))
        tile_ref[field] = tile.astype(BF)
        send_ref[field] = dot(chooser, tile.astype(BF), NN).astype(BF)


def standardize(values_full):
    center = values_full - jnp.mean(values_full, axis=1, keepdims=True)
    variance = jnp.mean(center * center, axis=1, keepdims=True)
    inv_scale = lax.rsqrt(variance + NORM_EPS)
    return center * inv_scale, inv_scale


def bars(shifts, ids, first_row, grid_rows, bar_q, bar_k):
    level, row, _ = place(1)
    wrapped = jnp.where(row < by_level(level, [shifts[n, 0] for n in range(LEV)]), WLAT, 0)
    at = first_row + row + wrapped
    at = jnp.where(at >= grid_rows, at - grid_rows, at)
    top = sum((ids[n] == ids[0]).astype(I32) for n in range(WLAT - 1))
    bottom = sum((ids[grid_rows - 1 - n] == ids[grid_rows - 1]).astype(I32) for n in range(WLAT - 1))
    kind = jnp.where(at < top, 1, jnp.where(at >= grid_rows - bottom, 2, 0))
    features = lax.broadcasted_iota(I32, (32, COUNT), 0)
    same = (features == kind).astype(F32)
    bar_q[...] = jnp.zeros_like(bar_q)
    bar_q[:, :COUNT] = (same * -BARRED).astype(BF)
    bar_k[...] = jnp.zeros_like(bar_k)
    bar_k[:, :COUNT] = jnp.where(features < 3, 1.0 - same, 0.0).astype(BF)


def attend(heads, size, bar_q, bar_k, q_s, k_s, v_s, g_s, ctx_ref, gp_ref):
    scale = 1.0 / math.sqrt(size)
    part = heads * size

    def head(h, carry):
        base = pl.multiple_of(h * size, size)
        rows = pl.ds(base, size)
        q_high, q_low = split_bf16(q_s[rows] * (scale * math.log2(math.e)))
        k_high, k_low = split_bf16(k_s[rows])
        value = v_s[rows]
        grad_ctx = g_s[rows]
        q_all = jnp.concatenate([q_high, q_low, q_high, bar_q[...]], axis=0)
        k_all = jnp.concatenate([k_high, k_high, k_low, bar_k[...]], axis=0)
        k_tok = k_all.T[:COUNT]
        others = jnp.concatenate([value, q_high, q_low, grad_ctx], axis=0).T
        lane = lax.broadcasted_iota(I32, others.shape, 1)
        empty = jnp.zeros_like(others)
        q_tok = jnp.where(lane < 3 * size, others, empty)
        g_tok = jnp.where(lane < 3 * size, empty, others)
        scores = dot(k_tok, q_all, NN)
        expo = jnp.exp2(scores - jnp.max(scores, axis=0, keepdims=True))
        weights = expo * (1.0 / jnp.sum(expo, axis=0, keepdims=True))
        rounded = weights.astype(BF)
        ctx_ref[rows] = dot(value[:, :COUNT], rounded, NN)[:, :COUNT].astype(BF)
        grad_w = dot(others[:COUNT, :size], grad_ctx, NN)
        grad_sc = weights * (grad_w - jnp.sum(weights * grad_w, axis=0, keepdims=True))
        high, low = split_bf16(grad_sc)
        k_pair = jnp.concatenate([k_high[:, :COUNT], k_low[:, :COUNT]], axis=0)
        gq = dot(
            jnp.concatenate([k_pair, k_pair], axis=1), jnp.concatenate([high, low], axis=0), NN
        )
        gq = gq[:size] + gq[size:]
        by_key = dot(
            jnp.concatenate([high, low, rounded], axis=1),
            jnp.concatenate([q_tok, q_tok, g_tok], axis=0),
            NN,
        ).T
        gk = by_key[size : 2 * size] + by_key[2 * size : 3 * size]
        gv = by_key[3 * size :]
        gp_ref[pl.ds(base, size)] = (gq[:, :COUNT] * scale).astype(BF)
        gp_ref[pl.ds(part + base, size)] = (gk * math.log(2.0)).astype(BF)
        gp_ref[pl.ds(2 * part + base, size)] = gv.astype(BF)
        return carry

    lax.fori_loop(0, heads, head, 0, unroll=2)


def project(first, part, width, w_ref, wp_ref, norm_s, cot_s, q_s, k_s, v_s, g_s):
    norm = norm_s[...]
    q_s[...] = dot(w_ref[first : first + part], norm, NT)
    k_s[...] = dot(w_ref[width + first : width + first + part], norm, NT)
    v_s[...] = dot(w_ref[2 * width + first : 2 * width + first + part], norm, NT).astype(BF)
    g_s[...] = dot(wp_ref[first : first + part], cot_s[...], NT).astype(BF)


def head_scratch(part, width):
    return [
        pltpu.VMEM((LANES, width), BF),
        pltpu.VMEM((LANES, width), BF),
        pltpu.VMEM((32, LANES), BF),
        pltpu.VMEM((32, LANES), BF),
        pltpu.VMEM((part, LANES), F32),
        pltpu.VMEM((part, LANES), F32),
        pltpu.VMEM((part, LANES), BF),
        pltpu.VMEM((part, LANES), BF),
    ]


def first_kernel(
    ahead, window, shifts, ids, spot, own_ref, got_ref, w_ref, wp_ref,
    tile_ref, norm_ref, ctx_ref, gp_ref,
    norm_s, cot_s, bar_q, bar_k, q_s, k_s, v_s, g_s,
):
    width = own_ref.shape[-1]
    size = width // HEADS
    start, heads = PHASES[0]
    taken, spread = unpack_matrix(shifts, ahead)
    x = select_other(taken, spread, got_ref[0], own_ref[0])
    cot = select_other(taken, spread, got_ref[1], own_ref[1]).astype(BF)
    tile_ref[0] = x.astype(BF)
    tile_ref[1] = cot
    normed = standardize(x)[0].astype(BF)
    norm_ref[...] = normed
    norm_s[:COUNT] = normed
    norm_s[COUNT:] = jnp.zeros((LANES - COUNT, width), BF)
    cot_s[:COUNT] = cot
    cot_s[COUNT:] = jnp.zeros((LANES - COUNT, width), BF)
    bars(shifts, ids, spot[0] + window * WLAT, ids.shape[0], bar_q, bar_k)
    project(start * size, heads * size, width, w_ref, wp_ref, norm_s, cot_s, q_s, k_s, v_s, g_s)
    attend(heads, size, bar_q, bar_k, q_s, k_s, v_s, g_s, ctx_ref, gp_ref)


def second_kernel(
    ahead, window, shifts, ids, spot, tile_ref, norm_ref, ctx_a, gp_a, w_ref, wp_ref,
    out_ref, send_ref, ctx_ref, gp_ref,
    norm_s, cot_s, bar_q, bar_k, q_s, k_s, v_s, g_s,
):
    width = norm_ref.shape[-1]
    size = width // HEADS
    start, heads = PHASES[1]
    norm_s[:COUNT] = norm_ref[...]
    norm_s[COUNT:] = jnp.zeros((LANES - COUNT, width), BF)
    cot_s[:COUNT] = tile_ref[1]
    cot_s[COUNT:] = jnp.zeros((LANES - COUNT, width), BF)
    bars(shifts, ids, spot[0] + window * WLAT, ids.shape[0], bar_q, bar_k)
    project(start * size, heads * size, width, w_ref, wp_ref, norm_s, cot_s, q_s, k_s, v_s, g_s)
    attend(heads, size, bar_q, bar_k, q_s, k_s, v_s, g_s, ctx_ref, gp_ref)
    context = jnp.concatenate([ctx_a[...], ctx_ref[...]], axis=0)
    update = dot(context, wp_ref[...], TN).astype(BF)
    parts = []
    for n in range(3):
        for ref in (gp_a, gp_ref):
            part = ref.shape[0] // 3
            parts.append(ref[n * part : (n + 1) * part])
    grad_normed = dot(jnp.concatenate(parts, axis=0), w_ref[...], TN)
    standard, inv_scale = standardize(tile_ref[0].astype(F32))
    grad = inv_scale * (
        grad_normed
        - jnp.mean(grad_normed, axis=1, keepdims=True)
        - standard * jnp.mean(grad_normed * standard, axis=1, keepdims=True)
    )
    grad = grad.astype(BF)
    chooser = pack_matrix(shifts, ahead)
    for field, value in enumerate((update, grad)):
        out_ref[field] = value
        send_ref[field] = dot(chooser, value, NN).astype(BF)


def weight_kernel(windows, kept, spot, *refs):
    norms, tiles, ctxs, gps = (refs[n * windows : (n + 1) * windows] for n in range(4))
    out_ref = refs[-1]
    part = ctxs[0].shape[0]
    width = norms[0].shape[-1]

    def total(left, right, dims):
        return functools.reduce(jnp.add, (dot(a, b, dims) for a, b in zip(left, right)))

    side = spot[1] if kept else 1 - spot[1]

    @pl.when(side == 0)
    def _():
        out_ref[...] = total([n[...] for n in norms], [g[: 2 * part] for g in gps], TT)

    @pl.when(side == 1)
    def _():
        out_ref[:, :part] = total([n[...] for n in norms], [g[2 * part :] for g in gps], TT)
        proj = total([c[...] for c in ctxs], [t[1] for t in tiles], NN)
        half = width // 2
        out_ref[:part, part:] = proj[:, :half]
        out_ref[part:, part:] = proj[:, half:]


def halve_kernel(bit, spot, mine_ref, got_ref, keep_ref, send_ref):
    rows = keep_ref.shape[0]
    for side, ref in ((spot[bit], keep_ref), (1 - spot[bit], send_ref)):
        at = pl.ds(pl.multiple_of(side * rows, rows), rows)
        ref[...] = mine_ref[at] + got_ref[at]


def spread_kernel(spot, mine_ref, got_ref, *out_refs):
    rows = out_refs[0].shape[0]
    for d, ref in enumerate(out_refs):
        at = pl.ds(pl.multiple_of((spot[4] ^ d) * rows, rows), rows)
        ref[...] = mine_ref[at] + got_ref[at]


def gather_sum_kernel(*refs):
    refs[-1][...] = functools.reduce(jnp.add, (r[...] for r in refs[:-1])).astype(BF)


def arrange_kernel(spot, *refs):
    *parts, out_ref = refs
    if len(out_ref.shape) == 4:
        out_ref[0] = parts.pop()[...]
        out_ref = out_ref.at[1]
    for d, ref in enumerate(parts):
        out_ref[spot[4] ^ d] = ref[...]


def join_kernel(bit, spot, mine_ref, got_ref, out_ref):
    count = mine_ref.shape[1]
    for side, ref in ((spot[bit], mine_ref), (1 - spot[bit], got_ref)):
        for phase in range(mine_ref.shape[0]):
            for n in range(count):
                out_ref[phase, side * count + n] = ref[phase, n]


def gradient_kernel(factor, spot, mine_ref, got_ref, qkv_ref, proj_ref):
    width = proj_ref.shape[0]
    half = width // 2
    first = spot[1] == 0

    def write(pair_ref, rest_ref):
        count, rows = mine_ref.shape[1:3]
        for phase in range(len(PHASES)):
            at = phase * half
            for n in range(count):
                here = slice(n * rows, (n + 1) * rows)
                pair = pair_ref[phase, n].astype(F32) * factor
                rest = rest_ref[phase, n].astype(F32) * factor
                qkv_ref[here, at : at + half] = pair[:, :half]
                qkv_ref[here, width + at : width + at + half] = pair[:, half:]
                qkv_ref[here, 2 * width + at : 2 * width + at + half] = rest[:, :half]
                lower = n * rows >= half
                there = at + n * rows - (half if lower else 0)
                columns = slice(half, width) if lower else slice(0, half)
                proj_ref[there : there + rows, columns] = rest[:, half:]

    @pl.when(first)
    def _():
        write(mine_ref, got_ref)

    @pl.when(jnp.logical_not(first))
    def _():
        write(got_ref, mine_ref)


def turn_kernel(w_ref, out_ref):
    out_ref[...] = w_ref[...].T


def last_back_kernel(ahead, shifts, own_ref, got_ref, out_ref):
    taken, spread = unpack_matrix(shifts, ahead)
    for field in range(2):
        out_ref[field] = select_other(taken, spread, got_ref[field], own_ref[field]).astype(BF)


def finish_kernel(ahead, windows, shifts, x_ref, cot_ref, above_ref, final_ref, *refs):
    owns, gots = refs[: windows - 1], refs[windows - 1 : 2 * windows - 2]
    outs = refs[2 * windows - 2 :]
    part = WLAT * WLON
    grid = x_ref.shape[1]
    taken, spread = unpack_matrix(shifts, ahead)
    movers = []
    for level in range(LEV):
        cut = shifts[level, 0]
        slot, first, row = level_slots(windows, cut, 1)
        slot = jnp.where(jnp.logical_and(first, row >= cut), -1, slot)
        cells = lax.broadcasted_iota(I32, (grid, (windows + 1) * part), 0)
        movers.append((cells == slot).astype(F32).astype(BF))
    for field, ref in enumerate((x_ref, cot_ref)):
        tiles = [
            select_other(taken, spread, gots[w][field], owns[w][field]) for w in range(windows - 1)
        ]
        tiles += [final_ref[field].astype(F32), above_ref[field].astype(F32)]
        for level in range(LEV):
            here = slice(level * part, (level + 1) * part)
            source = jnp.concatenate([t[here] for t in tiles], axis=0).astype(BF)
            value = ref[level].astype(F32) + dot(movers[level], source, NN)
            outs[field][level] = value.astype(BF)


def route(pairs_of, lat, lon):
    return [
        (a * lon + o, pairs_of(a, o)[0] * lon + pairs_of(a, o)[1])
        for a in range(lat)
        for o in range(lon)
    ]


def across_core(a, o):
    return a ^ 1, o


def step_one(a, o):
    return (a, o ^ 1) if a % 2 else (a ^ 2, o)


def step_two(a, o):
    return (a ^ 2, o) if a % 2 else (a, o ^ 1)


def all_sum(weights, operands, spot, beside, earlier):
    lat, lon = lax.axis_size("lat"), lax.axis_size("lon")
    reach = lon // 2
    width = operands[0].shape[-1]

    def swap(value, pairs_of):
        return lax.ppermute(value, ("lat", "lon"), route(pairs_of, lat, lon))

    def along(d):
        return lambda a, o: (a, o ^ (2 * d))

    sent = weights(False, operands, earlier)
    got = swap(sent, across_core)
    held = weights(True, operands, (sent,))
    after = ()
    for bit, pairs_of in ((2, step_one), (3, step_two)):
        rows = held.shape[0] // 2
        held, sent = call(
            functools.partial(halve_kernel, bit),
            (spot, held, got),
            [shape_of(F32, rows, width)] * 2,
            scalars=1,
            after=after,
        )
        got = swap(sent, pairs_of)
        after = beside(held)
    rows = held.shape[0] // reach
    pieces = call(
        spread_kernel, (spot, held, got), [shape_of(F32, rows, width)] * reach, scalars=1, after=after
    )
    gots = [swap(pieces[d], along(d)) for d in range(1, reach)]
    after = beside(pieces[0])
    sums = call(gather_sum_kernel, (pieces[0], *gots), [shape_of(BF, rows, width)], after=after)[0]
    gots = [swap(sums, along(d)) for d in range(1, reach)]
    after = beside(sums)
    other = tuple(e for e in earlier if e.ndim == 3 and e.shape[1:] == sums.shape)
    return call(
        arrange_kernel,
        (spot, sums, *gots, *other),
        [shape_of(BF, *[2] * len(other), reach, rows, width)],
        scalars=1,
        after=after,
    )[0]


def all_gather(parts, spot, factor):
    lat, lon = lax.axis_size("lat"), lax.axis_size("lon")
    _, reach, rows, width = parts.shape
    held = parts.reshape(len(PHASES), 1, reach * rows, width)

    def swap(value, pairs_of):
        return lax.ppermute(value, ("lat", "lon"), route(pairs_of, lat, lon))

    for bit, pairs_of in ((3, step_two), (2, step_one)):
        phases, count, rows, width = held.shape
        held = call(
            functools.partial(join_kernel, bit),
            (spot, held, swap(held, pairs_of)),
            [shape_of(BF, phases, 2 * count, rows, width)],
            scalars=1,
        )[0]
    return call(
        functools.partial(gradient_kernel, factor),
        (spot, held, swap(held, across_core)),
        [shape_of(F32, width, 3 * width), shape_of(F32, width, width)],
        scalars=1,
    )


def body(ahead, tokens, cotangent, w_qkv, w_proj, shifts, region_ids):
    levels, lat_rows, lon_cols, width = tokens.shape

    def by_column(grid_field):
        return grid_field.transpose(0, 2, 1, 3).reshape(levels, lon_cols * lat_rows, width)

    tokens, cotangent = by_column(tokens), by_column(cotangent)
    windows = lat_rows // WLAT
    size = width // HEADS
    my_lat, my_lon = lax.axis_index("lat"), lax.axis_index("lon")
    core, high, low = my_lat & 1, my_lat >> 1, my_lon & 1
    spot = jnp.stack(
        [
            my_lat * lat_rows,
            core,
            jnp.where(core == 1, low, high),
            jnp.where(core == 1, high, low),
            my_lon >> 1,
        ]
    ).astype(I32)

    def ring(value, axis, step):
        count = lax.axis_size(axis)
        return lax.ppermute(value, axis, [(i, (i + step) % count) for i in range(count)])

    out_step = -1 if ahead else 1
    pair = shape_of(BF, 2, COUNT, width)
    packed = shape_of(BF, 2, PACKED, width)
    made = call(
        functools.partial(pack_kernel, ahead, windows),
        (shifts, tokens, cotangent),
        [pair, pair] + [pair] * (windows - 1) + [packed] * (windows - 1),
        scalars=1,
    )
    halo, last, tiles, sends = made[0], made[1], made[2 : windows + 1], made[windows + 1 :]
    w_t = call(turn_kernel, (w_qkv,), [shape_of(BF, 3 * width, width)], after=(halo,))[0]
    below = ring(halo, "lat", -1)
    gots = [ring(s, "lon", out_step) for s in sends]
    def parts(phase):
        part = PHASES[phase][1] * size
        return part, [shape_of(BF, part, COUNT), shape_of(BF, 3 * part, COUNT)]

    part, shapes = parts(0)
    firsts = []
    tiles = list(tiles)
    for w in range(windows):
        if w == windows - 2:
            last_tile, last_send = call(
                functools.partial(pack_last_kernel, ahead),
                (shifts, last, below),
                [pair, packed],
                scalars=1,
                after=firsts[0][1:2],
            )
            gots.append(ring(last_send, "lon", out_step))
            tiles.append(last_tile)
            after_last = [last_send]
        firsts.append(
            call(
                functools.partial(first_kernel, ahead, w),
                (shifts, region_ids, spot, tiles[w], gots[w], w_t, w_proj),
                [pair, shape_of(BF, COUNT, width), *shapes],
                head_scratch(part, width),
                3,
                9_000_000_000,
                700_000,
                [f[1] for f in firsts[-1:]] + (after_last if w == windows - 2 else []),
            )
        )
    norms = [f[1] for f in firsts]
    whole_tiles = [f[0] for f in firsts]

    def weights(kept, operands, after):
        return call(
            functools.partial(weight_kernel, windows, kept),
            (spot, *operands),
            [shape_of(F32, width, width)],
            scalars=1,
            flops=1_000_000_000,
            after=after,
        )[0]

    part, shapes = parts(1)
    order = [windows - 1, *range(windows - 1)]
    seconds, backs = {}, {}

    ends = []

    def next_second(value):
        done = [seconds[w] for w in order[: len(seconds)]]
        w = order[len(done)]
        waits = [value]
        if len(done) == 2:
            final = call(
                functools.partial(last_back_kernel, ahead),
                (shifts, done[0][0], backs[order[0]]),
                [pair],
                scalars=1,
                after=(done[1][2],),
            )[0]
            ends.extend([final, ring(final, "lat", 1)])
            waits.append(final)
        if len(done) == 3:
            waits += [backs[order[1]], ends[1]]
        seconds[w] = call(
            functools.partial(second_kernel, ahead, w),
            (shifts, region_ids, spot, *firsts[w], w_t, w_proj),
            [pair, packed, *shapes],
            head_scratch(part, width),
            3,
            10_000_000_000,
            700_000,
            waits,
        )
        backs[w] = ring(seconds[w][1], "lon", -out_step)
        return (seconds[w][2],)

    sum_a = all_sum(
        weights,
        (*norms, *whole_tiles, *[f[2] for f in firsts], *[f[3] for f in firsts]),
        spot,
        next_second,
        (),
    )
    while len(seconds) < windows:
        next_second(seconds[order[len(seconds) - 1]][2])
    results = []

    def finish(value):
        if not results:
            results.extend(
                call(
                    functools.partial(finish_kernel, ahead, windows),
                    (
                        shifts, tokens, cotangent, ends[1], ends[0],
                        *[seconds[w][0] for w in range(windows - 1)],
                        *[backs[w] for w in range(windows - 1)],
                    ),
                    [shape_of(BF, *tokens.shape)] * 2,
                    scalars=1,
                    after=(value,),
                )
            )
            return ()
        return results[:1]

    sum_b = all_sum(
        weights,
        (
            *norms,
            *whole_tiles,
            *[seconds[w][2] for w in range(windows)],
            *[seconds[w][3] for w in range(windows)],
        ),
        spot,
        finish,
        (sum_a, backs[order[2]]),
    )
    mixed, grad_tokens = (
        r.reshape(levels, lon_cols, lat_rows, width).transpose(0, 2, 1, 3) for r in results
    )

    total_tokens = levels * lat_rows * lax.axis_size("lat") * lon_cols * lax.axis_size("lon")
    gradients = all_gather(sum_b, spot, 1.0 / math.sqrt(total_tokens))
    return (mixed, grad_tokens, *gradients)


def local(tokens, cotangent, w_qkv, w_proj, shifts, region_ids):
    return lax.cond(
        jnp.sum(shifts[:, 1]) <= ENTRIES,
        functools.partial(body, True),
        functools.partial(body, False),
        tokens, cotangent, w_qkv, w_proj, shifts, region_ids,
    )


def solution(mesh):
    return jax.shard_map(
        local,
        mesh=mesh,
        in_specs=(P(None, "lat", "lon", None), P(None, "lat", "lon", None), P(), P(), P(), P()),
        out_specs=(P(None, "lat", "lon", None), P(None, "lat", "lon", None), P(), P()),
        check_vma=False,
    )
```

```python
import functools
import math

import jax
import jax.numpy as jnp
from jax import lax
from jax.experimental import pallas as pl
from jax.experimental.pallas import tpu as pltpu
from jax.sharding import PartitionSpec as P

HEADS = 16
WLAT = 6
WLON = 12
LEV = 4
COUNT = LEV * WLAT * WLON
LANES = 384
ENTRIES = LEV * WLON // 2
PACKED = ENTRIES * WLAT
PHASES = ((0, 8), (8, 8))
NORM_EPS = 1e-05
BARRED = 2.0**100
BF = jnp.bfloat16
F32 = jnp.float32
I32 = jnp.int32

NN = (((1,), (0,)), ((), ()))
NT = (((1,), (1,)), ((), ()))
TN = (((0,), (0,)), ((), ()))
TT = (((0,), (1,)), ((), ()))

SMEM = pl.BlockSpec(memory_space=pltpu.SMEM)
VMEM = pl.BlockSpec(memory_space=pltpu.VMEM)
ANY = pl.BlockSpec(memory_space=pl.ANY)


def dot(a, b, dims):
    return lax.dot_general(a, b, dims, preferred_element_type=F32)


def split_bf16(value):
    high = value.astype(BF)
    low = (value - high.astype(F32)).astype(BF)
    return high, low


def call(kernel, ins, outs, scratch=(), scalars=0, flops=0, transcendentals=0, after=()):
    size = sum(math.prod(a.shape) * a.dtype.itemsize for a in (*ins, *outs))

    def ordered(*refs):
        kernel(*refs[: len(ins)], *refs[len(ins) + len(after) :])

    return pl.pallas_call(
        ordered,
        in_specs=[SMEM] * scalars + [VMEM] * (len(ins) - scalars) + [ANY] * len(after),
        out_specs=[VMEM] * len(outs),
        out_shape=list(outs),
        scratch_shapes=list(scratch),
        compiler_params=pltpu.CompilerParams(vmem_limit_bytes=24 * 1024 * 1024),
        cost_estimate=pl.CostEstimate(
            flops=flops, bytes_accessed=size, transcendentals=transcendentals
        ),
    )(*ins, *after)


def shape_of(dtype, *dims):
    return jax.ShapeDtypeStruct(dims, dtype)


def place(axis):
    dims = (COUNT, 1) if axis == 0 else (1, COUNT)
    token = lax.broadcasted_iota(I32, dims, axis)
    level = sum((token >= n * WLAT * WLON).astype(I32) for n in range(1, LEV))
    column, row = column_and_row(token - level * (WLAT * WLON))
    return level, row, column


def column_and_row(rest):
    column = sum((rest >= n * WLAT).astype(I32) for n in range(1, WLON))
    return column, rest - column * WLAT


def level_slots(windows, cut, axis):
    part = WLAT * WLON
    size = (windows + 1) * part
    dims = (size, 1) if axis == 0 else (1, size)
    token = lax.broadcasted_iota(I32, dims, axis)
    window = sum((token >= n * part).astype(I32) for n in range(1, windows + 1))
    column, row = column_and_row(token - window * part)
    at = window * WLAT + row + jnp.where(row < cut, WLAT, 0)
    slot = jnp.where(at < windows * WLAT, column * (windows * WLAT) + at, -1)
    first = window == windows
    return jnp.where(first, column * (windows * WLAT) + row, slot), first, row


def by_level(level, values):
    result = jnp.full(level.shape, values[0], I32)
    for n in range(1, LEV):
        result = jnp.where(level == n, values[n], result)
    return result


def from_next_row(shifts, axis):
    level, row, _ = place(axis)
    return row < by_level(level, [shifts[n, 0] for n in range(LEV)])


def from_other_side(shifts, ahead, axis):
    level, row, column = place(axis)
    cut = [shifts[n, 1] for n in range(LEV)]
    counts = cut if ahead else [WLON - c for c in cut]
    starts = [0] * LEV if ahead else cut
    offsets = [0]
    for n in range(LEV - 1):
        offsets.append(offsets[-1] + counts[n])
    at = by_level(level, cut)
    taken = (column < at) if ahead else (column >= at)
    entry = by_level(level, [o - s for o, s in zip(offsets, starts)]) + column
    return taken, jnp.where(taken, entry * WLAT + row, -1)


def pack_matrix(shifts, ahead):
    _, slot = from_other_side(shifts, ahead, 1)
    rows = lax.broadcasted_iota(I32, (PACKED, COUNT), 0)
    return (rows == slot).astype(F32).astype(BF)


def unpack_matrix(shifts, ahead):
    taken, slot = from_other_side(shifts, ahead, 0)
    columns = lax.broadcasted_iota(I32, (COUNT, PACKED), 1)
    return taken, (columns == slot).astype(F32).astype(BF)


def select_other(taken, spread, packed, own):
    return jnp.where(taken, dot(spread, packed, NN), own.astype(F32))


def pack_kernel(ahead, windows, first, shifts, x_ref, cot_ref, *refs):
    part = WLAT * WLON
    grid = x_ref.shape[1]
    if first:
        count = 2
        tile_refs, send_refs, (halo_ref,) = refs[:1], refs[1:2], refs[2:]
    else:
        count = windows - 1
        tile_refs, send_refs = refs[:count], refs[count:]
    chooser = pack_matrix(shifts, ahead)
    parts = [[[None] * LEV for _ in range(count)] for _ in range(2)]
    for level in range(LEV):
        slot, _, _ = level_slots(windows, shifts[level, 0], 0)
        if first:
            slot = jnp.concatenate([slot[:part], slot[windows * part :]], axis=0)
        else:
            slot = slot[part : windows * part]
        cells = lax.broadcasted_iota(I32, (count * part, grid), 1)
        mover = (cells == slot).astype(F32).astype(BF)
        for field, ref in enumerate((x_ref, cot_ref)):
            moved = dot(mover, ref[level], NN)
            for w in range(count):
                parts[field][w][level] = moved[w * part : (w + 1) * part]
    for field in range(2):
        whole = [jnp.concatenate(p, axis=0).astype(BF) for p in parts[field]]
        for tile_ref, tile in zip(tile_refs, whole):
            tile_ref[field] = tile
        for send_ref, tile in zip(send_refs, whole):
            send_ref[field] = dot(chooser, tile, NN).astype(BF)
        if first:
            halo_ref[field] = whole[1]


def pack_last_kernel(ahead, shifts, last_ref, halo_ref, tile_ref, send_ref):
    lower = from_next_row(shifts, 0)
    chooser = pack_matrix(shifts, ahead)
    for field in range(2):
        tile = jnp.where(lower, halo_ref[field].astype(F32), last_ref[field].astype(F32))
        tile_ref[field] = tile.astype(BF)
        send_ref[field] = dot(chooser, tile.astype(BF), NN).astype(BF)


def standardize(values_full):
    center = values_full - jnp.mean(values_full, axis=1, keepdims=True)
    variance = jnp.mean(center * center, axis=1, keepdims=True)
    inv_scale = lax.rsqrt(variance + NORM_EPS)
    return center * inv_scale, inv_scale


def bars(shifts, ids, first_row, grid_rows, bar_q, bar_k):
    level, row, _ = place(1)
    wrapped = jnp.where(row < by_level(level, [shifts[n, 0] for n in range(LEV)]), WLAT, 0)
    at = first_row + row + wrapped
    at = jnp.where(at >= grid_rows, at - grid_rows, at)
    top = sum((ids[n] == ids[0]).astype(I32) for n in range(WLAT - 1))
    bottom = sum((ids[grid_rows - 1 - n] == ids[grid_rows - 1]).astype(I32) for n in range(WLAT - 1))
    kind = jnp.where(at < top, 1, jnp.where(at >= grid_rows - bottom, 2, 0))
    features = lax.broadcasted_iota(I32, (32, COUNT), 0)
    same = (features == kind).astype(F32)
    bar_q[...] = jnp.zeros_like(bar_q)
    bar_q[:, :COUNT] = (same * -BARRED).astype(BF)
    bar_k[...] = jnp.zeros_like(bar_k)
    bar_k[:, :COUNT] = jnp.where(features < 3, 1.0 - same, 0.0).astype(BF)


def attend(heads, size, bar_q, bar_k, q_s, k_s, v_s, g_s, buffers, ctx_ref, gp_ref):
    scale = 1.0 / math.sqrt(size)
    part = heads * size

    def rows_of(h):
        return pl.ds(pl.multiple_of(h * size, size), size)

    def products(h, buffer):
        score_b, grad_b = buffer[:2]
        rows = rows_of(h)
        q_high, q_low = split_bf16(q_s[rows])
        k_high, k_low = split_bf16(k_s[rows])
        q_all = jnp.concatenate([q_high, q_low, q_high, bar_q[...]], axis=0)
        k_all = jnp.concatenate([k_high, k_high, k_low, bar_k[...]], axis=0)
        score_b[...] = dot(k_all.T[:COUNT], q_all, NN)
        grad_b[...] = dot(v_s[rows].T[:COUNT], g_s[rows], NN)

    def soften(buffer):
        score_b, grad_b, weight_b, high_b, low_b = buffer
        for start in range(0, LANES, 128):
            lanes = slice(start, start + 128)
            scores = score_b[:, lanes]
            expo = jnp.exp2(scores - jnp.max(scores, axis=0, keepdims=True))
            weights = expo * (1.0 / jnp.sum(expo, axis=0, keepdims=True))
            weight_b[:, lanes] = weights.astype(BF)
            grad_w = grad_b[:, lanes]
            grad_sc = weights * (grad_w - jnp.sum(weights * grad_w, axis=0, keepdims=True))
            high_b[:, lanes], low_b[:, lanes] = split_bf16(grad_sc)

    def results(h, buffer):
        weight_b, high_b, low_b = buffer[2:]
        rows = rows_of(h)
        q_high, q_low = split_bf16(q_s[rows])
        k_high, k_low = split_bf16(k_s[rows])
        rounded, high, low = weight_b[...], high_b[...], low_b[...]
        ctx_ref[rows] = dot(v_s[rows][:, :COUNT], rounded, NN)[:, :COUNT].astype(BF)
        k_pair = jnp.concatenate([k_high[:, :COUNT], k_low[:, :COUNT]], axis=0)
        q_pair = jnp.concatenate([q_high, q_low], axis=0)
        gq = dot(k_pair, high, NN)
        gq = gq[:size] + gq[size:] + dot(k_high[:, :COUNT], low, NN)
        gk = dot(q_pair, high, NT)
        gk = gk[:size] + gk[size:] + dot(q_high, low, NT)
        gv = dot(g_s[rows], rounded, NT)
        base = pl.multiple_of(h * size, size)
        gp_ref[pl.ds(base, size)] = (gq[:, :COUNT] * scale).astype(BF)
        gp_ref[pl.ds(part + base, size)] = (gk * math.log(2.0)).astype(BF)
        gp_ref[pl.ds(2 * part + base, size)] = gv.astype(BF)

    even, odd = buffers[:5], buffers[5:]
    products(0, even)

    def pair(p, carry):
        h = 2 * p
        products(h + 1, odd)
        soften(even)
        results(jnp.maximum(h - 1, 0), odd)
        products(jnp.minimum(h + 2, heads - 1), even)
        soften(odd)
        results(h, even)
        return carry

    lax.fori_loop(0, heads // 2, pair, 0)
    results(heads - 1, odd)


def project(first, part, width, w_ref, wp_ref, norm_s, cot_s, q_s, k_s, v_s, g_s):
    norm = norm_s[...]
    factor = math.log2(math.e) / math.sqrt(width // HEADS)
    q_s[...] = dot(w_ref[first : first + part], norm, NT) * factor
    k_s[...] = dot(w_ref[width + first : width + first + part], norm, NT)
    v_s[...] = dot(w_ref[2 * width + first : 2 * width + first + part], norm, NT).astype(BF)
    g_s[...] = dot(wp_ref[first : first + part], cot_s[...], NT).astype(BF)


def head_scratch(part, width):
    return [
        pltpu.VMEM((LANES, width), BF),
        pltpu.VMEM((LANES, width), BF),
        pltpu.VMEM((32, LANES), BF),
        pltpu.VMEM((32, LANES), BF),
        pltpu.VMEM((part, LANES), F32),
        pltpu.VMEM((part, LANES), F32),
        pltpu.VMEM((part, LANES), BF),
        pltpu.VMEM((part, LANES), BF),
    ] + [
        pltpu.VMEM((COUNT, LANES), kind) for _ in range(2) for kind in (F32, F32, BF, BF, BF)
    ]


def first_kernel(
    ahead, window, shifts, ids, spot, own_ref, got_ref, w_ref, wp_ref,
    tile_ref, norm_ref, ctx_ref, gp_ref,
    norm_s, cot_s, bar_q, bar_k, q_s, k_s, v_s, g_s, *buffers,
):
    width = own_ref.shape[-1]
    size = width // HEADS
    start, heads = PHASES[0]
    taken, spread = unpack_matrix(shifts, ahead)
    x = select_other(taken, spread, got_ref[0], own_ref[0])
    cot = select_other(taken, spread, got_ref[1], own_ref[1]).astype(BF)
    tile_ref[0] = x.astype(BF)
    tile_ref[1] = cot
    normed = standardize(x)[0].astype(BF)
    norm_ref[...] = normed
    norm_s[:COUNT] = normed
    norm_s[COUNT:] = jnp.zeros((LANES - COUNT, width), BF)
    cot_s[:COUNT] = cot
    cot_s[COUNT:] = jnp.zeros((LANES - COUNT, width), BF)
    bars(shifts, ids, spot[0] + window * WLAT, ids.shape[0], bar_q, bar_k)
    project(start * size, heads * size, width, w_ref, wp_ref, norm_s, cot_s, q_s, k_s, v_s, g_s)
    attend(heads, size, bar_q, bar_k, q_s, k_s, v_s, g_s, buffers, ctx_ref, gp_ref)


def second_kernel(
    ahead, window, shifts, ids, spot, tile_ref, norm_ref, ctx_a, gp_a, w_ref, wp_ref,
    out_ref, send_ref, ctx_ref, gp_ref,
    norm_s, cot_s, bar_q, bar_k, q_s, k_s, v_s, g_s, *buffers,
):
    width = norm_ref.shape[-1]
    size = width // HEADS
    start, heads = PHASES[1]
    norm_s[:COUNT] = norm_ref[...]
    norm_s[COUNT:] = jnp.zeros((LANES - COUNT, width), BF)
    cot_s[:COUNT] = tile_ref[1]
    cot_s[COUNT:] = jnp.zeros((LANES - COUNT, width), BF)
    bars(shifts, ids, spot[0] + window * WLAT, ids.shape[0], bar_q, bar_k)
    project(start * size, heads * size, width, w_ref, wp_ref, norm_s, cot_s, q_s, k_s, v_s, g_s)
    attend(heads, size, bar_q, bar_k, q_s, k_s, v_s, g_s, buffers, ctx_ref, gp_ref)
    context = jnp.concatenate([ctx_a[...], ctx_ref[...]], axis=0)
    update = dot(context, wp_ref[...], TN).astype(BF)
    parts = []
    for n in range(3):
        for ref in (gp_a, gp_ref):
            part = ref.shape[0] // 3
            parts.append(ref[n * part : (n + 1) * part])
    grad_normed = dot(jnp.concatenate(parts, axis=0), w_ref[...], TN)
    standard, inv_scale = standardize(tile_ref[0].astype(F32))
    grad = inv_scale * (
        grad_normed
        - jnp.mean(grad_normed, axis=1, keepdims=True)
        - standard * jnp.mean(grad_normed * standard, axis=1, keepdims=True)
    )
    grad = grad.astype(BF)
    chooser = pack_matrix(shifts, ahead)
    for field, value in enumerate((update, grad)):
        out_ref[field] = value
        send_ref[field] = dot(chooser, value, NN).astype(BF)


def weight_kernel(windows, kept, spot, *refs):
    norms, tiles, ctxs, gps = (refs[n * windows : (n + 1) * windows] for n in range(4))
    out_ref = refs[-1]
    part = ctxs[0].shape[0]
    width = norms[0].shape[-1]

    def total(left, right, dims):
        return functools.reduce(jnp.add, (dot(a, b, dims) for a, b in zip(left, right)))

    side = spot[1] if kept else 1 - spot[1]

    @pl.when(side == 0)
    def _():
        out_ref[...] = total([n[...] for n in norms], [g[: 2 * part] for g in gps], TT)

    @pl.when(side == 1)
    def _():
        out_ref[:, :part] = total([n[...] for n in norms], [g[2 * part :] for g in gps], TT)
        proj = total([c[...] for c in ctxs], [t[1] for t in tiles], NN)
        half = width // 2
        out_ref[:part, part:] = proj[:, :half]
        out_ref[part:, part:] = proj[:, half:]


def halve_kernel(bit, spot, mine_ref, got_ref, keep_ref, send_ref):
    rows = keep_ref.shape[0]
    for side, ref in ((spot[bit], keep_ref), (1 - spot[bit], send_ref)):
        at = pl.ds(pl.multiple_of(side * rows, rows), rows)
        ref[...] = mine_ref[at] + got_ref[at]


def spread_kernel(spot, mine_ref, got_ref, *out_refs):
    rows = out_refs[0].shape[0]
    for d, ref in enumerate(out_refs):
        at = pl.ds(pl.multiple_of((spot[4] ^ d) * rows, rows), rows)
        ref[...] = mine_ref[at] + got_ref[at]


def gather_sum_kernel(*refs):
    refs[-1][...] = functools.reduce(jnp.add, (r[...] for r in refs[:-1])).astype(BF)


def arrange_kernel(spot, *refs):
    *parts, out_ref = refs
    if len(out_ref.shape) == 4:
        out_ref[0] = parts.pop()[...]
        out_ref = out_ref.at[1]
    for d, ref in enumerate(parts):
        out_ref[spot[4] ^ d] = ref[...]


def join_kernel(bit, spot, mine_ref, got_ref, out_ref):
    count = mine_ref.shape[1]
    for side, ref in ((spot[bit], mine_ref), (1 - spot[bit], got_ref)):
        for phase in range(mine_ref.shape[0]):
            for n in range(count):
                out_ref[phase, side * count + n] = ref[phase, n]


def gradient_kernel(factor, spot, mine_ref, got_ref, qkv_ref, proj_ref):
    width = proj_ref.shape[0]
    half = width // 2
    first = spot[1] == 0

    def write(pair_ref, rest_ref):
        count, rows = mine_ref.shape[1:3]
        for phase in range(len(PHASES)):
            at = phase * half
            for n in range(count):
                here = slice(n * rows, (n + 1) * rows)
                pair = pair_ref[phase, n].astype(F32) * factor
                rest = rest_ref[phase, n].astype(F32) * factor
                qkv_ref[here, at : at + half] = pair[:, :half]
                qkv_ref[here, width + at : width + at + half] = pair[:, half:]
                qkv_ref[here, 2 * width + at : 2 * width + at + half] = rest[:, :half]
                lower = n * rows >= half
                there = at + n * rows - (half if lower else 0)
                columns = slice(half, width) if lower else slice(0, half)
                proj_ref[there : there + rows, columns] = rest[:, half:]

    @pl.when(first)
    def _():
        write(mine_ref, got_ref)

    @pl.when(jnp.logical_not(first))
    def _():
        write(got_ref, mine_ref)


def turn_kernel(w_ref, out_ref):
    out_ref[...] = w_ref[...].T


def last_back_kernel(ahead, shifts, own_ref, got_ref, out_ref):
    taken, spread = unpack_matrix(shifts, ahead)
    for field in range(2):
        out_ref[field] = select_other(taken, spread, got_ref[field], own_ref[field]).astype(BF)


def finish_kernel(ahead, windows, shifts, x_ref, cot_ref, above_ref, final_ref, *refs):
    owns, gots = refs[: windows - 1], refs[windows - 1 : 2 * windows - 2]
    outs = refs[2 * windows - 2 :]
    part = WLAT * WLON
    grid = x_ref.shape[1]
    taken, spread = unpack_matrix(shifts, ahead)
    movers = []
    for level in range(LEV):
        cut = shifts[level, 0]
        slot, first, row = level_slots(windows, cut, 1)
        slot = jnp.where(jnp.logical_and(first, row >= cut), -1, slot)
        cells = lax.broadcasted_iota(I32, (grid, (windows + 1) * part), 0)
        movers.append((cells == slot).astype(F32).astype(BF))
    for field, ref in enumerate((x_ref, cot_ref)):
        tiles = [
            select_other(taken, spread, gots[w][field], owns[w][field]) for w in range(windows - 1)
        ]
        tiles += [final_ref[field].astype(F32), above_ref[field].astype(F32)]
        for level in range(LEV):
            here = slice(level * part, (level + 1) * part)
            source = jnp.concatenate([t[here] for t in tiles], axis=0).astype(BF)
            value = ref[level].astype(F32) + dot(movers[level], source, NN)
            outs[field][level] = value.astype(BF)


def route(pairs_of, lat, lon):
    return [
        (a * lon + o, pairs_of(a, o)[0] * lon + pairs_of(a, o)[1])
        for a in range(lat)
        for o in range(lon)
    ]


def across_core(a, o):
    return a ^ 1, o


def step_one(a, o):
    return (a, o ^ 1) if a % 2 else (a ^ 2, o)


def step_two(a, o):
    return (a ^ 2, o) if a % 2 else (a, o ^ 1)


def all_sum(weights, operands, spot, beside, earlier):
    lat, lon = lax.axis_size("lat"), lax.axis_size("lon")
    reach = lon // 2
    width = operands[0].shape[-1]

    def swap(value, pairs_of):
        return lax.ppermute(value, ("lat", "lon"), route(pairs_of, lat, lon))

    def along(d):
        return lambda a, o: (a, o ^ (2 * d))

    sent = weights(False, operands, earlier)
    got = swap(sent, across_core)
    held = weights(True, operands, (sent,))
    after = ()
    for bit, pairs_of in ((2, step_one), (3, step_two)):
        rows = held.shape[0] // 2
        held, sent = call(
            functools.partial(halve_kernel, bit),
            (spot, held, got),
            [shape_of(F32, rows, width)] * 2,
            scalars=1,
            after=after,
        )
        got = swap(sent, pairs_of)
        after = beside(held)
    rows = held.shape[0] // reach
    pieces = call(
        spread_kernel, (spot, held, got), [shape_of(F32, rows, width)] * reach, scalars=1, after=after
    )
    gots = [swap(pieces[d], along(d)) for d in range(1, reach)]
    after = beside(pieces[0])
    sums = call(gather_sum_kernel, (pieces[0], *gots), [shape_of(BF, rows, width)], after=after)[0]
    gots = [swap(sums, along(d)) for d in range(1, reach)]
    after = beside(sums)
    other = tuple(e for e in earlier if e.ndim == 3 and e.shape[1:] == sums.shape)
    return call(
        arrange_kernel,
        (spot, sums, *gots, *other),
        [shape_of(BF, *[2] * len(other), reach, rows, width)],
        scalars=1,
        after=after,
    )[0]


def all_gather(parts, spot, factor):
    lat, lon = lax.axis_size("lat"), lax.axis_size("lon")
    _, reach, rows, width = parts.shape
    held = parts.reshape(len(PHASES), 1, reach * rows, width)

    def swap(value, pairs_of):
        return lax.ppermute(value, ("lat", "lon"), route(pairs_of, lat, lon))

    for bit, pairs_of in ((3, step_two), (2, step_one)):
        phases, count, rows, width = held.shape
        held = call(
            functools.partial(join_kernel, bit),
            (spot, held, swap(held, pairs_of)),
            [shape_of(BF, phases, 2 * count, rows, width)],
            scalars=1,
        )[0]
    return call(
        functools.partial(gradient_kernel, factor),
        (spot, held, swap(held, across_core)),
        [shape_of(F32, width, 3 * width), shape_of(F32, width, width)],
        scalars=1,
    )


def body(ahead, tokens, cotangent, w_qkv, w_proj, shifts, region_ids):
    levels, lat_rows, lon_cols, width = tokens.shape

    def by_column(grid_field):
        return grid_field.transpose(0, 2, 1, 3).reshape(levels, lon_cols * lat_rows, width)

    tokens, cotangent = by_column(tokens), by_column(cotangent)
    windows = lat_rows // WLAT
    size = width // HEADS
    my_lat, my_lon = lax.axis_index("lat"), lax.axis_index("lon")
    core, high, low = my_lat & 1, my_lat >> 1, my_lon & 1
    spot = jnp.stack(
        [
            my_lat * lat_rows,
            core,
            jnp.where(core == 1, low, high),
            jnp.where(core == 1, high, low),
            my_lon >> 1,
        ]
    ).astype(I32)

    def ring(value, axis, step):
        count = lax.axis_size(axis)
        return lax.ppermute(value, axis, [(i, (i + step) % count) for i in range(count)])

    out_step = -1 if ahead else 1
    pair = shape_of(BF, 2, COUNT, width)
    packed = shape_of(BF, 2, PACKED, width)
    arrays = (shifts, tokens, cotangent)
    tile, send, halo = call(
        functools.partial(pack_kernel, ahead, windows, True), arrays, [pair, packed, pair], scalars=1
    )
    made = call(
        functools.partial(pack_kernel, ahead, windows, False),
        arrays,
        [pair] * (windows - 1) + [packed] * (windows - 2),
        scalars=1,
        after=(tile,),
    )
    tiles, last = [tile, *made[: windows - 2]], made[windows - 2]
    sends = [send, *made[windows - 1 :]]
    w_t = call(turn_kernel, (w_qkv,), [shape_of(BF, 3 * width, width)], after=(last,))[0]
    below = ring(halo, "lat", -1)
    gots = [ring(s, "lon", out_step) for s in sends]
    def parts(phase):
        part = PHASES[phase][1] * size
        return part, [shape_of(BF, part, COUNT), shape_of(BF, 3 * part, COUNT)]

    part, shapes = parts(0)
    firsts = []
    tiles = list(tiles)
    for w in range(windows):
        if w == windows - 2:
            last_tile, last_send = call(
                functools.partial(pack_last_kernel, ahead),
                (shifts, last, below),
                [pair, packed],
                scalars=1,
                after=firsts[0][1:2],
            )
            gots.append(ring(last_send, "lon", out_step))
            tiles.append(last_tile)
            after_last = [last_send]
        firsts.append(
            call(
                functools.partial(first_kernel, ahead, w),
                (shifts, region_ids, spot, tiles[w], gots[w], w_t, w_proj),
                [pair, shape_of(BF, COUNT, width), *shapes],
                head_scratch(part, width),
                3,
                9_000_000_000,
                700_000,
                [f[1] for f in firsts[-1:]] + (after_last if w == windows - 2 else []),
            )
        )
    norms = [f[1] for f in firsts]
    whole_tiles = [f[0] for f in firsts]

    def weights(kept, operands, after):
        return call(
            functools.partial(weight_kernel, windows, kept),
            (spot, *operands),
            [shape_of(F32, width, width)],
            scalars=1,
            flops=1_000_000_000,
            after=after,
        )[0]

    part, shapes = parts(1)
    order = [windows - 1, *range(windows - 1)]
    seconds, backs = {}, {}

    ends = []

    def next_second(value):
        done = [seconds[w] for w in order[: len(seconds)]]
        w = order[len(done)]
        waits = [value]
        if len(done) == 2:
            final = call(
                functools.partial(last_back_kernel, ahead),
                (shifts, done[0][0], backs[order[0]]),
                [pair],
                scalars=1,
                after=(done[1][2],),
            )[0]
            ends.extend([final, ring(final, "lat", 1)])
            waits.append(final)
        if len(done) == 3:
            waits += [backs[order[1]], ends[1]]
        seconds[w] = call(
            functools.partial(second_kernel, ahead, w),
            (shifts, region_ids, spot, *firsts[w], w_t, w_proj),
            [pair, packed, *shapes],
            head_scratch(part, width),
            3,
            10_000_000_000,
            700_000,
            waits,
        )
        backs[w] = ring(seconds[w][1], "lon", -out_step)
        return (seconds[w][2],)

    sum_a = all_sum(
        weights,
        (*norms, *whole_tiles, *[f[2] for f in firsts], *[f[3] for f in firsts]),
        spot,
        next_second,
        (),
    )
    while len(seconds) < windows:
        next_second(seconds[order[len(seconds) - 1]][2])
    results = []

    def finish(value):
        if not results:
            results.extend(
                call(
                    functools.partial(finish_kernel, ahead, windows),
                    (
                        shifts, tokens, cotangent, ends[1], ends[0],
                        *[seconds[w][0] for w in range(windows - 1)],
                        *[backs[w] for w in range(windows - 1)],
                    ),
                    [shape_of(BF, *tokens.shape)] * 2,
                    scalars=1,
                    after=(value,),
                )
            )
            return ()
        return results[:1]

    sum_b = all_sum(
        weights,
        (
            *norms,
            *whole_tiles,
            *[seconds[w][2] for w in range(windows)],
            *[seconds[w][3] for w in range(windows)],
        ),
        spot,
        finish,
        (sum_a, backs[order[2]]),
    )
    mixed, grad_tokens = (
        r.reshape(levels, lon_cols, lat_rows, width).transpose(0, 2, 1, 3) for r in results
    )

    total_tokens = levels * lat_rows * lax.axis_size("lat") * lon_cols * lax.axis_size("lon")
    gradients = all_gather(sum_b, spot, 1.0 / math.sqrt(total_tokens))
    return (mixed, grad_tokens, *gradients)


def local(tokens, cotangent, w_qkv, w_proj, shifts, region_ids):
    return lax.cond(
        jnp.sum(shifts[:, 1]) <= ENTRIES,
        functools.partial(body, True),
        functools.partial(body, False),
        tokens, cotangent, w_qkv, w_proj, shifts, region_ids,
    )


def solution(mesh):
    return jax.shard_map(
        local,
        mesh=mesh,
        in_specs=(P(None, "lat", "lon", None), P(None, "lat", "lon", None), P(), P(), P(), P()),
        out_specs=(P(None, "lat", "lon", None), P(None, "lat", "lon", None), P(), P()),
        check_vma=False,
    )
```

```python
import functools
import math

import jax
import jax.numpy as jnp
from jax import lax
from jax.experimental import pallas as pl
from jax.experimental.pallas import tpu as pltpu
from jax.sharding import PartitionSpec as P

HEADS = 16
WLAT = 6
WLON = 12
LEV = 4
COUNT = LEV * WLAT * WLON
LANES = 384
ENTRIES = LEV * WLON // 2
PACKED = ENTRIES * WLAT
PHASES = ((0, 12), (12, 4))
NORM_EPS = 1e-05
BARRED = 2.0**100
BF = jnp.bfloat16
F32 = jnp.float32
I32 = jnp.int32

NN = (((1,), (0,)), ((), ()))
NT = (((1,), (1,)), ((), ()))
TN = (((0,), (0,)), ((), ()))
TT = (((0,), (1,)), ((), ()))

SMEM = pl.BlockSpec(memory_space=pltpu.SMEM)
VMEM = pl.BlockSpec(memory_space=pltpu.VMEM)
ANY = pl.BlockSpec(memory_space=pl.ANY)


def dot(a, b, dims):
    return lax.dot_general(a, b, dims, preferred_element_type=F32)


def split_bf16(value):
    high = value.astype(BF)
    low = (value - high.astype(F32)).astype(BF)
    return high, low


def call(kernel, ins, outs, scratch=(), scalars=0, flops=0, transcendentals=0, after=()):
    size = sum(math.prod(a.shape) * a.dtype.itemsize for a in (*ins, *outs))

    def ordered(*refs):
        kernel(*refs[: len(ins)], *refs[len(ins) + len(after) :])

    return pl.pallas_call(
        ordered,
        in_specs=[SMEM] * scalars + [VMEM] * (len(ins) - scalars) + [ANY] * len(after),
        out_specs=[VMEM] * len(outs),
        out_shape=list(outs),
        scratch_shapes=list(scratch),
        compiler_params=pltpu.CompilerParams(vmem_limit_bytes=24 * 1024 * 1024),
        cost_estimate=pl.CostEstimate(
            flops=flops, bytes_accessed=size, transcendentals=transcendentals
        ),
    )(*ins, *after)


def shape_of(dtype, *dims):
    return jax.ShapeDtypeStruct(dims, dtype)


def place(axis):
    dims = (COUNT, 1) if axis == 0 else (1, COUNT)
    token = lax.broadcasted_iota(I32, dims, axis)
    level = sum((token >= n * WLAT * WLON).astype(I32) for n in range(1, LEV))
    column, row = column_and_row(token - level * (WLAT * WLON))
    return level, row, column


def column_and_row(rest):
    column = sum((rest >= n * WLAT).astype(I32) for n in range(1, WLON))
    return column, rest - column * WLAT


def level_slots(windows, cut, axis):
    part = WLAT * WLON
    size = (windows + 1) * part
    dims = (size, 1) if axis == 0 else (1, size)
    token = lax.broadcasted_iota(I32, dims, axis)
    window = sum((token >= n * part).astype(I32) for n in range(1, windows + 1))
    column, row = column_and_row(token - window * part)
    at = window * WLAT + row + jnp.where(row < cut, WLAT, 0)
    slot = jnp.where(at < windows * WLAT, column * (windows * WLAT) + at, -1)
    first = window == windows
    return jnp.where(first, column * (windows * WLAT) + row, slot), first, row


def by_level(level, values):
    result = jnp.full(level.shape, values[0], I32)
    for n in range(1, LEV):
        result = jnp.where(level == n, values[n], result)
    return result


def from_next_row(shifts, axis):
    level, row, _ = place(axis)
    return row < by_level(level, [shifts[n, 0] for n in range(LEV)])


def from_other_side(shifts, ahead, axis):
    level, row, column = place(axis)
    cut = [shifts[n, 1] for n in range(LEV)]
    counts = cut if ahead else [WLON - c for c in cut]
    starts = [0] * LEV if ahead else cut
    offsets = [0]
    for n in range(LEV - 1):
        offsets.append(offsets[-1] + counts[n])
    at = by_level(level, cut)
    taken = (column < at) if ahead else (column >= at)
    entry = by_level(level, [o - s for o, s in zip(offsets, starts)]) + column
    return taken, jnp.where(taken, entry * WLAT + row, -1)


def pack_matrix(shifts, ahead):
    _, slot = from_other_side(shifts, ahead, 1)
    rows = lax.broadcasted_iota(I32, (PACKED, COUNT), 0)
    return (rows == slot).astype(F32).astype(BF)


def unpack_matrix(shifts, ahead):
    taken, slot = from_other_side(shifts, ahead, 0)
    columns = lax.broadcasted_iota(I32, (COUNT, PACKED), 1)
    return taken, (columns == slot).astype(F32).astype(BF)


def select_other(taken, spread, packed, own):
    return jnp.where(taken, dot(spread, packed, NN), own.astype(F32))


def pack_kernel(ahead, windows, first, shifts, x_ref, cot_ref, *refs):
    part = WLAT * WLON
    grid = x_ref.shape[1]
    if first:
        count = 2
        tile_refs, send_refs, (halo_ref,) = refs[:1], refs[1:2], refs[2:]
    else:
        count = windows - 1
        tile_refs, send_refs = refs[:count], refs[count:]
    chooser = pack_matrix(shifts, ahead)
    parts = [[[None] * LEV for _ in range(count)] for _ in range(2)]
    for level in range(LEV):
        slot, _, _ = level_slots(windows, shifts[level, 0], 0)
        if first:
            slot = jnp.concatenate([slot[:part], slot[windows * part :]], axis=0)
        else:
            slot = slot[part : windows * part]
        cells = lax.broadcasted_iota(I32, (count * part, grid), 1)
        mover = (cells == slot).astype(F32).astype(BF)
        for field, ref in enumerate((x_ref, cot_ref)):
            moved = dot(mover, ref[level], NN)
            for w in range(count):
                parts[field][w][level] = moved[w * part : (w + 1) * part]
    for field in range(2):
        whole = [jnp.concatenate(p, axis=0).astype(BF) for p in parts[field]]
        for tile_ref, tile in zip(tile_refs, whole):
            tile_ref[field] = tile
        for send_ref, tile in zip(send_refs, whole):
            send_ref[field] = dot(chooser, tile, NN).astype(BF)
        if first:
            halo_ref[field] = whole[1]


def pack_last_kernel(ahead, shifts, last_ref, halo_ref, tile_ref, send_ref):
    lower = from_next_row(shifts, 0)
    chooser = pack_matrix(shifts, ahead)
    for field in range(2):
        tile = jnp.where(lower, halo_ref[field].astype(F32), last_ref[field].astype(F32))
        tile_ref[field] = tile.astype(BF)
        send_ref[field] = dot(chooser, tile.astype(BF), NN).astype(BF)


def standardize(values_full):
    center = values_full - jnp.mean(values_full, axis=1, keepdims=True)
    variance = jnp.mean(center * center, axis=1, keepdims=True)
    inv_scale = lax.rsqrt(variance + NORM_EPS)
    return center * inv_scale, inv_scale


def bars(shifts, ids, first_row, grid_rows, bar_q, bar_k):
    level, row, _ = place(1)
    wrapped = jnp.where(row < by_level(level, [shifts[n, 0] for n in range(LEV)]), WLAT, 0)
    at = first_row + row + wrapped
    at = jnp.where(at >= grid_rows, at - grid_rows, at)
    top = sum((ids[n] == ids[0]).astype(I32) for n in range(WLAT - 1))
    bottom = sum((ids[grid_rows - 1 - n] == ids[grid_rows - 1]).astype(I32) for n in range(WLAT - 1))
    kind = jnp.where(at < top, 1, jnp.where(at >= grid_rows - bottom, 2, 0))
    features = lax.broadcasted_iota(I32, (32, COUNT), 0)
    same = (features == kind).astype(F32)
    bar_q[...] = jnp.zeros_like(bar_q)
    bar_q[:, :COUNT] = (same * -BARRED).astype(BF)
    bar_k[...] = jnp.zeros_like(bar_k)
    bar_k[:, :COUNT] = jnp.where(features < 3, 1.0 - same, 0.0).astype(BF)


def attend(heads, size, bar_q, bar_k, q_s, k_s, v_s, g_s, buffers, ctx_ref, gp_ref):
    scale = 1.0 / math.sqrt(size)
    part = heads * size

    def rows_of(h):
        return pl.ds(pl.multiple_of(h * size, size), size)

    def products(h, buffer):
        score_b, grad_b = buffer[:2]
        rows = rows_of(h)
        q_high, q_low = split_bf16(q_s[rows])
        k_high, k_low = split_bf16(k_s[rows])
        q_all = jnp.concatenate([q_high, q_low, q_high, bar_q[...]], axis=0)
        k_all = jnp.concatenate([k_high, k_high, k_low, bar_k[...]], axis=0)
        score_b[...] = dot(k_all.T[:COUNT], q_all, NN)
        grad_b[...] = dot(v_s[rows].T[:COUNT], g_s[rows], NN)

    def soften(buffer):
        score_b, grad_b, weight_b, high_b, low_b = buffer
        for start in range(0, LANES, 128):
            lanes = slice(start, start + 128)
            scores = score_b[:, lanes]
            expo = jnp.exp2(scores - jnp.max(scores, axis=0, keepdims=True))
            weights = expo * (1.0 / jnp.sum(expo, axis=0, keepdims=True))
            weight_b[:, lanes] = weights.astype(BF)
            grad_w = grad_b[:, lanes]
            grad_sc = weights * (grad_w - jnp.sum(weights * grad_w, axis=0, keepdims=True))
            high_b[:, lanes], low_b[:, lanes] = split_bf16(grad_sc)

    def results(h, buffer):
        weight_b, high_b, low_b = buffer[2:]
        rows = rows_of(h)
        q_high, q_low = split_bf16(q_s[rows])
        k_high, k_low = split_bf16(k_s[rows])
        rounded, high, low = weight_b[...], high_b[...], low_b[...]
        ctx_ref[rows] = dot(v_s[rows][:, :COUNT], rounded, NN)[:, :COUNT].astype(BF)
        k_pair = jnp.concatenate([k_high[:, :COUNT], k_low[:, :COUNT]], axis=0)
        q_pair = jnp.concatenate([q_high, q_low], axis=0)
        gq = dot(k_pair, high, NN)
        gq = gq[:size] + gq[size:] + dot(k_high[:, :COUNT], low, NN)
        gk = dot(q_pair, high, NT)
        gk = gk[:size] + gk[size:] + dot(q_high, low, NT)
        gv = dot(g_s[rows], rounded, NT)
        base = pl.multiple_of(h * size, size)
        gp_ref[pl.ds(base, size)] = (gq[:, :COUNT] * scale).astype(BF)
        gp_ref[pl.ds(part + base, size)] = (gk * math.log(2.0)).astype(BF)
        gp_ref[pl.ds(2 * part + base, size)] = gv.astype(BF)

    even, odd = buffers[:5], buffers[5:]
    products(0, even)

    def pair(p, carry):
        h = 2 * p
        products(h + 1, odd)
        soften(even)
        results(jnp.maximum(h - 1, 0), odd)
        products(jnp.minimum(h + 2, heads - 1), even)
        soften(odd)
        results(h, even)
        return carry

    lax.fori_loop(0, heads // 2, pair, 0)
    results(heads - 1, odd)


def project(part, width, w_ref, wp_rows, norm_s, cot_s, q_s, k_s, v_s, g_s):
    norm = norm_s[...]
    factor = math.log2(math.e) / math.sqrt(width // HEADS)
    q_s[...] = dot(w_ref[:part], norm, NT) * factor
    k_s[...] = dot(w_ref[part : 2 * part], norm, NT)
    v_s[...] = dot(w_ref[2 * part :], norm, NT).astype(BF)
    g_s[...] = dot(wp_rows, cot_s[...], NT).astype(BF)


def head_scratch(part, width):
    return [
        pltpu.VMEM((LANES, width), BF),
        pltpu.VMEM((LANES, width), BF),
        pltpu.VMEM((32, LANES), BF),
        pltpu.VMEM((32, LANES), BF),
        pltpu.VMEM((part, LANES), F32),
        pltpu.VMEM((part, LANES), F32),
        pltpu.VMEM((part, LANES), BF),
        pltpu.VMEM((part, LANES), BF),
    ] + [
        pltpu.VMEM((COUNT, LANES), kind) for _ in range(2) for kind in (F32, F32, BF, BF, BF)
    ]


def first_kernel(
    ahead, window, shifts, ids, spot, own_ref, got_ref, w_ref, wp_ref,
    tile_ref, norm_ref, ctx_ref, gp_ref,
    norm_s, cot_s, bar_q, bar_k, q_s, k_s, v_s, g_s, *buffers,
):
    width = own_ref.shape[-1]
    size = width // HEADS
    start, heads = PHASES[0]
    taken, spread = unpack_matrix(shifts, ahead)
    x = select_other(taken, spread, got_ref[0], own_ref[0])
    cot = select_other(taken, spread, got_ref[1], own_ref[1]).astype(BF)
    tile_ref[0] = x.astype(BF)
    tile_ref[1] = cot
    normed = standardize(x)[0].astype(BF)
    norm_ref[...] = normed
    norm_s[:COUNT] = normed
    norm_s[COUNT:] = jnp.zeros((LANES - COUNT, width), BF)
    cot_s[:COUNT] = cot
    cot_s[COUNT:] = jnp.zeros((LANES - COUNT, width), BF)
    bars(shifts, ids, spot[0] + window * WLAT, ids.shape[0], bar_q, bar_k)
    part = heads * size
    wp_rows = wp_ref[start * size : start * size + part]
    project(part, width, w_ref, wp_rows, norm_s, cot_s, q_s, k_s, v_s, g_s)
    attend(heads, size, bar_q, bar_k, q_s, k_s, v_s, g_s, buffers, ctx_ref, gp_ref)


def second_kernel(
    ahead, window, shifts, ids, spot, tile_ref, norm_ref, ctx_a, gp_a, w_a, w_ref, wp_ref,
    out_ref, send_ref, ctx_ref, gp_ref,
    norm_s, cot_s, bar_q, bar_k, q_s, k_s, v_s, g_s, *buffers,
):
    width = norm_ref.shape[-1]
    size = width // HEADS
    start, heads = PHASES[1]
    norm_s[:COUNT] = norm_ref[...]
    norm_s[COUNT:] = jnp.zeros((LANES - COUNT, width), BF)
    cot_s[:COUNT] = tile_ref[1]
    cot_s[COUNT:] = jnp.zeros((LANES - COUNT, width), BF)
    bars(shifts, ids, spot[0] + window * WLAT, ids.shape[0], bar_q, bar_k)
    part = heads * size
    wp_rows = wp_ref[start * size : start * size + part]
    project(part, width, w_ref, wp_rows, norm_s, cot_s, q_s, k_s, v_s, g_s)
    attend(heads, size, bar_q, bar_k, q_s, k_s, v_s, g_s, buffers, ctx_ref, gp_ref)
    context = jnp.concatenate([ctx_a[...], ctx_ref[...]], axis=0)
    update = dot(context, wp_ref[...], TN).astype(BF)
    grad_normed = dot(gp_a[...], w_a[...], TN) + dot(gp_ref[...], w_ref[...], TN)
    standard, inv_scale = standardize(tile_ref[0].astype(F32))
    grad = inv_scale * (
        grad_normed
        - jnp.mean(grad_normed, axis=1, keepdims=True)
        - standard * jnp.mean(grad_normed * standard, axis=1, keepdims=True)
    )
    grad = grad.astype(BF)
    chooser = pack_matrix(shifts, ahead)
    for field, value in enumerate((update, grad)):
        out_ref[field] = value
        send_ref[field] = dot(chooser, value, NN).astype(BF)


def weight_kernel(windows, kept, spot, *refs):
    norms, tiles, ctxs, gps = (refs[n * windows : (n + 1) * windows] for n in range(4))
    out_ref = refs[-1]
    part = ctxs[0].shape[0]

    def total(left, right):
        return functools.reduce(jnp.add, (dot(a, b, TT) for a, b in zip(left, right)))

    side = spot[1] if kept else 1 - spot[1]

    @pl.when(side == 0)
    def _():
        out_ref[...] = total([n[...] for n in norms], [g[: 2 * part] for g in gps])

    @pl.when(side == 1)
    def _():
        out_ref[:, :part] = total([n[...] for n in norms], [g[2 * part :] for g in gps])
        out_ref[:, part:] = total([t[1] for t in tiles], [c[...] for c in ctxs])


def halve_kernel(bit, gots, spot, mine_ref, *refs):
    got_refs, (keep_ref, *send_refs), total = refs[:gots], refs[gots:-1], refs[-1]
    rows = keep_ref.shape[0]
    piece = got_refs[0].shape[0]
    for n, got_ref in enumerate(got_refs):
        here = slice(n * piece, (n + 1) * piece)
        total[here] = mine_ref[here] + got_ref[...]
    keep_ref[...] = total[pl.ds(pl.multiple_of(spot[bit] * rows, rows), rows)]
    part = send_refs[0].shape[0]
    for n, ref in enumerate(send_refs):
        ref[...] = total[pl.ds(pl.multiple_of((1 - spot[bit]) * rows + n * part, part), part)]


def spread_kernel(spot, mine_ref, got_ref, *out_refs):
    rows = out_refs[0].shape[0]
    for d, ref in enumerate(out_refs):
        at = pl.ds(pl.multiple_of((spot[4] ^ d) * rows, rows), rows)
        ref[...] = mine_ref[at] + got_ref[at]


def gather_sum_kernel(*refs):
    refs[-1][...] = functools.reduce(jnp.add, (r[...] for r in refs[:-1])).astype(BF)


def arrange_kernel(spot, *refs):
    *parts, out_ref = refs
    columns = parts[0].shape[1]
    before = out_ref.shape[2] - columns
    if before:
        out_ref[:, :, :before] = parts.pop()[...]
    for d, ref in enumerate(parts):
        out_ref[spot[4] ^ d, :, before:] = ref[...]


def join_two_kernel(bit, spot, mine_ref, got_ref, low_ref, high_ref):
    for value, ref, other in ((0, low_ref, high_ref), (1, high_ref, low_ref)):

        @pl.when(spot[bit] == value)
        def _(ref=ref, other=other):
            ref[...] = mine_ref[...]
            other[...] = got_ref[...]


def join_kernel(bit, spot, *refs):
    *parts, out_ref = refs
    count = len(parts) // 2
    for side, pieces in ((spot[bit], parts[:count]), (1 - spot[bit], parts[count:])):
        for n, ref in enumerate(pieces):
            out_ref[side * count + n] = ref[...]


def gradient_kernel(factor, spot, mine_ref, got_ref, qkv_ref, proj_ref):
    width = proj_ref.shape[0]
    size = width // HEADS
    count, rows = mine_ref.shape[:2]

    def write(pair_ref, rest_ref):
        for n in range(count):
            here = slice(n * rows, (n + 1) * rows)
            pair = pair_ref[n].astype(F32) * factor
            rest = rest_ref[n].astype(F32) * factor
            at = 0
            for start, heads in PHASES:
                low, part = start * size, heads * size
                qkv_ref[here, low : low + part] = pair[:, at : at + part]
                qkv_ref[here, width + low : width + low + part] = pair[:, at + part : at + 2 * part]
                qkv_ref[here, 2 * width + low : 2 * width + low + part] = rest[:, at : at + part]
                proj_ref[low : low + part, here] = rest[:, at + part : at + 2 * part].T
                at += 2 * part

    first = spot[1] == 0

    @pl.when(first)
    def _():
        write(mine_ref, got_ref)

    @pl.when(jnp.logical_not(first))
    def _():
        write(got_ref, mine_ref)


def turn_kernel(phase, w_ref, out_ref):
    width = w_ref.shape[0]
    start, heads = PHASES[phase]
    low, part = start * width // HEADS, heads * width // HEADS
    for n in range(3):
        out_ref[n * part : (n + 1) * part] = w_ref[:, n * width + low : n * width + low + part].T


def last_back_kernel(ahead, shifts, own_ref, got_ref, out_ref):
    taken, spread = unpack_matrix(shifts, ahead)
    for field in range(2):
        out_ref[field] = select_other(taken, spread, got_ref[field], own_ref[field]).astype(BF)


def finish_kernel(ahead, windows, shifts, x_ref, cot_ref, above_ref, final_ref, *refs):
    owns, gots = refs[: windows - 1], refs[windows - 1 : 2 * windows - 2]
    outs = refs[2 * windows - 2 :]
    part = WLAT * WLON
    grid = x_ref.shape[1]
    taken, spread = unpack_matrix(shifts, ahead)
    movers = []
    for level in range(LEV):
        cut = shifts[level, 0]
        slot, first, row = level_slots(windows, cut, 1)
        slot = jnp.where(jnp.logical_and(first, row >= cut), -1, slot)
        cells = lax.broadcasted_iota(I32, (grid, (windows + 1) * part), 0)
        movers.append((cells == slot).astype(F32).astype(BF))
    for field, ref in enumerate((x_ref, cot_ref)):
        tiles = [
            select_other(taken, spread, gots[w][field], owns[w][field]) for w in range(windows - 1)
        ]
        tiles += [final_ref[field].astype(F32), above_ref[field].astype(F32)]
        for level in range(LEV):
            here = slice(level * part, (level + 1) * part)
            source = jnp.concatenate([t[here] for t in tiles], axis=0).astype(BF)
            value = ref[level].astype(F32) + dot(movers[level], source, NN)
            outs[field][level] = value.astype(BF)


def route(pairs_of, lat, lon):
    return [
        (a * lon + o, pairs_of(a, o)[0] * lon + pairs_of(a, o)[1])
        for a in range(lat)
        for o in range(lon)
    ]


def across_core(a, o):
    return a ^ 1, o


def step_one(a, o):
    return (a, o ^ 1) if a % 2 else (a ^ 2, o)


def step_two(a, o):
    return (a ^ 2, o) if a % 2 else (a, o ^ 1)


def all_sum(weights, operands, spot, beside, earlier):
    lat, lon = lax.axis_size("lat"), lax.axis_size("lon")
    reach = lon // 2

    def swap(value, pairs_of):
        return lax.ppermute(value, ("lat", "lon"), route(pairs_of, lat, lon))

    def along(d):
        return lambda a, o: (a, o ^ (2 * d))

    sent = weights(False, operands, earlier)
    gots = [swap(sent, across_core)]
    held = weights(True, operands, (sent,))
    after = ()
    for bit, pairs_of, flows in ((2, step_one, 2), (3, step_two, 1)):
        rows, width = held.shape[0] // 2, held.shape[1]
        held, *sends = call(
            functools.partial(halve_kernel, bit, len(gots)),
            (spot, held, *gots),
            [shape_of(F32, rows, width)] + [shape_of(F32, rows // flows, width)] * flows,
            [pltpu.VMEM(held.shape, F32)],
            scalars=1,
            after=after,
        )
        gots = [swap(value, pairs_of) for value in sends]
        after = beside(held)
    rows = held.shape[0] // reach
    pieces = call(
        spread_kernel,
        (spot, held, *gots),
        [shape_of(F32, rows, width)] * reach,
        scalars=1,
        after=after,
    )
    gots = [swap(pieces[d], along(d)) for d in range(1, reach)]
    after = beside(pieces[0])
    sums = call(gather_sum_kernel, (pieces[0], *gots), [shape_of(BF, rows, width)], after=after)[0]
    gots = [swap(sums, along(d)) for d in range(1, reach)]
    after = beside(sums)
    other = tuple(e for e in earlier if e.shape[:2] == (reach, rows))
    return call(
        arrange_kernel,
        (spot, sums, *gots, *other),
        [shape_of(BF, reach, rows, width + sum(e.shape[2] for e in other))],
        scalars=1,
        after=after,
    )[0]


def all_gather(part, spot, factor):
    lat, lon = lax.axis_size("lat"), lax.axis_size("lon")
    reach, rows, width = part.shape
    held = part.reshape(reach * rows, width)
    block = shape_of(BF, *held.shape)

    def swap(value, pairs_of):
        return lax.ppermute(value, ("lat", "lon"), route(pairs_of, lat, lon))

    pair = call(
        functools.partial(join_two_kernel, 3),
        (spot, held, swap(held, step_two)),
        [block] * 2,
        scalars=1,
    )
    held = call(
        functools.partial(join_kernel, 2),
        (spot, *pair, *[swap(p, step_one) for p in pair]),
        [shape_of(BF, 4, *block.shape)],
        scalars=1,
    )[0]
    full = 4 * block.shape[0]
    return call(
        functools.partial(gradient_kernel, factor),
        (spot, held, swap(held, across_core)),
        [shape_of(F32, full, 3 * full), shape_of(F32, full, full)],
        scalars=1,
    )


def body(ahead, tokens, cotangent, w_qkv, w_proj, shifts, region_ids):
    levels, lat_rows, lon_cols, width = tokens.shape

    def by_column(grid_field):
        return grid_field.transpose(0, 2, 1, 3).reshape(levels, lon_cols * lat_rows, width)

    tokens, cotangent = by_column(tokens), by_column(cotangent)
    windows = lat_rows // WLAT
    size = width // HEADS
    my_lat, my_lon = lax.axis_index("lat"), lax.axis_index("lon")
    core, high, low = my_lat & 1, my_lat >> 1, my_lon & 1
    spot = jnp.stack(
        [
            my_lat * lat_rows,
            core,
            jnp.where(core == 1, low, high),
            jnp.where(core == 1, high, low),
            my_lon >> 1,
        ]
    ).astype(I32)

    def ring(value, axis, step):
        count = lax.axis_size(axis)
        return lax.ppermute(value, axis, [(i, (i + step) % count) for i in range(count)])

    out_step = -1 if ahead else 1
    pair = shape_of(BF, 2, COUNT, width)
    packed = shape_of(BF, 2, PACKED, width)
    arrays = (shifts, tokens, cotangent)
    tile, send, halo = call(
        functools.partial(pack_kernel, ahead, windows, True), arrays, [pair, packed, pair], scalars=1
    )
    made = call(
        functools.partial(pack_kernel, ahead, windows, False),
        arrays,
        [pair] * (windows - 1) + [packed] * (windows - 2),
        scalars=1,
        after=(tile,),
    )
    tiles, last = [tile, *made[: windows - 2]], made[windows - 2]
    sends = [send, *made[windows - 1 :]]

    def turned(phase, after):
        rows = 3 * PHASES[phase][1] * size
        kernel = functools.partial(turn_kernel, phase)
        return call(kernel, (w_qkv,), [shape_of(BF, rows, width)], after=after)[0]

    w_a = turned(0, (last,))
    below = ring(halo, "lat", -1)
    gots = [ring(s, "lon", out_step) for s in sends]
    def parts(phase):
        part = PHASES[phase][1] * size
        return part, [shape_of(BF, part, COUNT), shape_of(BF, 3 * part, COUNT)]

    part, shapes = parts(0)
    firsts = []
    tiles = list(tiles)
    for w in range(windows):
        if w == windows - 2:
            last_tile, last_send = call(
                functools.partial(pack_last_kernel, ahead),
                (shifts, last, below),
                [pair, packed],
                scalars=1,
                after=firsts[0][1:2],
            )
            gots.append(ring(last_send, "lon", out_step))
            tiles.append(last_tile)
            after_last = [last_send]
        firsts.append(
            call(
                functools.partial(first_kernel, ahead, w),
                (shifts, region_ids, spot, tiles[w], gots[w], w_a, w_proj),
                [pair, shape_of(BF, COUNT, width), *shapes],
                head_scratch(part, width),
                3,
                12_000_000_000,
                700_000,
                [f[1] for f in firsts[-1:]] + (after_last if w == windows - 2 else []),
            )
        )
    w_b = turned(1, (firsts[0][1],))
    norms = [f[1] for f in firsts]
    whole_tiles = [f[0] for f in firsts]

    def weights(kept, operands, after):
        columns = 2 * operands[2 * windows].shape[0]
        return call(
            functools.partial(weight_kernel, windows, kept),
            (spot, *operands),
            [shape_of(F32, width, columns)],
            scalars=1,
            flops=1_000_000_000,
            after=after,
        )[0]

    part, shapes = parts(1)
    order = [windows - 1, *range(windows - 1)]
    seconds, backs = {}, {}

    ends = []

    def next_second(value):
        done = [seconds[w] for w in order[: len(seconds)]]
        w = order[len(done)]
        waits = [value]
        if len(done) == 2:
            final = call(
                functools.partial(last_back_kernel, ahead),
                (shifts, done[0][0], backs[order[0]]),
                [pair],
                scalars=1,
                after=(done[1][2],),
            )[0]
            ends.extend([final, ring(final, "lat", 1)])
            waits.append(final)
        if len(done) == 3:
            waits += [backs[order[1]], ends[1]]
        seconds[w] = call(
            functools.partial(second_kernel, ahead, w),
            (shifts, region_ids, spot, *firsts[w], w_a, w_b, w_proj),
            [pair, packed, *shapes],
            head_scratch(part, width),
            3,
            8_000_000_000,
            700_000,
            waits,
        )
        backs[w] = ring(seconds[w][1], "lon", -out_step)
        return (seconds[w][2],)

    sum_a = all_sum(
        weights,
        (*norms, *whole_tiles, *[f[2] for f in firsts], *[f[3] for f in firsts]),
        spot,
        next_second,
        (),
    )
    while len(seconds) < windows:
        next_second(seconds[order[len(seconds) - 1]][2])
    results = []

    def finish(value):
        if not results:
            results.extend(
                call(
                    functools.partial(finish_kernel, ahead, windows),
                    (
                        shifts, tokens, cotangent, ends[1], ends[0],
                        *[seconds[w][0] for w in range(windows - 1)],
                        *[backs[w] for w in range(windows - 1)],
                    ),
                    [shape_of(BF, *tokens.shape)] * 2,
                    scalars=1,
                    after=(value,),
                )
            )
            return ()
        return results[:1]

    sum_b = all_sum(
        weights,
        (
            *norms,
            *whole_tiles,
            *[seconds[w][2] for w in range(windows)],
            *[seconds[w][3] for w in range(windows)],
        ),
        spot,
        finish,
        (sum_a, backs[order[2]]),
    )
    mixed, grad_tokens = (
        r.reshape(levels, lon_cols, lat_rows, width).transpose(0, 2, 1, 3) for r in results
    )

    total_tokens = levels * lat_rows * lax.axis_size("lat") * lon_cols * lax.axis_size("lon")
    gradients = all_gather(sum_b, spot, 1.0 / math.sqrt(total_tokens))
    return (mixed, grad_tokens, *gradients)


def local(tokens, cotangent, w_qkv, w_proj, shifts, region_ids):
    return lax.cond(
        jnp.sum(shifts[:, 1]) <= ENTRIES,
        functools.partial(body, True),
        functools.partial(body, False),
        tokens, cotangent, w_qkv, w_proj, shifts, region_ids,
    )


def solution(mesh):
    return jax.shard_map(
        local,
        mesh=mesh,
        in_specs=(P(None, "lat", "lon", None), P(None, "lat", "lon", None), P(), P(), P(), P()),
        out_specs=(P(None, "lat", "lon", None), P(None, "lat", "lon", None), P(), P()),
        check_vma=False,
    )
```

```python
import functools
import math

import jax
import jax.numpy as jnp
from jax import lax
from jax.experimental import pallas as pl
from jax.experimental.pallas import tpu as pltpu
from jax.sharding import PartitionSpec as P

HEADS = 16
WLAT = 6
WLON = 12
LEV = 4
COUNT = LEV * WLAT * WLON
LANES = 384
ENTRIES = LEV * WLON // 2
PACKED = ENTRIES * WLAT
PHASES = ((0, 8), (8, 8))
NORM_EPS = 1e-05
BARRED = 2.0**100
BF = jnp.bfloat16
F32 = jnp.float32
I32 = jnp.int32

NN = (((1,), (0,)), ((), ()))
NT = (((1,), (1,)), ((), ()))
TN = (((0,), (0,)), ((), ()))
TT = (((0,), (1,)), ((), ()))

SMEM = pl.BlockSpec(memory_space=pltpu.SMEM)
VMEM = pl.BlockSpec(memory_space=pltpu.VMEM)
ANY = pl.BlockSpec(memory_space=pl.ANY)


def dot(a, b, dims):
    return lax.dot_general(a, b, dims, preferred_element_type=F32)


def split_bf16(value):
    high = value.astype(BF)
    low = (value - high.astype(F32)).astype(BF)
    return high, low


def call(kernel, ins, outs, scratch=(), scalars=0, after=()):

    def ordered(*refs):
        kernel(*refs[: len(ins)], *refs[len(ins) + len(after) :])

    return pl.pallas_call(
        ordered,
        in_specs=[SMEM] * scalars + [VMEM] * (len(ins) - scalars) + [ANY] * len(after),
        out_specs=[VMEM] * len(outs),
        out_shape=list(outs),
        scratch_shapes=list(scratch),
        compiler_params=pltpu.CompilerParams(vmem_limit_bytes=24 * 1024 * 1024),
        cost_estimate=pl.CostEstimate(
            flops=1_000_000, bytes_accessed=10_000, transcendentals=0
        ),
    )(*ins, *after)


def shape_of(dtype, *dims):
    return jax.ShapeDtypeStruct(dims, dtype)


def place(axis):
    dims = (COUNT, 1) if axis == 0 else (1, COUNT)
    token = lax.broadcasted_iota(I32, dims, axis)
    level = sum((token >= n * WLAT * WLON).astype(I32) for n in range(1, LEV))
    column, row = column_and_row(token - level * (WLAT * WLON))
    return level, row, column


def column_and_row(rest):
    column = sum((rest >= n * WLAT).astype(I32) for n in range(1, WLON))
    return column, rest - column * WLAT


def level_slots(windows, cut, axis):
    part = WLAT * WLON
    size = (windows + 1) * part
    dims = (size, 1) if axis == 0 else (1, size)
    token = lax.broadcasted_iota(I32, dims, axis)
    window = sum((token >= n * part).astype(I32) for n in range(1, windows + 1))
    column, row = column_and_row(token - window * part)
    at = window * WLAT + row + jnp.where(row < cut, WLAT, 0)
    slot = jnp.where(at < windows * WLAT, column * (windows * WLAT) + at, -1)
    first = window == windows
    return jnp.where(first, column * (windows * WLAT) + row, slot), first, row


def by_level(level, values):
    result = jnp.full(level.shape, values[0], I32)
    for n in range(1, LEV):
        result = jnp.where(level == n, values[n], result)
    return result


def from_next_row(shifts, axis):
    level, row, _ = place(axis)
    return row < by_level(level, [shifts[n, 0] for n in range(LEV)])


def from_other_side(shifts, ahead, axis):
    level, row, column = place(axis)
    cut = [shifts[n, 1] for n in range(LEV)]
    counts = cut if ahead else [WLON - c for c in cut]
    starts = [0] * LEV if ahead else cut
    offsets = [0]
    for n in range(LEV - 1):
        offsets.append(offsets[-1] + counts[n])
    at = by_level(level, cut)
    taken = (column < at) if ahead else (column >= at)
    entry = by_level(level, [o - s for o, s in zip(offsets, starts)]) + column
    return taken, jnp.where(taken, entry * WLAT + row, -1)


def pack_matrix(shifts, ahead):
    _, slot = from_other_side(shifts, ahead, 1)
    rows = lax.broadcasted_iota(I32, (PACKED, COUNT), 0)
    return (rows == slot).astype(F32).astype(BF)


def unpack_matrix(shifts, ahead):
    taken, slot = from_other_side(shifts, ahead, 0)
    columns = lax.broadcasted_iota(I32, (COUNT, PACKED), 1)
    return taken, (columns == slot).astype(F32).astype(BF)


def select_other(taken, spread, packed, own):
    return jnp.where(taken, dot(spread, packed, NN), own.astype(F32))


def pack_kernel(ahead, windows, first, shifts, x_ref, cot_ref, *refs):
    part = WLAT * WLON
    grid = x_ref.shape[1]
    if first:
        count = 2
        tile_refs, send_refs, (halo_ref,) = refs[:1], refs[1:2], refs[2:]
    else:
        count = windows - 1
        tile_refs, send_refs = refs[:count], refs[count:]
    chooser = pack_matrix(shifts, ahead)
    parts = [[[None] * LEV for _ in range(count)] for _ in range(2)]
    for level in range(LEV):
        slot, _, _ = level_slots(windows, shifts[level, 0], 0)
        if first:
            slot = jnp.concatenate([slot[:part], slot[windows * part :]], axis=0)
        else:
            slot = slot[part : windows * part]
        cells = lax.broadcasted_iota(I32, (count * part, grid), 1)
        mover = (cells == slot).astype(F32).astype(BF)
        for field, ref in enumerate((x_ref, cot_ref)):
            moved = dot(mover, ref[level], NN)
            for w in range(count):
                parts[field][w][level] = moved[w * part : (w + 1) * part]
    for field in range(2):
        whole = [jnp.concatenate(p, axis=0).astype(BF) for p in parts[field]]
        for tile_ref, tile in zip(tile_refs, whole):
            tile_ref[field] = tile
        for send_ref, tile in zip(send_refs, whole):
            send_ref[field] = dot(chooser, tile, NN).astype(BF)
        if first:
            halo_ref[field] = whole[1]


def pack_last_kernel(ahead, shifts, last_ref, halo_ref, tile_ref, send_ref):
    lower = from_next_row(shifts, 0)
    chooser = pack_matrix(shifts, ahead)
    for field in range(2):
        tile = jnp.where(lower, halo_ref[field].astype(F32), last_ref[field].astype(F32))
        tile_ref[field] = tile.astype(BF)
        send_ref[field] = dot(chooser, tile.astype(BF), NN).astype(BF)


def standardize(values_full):
    center = values_full - jnp.mean(values_full, axis=1, keepdims=True)
    variance = jnp.mean(center * center, axis=1, keepdims=True)
    inv_scale = lax.rsqrt(variance + NORM_EPS)
    return center * inv_scale, inv_scale


def bars(shifts, ids, first_row, grid_rows, bar_q, bar_k):
    level, row, _ = place(1)
    wrapped = jnp.where(row < by_level(level, [shifts[n, 0] for n in range(LEV)]), WLAT, 0)
    at = first_row + row + wrapped
    at = jnp.where(at >= grid_rows, at - grid_rows, at)
    top = sum((ids[n] == ids[0]).astype(I32) for n in range(WLAT - 1))
    bottom = sum((ids[grid_rows - 1 - n] == ids[grid_rows - 1]).astype(I32) for n in range(WLAT - 1))
    kind = jnp.where(at < top, 1, jnp.where(at >= grid_rows - bottom, 2, 0))
    features = lax.broadcasted_iota(I32, (32, COUNT), 0)
    same = (features == kind).astype(F32)
    bar_q[...] = jnp.zeros_like(bar_q)
    bar_q[:, :COUNT] = (same * -BARRED).astype(BF)
    bar_k[...] = jnp.zeros_like(bar_k)
    bar_k[:, :COUNT] = jnp.where(features < 3, 1.0 - same, 0.0).astype(BF)


def attend(heads, size, bar_q, bar_k, q_s, k_s, v_s, g_s, buffers, ctx_ref, gp_ref):
    scale = 1.0 / math.sqrt(size)
    part = heads * size

    def rows_of(h):
        return pl.ds(pl.multiple_of(h * size, size), size)

    def products(h, buffer):
        score_b, grad_b = buffer[:2]
        rows = rows_of(h)
        q_high, q_low = split_bf16(q_s[rows])
        k_high, k_low = split_bf16(k_s[rows])
        q_all = jnp.concatenate([q_high, q_low, q_high, bar_q[...]], axis=0)
        k_all = jnp.concatenate([k_high, k_high, k_low, bar_k[...]], axis=0)
        score_b[...] = dot(k_all.T[:COUNT], q_all, NN)
        grad_b[...] = dot(v_s[rows].T[:COUNT], g_s[rows], NN)

    def soften(buffer):
        score_b, grad_b, weight_b, high_b, low_b = buffer
        for start in range(0, LANES, 128):
            lanes = slice(start, start + 128)
            scores = score_b[:, lanes]
            expo = jnp.exp2(scores - jnp.max(scores, axis=0, keepdims=True))
            weights = expo * (1.0 / jnp.sum(expo, axis=0, keepdims=True))
            weight_b[:, lanes] = weights.astype(BF)
            grad_w = grad_b[:, lanes]
            grad_sc = weights * (grad_w - jnp.sum(weights * grad_w, axis=0, keepdims=True))
            high_b[:, lanes], low_b[:, lanes] = split_bf16(grad_sc)

    def results(h, buffer):
        weight_b, high_b, low_b = buffer[2:]
        rows = rows_of(h)
        q_high, q_low = split_bf16(q_s[rows])
        k_high, k_low = split_bf16(k_s[rows])
        rounded, high, low = weight_b[...], high_b[...], low_b[...]
        ctx_ref[rows] = dot(v_s[rows][:, :COUNT], rounded, NN)[:, :COUNT].astype(BF)
        k_pair = jnp.concatenate([k_high[:, :COUNT], k_low[:, :COUNT]], axis=0)
        q_pair = jnp.concatenate([q_high, q_low], axis=0)
        gq = dot(k_pair, high, NN)
        gq = gq[:size] + gq[size:] + dot(k_high[:, :COUNT], low, NN)
        gk = dot(q_pair, high, NT)
        gk = gk[:size] + gk[size:] + dot(q_high, low, NT)
        gv = dot(g_s[rows], rounded, NT)
        base = pl.multiple_of(h * size, size)
        gp_ref[pl.ds(base, size)] = (gq[:, :COUNT] * scale).astype(BF)
        gp_ref[pl.ds(part + base, size)] = (gk * math.log(2.0)).astype(BF)
        gp_ref[pl.ds(2 * part + base, size)] = gv.astype(BF)

    even, odd = buffers[:5], buffers[5:]
    products(0, even)

    def pair(p, carry):
        h = 2 * p
        products(h + 1, odd)
        soften(even)
        results(jnp.maximum(h - 1, 0), odd)
        products(jnp.minimum(h + 2, heads - 1), even)
        soften(odd)
        results(h, even)
        return carry

    lax.fori_loop(0, heads // 2, pair, 0)
    results(heads - 1, odd)


def project(part, width, w_ref, wp_rows, norm_s, cot_s, q_s, k_s, v_s, g_s):
    norm = norm_s[...]
    factor = math.log2(math.e) / math.sqrt(width // HEADS)
    q_s[...] = dot(w_ref[:part], norm, NT) * factor
    k_s[...] = dot(w_ref[part : 2 * part], norm, NT)
    v_s[...] = dot(w_ref[2 * part :], norm, NT).astype(BF)
    g_s[...] = dot(wp_rows, cot_s[...], NT).astype(BF)


def head_scratch(part, width):
    return [
        pltpu.VMEM((LANES, width), BF),
        pltpu.VMEM((LANES, width), BF),
        pltpu.VMEM((32, LANES), BF),
        pltpu.VMEM((32, LANES), BF),
        pltpu.VMEM((part, LANES), F32),
        pltpu.VMEM((part, LANES), F32),
        pltpu.VMEM((part, LANES), BF),
        pltpu.VMEM((part, LANES), BF),
    ] + [
        pltpu.VMEM((COUNT, LANES), kind) for _ in range(2) for kind in (F32, F32, BF, BF, BF)
    ]


def first_kernel(
    ahead, window, shifts, ids, spot, own_ref, got_ref, w_ref, wp_ref,
    tile_ref, norm_ref, ctx_ref, gp_ref,
    norm_s, cot_s, bar_q, bar_k, q_s, k_s, v_s, g_s, *buffers,
):
    width = own_ref.shape[-1]
    size = width // HEADS
    start, heads = PHASES[0]
    taken, spread = unpack_matrix(shifts, ahead)
    x = select_other(taken, spread, got_ref[0], own_ref[0])
    cot = select_other(taken, spread, got_ref[1], own_ref[1]).astype(BF)
    tile_ref[0] = x.astype(BF)
    tile_ref[1] = cot
    normed = standardize(x)[0].astype(BF)
    norm_ref[...] = normed
    norm_s[:COUNT] = normed
    norm_s[COUNT:] = jnp.zeros((LANES - COUNT, width), BF)
    cot_s[:COUNT] = cot
    cot_s[COUNT:] = jnp.zeros((LANES - COUNT, width), BF)
    bars(shifts, ids, spot[0] + window * WLAT, ids.shape[0], bar_q, bar_k)
    part = heads * size
    wp_rows = wp_ref[start * size : start * size + part]
    project(part, width, w_ref, wp_rows, norm_s, cot_s, q_s, k_s, v_s, g_s)
    attend(heads, size, bar_q, bar_k, q_s, k_s, v_s, g_s, buffers, ctx_ref, gp_ref)


def second_kernel(
    ahead, window, shifts, ids, spot, tile_ref, norm_ref, ctx_a, gp_a, w_a, w_ref, wp_ref,
    out_ref, send_ref, ctx_ref, gp_ref,
    norm_s, cot_s, bar_q, bar_k, q_s, k_s, v_s, g_s, *buffers,
):
    width = norm_ref.shape[-1]
    size = width // HEADS
    start, heads = PHASES[1]
    norm_s[:COUNT] = norm_ref[...]
    norm_s[COUNT:] = jnp.zeros((LANES - COUNT, width), BF)
    cot_s[:COUNT] = tile_ref[1]
    cot_s[COUNT:] = jnp.zeros((LANES - COUNT, width), BF)
    bars(shifts, ids, spot[0] + window * WLAT, ids.shape[0], bar_q, bar_k)
    part = heads * size
    wp_rows = wp_ref[start * size : start * size + part]
    project(part, width, w_ref, wp_rows, norm_s, cot_s, q_s, k_s, v_s, g_s)
    attend(heads, size, bar_q, bar_k, q_s, k_s, v_s, g_s, buffers, ctx_ref, gp_ref)
    context = jnp.concatenate([ctx_a[...], ctx_ref[...]], axis=0)
    update = dot(context, wp_ref[...], TN).astype(BF)
    grad_normed = dot(gp_a[...], w_a[...], TN) + dot(gp_ref[...], w_ref[...], TN)
    standard, inv_scale = standardize(tile_ref[0].astype(F32))
    grad = inv_scale * (
        grad_normed
        - jnp.mean(grad_normed, axis=1, keepdims=True)
        - standard * jnp.mean(grad_normed * standard, axis=1, keepdims=True)
    )
    grad = grad.astype(BF)
    chooser = pack_matrix(shifts, ahead)
    for field, value in enumerate((update, grad)):
        out_ref[field] = value
        send_ref[field] = dot(chooser, value, NN).astype(BF)


def weight_kernel(windows, kept, *refs):
    spot, refs = (None, refs) if kept is None else (refs[0], refs[1:])
    norms, tiles, ctxs, gps = (refs[n * windows : (n + 1) * windows] for n in range(4))
    out_refs = refs[4 * windows :]
    part = ctxs[0].shape[0]

    def total(left, right):
        return functools.reduce(jnp.add, (dot(a, b, TT) for a, b in zip(left, right)))

    def queries_keys(ref):
        ref[...] = total([n[...] for n in norms], [g[: 2 * part] for g in gps])

    def values_proj(ref):
        ref[:, :part] = total([n[...] for n in norms], [g[2 * part :] for g in gps])
        ref[:, part:] = total([t[1] for t in tiles], [c[...] for c in ctxs])

    if len(out_refs) == 2:
        queries_keys(out_refs[0])
        values_proj(out_refs[1])
        return
    side = spot[1] if kept else 1 - spot[1]
    pl.when(side == 0)(functools.partial(queries_keys, out_refs[0]))
    pl.when(side == 1)(functools.partial(values_proj, out_refs[0]))


def halve_kernel(bit, gots, spot, mine_ref, *refs):
    got_refs, (keep_ref, *send_refs), total = refs[:gots], refs[gots:-1], refs[-1]
    rows = keep_ref.shape[0]
    piece = got_refs[0].shape[0]
    for n, got_ref in enumerate(got_refs):
        here = slice(n * piece, (n + 1) * piece)
        total[here] = mine_ref[here] + got_ref[...]
    keep_ref[...] = total[pl.ds(pl.multiple_of(spot[bit] * rows, rows), rows)]
    part = send_refs[0].shape[0]
    for n, ref in enumerate(send_refs):
        ref[...] = total[pl.ds(pl.multiple_of((1 - spot[bit]) * rows + n * part, part), part)]


def spread_kernel(spot, mine_ref, got_ref, *out_refs):
    rows = out_refs[0].shape[0]
    for d, ref in enumerate(out_refs):
        at = pl.ds(pl.multiple_of((spot[4] ^ d) * rows, rows), rows)
        ref[...] = mine_ref[at] + got_ref[at]


def gather_sum_kernel(*refs):
    refs[-1][...] = functools.reduce(jnp.add, (r[...] for r in refs[:-1])).astype(BF)


def arrange_kernel(spot, *refs):
    for d, ref in enumerate(refs[:-1]):
        refs[-1][spot[4] ^ d] = ref[...]


def join_kernel(bit, spot, mine_ref, got_ref, out_ref):
    count = mine_ref.shape[0]
    for side, ref in ((spot[bit], mine_ref), (1 - spot[bit], got_ref)):
        for n in range(count):
            out_ref[side * count + n] = ref[n]


def gradient_kernel(factor, spot, pair_a, rest_a, mine_ref, got_ref, qkv_ref, proj_ref):
    width = proj_ref.shape[0]
    size = width // HEADS
    count, rows = mine_ref.shape[:2]

    def write(phase, here, pair, rest):
        low, part = (n * size for n in PHASES[phase])
        qkv_ref[here, low : low + part] = pair[:, :part]
        qkv_ref[here, width + low : width + low + part] = pair[:, part:]
        qkv_ref[here, 2 * width + low : 2 * width + low + part] = rest[:, :part]
        proj_ref[low : low + part, here] = rest[:, part:].T

    def second(pair_ref, rest_ref):
        for n in range(count):
            here = slice(n * rows, (n + 1) * rows)
            write(1, here, pair_ref[n].astype(F32) * factor, rest_ref[n].astype(F32) * factor)

    for n in range(count):
        here = slice(n * rows, (n + 1) * rows)
        write(0, here, pair_a[here] * factor, rest_a[here] * factor)
    first = spot[1] == 0

    @pl.when(first)
    def _():
        second(mine_ref, got_ref)

    @pl.when(jnp.logical_not(first))
    def _():
        second(got_ref, mine_ref)


def turn_kernel(phase, w_ref, out_ref):
    width = w_ref.shape[0]
    start, heads = PHASES[phase]
    low, part = start * width // HEADS, heads * width // HEADS
    for n in range(3):
        out_ref[n * part : (n + 1) * part] = w_ref[:, n * width + low : n * width + low + part].T


def last_back_kernel(ahead, shifts, own_ref, got_ref, out_ref):
    taken, spread = unpack_matrix(shifts, ahead)
    for field in range(2):
        out_ref[field] = select_other(taken, spread, got_ref[field], own_ref[field]).astype(BF)


def finish_kernel(ahead, windows, shifts, x_ref, cot_ref, above_ref, final_ref, *refs):
    owns, gots = refs[: windows - 1], refs[windows - 1 : 2 * windows - 2]
    outs = refs[2 * windows - 2 :]
    part = WLAT * WLON
    grid = x_ref.shape[1]
    taken, spread = unpack_matrix(shifts, ahead)
    movers = []
    for level in range(LEV):
        cut = shifts[level, 0]
        slot, first, row = level_slots(windows, cut, 1)
        slot = jnp.where(jnp.logical_and(first, row >= cut), -1, slot)
        cells = lax.broadcasted_iota(I32, (grid, (windows + 1) * part), 0)
        movers.append((cells == slot).astype(F32).astype(BF))
    for field, ref in enumerate((x_ref, cot_ref)):
        tiles = [
            select_other(taken, spread, gots[w][field], owns[w][field]) for w in range(windows - 1)
        ]
        tiles += [final_ref[field].astype(F32), above_ref[field].astype(F32)]
        for level in range(LEV):
            here = slice(level * part, (level + 1) * part)
            source = jnp.concatenate([t[here] for t in tiles], axis=0).astype(BF)
            value = ref[level].astype(F32) + dot(movers[level], source, NN)
            outs[field][level] = value.astype(BF)


def route(pairs_of, lat, lon):
    return [
        (a * lon + o, pairs_of(a, o)[0] * lon + pairs_of(a, o)[1])
        for a in range(lat)
        for o in range(lon)
    ]


def across_core(a, o):
    return a ^ 1, o


def step_one(a, o):
    return (a, o ^ 1) if a % 2 else (a ^ 2, o)


def step_two(a, o):
    return (a ^ 2, o) if a % 2 else (a, o ^ 1)


def all_sum(operands, spot, beside, earlier):
    lat, lon = lax.axis_size("lat"), lax.axis_size("lon")
    reach = lon // 2

    def swap(value, pairs_of):
        return lax.ppermute(value, ("lat", "lon"), route(pairs_of, lat, lon))

    def along(d):
        return lambda a, o: (a, o ^ (2 * d))

    (sent,) = weights(False, operands, earlier, spot)
    gots = [swap(sent, across_core)]
    (held,) = weights(True, operands, (sent,), spot)
    after = ()
    for bit, pairs_of, flows in ((2, step_one, 1), (3, step_two, 1)):
        rows, width = held.shape[0] // 2, held.shape[1]
        held, *sends = call(
            functools.partial(halve_kernel, bit, len(gots)),
            (spot, held, *gots),
            [shape_of(F32, rows, width)] + [shape_of(F32, rows // flows, width)] * flows,
            [pltpu.VMEM(held.shape, F32)],
            scalars=1,
            after=after,
        )
        gots = [swap(value, pairs_of) for value in sends]
        after = beside(held)
    rows = held.shape[0] // reach
    pieces = call(
        spread_kernel,
        (spot, held, *gots),
        [shape_of(F32, rows, width)] * reach,
        scalars=1,
        after=after,
    )
    gots = [swap(pieces[d], along(d)) for d in range(1, reach)]
    after = beside(pieces[0])
    sums = call(gather_sum_kernel, (pieces[0], *gots), [shape_of(BF, rows, width)], after=after)[0]
    gots = [swap(sums, along(d)) for d in range(1, reach)]
    after = beside(sums)
    return call(
        arrange_kernel, (spot, sums, *gots), [shape_of(BF, reach, rows, width)], scalars=1, after=after
    )[0]


def all_gather(part, spot):
    lat, lon = lax.axis_size("lat"), lax.axis_size("lon")
    reach, rows, columns = part.shape
    held = part.reshape(1, reach * rows, columns)

    def swap(value, pairs_of):
        return lax.ppermute(value, ("lat", "lon"), route(pairs_of, lat, lon))

    for bit, pairs_of in ((3, step_two), (2, step_one)):
        count = 2 * held.shape[0]
        held = call(
            functools.partial(join_kernel, bit),
            (spot, held, swap(held, pairs_of)),
            [shape_of(BF, count, *held.shape[1:])],
            scalars=1,
        )[0]
    return held, swap(held, across_core)


def ring(value, axis, step):
    count = lax.axis_size(axis)
    return lax.ppermute(value, axis, [(i, (i + step) % count) for i in range(count)])


def part_shapes(phase, width):
    part = PHASES[phase][1] * width // HEADS
    return part, [shape_of(BF, part, COUNT), shape_of(BF, 3 * part, COUNT)]


def first_phase(ahead, tokens, cotangent, w_qkv, w_proj, shifts, region_ids, spot):
    width = tokens.shape[-1]
    windows = tokens.shape[1] // (WLAT * WLON)
    out_step = -1 if ahead else 1
    pair = shape_of(BF, 2, COUNT, width)
    packed = shape_of(BF, 2, PACKED, width)
    arrays = (shifts, tokens, cotangent)
    tile, send, halo = call(
        functools.partial(pack_kernel, ahead, windows, True), arrays, [pair, packed, pair], scalars=1
    )
    made = call(
        functools.partial(pack_kernel, ahead, windows, False),
        arrays,
        [pair] * (windows - 1) + [packed] * (windows - 2),
        scalars=1,
        after=(tile,),
    )
    tiles, last = [tile, *made[: windows - 2]], made[windows - 2]
    sends = [send, *made[windows - 1 :]]

    def turned(phase, after):
        rows = 3 * part_shapes(phase, width)[0]
        kernel = functools.partial(turn_kernel, phase)
        return call(kernel, (w_qkv,), [shape_of(BF, rows, width)], after=after)[0]

    w_a = turned(0, (last,))
    below = ring(halo, "lat", -1)
    gots = [ring(s, "lon", out_step) for s in sends]
    part, shapes = part_shapes(0, width)
    firsts = []
    for w in range(windows):
        if w == windows - 2:
            last_tile, last_send = call(
                functools.partial(pack_last_kernel, ahead),
                (shifts, last, below),
                [pair, packed],
                scalars=1,
                after=firsts[0][1:2],
            )
            gots.append(ring(last_send, "lon", out_step))
            tiles.append(last_tile)
            after_last = [last_send]
        firsts.append(
            call(
                functools.partial(first_kernel, ahead, w),
                (shifts, region_ids, spot, tiles[w], gots[w], w_a, w_proj),
                [pair, shape_of(BF, COUNT, width), *shapes],
                head_scratch(part, width),
                3,
                [f[1] for f in firsts[-1:]] + (after_last if w == windows - 2 else []),
            )
        )
    return firsts, w_a, turned(1, (firsts[0][1],))


def weights(kept, operands, after, spot=None):
    columns = 2 * operands[-1].shape[0] // 3
    width = operands[0].shape[-1]
    return call(
        functools.partial(weight_kernel, len(operands) // 4, kept),
        operands if kept is None else (spot, *operands),
        [shape_of(F32, width, columns)] * (2 if kept is None else 1),
        scalars=0 if kept is None else 1,
        after=after,
    )


def second_phase(ahead, tokens, cotangent, w_a, w_b, w_proj, shifts, region_ids, spot, firsts):
    width = tokens.shape[-1]
    windows = len(firsts)
    out_step = -1 if ahead else 1
    pair = shape_of(BF, 2, COUNT, width)
    packed = shape_of(BF, 2, PACKED, width)
    part, shapes = part_shapes(1, width)
    order = [windows - 1, *range(windows - 1)]
    seconds, backs, ends = {}, {}, []
    for w in order:
        done = [seconds[n] for n in seconds]
        waits = [d[2] for d in done[-1:]]
        if len(done) == 2:
            final = call(
                functools.partial(last_back_kernel, ahead),
                (shifts, done[0][0], backs[order[0]]),
                [pair],
                scalars=1,
                after=(done[1][2],),
            )[0]
            ends = [final, ring(final, "lat", 1)]
            waits.append(final)
        if len(done) == 3:
            waits += [backs[order[1]], ends[1]]
        seconds[w] = call(
            functools.partial(second_kernel, ahead, w),
            (shifts, region_ids, spot, *firsts[w], w_a, w_b, w_proj),
            [pair, packed, *shapes],
            head_scratch(part, width),
            3,
            waits,
        )
        backs[w] = ring(seconds[w][1], "lon", -out_step)
    results = []

    def finish(value):
        if not results:
            results.extend(
                call(
                    functools.partial(finish_kernel, ahead, windows),
                    (
                        shifts, tokens, cotangent, ends[1], ends[0],
                        *[seconds[w][0] for w in range(windows - 1)],
                        *[backs[w] for w in range(windows - 1)],
                    ),
                    [shape_of(BF, *tokens.shape)] * 2,
                    scalars=1,
                    after=(value,),
                )
            )
            return ()
        return results[:1]

    operands = weight_operands(firsts, [seconds[w] for w in range(windows)])
    summed = all_sum(operands, spot, finish, (backs[order[2]],))
    return (*results, *all_gather(summed, spot))


def weight_operands(firsts, made):
    return (
        *[f[1] for f in firsts],
        *[f[0] for f in firsts],
        *[m[2] for m in made],
        *[m[3] for m in made],
    )


def local(tokens, cotangent, w_qkv, w_proj, shifts, region_ids):
    levels, lat_rows, lon_cols, width = tokens.shape

    def by_column(grid_field):
        return grid_field.transpose(0, 2, 1, 3).reshape(levels, lon_cols * lat_rows, width)

    fields = by_column(tokens), by_column(cotangent)
    my_lat, my_lon = lax.axis_index("lat"), lax.axis_index("lon")
    core, high, low = my_lat & 1, my_lat >> 1, my_lon & 1
    spot = jnp.stack(
        [
            my_lat * lat_rows,
            core,
            jnp.where(core == 1, low, high),
            jnp.where(core == 1, high, low),
            my_lon >> 1,
        ]
    ).astype(I32)
    ahead = jnp.sum(shifts[:, 1]) <= ENTRIES

    def either(function, *operands):
        return lax.cond(
            ahead, functools.partial(function, True), functools.partial(function, False), *operands
        )

    firsts, w_a, w_b = either(first_phase, *fields, w_qkv, w_proj, shifts, region_ids, spot)
    sums_a = weights(None, weight_operands(firsts, firsts), ())
    sums_a = lax.psum(tuple(sums_a), ("lat", "lon"))
    *results, held, got = either(
        second_phase, *fields, w_a, w_b, w_proj, shifts, region_ids, spot, firsts
    )
    mixed, grad_tokens = (
        r.reshape(levels, lon_cols, lat_rows, width).transpose(0, 2, 1, 3) for r in results
    )
    total_tokens = levels * lat_rows * lax.axis_size("lat") * lon_cols * lax.axis_size("lon")
    gradients = call(
        functools.partial(gradient_kernel, 1.0 / math.sqrt(total_tokens)),
        (spot, *sums_a, held, got),
        [shape_of(F32, width, 3 * width), shape_of(F32, width, width)],
        scalars=1,
    )
    return (mixed, grad_tokens, *gradients)


def solution(mesh):
    return jax.shard_map(
        local,
        mesh=mesh,
        in_specs=(P(None, "lat", "lon", None), P(None, "lat", "lon", None), P(), P(), P(), P()),
        out_specs=(P(None, "lat", "lon", None), P(None, "lat", "lon", None), P(), P()),
        check_vma=False,
    )
```

```python
import functools
import math

import jax
import jax.numpy as jnp
from jax import lax
from jax.experimental import pallas as pl
from jax.experimental.pallas import tpu as pltpu
from jax.sharding import PartitionSpec as P

HEADS = 16
WLAT = 6
WLON = 12
LEV = 4
COUNT = LEV * WLAT * WLON
LANES = 384
ENTRIES = LEV * WLON // 2
PACKED = ENTRIES * WLAT
PHASES = ((0, 8), (8, 8))
NORM_EPS = 1e-05
BARRED = 2.0**100
BF = jnp.bfloat16
F32 = jnp.float32
I32 = jnp.int32

NN = (((1,), (0,)), ((), ()))
NT = (((1,), (1,)), ((), ()))
TN = (((0,), (0,)), ((), ()))
TT = (((0,), (1,)), ((), ()))

SMEM = pl.BlockSpec(memory_space=pltpu.SMEM)
VMEM = pl.BlockSpec(memory_space=pltpu.VMEM)
ANY = pl.BlockSpec(memory_space=pl.ANY)


def dot(a, b, dims):
    return lax.dot_general(a, b, dims, preferred_element_type=F32)


def split_bf16(value):
    high = value.astype(BF)
    low = (value - high.astype(F32)).astype(BF)
    return high, low


def call(kernel, ins, outs, scratch=(), scalars=0, after=()):

    def ordered(*refs):
        kernel(*refs[: len(ins)], *refs[len(ins) + len(after) :])

    return pl.pallas_call(
        ordered,
        in_specs=[SMEM] * scalars + [VMEM] * (len(ins) - scalars) + [ANY] * len(after),
        out_specs=[VMEM] * len(outs),
        out_shape=list(outs),
        scratch_shapes=list(scratch),
        compiler_params=pltpu.CompilerParams(vmem_limit_bytes=24 * 1024 * 1024),
        cost_estimate=pl.CostEstimate(
            flops=1_000_000, bytes_accessed=10_000, transcendentals=0
        ),
    )(*ins, *after)


def shape_of(dtype, *dims):
    return jax.ShapeDtypeStruct(dims, dtype)


def place(axis):
    dims = (COUNT, 1) if axis == 0 else (1, COUNT)
    token = lax.broadcasted_iota(I32, dims, axis)
    level = sum((token >= n * WLAT * WLON).astype(I32) for n in range(1, LEV))
    column, row = column_and_row(token - level * (WLAT * WLON))
    return level, row, column


def column_and_row(rest):
    column = sum((rest >= n * WLAT).astype(I32) for n in range(1, WLON))
    return column, rest - column * WLAT


def level_slots(windows, cut, axis):
    part = WLAT * WLON
    size = (windows + 1) * part
    dims = (size, 1) if axis == 0 else (1, size)
    token = lax.broadcasted_iota(I32, dims, axis)
    window = sum((token >= n * part).astype(I32) for n in range(1, windows + 1))
    column, row = column_and_row(token - window * part)
    at = window * WLAT + row + jnp.where(row < cut, WLAT, 0)
    slot = jnp.where(at < windows * WLAT, column * (windows * WLAT) + at, -1)
    first = window == windows
    return jnp.where(first, column * (windows * WLAT) + row, slot), first, row


def by_level(level, values):
    result = jnp.full(level.shape, values[0], I32)
    for n in range(1, LEV):
        result = jnp.where(level == n, values[n], result)
    return result


def from_next_row(shifts, axis):
    level, row, _ = place(axis)
    return row < by_level(level, [shifts[n, 0] for n in range(LEV)])


def from_other_side(shifts, ahead, axis):
    level, row, column = place(axis)
    cut = [shifts[n, 1] for n in range(LEV)]
    counts = cut if ahead else [WLON - c for c in cut]
    starts = [0] * LEV if ahead else cut
    offsets = [0]
    for n in range(LEV - 1):
        offsets.append(offsets[-1] + counts[n])
    at = by_level(level, cut)
    taken = (column < at) if ahead else (column >= at)
    entry = by_level(level, [o - s for o, s in zip(offsets, starts)]) + column
    return taken, jnp.where(taken, entry * WLAT + row, -1)


def pack_matrix(shifts, ahead):
    _, slot = from_other_side(shifts, ahead, 1)
    rows = lax.broadcasted_iota(I32, (PACKED, COUNT), 0)
    return (rows == slot).astype(F32).astype(BF)


def unpack_matrix(shifts, ahead):
    taken, slot = from_other_side(shifts, ahead, 0)
    columns = lax.broadcasted_iota(I32, (COUNT, PACKED), 1)
    return taken, (columns == slot).astype(F32).astype(BF)


def select_other(taken, spread, packed, own):
    return jnp.where(taken, dot(spread, packed, NN), own.astype(F32))


def pack_kernel(ahead, windows, chosen, sent, shifts, x_ref, cot_ref, *refs):
    part = WLAT * WLON
    grid = x_ref.shape[1]
    count = len(chosen)
    tile_refs, send_refs = refs[:count], refs[count:]
    chooser = pack_matrix(shifts, ahead)
    parts = [[[None] * LEV for _ in range(count)] for _ in range(2)]
    for level in range(LEV):
        slot, _, _ = level_slots(windows, shifts[level, 0], 0)
        slot = jnp.concatenate([slot[w * part : (w + 1) * part] for w in chosen], axis=0)
        cells = lax.broadcasted_iota(I32, (count * part, grid), 1)
        mover = (cells == slot).astype(F32).astype(BF)
        for field, ref in enumerate((x_ref, cot_ref)):
            moved = dot(mover, ref[level], NN)
            for w in range(count):
                parts[field][w][level] = moved[w * part : (w + 1) * part]
    for field in range(2):
        whole = [jnp.concatenate(p, axis=0).astype(BF) for p in parts[field]]
        for tile_ref, tile in zip(tile_refs, whole):
            tile_ref[field] = tile
        for n, send_ref in zip(sent, send_refs):
            send_ref[field] = dot(chooser, whole[n], NN).astype(BF)


def pack_last_kernel(ahead, shifts, last_ref, halo_ref, tile_ref, send_ref):
    lower = from_next_row(shifts, 0)
    chooser = pack_matrix(shifts, ahead)
    for field in range(2):
        tile = jnp.where(lower, halo_ref[field].astype(F32), last_ref[field].astype(F32))
        tile_ref[field] = tile.astype(BF)
        send_ref[field] = dot(chooser, tile.astype(BF), NN).astype(BF)


def standardize(values_full):
    center = values_full - jnp.mean(values_full, axis=1, keepdims=True)
    variance = jnp.mean(center * center, axis=1, keepdims=True)
    inv_scale = lax.rsqrt(variance + NORM_EPS)
    return center * inv_scale, inv_scale


def bars(shifts, ids, first_row, grid_rows, bar_q, bar_k):
    level, row, _ = place(1)
    wrapped = jnp.where(row < by_level(level, [shifts[n, 0] for n in range(LEV)]), WLAT, 0)
    at = first_row + row + wrapped
    at = jnp.where(at >= grid_rows, at - grid_rows, at)
    top = sum((ids[n] == ids[0]).astype(I32) for n in range(WLAT - 1))
    bottom = sum((ids[grid_rows - 1 - n] == ids[grid_rows - 1]).astype(I32) for n in range(WLAT - 1))
    kind = jnp.where(at < top, 1, jnp.where(at >= grid_rows - bottom, 2, 0))
    features = lax.broadcasted_iota(I32, (32, COUNT), 0)
    same = (features == kind).astype(F32)
    bar_q[...] = jnp.zeros_like(bar_q)
    bar_q[:, :COUNT] = (same * -BARRED).astype(BF)
    bar_k[...] = jnp.zeros_like(bar_k)
    bar_k[:, :COUNT] = jnp.where(features < 3, 1.0 - same, 0.0).astype(BF)


def attend(heads, size, bar_q, bar_k, q_s, k_s, v_s, g_s, buffers, ctx_ref, gp_ref):
    scale = 1.0 / math.sqrt(size)
    part = heads * size

    def rows_of(h):
        return pl.ds(pl.multiple_of(h * size, size), size)

    def products(h, buffer):
        score_b, grad_b = buffer[:2]
        rows = rows_of(h)
        q_high, q_low = split_bf16(q_s[rows])
        k_high, k_low = split_bf16(k_s[rows])
        q_all = jnp.concatenate([q_high, q_low, q_high, bar_q[...]], axis=0)
        k_all = jnp.concatenate([k_high, k_high, k_low, bar_k[...]], axis=0)
        score_b[...] = dot(k_all.T[:COUNT], q_all, NN)
        grad_b[...] = dot(v_s[rows].T[:COUNT], g_s[rows], NN)

    def soften(buffer):
        score_b, grad_b, weight_b, high_b, low_b = buffer
        for start in range(0, LANES, 128):
            lanes = slice(start, start + 128)
            scores = score_b[:, lanes]
            expo = jnp.exp2(scores - jnp.max(scores, axis=0, keepdims=True))
            weights = expo * (1.0 / jnp.sum(expo, axis=0, keepdims=True))
            weight_b[:, lanes] = weights.astype(BF)
            grad_w = grad_b[:, lanes]
            grad_sc = weights * (grad_w - jnp.sum(weights * grad_w, axis=0, keepdims=True))
            high_b[:, lanes], low_b[:, lanes] = split_bf16(grad_sc)

    def results(h, buffer):
        weight_b, high_b, low_b = buffer[2:]
        rows = rows_of(h)
        q_high, q_low = split_bf16(q_s[rows])
        k_high, k_low = split_bf16(k_s[rows])
        rounded, high, low = weight_b[...], high_b[...], low_b[...]
        ctx_ref[rows] = dot(v_s[rows][:, :COUNT], rounded, NN)[:, :COUNT].astype(BF)
        k_pair = jnp.concatenate([k_high[:, :COUNT], k_low[:, :COUNT]], axis=0)
        q_pair = jnp.concatenate([q_high, q_low], axis=0)
        gq = dot(k_pair, high, NN)
        gq = gq[:size] + gq[size:] + dot(k_high[:, :COUNT], low, NN)
        gk = dot(q_pair, high, NT)
        gk = gk[:size] + gk[size:] + dot(q_high, low, NT)
        gv = dot(g_s[rows], rounded, NT)
        base = pl.multiple_of(h * size, size)
        gp_ref[pl.ds(base, size)] = (gq[:, :COUNT] * scale).astype(BF)
        gp_ref[pl.ds(part + base, size)] = (gk * math.log(2.0)).astype(BF)
        gp_ref[pl.ds(2 * part + base, size)] = gv.astype(BF)

    even, odd = buffers[:5], buffers[5:]
    products(0, even)

    def pair(p, carry):
        h = 2 * p
        products(h + 1, odd)
        soften(even)
        results(jnp.maximum(h - 1, 0), odd)
        products(jnp.minimum(h + 2, heads - 1), even)
        soften(odd)
        results(h, even)
        return carry

    lax.fori_loop(0, heads // 2, pair, 0)
    results(heads - 1, odd)


def project(first, part, width, w_ref, wp_ref, norm_s, cot_s, q_s, k_s, v_s, g_s):
    norm = norm_s[...]
    factor = math.log2(math.e) / math.sqrt(width // HEADS)
    q_s[...] = dot(w_ref[first : first + part], norm, NT) * factor
    k_s[...] = dot(w_ref[width + first : width + first + part], norm, NT)
    v_s[...] = dot(w_ref[2 * width + first : 2 * width + first + part], norm, NT).astype(BF)
    g_s[...] = dot(wp_ref[first : first + part], cot_s[...], NT).astype(BF)


def head_scratch(part, width):
    return [
        pltpu.VMEM((LANES, width), BF),
        pltpu.VMEM((LANES, width), BF),
        pltpu.VMEM((32, LANES), BF),
        pltpu.VMEM((32, LANES), BF),
        pltpu.VMEM((part, LANES), F32),
        pltpu.VMEM((part, LANES), F32),
        pltpu.VMEM((part, LANES), BF),
        pltpu.VMEM((part, LANES), BF),
    ] + [
        pltpu.VMEM((COUNT, LANES), kind) for _ in range(2) for kind in (F32, F32, BF, BF, BF)
    ]


def first_kernel(
    ahead, window, shifts, ids, spot, own_ref, got_ref, w_ref, wp_ref,
    tile_ref, norm_ref, ctx_ref, gp_ref,
    norm_s, cot_s, bar_q, bar_k, q_s, k_s, v_s, g_s, *buffers,
):
    width = own_ref.shape[-1]
    size = width // HEADS
    start, heads = PHASES[0]
    taken, spread = unpack_matrix(shifts, ahead)
    x = select_other(taken, spread, got_ref[0], own_ref[0])
    cot = select_other(taken, spread, got_ref[1], own_ref[1]).astype(BF)
    tile_ref[0] = x.astype(BF)
    tile_ref[1] = cot
    normed = standardize(x)[0].astype(BF)
    norm_ref[...] = normed
    norm_s[:COUNT] = normed
    norm_s[COUNT:] = jnp.zeros((LANES - COUNT, width), BF)
    cot_s[:COUNT] = cot
    cot_s[COUNT:] = jnp.zeros((LANES - COUNT, width), BF)
    bars(shifts, ids, spot[0] + window * WLAT, ids.shape[0], bar_q, bar_k)
    project(start * size, heads * size, width, w_ref, wp_ref, norm_s, cot_s, q_s, k_s, v_s, g_s)
    attend(heads, size, bar_q, bar_k, q_s, k_s, v_s, g_s, buffers, ctx_ref, gp_ref)


def second_kernel(
    ahead, window, shifts, ids, spot, tile_ref, norm_ref, ctx_a, gp_a, w_ref, wp_ref,
    out_ref, send_ref, ctx_ref, gp_ref,
    norm_s, cot_s, bar_q, bar_k, q_s, k_s, v_s, g_s, *buffers,
):
    width = norm_ref.shape[-1]
    size = width // HEADS
    start, heads = PHASES[1]
    norm_s[:COUNT] = norm_ref[...]
    norm_s[COUNT:] = jnp.zeros((LANES - COUNT, width), BF)
    cot_s[:COUNT] = tile_ref[1]
    cot_s[COUNT:] = jnp.zeros((LANES - COUNT, width), BF)
    bars(shifts, ids, spot[0] + window * WLAT, ids.shape[0], bar_q, bar_k)
    project(start * size, heads * size, width, w_ref, wp_ref, norm_s, cot_s, q_s, k_s, v_s, g_s)
    attend(heads, size, bar_q, bar_k, q_s, k_s, v_s, g_s, buffers, ctx_ref, gp_ref)
    context = jnp.concatenate([ctx_a[...], ctx_ref[...]], axis=0)
    update = dot(context, wp_ref[...], TN).astype(BF)
    parts = []
    for n in range(3):
        for ref in (gp_a, gp_ref):
            part = ref.shape[0] // 3
            parts.append(ref[n * part : (n + 1) * part])
    grad_normed = dot(jnp.concatenate(parts, axis=0), w_ref[...], TN)
    standard, inv_scale = standardize(tile_ref[0].astype(F32))
    grad = inv_scale * (
        grad_normed
        - jnp.mean(grad_normed, axis=1, keepdims=True)
        - standard * jnp.mean(grad_normed * standard, axis=1, keepdims=True)
    )
    grad = grad.astype(BF)
    chooser = pack_matrix(shifts, ahead)
    for field, value in enumerate((update, grad)):
        out_ref[field] = value
        send_ref[field] = dot(chooser, value, NN).astype(BF)


def weight_kernel(windows, kept, spot, *refs):
    norms, tiles, ctxs, gps = (refs[n * windows : (n + 1) * windows] for n in range(4))
    out_ref = refs[-1]
    part = ctxs[0].shape[0]
    width = norms[0].shape[-1]

    def total(left, right, dims):
        return functools.reduce(jnp.add, (dot(a, b, dims) for a, b in zip(left, right)))

    side = spot[1] if kept else 1 - spot[1]

    @pl.when(side == 0)
    def _():
        out_ref[...] = total([n[...] for n in norms], [g[: 2 * part] for g in gps], TT)

    @pl.when(side == 1)
    def _():
        out_ref[:, :part] = total([n[...] for n in norms], [g[2 * part :] for g in gps], TT)
        proj = total([c[...] for c in ctxs], [t[1] for t in tiles], NN)
        half = width // 2
        out_ref[:part, part:] = proj[:, :half]
        out_ref[part:, part:] = proj[:, half:]


def halve_kernel(bit, spot, mine_ref, got_ref, keep_ref, send_ref):
    rows = keep_ref.shape[0]
    for side, ref in ((spot[bit], keep_ref), (1 - spot[bit], send_ref)):
        at = pl.ds(pl.multiple_of(side * rows, rows), rows)
        ref[...] = mine_ref[at] + got_ref[at]


def spread_kernel(spot, mine_ref, got_ref, out_ref):
    reach, rows = out_ref.shape[:2]
    for n in range(reach):
        here = slice(n * rows, (n + 1) * rows)
        out_ref[n] = mine_ref[here] + got_ref[here]


def gather_sum_kernel(got_ref, out_ref):
    total = functools.reduce(jnp.add, (got_ref[n] for n in range(got_ref.shape[0]))).astype(BF)
    for n in range(out_ref.shape[0]):
        out_ref[n] = total


def stack_kernel(first_ref, second_ref, out_ref):
    out_ref[0] = first_ref[...]
    out_ref[1] = second_ref[...]


def join_kernel(bit, spot, mine_ref, got_ref, out_ref):
    count = mine_ref.shape[1]
    for side, ref in ((spot[bit], mine_ref), (1 - spot[bit], got_ref)):
        for phase in range(mine_ref.shape[0]):
            for n in range(count):
                out_ref[phase, side * count + n] = ref[phase, n]


def gradient_kernel(factor, spot, mine_ref, got_ref, qkv_ref, proj_ref):
    width = proj_ref.shape[0]
    half = width // 2
    first = spot[1] == 0

    def write(pair_ref, rest_ref):
        count, rows = mine_ref.shape[1:3]
        for phase in range(len(PHASES)):
            at = phase * half
            for n in range(count):
                here = slice(n * rows, (n + 1) * rows)
                pair = pair_ref[phase, n].astype(F32) * factor
                rest = rest_ref[phase, n].astype(F32) * factor
                qkv_ref[here, at : at + half] = pair[:, :half]
                qkv_ref[here, width + at : width + at + half] = pair[:, half:]
                qkv_ref[here, 2 * width + at : 2 * width + at + half] = rest[:, :half]
                lower = n * rows >= half
                there = at + n * rows - (half if lower else 0)
                columns = slice(half, width) if lower else slice(0, half)
                proj_ref[there : there + rows, columns] = rest[:, half:]

    @pl.when(first)
    def _():
        write(mine_ref, got_ref)

    @pl.when(jnp.logical_not(first))
    def _():
        write(got_ref, mine_ref)


def turn_kernel(w_ref, out_ref):
    out_ref[...] = w_ref[...].T


def last_back_kernel(ahead, shifts, own_ref, got_ref, out_ref):
    taken, spread = unpack_matrix(shifts, ahead)
    for field in range(2):
        out_ref[field] = select_other(taken, spread, got_ref[field], own_ref[field]).astype(BF)


def finish_kernel(ahead, windows, shifts, x_ref, cot_ref, above_ref, final_ref, *refs):
    owns, gots = refs[: windows - 1], refs[windows - 1 : 2 * windows - 2]
    outs = refs[2 * windows - 2 :]
    part = WLAT * WLON
    grid = x_ref.shape[1]
    taken, spread = unpack_matrix(shifts, ahead)
    movers = []
    for level in range(LEV):
        cut = shifts[level, 0]
        slot, first, row = level_slots(windows, cut, 1)
        slot = jnp.where(jnp.logical_and(first, row >= cut), -1, slot)
        cells = lax.broadcasted_iota(I32, (grid, (windows + 1) * part), 0)
        movers.append((cells == slot).astype(F32).astype(BF))
    for field, ref in enumerate((x_ref, cot_ref)):
        tiles = [
            select_other(taken, spread, gots[w][field], owns[w][field]) for w in range(windows - 1)
        ]
        tiles += [final_ref[field].astype(F32), above_ref[field].astype(F32)]
        for level in range(LEV):
            here = slice(level * part, (level + 1) * part)
            source = jnp.concatenate([t[here] for t in tiles], axis=0).astype(BF)
            value = ref[level].astype(F32) + dot(movers[level], source, NN)
            outs[field][level] = value.astype(BF)


def route(pairs_of, lat, lon):
    return [
        (a * lon + o, pairs_of(a, o)[0] * lon + pairs_of(a, o)[1])
        for a in range(lat)
        for o in range(lon)
    ]


def across_core(a, o):
    return a ^ 1, o


def step_one(a, o):
    return (a, o ^ 1) if a % 2 else (a ^ 2, o)


def step_two(a, o):
    return (a ^ 2, o) if a % 2 else (a, o ^ 1)


def all_sum(weights, operands, spot, beside, earlier):
    lat, lon = lax.axis_size("lat"), lax.axis_size("lon")
    reach = lon // 2
    width = operands[0].shape[-1]

    def swap(value, pairs_of):
        return lax.ppermute(value, ("lat", "lon"), route(pairs_of, lat, lon))

    groups = [[o for o in range(lon) if o % 2 == side] for side in range(2)]

    def exchange(value):
        return lax.all_to_all(value, "lon", 0, 0, axis_index_groups=groups)

    sent = weights(False, operands, earlier)
    got = swap(sent, across_core)
    held = weights(True, operands, (sent,))
    after = ()
    for bit, pairs_of in ((2, step_one), (3, step_two)):
        rows = held.shape[0] // 2
        held, sent = call(
            functools.partial(halve_kernel, bit),
            (spot, held, got),
            [shape_of(F32, rows, width)] * 2,
            scalars=1,
            after=after,
        )
        got = swap(sent, pairs_of)
        after = beside(held)
    rows = held.shape[0] // reach
    pieces = call(
        spread_kernel, (spot, held, got), [shape_of(F32, reach, rows, width)], scalars=1, after=after
    )[0]
    got = exchange(pieces)
    after = beside(pieces)
    sums = call(gather_sum_kernel, (got,), [shape_of(BF, reach, rows, width)], after=after)[0]
    got = exchange(sums)
    after = beside(sums)
    other = tuple(e for e in earlier if e.shape == (reach, rows, width))
    if not other:
        return got
    return call(stack_kernel, (*other, got), [shape_of(BF, 2, reach, rows, width)], after=after)[0]


def all_gather(parts, spot, factor):
    lat, lon = lax.axis_size("lat"), lax.axis_size("lon")
    _, reach, rows, width = parts.shape
    held = parts.reshape(len(PHASES), 1, reach * rows, width)

    def swap(value, pairs_of):
        return lax.ppermute(value, ("lat", "lon"), route(pairs_of, lat, lon))

    for bit, pairs_of in ((3, step_two), (2, step_one)):
        phases, count, rows, width = held.shape
        held = call(
            functools.partial(join_kernel, bit),
            (spot, held, swap(held, pairs_of)),
            [shape_of(BF, phases, 2 * count, rows, width)],
            scalars=1,
        )[0]
    return call(
        functools.partial(gradient_kernel, factor),
        (spot, held, swap(held, across_core)),
        [shape_of(F32, width, 3 * width), shape_of(F32, width, width)],
        scalars=1,
    )


def body(ahead, tokens, cotangent, w_qkv, w_proj, shifts, region_ids):
    levels, lat_rows, lon_cols, width = tokens.shape

    def by_column(grid_field):
        return grid_field.transpose(0, 2, 1, 3).reshape(levels, lon_cols * lat_rows, width)

    tokens, cotangent = by_column(tokens), by_column(cotangent)
    windows = lat_rows // WLAT
    size = width // HEADS
    my_lat, my_lon = lax.axis_index("lat"), lax.axis_index("lon")
    core, high, low = my_lat & 1, my_lat >> 1, my_lon & 1
    spot = jnp.stack(
        [
            my_lat * lat_rows,
            core,
            jnp.where(core == 1, low, high),
            jnp.where(core == 1, high, low),
            my_lon >> 1,
        ]
    ).astype(I32)

    def ring(value, axis, step):
        count = lax.axis_size(axis)
        return lax.ppermute(value, axis, [(i, (i + step) % count) for i in range(count)])

    out_step = -1 if ahead else 1
    pair = shape_of(BF, 2, COUNT, width)
    packed = shape_of(BF, 2, PACKED, width)

    def packs(chosen, sent, after):
        return call(
            functools.partial(pack_kernel, ahead, windows, chosen, sent),
            (shifts, tokens, cotangent),
            [pair] * len(chosen) + [packed] * len(sent),
            scalars=1,
            after=after,
        )

    tile, send = packs((0,), (0,), ())
    gots = [ring(send, "lon", out_step)]
    next_tile, last, halo, send = packs((1, windows - 1, windows), (0,), (tile,))
    gots.append(ring(send, "lon", out_step))
    tiles = [tile, next_tile]
    w_t = call(turn_kernel, (w_qkv,), [shape_of(BF, 3 * width, width)], after=(last,))[0]
    below = ring(halo, "lat", -1)
    def parts(phase):
        part = PHASES[phase][1] * size
        return part, [shape_of(BF, part, COUNT), shape_of(BF, 3 * part, COUNT)]

    part, shapes = parts(0)
    firsts = []
    for w in range(windows):
        waits = [f[1] for f in firsts[-1:]]
        if 1 <= w < windows - 1:
            if w + 1 < windows - 1:
                tile, send = packs((w + 1,), (0,), waits)
            else:
                tile, send = call(
                    functools.partial(pack_last_kernel, ahead),
                    (shifts, last, below),
                    [pair, packed],
                    scalars=1,
                    after=waits,
                )
            gots.append(ring(send, "lon", out_step))
            tiles.append(tile)
            waits.append(send)
        firsts.append(
            call(
                functools.partial(first_kernel, ahead, w),
                (shifts, region_ids, spot, tiles[w], gots[w], w_t, w_proj),
                [pair, shape_of(BF, COUNT, width), *shapes],
                head_scratch(part, width),
                3,
                waits,
            )
        )
    norms = [f[1] for f in firsts]
    whole_tiles = [f[0] for f in firsts]

    def weights(kept, operands, after):
        return call(
            functools.partial(weight_kernel, windows, kept),
            (spot, *operands),
            [shape_of(F32, width, width)],
            scalars=1,
            after=after,
        )[0]

    part, shapes = parts(1)
    order = [windows - 1, *range(windows - 1)]
    seconds, backs = {}, {}

    ends = []

    def next_second(value):
        done = [seconds[w] for w in order[: len(seconds)]]
        w = order[len(done)]
        waits = [value]
        if len(done) == 2:
            final = call(
                functools.partial(last_back_kernel, ahead),
                (shifts, done[0][0], backs[order[0]]),
                [pair],
                scalars=1,
                after=(done[1][2],),
            )[0]
            ends.extend([final, ring(final, "lat", 1)])
            waits.append(final)
        if len(done) == 3:
            waits += [backs[order[1]], ends[1]]
        seconds[w] = call(
            functools.partial(second_kernel, ahead, w),
            (shifts, region_ids, spot, *firsts[w], w_t, w_proj),
            [pair, packed, *shapes],
            head_scratch(part, width),
            3,
            waits,
        )
        backs[w] = ring(seconds[w][1], "lon", -out_step)
        return (seconds[w][2],)

    sum_a = all_sum(
        weights,
        (*norms, *whole_tiles, *[f[2] for f in firsts], *[f[3] for f in firsts]),
        spot,
        next_second,
        (),
    )
    while len(seconds) < windows:
        next_second(seconds[order[len(seconds) - 1]][2])
    results = []

    def finish(value):
        if not results:
            results.extend(
                call(
                    functools.partial(finish_kernel, ahead, windows),
                    (
                        shifts, tokens, cotangent, ends[1], ends[0],
                        *[seconds[w][0] for w in range(windows - 1)],
                        *[backs[w] for w in range(windows - 1)],
                    ),
                    [shape_of(BF, *tokens.shape)] * 2,
                    scalars=1,
                    after=(value,),
                )
            )
            return ()
        return results[:1]

    sum_b = all_sum(
        weights,
        (
            *norms,
            *whole_tiles,
            *[seconds[w][2] for w in range(windows)],
            *[seconds[w][3] for w in range(windows)],
        ),
        spot,
        finish,
        (sum_a, backs[order[2]]),
    )
    mixed, grad_tokens = (
        r.reshape(levels, lon_cols, lat_rows, width).transpose(0, 2, 1, 3) for r in results
    )

    total_tokens = levels * lat_rows * lax.axis_size("lat") * lon_cols * lax.axis_size("lon")
    gradients = all_gather(sum_b, spot, 1.0 / math.sqrt(total_tokens))
    return (mixed, grad_tokens, *gradients)


def local(tokens, cotangent, w_qkv, w_proj, shifts, region_ids):
    return lax.cond(
        jnp.sum(shifts[:, 1]) <= ENTRIES,
        functools.partial(body, True),
        functools.partial(body, False),
        tokens, cotangent, w_qkv, w_proj, shifts, region_ids,
    )


def solution(mesh):
    return jax.shard_map(
        local,
        mesh=mesh,
        in_specs=(P(None, "lat", "lon", None), P(None, "lat", "lon", None), P(), P(), P(), P()),
        out_specs=(P(None, "lat", "lon", None), P(None, "lat", "lon", None), P(), P()),
        check_vma=False,
    )
```

```python
import functools
import math

import jax
import jax.numpy as jnp
from jax import lax
from jax.experimental import pallas as pl
from jax.experimental.pallas import tpu as pltpu
from jax.sharding import PartitionSpec as P

HEADS = 16
WLAT = 6
WLON = 12
LEV = 4
COUNT = LEV * WLAT * WLON
LANES = 384
ENTRIES = LEV * WLON // 2
PACKED = ENTRIES * WLAT
NORM_EPS = 1e-05
BARRED = 2.0**100
BF = jnp.bfloat16
F32 = jnp.float32
I32 = jnp.int32

NN = (((1,), (0,)), ((), ()))
NT = (((1,), (1,)), ((), ()))
TN = (((0,), (0,)), ((), ()))
TT = (((0,), (1,)), ((), ()))

SMEM = pl.BlockSpec(memory_space=pltpu.SMEM)
VMEM = pl.BlockSpec(memory_space=pltpu.VMEM)
ANY = pl.BlockSpec(memory_space=pl.ANY)


def dot(a, b, dims):
    return lax.dot_general(a, b, dims, preferred_element_type=F32)


def split_bf16(value):
    high = value.astype(BF)
    low = (value - high.astype(F32)).astype(BF)
    return high, low


def call(kernel, ins, outs, scratch=(), scalars=0, after=()):

    def ordered(*refs):
        kernel(*refs[: len(ins)], *refs[len(ins) + len(after) :])

    return pl.pallas_call(
        ordered,
        in_specs=[SMEM] * scalars + [VMEM] * (len(ins) - scalars) + [ANY] * len(after),
        out_specs=[VMEM] * len(outs),
        out_shape=list(outs),
        scratch_shapes=list(scratch),
        compiler_params=pltpu.CompilerParams(vmem_limit_bytes=24 * 1024 * 1024),
        cost_estimate=pl.CostEstimate(
            flops=1_000_000, bytes_accessed=10_000, transcendentals=0
        ),
    )(*ins, *after)


def shape_of(dtype, *dims):
    return jax.ShapeDtypeStruct(dims, dtype)


def place(axis):
    dims = (COUNT, 1) if axis == 0 else (1, COUNT)
    token = lax.broadcasted_iota(I32, dims, axis)
    level = sum((token >= n * WLAT * WLON).astype(I32) for n in range(1, LEV))
    column, row = column_and_row(token - level * (WLAT * WLON))
    return level, row, column


def column_and_row(rest):
    column = sum((rest >= n * WLAT).astype(I32) for n in range(1, WLON))
    return column, rest - column * WLAT


def level_slots(windows, cut, axis):
    part = WLAT * WLON
    size = (windows + 1) * part
    dims = (size, 1) if axis == 0 else (1, size)
    token = lax.broadcasted_iota(I32, dims, axis)
    window = sum((token >= n * part).astype(I32) for n in range(1, windows + 1))
    column, row = column_and_row(token - window * part)
    at = window * WLAT + row + jnp.where(row < cut, WLAT, 0)
    slot = jnp.where(at < windows * WLAT, column * (windows * WLAT) + at, -1)
    first = window == windows
    return jnp.where(first, column * (windows * WLAT) + row, slot), first, row


def by_level(level, values):
    result = jnp.full(level.shape, values[0], I32)
    for n in range(1, LEV):
        result = jnp.where(level == n, values[n], result)
    return result


def from_next_row(shifts, axis):
    level, row, _ = place(axis)
    return row < by_level(level, [shifts[n, 0] for n in range(LEV)])


def from_other_side(shifts, ahead, axis):
    level, row, column = place(axis)
    cut = [shifts[n, 1] for n in range(LEV)]
    counts = cut if ahead else [WLON - c for c in cut]
    starts = [0] * LEV if ahead else cut
    offsets = [0]
    for n in range(LEV - 1):
        offsets.append(offsets[-1] + counts[n])
    at = by_level(level, cut)
    taken = (column < at) if ahead else (column >= at)
    entry = by_level(level, [o - s for o, s in zip(offsets, starts)]) + column
    return taken, jnp.where(taken, entry * WLAT + row, -1)


def pack_matrix(shifts, ahead):
    _, slot = from_other_side(shifts, ahead, 1)
    rows = lax.broadcasted_iota(I32, (PACKED, COUNT), 0)
    return (rows == slot).astype(F32).astype(BF)


def unpack_matrix(shifts, ahead):
    taken, slot = from_other_side(shifts, ahead, 0)
    columns = lax.broadcasted_iota(I32, (COUNT, PACKED), 1)
    return taken, (columns == slot).astype(F32).astype(BF)


def select_other(taken, spread, packed, own):
    return jnp.where(taken, dot(spread, packed, NN), own.astype(F32))


def pack_kernel(ahead, windows, first, shifts, x_ref, cot_ref, *refs):
    part = WLAT * WLON
    grid = x_ref.shape[1]
    if first:
        count = 2
        tile_refs, send_refs, (halo_ref,) = refs[:1], refs[1:2], refs[2:]
    else:
        count = windows - 1
        tile_refs, send_refs = refs[:count], refs[count:]
    chooser = pack_matrix(shifts, ahead)
    parts = [[[None] * LEV for _ in range(count)] for _ in range(2)]
    for level in range(LEV):
        slot, _, _ = level_slots(windows, shifts[level, 0], 0)
        if first:
            slot = jnp.concatenate([slot[:part], slot[windows * part :]], axis=0)
        else:
            slot = slot[part : windows * part]
        cells = lax.broadcasted_iota(I32, (count * part, grid), 1)
        mover = (cells == slot).astype(F32).astype(BF)
        for field, ref in enumerate((x_ref, cot_ref)):
            moved = dot(mover, ref[level], NN)
            for w in range(count):
                parts[field][w][level] = moved[w * part : (w + 1) * part]
    for field in range(2):
        whole = [jnp.concatenate(p, axis=0).astype(BF) for p in parts[field]]
        for tile_ref, tile in zip(tile_refs, whole):
            tile_ref[field] = tile
        for send_ref, tile in zip(send_refs, whole):
            send_ref[field] = dot(chooser, tile, NN).astype(BF)
        if first:
            halo_ref[field] = whole[1]


def pack_last_kernel(ahead, shifts, last_ref, halo_ref, tile_ref, send_ref):
    lower = from_next_row(shifts, 0)
    chooser = pack_matrix(shifts, ahead)
    for field in range(2):
        tile = jnp.where(lower, halo_ref[field].astype(F32), last_ref[field].astype(F32))
        tile_ref[field] = tile.astype(BF)
        send_ref[field] = dot(chooser, tile.astype(BF), NN).astype(BF)


def standardize(values_full):
    center = values_full - jnp.mean(values_full, axis=1, keepdims=True)
    variance = jnp.mean(center * center, axis=1, keepdims=True)
    inv_scale = lax.rsqrt(variance + NORM_EPS)
    return center * inv_scale, inv_scale


def bars(shifts, ids, first_row, grid_rows, bar_q, bar_k):
    level, row, _ = place(1)
    wrapped = jnp.where(row < by_level(level, [shifts[n, 0] for n in range(LEV)]), WLAT, 0)
    at = first_row + row + wrapped
    at = jnp.where(at >= grid_rows, at - grid_rows, at)
    top = sum((ids[n] == ids[0]).astype(I32) for n in range(WLAT - 1))
    bottom = sum((ids[grid_rows - 1 - n] == ids[grid_rows - 1]).astype(I32) for n in range(WLAT - 1))
    kind = jnp.where(at < top, 1, jnp.where(at >= grid_rows - bottom, 2, 0))
    features = lax.broadcasted_iota(I32, (32, COUNT), 0)
    same = (features == kind).astype(F32)
    bar_q[...] = jnp.zeros_like(bar_q)
    bar_q[:, :COUNT] = (same * -BARRED).astype(BF)
    bar_k[...] = jnp.zeros_like(bar_k)
    bar_k[:, :COUNT] = jnp.where(features < 3, 1.0 - same, 0.0).astype(BF)


def attend(size, bar_q, bar_k, q_s, k_s, v_s, g_s, buffers, ctx_ref, gp_ref):
    scale = 1.0 / math.sqrt(size)
    heads = HEADS
    part = heads * size

    def rows_of(h):
        return pl.ds(pl.multiple_of(h * size, size), size)

    def products(h, buffer):
        score_b, grad_b = buffer[:2]
        rows = rows_of(h)
        q_high, q_low = split_bf16(q_s[rows])
        k_high, k_low = split_bf16(k_s[rows])
        q_all = jnp.concatenate([q_high, q_low, q_high, bar_q[...]], axis=0)
        k_all = jnp.concatenate([k_high, k_high, k_low, bar_k[...]], axis=0)
        score_b[...] = dot(k_all.T[:COUNT], q_all, NN)
        grad_b[...] = dot(v_s[rows].T[:COUNT], g_s[rows], NN)

    def soften(buffer):
        score_b, grad_b, weight_b, high_b, low_b = buffer
        for start in range(0, LANES, 128):
            lanes = slice(start, start + 128)
            scores = score_b[:, lanes]
            expo = jnp.exp2(scores - jnp.max(scores, axis=0, keepdims=True))
            weights = expo * (1.0 / jnp.sum(expo, axis=0, keepdims=True))
            weight_b[:, lanes] = weights.astype(BF)
            grad_w = grad_b[:, lanes]
            grad_sc = weights * (grad_w - jnp.sum(weights * grad_w, axis=0, keepdims=True))
            high_b[:, lanes], low_b[:, lanes] = split_bf16(grad_sc)

    def results(h, buffer):
        weight_b, high_b, low_b = buffer[2:]
        rows = rows_of(h)
        q_high, q_low = split_bf16(q_s[rows])
        k_high, k_low = split_bf16(k_s[rows])
        rounded, high, low = weight_b[...], high_b[...], low_b[...]
        ctx_ref[rows] = dot(v_s[rows][:, :COUNT], rounded, NN)[:, :COUNT].astype(BF)
        k_pair = jnp.concatenate([k_high[:, :COUNT], k_low[:, :COUNT]], axis=0)
        q_pair = jnp.concatenate([q_high, q_low], axis=0)
        gq = dot(k_pair, high, NN)
        gq = gq[:size] + gq[size:] + dot(k_high[:, :COUNT], low, NN)
        gk = dot(q_pair, high, NT)
        gk = gk[:size] + gk[size:] + dot(q_high, low, NT)
        gv = dot(g_s[rows], rounded, NT)
        base = pl.multiple_of(h * size, size)
        gp_ref[pl.ds(base, size)] = (gq[:, :COUNT] * scale).astype(BF)
        gp_ref[pl.ds(part + base, size)] = (gk * math.log(2.0)).astype(BF)
        gp_ref[pl.ds(2 * part + base, size)] = gv.astype(BF)

    even, odd = buffers[:5], buffers[5:]
    products(0, even)

    def pair(p, carry):
        h = 2 * p
        products(h + 1, odd)
        soften(even)
        results(jnp.maximum(h - 1, 0), odd)
        products(jnp.minimum(h + 2, heads - 1), even)
        soften(odd)
        results(h, even)
        return carry

    lax.fori_loop(0, heads // 2, pair, 0)
    results(heads - 1, odd)


def project(w_ref, wp_ref, norm_s, cot_s, q_s, k_s, v_s, g_s):
    norm = norm_s[...]
    width = norm.shape[1]
    factor = math.log2(math.e) / math.sqrt(width // HEADS)
    q_s[...] = dot(w_ref[:width], norm, NT) * factor
    k_s[...] = dot(w_ref[width : 2 * width], norm, NT)
    v_s[...] = dot(w_ref[2 * width :], norm, NT).astype(BF)
    g_s[...] = dot(wp_ref[...], cot_s[...], NT).astype(BF)


def head_scratch(width):
    return [
        pltpu.VMEM((LANES, width), BF),
        pltpu.VMEM((LANES, width), BF),
        pltpu.VMEM((32, LANES), BF),
        pltpu.VMEM((32, LANES), BF),
        pltpu.VMEM((width, LANES), F32),
        pltpu.VMEM((width, LANES), F32),
        pltpu.VMEM((width, LANES), BF),
        pltpu.VMEM((width, LANES), BF),
    ] + [
        pltpu.VMEM((COUNT, LANES), kind) for _ in range(2) for kind in (F32, F32, BF, BF, BF)
    ]


def window_kernel(
    ahead, window, shifts, ids, spot, own_ref, got_ref, w_ref, wp_ref,
    tile_ref, norm_ref, ctx_ref, gp_ref,
    norm_s, cot_s, bar_q, bar_k, q_s, k_s, v_s, g_s, *buffers,
):
    width = own_ref.shape[-1]
    taken, spread = unpack_matrix(shifts, ahead)
    x = select_other(taken, spread, got_ref[0], own_ref[0])
    cot = select_other(taken, spread, got_ref[1], own_ref[1]).astype(BF)
    tile_ref[0] = x.astype(BF)
    tile_ref[1] = cot
    normed = standardize(x)[0].astype(BF)
    norm_ref[...] = normed
    norm_s[:COUNT] = normed
    norm_s[COUNT:] = jnp.zeros((LANES - COUNT, width), BF)
    cot_s[:COUNT] = cot
    cot_s[COUNT:] = jnp.zeros((LANES - COUNT, width), BF)
    bars(shifts, ids, spot[0] + window * WLAT, ids.shape[0], bar_q, bar_k)
    project(w_ref, wp_ref, norm_s, cot_s, q_s, k_s, v_s, g_s)
    attend(width // HEADS, bar_q, bar_k, q_s, k_s, v_s, g_s, buffers, ctx_ref, gp_ref)


def close_kernel(ahead, shifts, tile_ref, ctx_ref, gp_ref, w_ref, wp_ref, out_ref, send_ref):
    update = dot(ctx_ref[...], wp_ref[...], TN).astype(BF)
    grad_normed = dot(gp_ref[...], w_ref[...], TN)
    standard, inv_scale = standardize(tile_ref[0].astype(F32))
    grad = inv_scale * (
        grad_normed
        - jnp.mean(grad_normed, axis=1, keepdims=True)
        - standard * jnp.mean(grad_normed * standard, axis=1, keepdims=True)
    )
    grad = grad.astype(BF)
    chooser = pack_matrix(shifts, ahead)
    for field, value in enumerate((update, grad)):
        out_ref[field] = value
        send_ref[field] = dot(chooser, value, NN).astype(BF)


def weight_kernel(windows, kept, spot, *refs):
    norms, tiles, ctxs, gps = (refs[n * windows : (n + 1) * windows] for n in range(4))
    out_ref = refs[-1]
    part = ctxs[0].shape[0]

    def total(left, right):
        return functools.reduce(jnp.add, (dot(a, b, TT) for a, b in zip(left, right)))

    side = spot[1] if kept else 1 - spot[1]

    @pl.when(side == 0)
    def _():
        out_ref[...] = total([n[...] for n in norms], [g[: 2 * part] for g in gps])

    @pl.when(side == 1)
    def _():
        out_ref[:, :part] = total([n[...] for n in norms], [g[2 * part :] for g in gps])
        out_ref[:, part:] = total([t[1] for t in tiles], [c[...] for c in ctxs])


def halve_kernel(bit, gots, spot, mine_ref, *refs):
    got_refs, (keep_ref, *send_refs), total = refs[:gots], refs[gots:-1], refs[-1]
    rows = keep_ref.shape[0]
    piece = got_refs[0].shape[0]
    for n, got_ref in enumerate(got_refs):
        here = slice(n * piece, (n + 1) * piece)
        total[here] = mine_ref[here] + got_ref[...]
    keep_ref[...] = total[pl.ds(pl.multiple_of(spot[bit] * rows, rows), rows)]
    part = send_refs[0].shape[0]
    for n, ref in enumerate(send_refs):
        ref[...] = total[pl.ds(pl.multiple_of((1 - spot[bit]) * rows + n * part, part), part)]


def spread_kernel(spot, mine_ref, got_ref, *out_refs):
    rows = out_refs[0].shape[0]
    for d, ref in enumerate(out_refs):
        at = pl.ds(pl.multiple_of((spot[4] ^ d) * rows, rows), rows)
        ref[...] = mine_ref[at] + got_ref[at]


def gather_sum_kernel(*refs):
    refs[-1][...] = functools.reduce(jnp.add, (r[...] for r in refs[:-1])).astype(BF)


def arrange_kernel(spot, *refs):
    for d, ref in enumerate(refs[:-1]):
        refs[-1][spot[4] ^ d] = ref[...]


def join_kernel(bit, spot, mine_ref, got_ref, out_ref):
    count = mine_ref.shape[0]
    for side, ref in ((spot[bit], mine_ref), (1 - spot[bit], got_ref)):
        for n in range(count):
            out_ref[side * count + n] = ref[n]


def gradient_kernel(factor, spot, mine_ref, got_ref, qkv_ref, proj_ref):
    width = proj_ref.shape[0]
    count, rows = mine_ref.shape[:2]

    def write(pair_ref, rest_ref):
        for n in range(count):
            here = slice(n * rows, (n + 1) * rows)
            rest = rest_ref[n].astype(F32) * factor
            qkv_ref[here, : 2 * width] = pair_ref[n].astype(F32) * factor
            qkv_ref[here, 2 * width :] = rest[:, :width]
            proj_ref[:, here] = rest[:, width:].T

    first = spot[1] == 0

    @pl.when(first)
    def _():
        write(mine_ref, got_ref)

    @pl.when(jnp.logical_not(first))
    def _():
        write(got_ref, mine_ref)


def turn_kernel(w_ref, out_ref):
    out_ref[...] = w_ref[...].T


def last_back_kernel(ahead, shifts, own_ref, got_ref, out_ref):
    taken, spread = unpack_matrix(shifts, ahead)
    for field in range(2):
        out_ref[field] = select_other(taken, spread, got_ref[field], own_ref[field]).astype(BF)


def finish_kernel(ahead, windows, shifts, x_ref, cot_ref, above_ref, final_ref, *refs):
    owns, gots = refs[: windows - 1], refs[windows - 1 : 2 * windows - 2]
    outs = refs[2 * windows - 2 :]
    part = WLAT * WLON
    grid = x_ref.shape[1]
    taken, spread = unpack_matrix(shifts, ahead)
    movers = []
    for level in range(LEV):
        cut = shifts[level, 0]
        slot, first, row = level_slots(windows, cut, 1)
        slot = jnp.where(jnp.logical_and(first, row >= cut), -1, slot)
        cells = lax.broadcasted_iota(I32, (grid, (windows + 1) * part), 0)
        movers.append((cells == slot).astype(F32).astype(BF))
    for field, ref in enumerate((x_ref, cot_ref)):
        tiles = [
            select_other(taken, spread, gots[w][field], owns[w][field]) for w in range(windows - 1)
        ]
        tiles += [final_ref[field].astype(F32), above_ref[field].astype(F32)]
        for level in range(LEV):
            here = slice(level * part, (level + 1) * part)
            source = jnp.concatenate([t[here] for t in tiles], axis=0).astype(BF)
            value = ref[level].astype(F32) + dot(movers[level], source, NN)
            outs[field][level] = value.astype(BF)


def route(pairs_of, lat, lon):
    return [
        (a * lon + o, pairs_of(a, o)[0] * lon + pairs_of(a, o)[1])
        for a in range(lat)
        for o in range(lon)
    ]


def across_core(a, o):
    return a ^ 1, o


def step_one(a, o):
    return (a, o ^ 1) if a % 2 else (a ^ 2, o)


def step_two(a, o):
    return (a ^ 2, o) if a % 2 else (a, o ^ 1)


def all_sum(weights, spot, beside, earlier):
    lat, lon = lax.axis_size("lat"), lax.axis_size("lon")
    reach = lon // 2

    def swap(value, pairs_of):
        return lax.ppermute(value, ("lat", "lon"), route(pairs_of, lat, lon))

    def along(d):
        return lambda a, o: (a, o ^ (2 * d))

    sent = weights(False, earlier)
    got = swap(sent, across_core)
    held = weights(True, (sent,))
    after = beside(held)
    for bit, pairs_of in ((2, step_one), (3, step_two)):
        rows, width = held.shape[0] // 2, held.shape[1]
        held, sent = call(
            functools.partial(halve_kernel, bit, 1),
            (spot, held, got),
            [shape_of(F32, rows, width)] * 2,
            [pltpu.VMEM(held.shape, F32)],
            scalars=1,
            after=after,
        )
        got = swap(sent, pairs_of)
        after = beside(held)
    rows = held.shape[0] // reach
    pieces = call(
        spread_kernel, (spot, held, got), [shape_of(F32, rows, width)] * reach, scalars=1, after=after
    )
    gots = [swap(pieces[d], along(d)) for d in range(1, reach)]
    after = beside(pieces[0])
    sums = call(gather_sum_kernel, (pieces[0], *gots), [shape_of(BF, rows, width)], after=after)[0]
    gots = [swap(sums, along(d)) for d in range(1, reach)]
    after = beside(sums)
    part = call(
        arrange_kernel, (spot, sums, *gots), [shape_of(BF, reach, rows, width)], scalars=1, after=after
    )[0]
    held = part.reshape(1, reach * rows, width)
    for bit, pairs_of in ((3, step_two), (2, step_one)):
        got = swap(held, pairs_of)
        after = beside(held)
        held = call(
            functools.partial(join_kernel, bit),
            (spot, held, got),
            [shape_of(BF, 2 * held.shape[0], *held.shape[1:])],
            scalars=1,
            after=after,
        )[0]
    return held, swap(held, across_core)


def ring(value, axis, step):
    count = lax.axis_size(axis)
    return lax.ppermute(value, axis, [(i, (i + step) % count) for i in range(count)])


def body(ahead, tokens, cotangent, w_qkv, w_proj, shifts, region_ids):
    levels, lat_rows, lon_cols, width = tokens.shape

    def by_column(grid_field):
        return grid_field.transpose(0, 2, 1, 3).reshape(levels, lon_cols * lat_rows, width)

    tokens, cotangent = by_column(tokens), by_column(cotangent)
    windows = lat_rows // WLAT
    my_lat, my_lon = lax.axis_index("lat"), lax.axis_index("lon")
    core, high, low = my_lat & 1, my_lat >> 1, my_lon & 1
    spot = jnp.stack(
        [
            my_lat * lat_rows,
            core,
            jnp.where(core == 1, low, high),
            jnp.where(core == 1, high, low),
            my_lon >> 1,
        ]
    ).astype(I32)

    out_step = -1 if ahead else 1
    pair = shape_of(BF, 2, COUNT, width)
    packed = shape_of(BF, 2, PACKED, width)
    arrays = (shifts, tokens, cotangent)
    tile, send, halo = call(
        functools.partial(pack_kernel, ahead, windows, True), arrays, [pair, packed, pair], scalars=1
    )
    made = call(
        functools.partial(pack_kernel, ahead, windows, False),
        arrays,
        [pair] * (windows - 1) + [packed] * (windows - 2),
        scalars=1,
        after=(tile,),
    )
    tiles, last = [tile, *made[: windows - 2]], made[windows - 2]
    w_t = call(turn_kernel, (w_qkv,), [shape_of(BF, 3 * width, width)], after=(last,))[0]
    below = ring(halo, "lat", -1)
    gots = [ring(s, "lon", out_step) for s in (send, *made[windows - 1 :])]
    firsts, closed = [], {}

    def window(w, after):
        firsts.append(
            call(
                functools.partial(window_kernel, ahead, w),
                (shifts, region_ids, spot, tiles[w], gots[w], w_t, w_proj),
                [
                    pair,
                    shape_of(BF, COUNT, width),
                    shape_of(BF, width, COUNT),
                    shape_of(BF, 3 * width, COUNT),
                ],
                head_scratch(width),
                scalars=3,
                after=after,
            )
        )
        return (firsts[w][1],)

    def close(w, after):
        tile, _, context, grads = firsts[w]
        out, send = call(
            functools.partial(close_kernel, ahead),
            (shifts, tile, context, grads, w_t, w_proj),
            [pair, packed],
            scalars=1,
            after=after,
        )
        closed[w] = out, ring(send, "lon", -out_step)
        return (send,)

    after = ()
    for w in range(windows):
        if w == 1:
            tile, send = call(
                functools.partial(pack_last_kernel, ahead),
                (shifts, last, below),
                [pair, packed],
                scalars=1,
                after=after,
            )
            tiles.append(tile)
            gots.append(ring(send, "lon", out_step))
            after = (send,)
        if w >= 2:
            after = (*after, closed[w - 2][1])
        after = window(w, after)
        if w < windows - 2:
            after = close(w, after)

    operands = [[f[n] for f in firsts] for n in (1, 0, 2, 3)]
    operands = [a for group in operands for a in group]

    def weights(kept, after):
        return call(
            functools.partial(weight_kernel, windows, kept),
            (spot, *operands),
            [shape_of(F32, width, 2 * width)],
            scalars=1,
            after=after,
        )[0]

    stage, ends = [], []

    def beside(value):
        stage.append(value)
        if len(stage) == 1:
            return close(windows - 1, (value,))
        if len(stage) == 2:
            return close(windows - 2, (value, closed[windows - 1][1]))
        if len(stage) == 3:
            final = call(
                functools.partial(last_back_kernel, ahead),
                (shifts, *closed[windows - 1]),
                [pair],
                scalars=1,
                after=(value,),
            )[0]
            ends.extend([final, ring(final, "lat", 1)])
            return (final, closed[windows - 2][1])
        if len(stage) == 4:
            return (ends[1],)
        if len(stage) == 5:
            ends.extend(
                call(
                    functools.partial(finish_kernel, ahead, windows),
                    (
                        shifts, tokens, cotangent, ends[1], ends[0],
                        *[closed[w][0] for w in range(windows - 1)],
                        *[closed[w][1] for w in range(windows - 1)],
                    ),
                    [shape_of(BF, *tokens.shape)] * 2,
                    scalars=1,
                    after=(value,),
                )
            )
            return (ends[2],)
        return ()

    summed = all_sum(weights, spot, beside, (closed[windows - 3][1],))
    mixed, grad_tokens = (
        r.reshape(levels, lon_cols, lat_rows, width).transpose(0, 2, 1, 3) for r in ends[2:]
    )
    total_tokens = levels * lat_rows * lax.axis_size("lat") * lon_cols * lax.axis_size("lon")
    gradients = call(
        functools.partial(gradient_kernel, 1.0 / math.sqrt(total_tokens)),
        (spot, *summed),
        [shape_of(F32, width, 3 * width), shape_of(F32, width, width)],
        scalars=1,
    )
    return (mixed, grad_tokens, *gradients)


def local(tokens, cotangent, w_qkv, w_proj, shifts, region_ids):
    return lax.cond(
        jnp.sum(shifts[:, 1]) <= ENTRIES,
        functools.partial(body, True),
        functools.partial(body, False),
        tokens, cotangent, w_qkv, w_proj, shifts, region_ids,
    )


def solution(mesh):
    return jax.shard_map(
        local,
        mesh=mesh,
        in_specs=(P(None, "lat", "lon", None), P(None, "lat", "lon", None), P(), P(), P(), P()),
        out_specs=(P(None, "lat", "lon", None), P(None, "lat", "lon", None), P(), P()),
        check_vma=False,
    )
```

```python
import functools
import math

import jax
import jax.numpy as jnp
from jax import lax
from jax.experimental import pallas as pl
from jax.experimental.pallas import tpu as pltpu
from jax.sharding import PartitionSpec as P

HEADS = 16
WLAT = 6
WLON = 12
LEV = 4
COUNT = LEV * WLAT * WLON
LANES = 384
ENTRIES = LEV * WLON // 2
PACKED = ENTRIES * WLAT
NORM_EPS = 1e-05
BARRED = 2.0**100
BF = jnp.bfloat16
F32 = jnp.float32
I32 = jnp.int32

NN = (((1,), (0,)), ((), ()))
NT = (((1,), (1,)), ((), ()))
TN = (((0,), (0,)), ((), ()))
TT = (((0,), (1,)), ((), ()))

SMEM = pl.BlockSpec(memory_space=pltpu.SMEM)
VMEM = pl.BlockSpec(memory_space=pltpu.VMEM)
ANY = pl.BlockSpec(memory_space=pl.ANY)


def dot(a, b, dims):
    return lax.dot_general(a, b, dims, preferred_element_type=F32)


def split_bf16(value):
    high = value.astype(BF)
    low = (value - high.astype(F32)).astype(BF)
    return high, low


def call(kernel, ins, outs, scratch=(), scalars=0, after=()):

    def ordered(*refs):
        kernel(*refs[: len(ins)], *refs[len(ins) + len(after) :])

    return pl.pallas_call(
        ordered,
        in_specs=[SMEM] * scalars + [VMEM] * (len(ins) - scalars) + [ANY] * len(after),
        out_specs=[VMEM] * len(outs),
        out_shape=list(outs),
        scratch_shapes=list(scratch),
        compiler_params=pltpu.CompilerParams(vmem_limit_bytes=24 * 1024 * 1024),
        cost_estimate=pl.CostEstimate(
            flops=1_000_000, bytes_accessed=10_000, transcendentals=0
        ),
    )(*ins, *after)


def shape_of(dtype, *dims):
    return jax.ShapeDtypeStruct(dims, dtype)


def place(axis):
    dims = (COUNT, 1) if axis == 0 else (1, COUNT)
    token = lax.broadcasted_iota(I32, dims, axis)
    level = sum((token >= n * WLAT * WLON).astype(I32) for n in range(1, LEV))
    column, row = column_and_row(token - level * (WLAT * WLON))
    return level, row, column


def column_and_row(rest):
    column = sum((rest >= n * WLAT).astype(I32) for n in range(1, WLON))
    return column, rest - column * WLAT


def level_slots(windows, cut, axis):
    part = WLAT * WLON
    size = (windows + 1) * part
    dims = (size, 1) if axis == 0 else (1, size)
    token = lax.broadcasted_iota(I32, dims, axis)
    window = sum((token >= n * part).astype(I32) for n in range(1, windows + 1))
    column, row = column_and_row(token - window * part)
    at = window * WLAT + row + jnp.where(row < cut, WLAT, 0)
    slot = jnp.where(at < windows * WLAT, column * (windows * WLAT) + at, -1)
    first = window == windows
    return jnp.where(first, column * (windows * WLAT) + row, slot), first, row


def by_level(level, values):
    result = jnp.full(level.shape, values[0], I32)
    for n in range(1, LEV):
        result = jnp.where(level == n, values[n], result)
    return result


def from_next_row(shifts, axis):
    level, row, _ = place(axis)
    return row < by_level(level, [shifts[n, 0] for n in range(LEV)])


def from_other_side(shifts, ahead, axis):
    level, row, column = place(axis)
    cut = [shifts[n, 1] for n in range(LEV)]
    counts = cut if ahead else [WLON - c for c in cut]
    starts = [0] * LEV if ahead else cut
    offsets = [0]
    for n in range(LEV - 1):
        offsets.append(offsets[-1] + counts[n])
    at = by_level(level, cut)
    taken = (column < at) if ahead else (column >= at)
    entry = by_level(level, [o - s for o, s in zip(offsets, starts)]) + column
    return taken, jnp.where(taken, entry * WLAT + row, -1)


def pack_matrix(shifts, ahead):
    _, slot = from_other_side(shifts, ahead, 1)
    rows = lax.broadcasted_iota(I32, (PACKED, COUNT), 0)
    return (rows == slot).astype(F32).astype(BF)


def unpack_matrix(shifts, ahead):
    taken, slot = from_other_side(shifts, ahead, 0)
    columns = lax.broadcasted_iota(I32, (COUNT, PACKED), 1)
    return taken, (columns == slot).astype(F32).astype(BF)


def select_other(taken, spread, packed, own):
    return jnp.where(taken, dot(spread, packed, NN), own.astype(F32))


def pack_kernel(ahead, windows, first, shifts, x_ref, cot_ref, *refs):
    part = WLAT * WLON
    grid = x_ref.shape[1]
    if first:
        count = 2
        tile_refs, send_refs, (halo_ref,) = refs[:1], refs[1:2], refs[2:]
    else:
        count = windows - 1
        tile_refs, send_refs = refs[:count], refs[count:]
    chooser = pack_matrix(shifts, ahead)
    parts = [[[None] * LEV for _ in range(count)] for _ in range(2)]
    for level in range(LEV):
        slot, _, _ = level_slots(windows, shifts[level, 0], 0)
        if first:
            slot = jnp.concatenate([slot[:part], slot[windows * part :]], axis=0)
        else:
            slot = slot[part : windows * part]
        cells = lax.broadcasted_iota(I32, (count * part, grid), 1)
        mover = (cells == slot).astype(F32).astype(BF)
        for field, ref in enumerate((x_ref, cot_ref)):
            moved = dot(mover, ref[level], NN)
            for w in range(count):
                parts[field][w][level] = moved[w * part : (w + 1) * part]
    for field in range(2):
        whole = [jnp.concatenate(p, axis=0).astype(BF) for p in parts[field]]
        for tile_ref, tile in zip(tile_refs, whole):
            tile_ref[field] = tile
        for send_ref, tile in zip(send_refs, whole):
            send_ref[field] = dot(chooser, tile, NN).astype(BF)
        if first:
            halo_ref[field] = whole[1]


def pack_last_kernel(ahead, shifts, last_ref, halo_ref, tile_ref, send_ref):
    lower = from_next_row(shifts, 0)
    chooser = pack_matrix(shifts, ahead)
    for field in range(2):
        tile = jnp.where(lower, halo_ref[field].astype(F32), last_ref[field].astype(F32))
        tile_ref[field] = tile.astype(BF)
        send_ref[field] = dot(chooser, tile.astype(BF), NN).astype(BF)


def standardize(values_full):
    center = values_full - jnp.mean(values_full, axis=1, keepdims=True)
    variance = jnp.mean(center * center, axis=1, keepdims=True)
    inv_scale = lax.rsqrt(variance + NORM_EPS)
    return center * inv_scale, inv_scale


def bars(shifts, ids, first_row, grid_rows, bar_q, bar_k):
    level, row, _ = place(1)
    wrapped = jnp.where(row < by_level(level, [shifts[n, 0] for n in range(LEV)]), WLAT, 0)
    at = first_row + row + wrapped
    at = jnp.where(at >= grid_rows, at - grid_rows, at)
    top = sum((ids[n] == ids[0]).astype(I32) for n in range(WLAT - 1))
    bottom = sum((ids[grid_rows - 1 - n] == ids[grid_rows - 1]).astype(I32) for n in range(WLAT - 1))
    kind = jnp.where(at < top, 1, jnp.where(at >= grid_rows - bottom, 2, 0))
    features = lax.broadcasted_iota(I32, (32, COUNT), 0)
    same = (features == kind).astype(F32)
    bar_q[...] = jnp.zeros_like(bar_q)
    bar_q[:, :COUNT] = (same * -BARRED).astype(BF)
    bar_k[...] = jnp.zeros_like(bar_k)
    bar_k[:, :COUNT] = jnp.where(features < 3, 1.0 - same, 0.0).astype(BF)


def attend(size, bar_q, bar_k, q_s, k_s, v_s, g_s, buffers, ctx_ref, gp_ref):
    scale = 1.0 / math.sqrt(size)
    heads = HEADS
    part = heads * size

    def rows_of(h):
        return pl.ds(pl.multiple_of(h * size, size), size)

    def products(h, buffer):
        score_b, grad_b = buffer[:2]
        rows = rows_of(h)
        q_high, q_low = split_bf16(q_s[rows])
        k_high, k_low = split_bf16(k_s[rows])
        q_all = jnp.concatenate([q_high, q_low, q_high, bar_q[...]], axis=0)
        k_all = jnp.concatenate([k_high, k_high, k_low, bar_k[...]], axis=0)
        score_b[...] = dot(k_all.T[:COUNT], q_all, NN)
        grad_b[...] = dot(v_s[rows].T[:COUNT], g_s[rows], NN)

    def soften(buffer):
        score_b, grad_b, weight_b, high_b, low_b = buffer
        for start in range(0, LANES, 128):
            lanes = slice(start, start + 128)
            scores = score_b[:, lanes]
            expo = jnp.exp2(scores - jnp.max(scores, axis=0, keepdims=True))
            weights = expo * (1.0 / jnp.sum(expo, axis=0, keepdims=True))
            weight_b[:, lanes] = weights.astype(BF)
            grad_w = grad_b[:, lanes]
            grad_sc = weights * (grad_w - jnp.sum(weights * grad_w, axis=0, keepdims=True))
            high_b[:, lanes], low_b[:, lanes] = split_bf16(grad_sc)

    def results(h, buffer):
        weight_b, high_b, low_b = buffer[2:]
        rows = rows_of(h)
        q_high, q_low = split_bf16(q_s[rows])
        k_high, k_low = split_bf16(k_s[rows])
        rounded, high, low = weight_b[...], high_b[...], low_b[...]
        ctx_ref[rows] = dot(v_s[rows][:, :COUNT], rounded, NN)[:, :COUNT].astype(BF)
        k_pair = jnp.concatenate([k_high[:, :COUNT], k_low[:, :COUNT]], axis=0)
        q_pair = jnp.concatenate([q_high, q_low], axis=0)
        gq = dot(k_pair, high, NN)
        gq = gq[:size] + gq[size:] + dot(k_high[:, :COUNT], low, NN)
        gk = dot(q_pair, high, NT)
        gk = gk[:size] + gk[size:] + dot(q_high, low, NT)
        gv = dot(g_s[rows], rounded, NT)
        base = pl.multiple_of(h * size, size)
        gp_ref[pl.ds(base, size)] = (gq[:, :COUNT] * scale).astype(BF)
        gp_ref[pl.ds(part + base, size)] = (gk * math.log(2.0)).astype(BF)
        gp_ref[pl.ds(2 * part + base, size)] = gv.astype(BF)

    even, odd = buffers[:5], buffers[5:]
    products(0, even)

    def pair(p, carry):
        h = 2 * p
        products(h + 1, odd)
        soften(even)
        results(jnp.maximum(h - 1, 0), odd)
        products(jnp.minimum(h + 2, heads - 1), even)
        soften(odd)
        results(h, even)
        return carry

    lax.fori_loop(0, heads // 2, pair, 0)
    results(heads - 1, odd)


def project(w_ref, wp_ref, norm_s, cot_s, q_s, k_s, v_s, g_s):
    norm = norm_s[...]
    width = norm.shape[1]
    factor = math.log2(math.e) / math.sqrt(width // HEADS)
    q_s[...] = dot(w_ref[:width], norm, NT) * factor
    k_s[...] = dot(w_ref[width : 2 * width], norm, NT)
    v_s[...] = dot(w_ref[2 * width :], norm, NT).astype(BF)
    g_s[...] = dot(wp_ref[...], cot_s[...], NT).astype(BF)


def head_scratch(width):
    return [
        pltpu.VMEM((LANES, width), BF),
        pltpu.VMEM((LANES, width), BF),
        pltpu.VMEM((32, LANES), BF),
        pltpu.VMEM((32, LANES), BF),
        pltpu.VMEM((width, LANES), F32),
        pltpu.VMEM((width, LANES), F32),
        pltpu.VMEM((width, LANES), BF),
        pltpu.VMEM((width, LANES), BF),
    ] + [
        pltpu.VMEM((COUNT, LANES), kind) for _ in range(2) for kind in (F32, F32, BF, BF, BF)
    ]


def window_kernel(
    ahead, window, shifts, ids, spot, own_ref, got_ref, w_ref, wp_ref,
    tile_ref, norm_ref, ctx_ref, gp_ref,
    norm_s, cot_s, bar_q, bar_k, q_s, k_s, v_s, g_s, *buffers,
):
    width = own_ref.shape[-1]
    taken, spread = unpack_matrix(shifts, ahead)
    x = select_other(taken, spread, got_ref[0], own_ref[0])
    cot = select_other(taken, spread, got_ref[1], own_ref[1]).astype(BF)
    tile_ref[0] = x.astype(BF)
    tile_ref[1] = cot
    normed = standardize(x)[0].astype(BF)
    norm_ref[...] = normed
    norm_s[:COUNT] = normed
    norm_s[COUNT:] = jnp.zeros((LANES - COUNT, width), BF)
    cot_s[:COUNT] = cot
    cot_s[COUNT:] = jnp.zeros((LANES - COUNT, width), BF)
    bars(shifts, ids, spot[0] + window * WLAT, ids.shape[0], bar_q, bar_k)
    project(w_ref, wp_ref, norm_s, cot_s, q_s, k_s, v_s, g_s)
    attend(width // HEADS, bar_q, bar_k, q_s, k_s, v_s, g_s, buffers, ctx_ref, gp_ref)


def close_kernel(ahead, shifts, tile_ref, ctx_ref, gp_ref, w_ref, wp_ref, out_ref, send_ref):
    update = dot(ctx_ref[...], wp_ref[...], TN).astype(BF)
    grad_normed = dot(gp_ref[...], w_ref[...], TN)
    standard, inv_scale = standardize(tile_ref[0].astype(F32))
    grad = inv_scale * (
        grad_normed
        - jnp.mean(grad_normed, axis=1, keepdims=True)
        - standard * jnp.mean(grad_normed * standard, axis=1, keepdims=True)
    )
    grad = grad.astype(BF)
    chooser = pack_matrix(shifts, ahead)
    for field, value in enumerate((update, grad)):
        out_ref[field] = value
        send_ref[field] = dot(chooser, value, NN).astype(BF)


def weight_kernel(windows, kept, spot, *refs):
    norms, tiles, ctxs, gps = (refs[n * windows : (n + 1) * windows] for n in range(4))
    out_ref = refs[-1]
    part = ctxs[0].shape[0]

    def total(left, right):
        return functools.reduce(jnp.add, (dot(a, b, TT) for a, b in zip(left, right)))

    side = spot[1] if kept else 1 - spot[1]

    @pl.when(side == 0)
    def _():
        out_ref[...] = total([n[...] for n in norms], [g[: 2 * part] for g in gps])

    @pl.when(side == 1)
    def _():
        out_ref[:, :part] = total([n[...] for n in norms], [g[2 * part :] for g in gps])
        out_ref[:, part:] = total([t[1] for t in tiles], [c[...] for c in ctxs])


def halve_kernel(bit, spot, mine_ref, got_ref, keep_ref, send_ref):
    rows = keep_ref.shape[0]
    for side, ref in ((spot[bit], keep_ref), (1 - spot[bit], send_ref)):
        at = pl.ds(pl.multiple_of(side * rows, rows), rows)
        ref[...] = mine_ref[at] + got_ref[at]


def round_kernel(mine_ref, got_ref, out_ref):
    out_ref[0] = (mine_ref[...] + got_ref[...]).astype(BF)


def join_kernel(bit, spot, mine_ref, got_ref, out_ref):
    count = mine_ref.shape[0]
    for side, ref in ((spot[bit], mine_ref), (1 - spot[bit], got_ref)):
        for n in range(count):
            out_ref[side * count + n] = ref[n]


def gradient_kernel(factor, spot, mine_ref, got_ref, qkv_ref, proj_ref):
    width = proj_ref.shape[0]
    count, rows = mine_ref.shape[:2]

    def write(pair_ref, rest_ref):
        for n in range(count):
            here = slice(n * rows, (n + 1) * rows)
            rest = rest_ref[n].astype(F32) * factor
            qkv_ref[here, : 2 * width] = pair_ref[n].astype(F32) * factor
            qkv_ref[here, 2 * width :] = rest[:, :width]
            proj_ref[:, here] = rest[:, width:].T

    first = spot[1] == 0

    @pl.when(first)
    def _():
        write(mine_ref, got_ref)

    @pl.when(jnp.logical_not(first))
    def _():
        write(got_ref, mine_ref)


def turn_kernel(w_ref, out_ref):
    out_ref[...] = w_ref[...].T


def last_back_kernel(ahead, shifts, own_ref, got_ref, out_ref):
    taken, spread = unpack_matrix(shifts, ahead)
    for field in range(2):
        out_ref[field] = select_other(taken, spread, got_ref[field], own_ref[field]).astype(BF)


def finish_kernel(ahead, windows, shifts, x_ref, cot_ref, above_ref, final_ref, *refs):
    owns, gots = refs[: windows - 1], refs[windows - 1 : 2 * windows - 2]
    outs = refs[2 * windows - 2 :]
    part = WLAT * WLON
    grid = x_ref.shape[1]
    taken, spread = unpack_matrix(shifts, ahead)
    movers = []
    for level in range(LEV):
        cut = shifts[level, 0]
        slot, first, row = level_slots(windows, cut, 1)
        slot = jnp.where(jnp.logical_and(first, row >= cut), -1, slot)
        cells = lax.broadcasted_iota(I32, (grid, (windows + 1) * part), 0)
        movers.append((cells == slot).astype(F32).astype(BF))
    for field, ref in enumerate((x_ref, cot_ref)):
        tiles = [
            select_other(taken, spread, gots[w][field], owns[w][field]) for w in range(windows - 1)
        ]
        tiles += [final_ref[field].astype(F32), above_ref[field].astype(F32)]
        for level in range(LEV):
            here = slice(level * part, (level + 1) * part)
            source = jnp.concatenate([t[here] for t in tiles], axis=0).astype(BF)
            value = ref[level].astype(F32) + dot(movers[level], source, NN)
            outs[field][level] = value.astype(BF)


def route(pairs_of, lat, lon):
    return [
        (a * lon + o, pairs_of(a, o)[0] * lon + pairs_of(a, o)[1])
        for a in range(lat)
        for o in range(lon)
    ]


def across_core(a, o):
    return a ^ 1, o


def tree_bits(core, lon):
    bits = [-1, *range(lon.bit_length() - 1)]
    if core and len(bits) > 2:
        bits = [1, -1, 0, *bits[3:]]
    return bits


def tree_step(k, lon):
    def pairs_of(a, o):
        bit = tree_bits(a % 2, lon)[k]
        return (a ^ 2, o) if bit < 0 else (a, o ^ (1 << bit))

    return pairs_of


def tree_spots(lon):
    my_lat, my_lon = lax.axis_index("lat"), lax.axis_index("lon")
    core = my_lat & 1

    def value(bit):
        return my_lat >> 1 if bit < 0 else (my_lon >> bit) & 1

    pairs = zip(tree_bits(0, lon), tree_bits(1, lon))
    return [core, *[jnp.where(core == 1, value(b), value(a)) for a, b in pairs]]


def all_sum(weights, spot, beside, earlier):
    lat, lon = lax.axis_size("lat"), lax.axis_size("lon")
    steps = range(lon.bit_length())

    def swap(value, pairs_of):
        return lax.ppermute(value, ("lat", "lon"), route(pairs_of, lat, lon))

    sent = weights(False, earlier)
    got = swap(sent, across_core)
    held = weights(True, (sent,))
    after = beside(held)
    for k in steps:
        rows, width = held.shape[0] // 2, held.shape[1]
        held, sent = call(
            functools.partial(halve_kernel, 2 + k),
            (spot, held, got),
            [shape_of(F32, rows, width)] * 2,
            scalars=1,
            after=after,
        )
        got = swap(sent, tree_step(k, lon))
        after = beside(held)
    held = call(round_kernel, (held, got), [shape_of(BF, 1, *held.shape)], after=after)[0]
    for k in reversed(steps):
        held = call(
            functools.partial(join_kernel, 2 + k),
            (spot, held, swap(held, tree_step(k, lon))),
            [shape_of(BF, 2 * held.shape[0], *held.shape[1:])],
            scalars=1,
        )[0]
    return held, swap(held, across_core)


def ring(value, axis, step):
    count = lax.axis_size(axis)
    return lax.ppermute(value, axis, [(i, (i + step) % count) for i in range(count)])


def body(ahead, tokens, cotangent, w_qkv, w_proj, shifts, region_ids):
    levels, lat_rows, lon_cols, width = tokens.shape

    def by_column(grid_field):
        return grid_field.transpose(0, 2, 1, 3).reshape(levels, lon_cols * lat_rows, width)

    tokens, cotangent = by_column(tokens), by_column(cotangent)
    windows = lat_rows // WLAT
    first_row = lax.axis_index("lat") * lat_rows
    spot = jnp.stack([first_row, *tree_spots(lax.axis_size("lon"))]).astype(I32)
    out_step = -1 if ahead else 1
    pair = shape_of(BF, 2, COUNT, width)
    packed = shape_of(BF, 2, PACKED, width)
    arrays = (shifts, tokens, cotangent)
    tile, send, halo = call(
        functools.partial(pack_kernel, ahead, windows, True), arrays, [pair, packed, pair], scalars=1
    )
    made = call(
        functools.partial(pack_kernel, ahead, windows, False),
        arrays,
        [pair] * (windows - 1) + [packed] * (windows - 2),
        scalars=1,
        after=(tile,),
    )
    tiles, last = [tile, *made[: windows - 2]], made[windows - 2]
    w_t = call(turn_kernel, (w_qkv,), [shape_of(BF, 3 * width, width)], after=(last,))[0]
    below = ring(halo, "lat", -1)
    gots = [ring(s, "lon", out_step) for s in (send, *made[windows - 1 :])]
    firsts, closed = {}, {}

    def window(w, after):
        firsts[w] = call(
            functools.partial(window_kernel, ahead, w),
            (shifts, region_ids, spot, tiles[w], gots[w], w_t, w_proj),
            [
                pair,
                shape_of(BF, COUNT, width),
                shape_of(BF, width, COUNT),
                shape_of(BF, 3 * width, COUNT),
            ],
            head_scratch(width),
            scalars=3,
            after=after,
        )
        return (firsts[w][1],)

    def close(w, after):
        tile, _, context, grads = firsts[w]
        out, send = call(
            functools.partial(close_kernel, ahead),
            (shifts, tile, context, grads, w_t, w_proj),
            [pair, packed],
            scalars=1,
            after=after,
        )
        closed[w] = out, ring(send, "lon", -out_step)
        return (send,)

    order = [*range(windows - 2), windows - 1, windows - 2]
    after = ()
    for n, w in enumerate(order):
        if n == 1:
            tile, send = call(
                functools.partial(pack_last_kernel, ahead),
                (shifts, last, below),
                [pair, packed],
                scalars=1,
                after=after,
            )
            tiles.append(tile)
            gots.append(ring(send, "lon", out_step))
            after = (send,)
        if n >= 2:
            after = (*after, closed[order[n - 2]][1])
        after = window(w, after)
        if n < windows - 1:
            after = close(w, after)
    final = call(
        functools.partial(last_back_kernel, ahead),
        (shifts, *closed[windows - 1]),
        [pair],
        scalars=1,
        after=after,
    )[0]
    above = ring(final, "lat", 1)

    operands = [[firsts[w][n] for w in range(windows)] for n in (1, 0, 2, 3)]
    operands = [a for group in operands for a in group]

    def weights(kept, after):
        return call(
            functools.partial(weight_kernel, windows, kept),
            (spot, *operands),
            [shape_of(F32, width, 2 * width)],
            scalars=1,
            after=after,
        )[0]

    stage, results = [], []

    def beside(value):
        stage.append(value)
        if len(stage) == 1:
            return close(windows - 2, (value, above))
        if len(stage) == 2:
            return (closed[windows - 2][1],)
        if len(stage) == 3:
            results.extend(
                call(
                    functools.partial(finish_kernel, ahead, windows),
                    (
                        shifts, tokens, cotangent, above, final,
                        *[closed[w][0] for w in range(windows - 1)],
                        *[closed[w][1] for w in range(windows - 1)],
                    ),
                    [shape_of(BF, *tokens.shape)] * 2,
                    scalars=1,
                    after=(value,),
                )
            )
            return (results[0],)
        return ()

    summed = all_sum(weights, spot, beside, (final,))
    mixed, grad_tokens = (
        r.reshape(levels, lon_cols, lat_rows, width).transpose(0, 2, 1, 3) for r in results
    )
    total_tokens = levels * lat_rows * lax.axis_size("lat") * lon_cols * lax.axis_size("lon")
    gradients = call(
        functools.partial(gradient_kernel, 1.0 / math.sqrt(total_tokens)),
        (spot, *summed),
        [shape_of(F32, width, 3 * width), shape_of(F32, width, width)],
        scalars=1,
    )
    return (mixed, grad_tokens, *gradients)


def local(tokens, cotangent, w_qkv, w_proj, shifts, region_ids):
    return lax.cond(
        jnp.sum(shifts[:, 1]) <= ENTRIES,
        functools.partial(body, True),
        functools.partial(body, False),
        tokens, cotangent, w_qkv, w_proj, shifts, region_ids,
    )


def solution(mesh):
    return jax.shard_map(
        local,
        mesh=mesh,
        in_specs=(P(None, "lat", "lon", None), P(None, "lat", "lon", None), P(), P(), P(), P()),
        out_specs=(P(None, "lat", "lon", None), P(None, "lat", "lon", None), P(), P()),
        check_vma=False,
    )
```

```python
import functools
import math

import jax
import jax.numpy as jnp
from jax import lax
from jax.experimental import pallas as pl
from jax.experimental.pallas import tpu as pltpu
from jax.sharding import PartitionSpec as P

HEADS = 16
WLAT = 6
WLON = 12
LEV = 4
COUNT = LEV * WLAT * WLON
LANES = 384
ENTRIES = LEV * WLON // 2
PACKED = ENTRIES * WLAT
NORM_EPS = 1e-05
BARRED = 2.0**100
BF = jnp.bfloat16
F32 = jnp.float32
I32 = jnp.int32

NN = (((1,), (0,)), ((), ()))
NT = (((1,), (1,)), ((), ()))
TN = (((0,), (0,)), ((), ()))
TT = (((0,), (1,)), ((), ()))

SMEM = pl.BlockSpec(memory_space=pltpu.SMEM)
VMEM = pl.BlockSpec(memory_space=pltpu.VMEM)
ANY = pl.BlockSpec(memory_space=pl.ANY)


def dot(a, b, dims):
    return lax.dot_general(a, b, dims, preferred_element_type=F32)


def split_bf16(value):
    high = value.astype(BF)
    low = (value - high.astype(F32)).astype(BF)
    return high, low


def call(kernel, ins, outs, scratch=(), scalars=0, after=()):

    def ordered(*refs):
        kernel(*refs[: len(ins)], *refs[len(ins) + len(after) :])

    return pl.pallas_call(
        ordered,
        in_specs=[SMEM] * scalars + [VMEM] * (len(ins) - scalars) + [ANY] * len(after),
        out_specs=[VMEM] * len(outs),
        out_shape=list(outs),
        scratch_shapes=list(scratch),
        compiler_params=pltpu.CompilerParams(vmem_limit_bytes=24 * 1024 * 1024),
        cost_estimate=pl.CostEstimate(
            flops=1_000_000, bytes_accessed=10_000, transcendentals=0
        ),
    )(*ins, *after)


def shape_of(dtype, *dims):
    return jax.ShapeDtypeStruct(dims, dtype)


def place(axis):
    dims = (COUNT, 1) if axis == 0 else (1, COUNT)
    token = lax.broadcasted_iota(I32, dims, axis)
    level = sum((token >= n * WLAT * WLON).astype(I32) for n in range(1, LEV))
    column, row = column_and_row(token - level * (WLAT * WLON))
    return level, row, column


def column_and_row(rest):
    column = sum((rest >= n * WLAT).astype(I32) for n in range(1, WLON))
    return column, rest - column * WLAT


def level_slots(windows, cut, axis):
    part = WLAT * WLON
    size = (windows + 1) * part
    dims = (size, 1) if axis == 0 else (1, size)
    token = lax.broadcasted_iota(I32, dims, axis)
    window = sum((token >= n * part).astype(I32) for n in range(1, windows + 1))
    column, row = column_and_row(token - window * part)
    at = window * WLAT + row + jnp.where(row < cut, WLAT, 0)
    slot = jnp.where(at < windows * WLAT, column * (windows * WLAT) + at, -1)
    first = window == windows
    return jnp.where(first, column * (windows * WLAT) + row, slot), first, row


def by_level(level, values):
    result = jnp.full(level.shape, values[0], I32)
    for n in range(1, LEV):
        result = jnp.where(level == n, values[n], result)
    return result


def from_next_row(shifts, axis):
    level, row, _ = place(axis)
    return row < by_level(level, [shifts[n, 0] for n in range(LEV)])


def from_other_side(shifts, ahead, axis):
    level, row, column = place(axis)
    cut = [shifts[n, 1] for n in range(LEV)]
    counts = cut if ahead else [WLON - c for c in cut]
    starts = [0] * LEV if ahead else cut
    offsets = [0]
    for n in range(LEV - 1):
        offsets.append(offsets[-1] + counts[n])
    at = by_level(level, cut)
    taken = (column < at) if ahead else (column >= at)
    entry = by_level(level, [o - s for o, s in zip(offsets, starts)]) + column
    return taken, jnp.where(taken, entry * WLAT + row, -1)


def pack_matrix(shifts, ahead):
    _, slot = from_other_side(shifts, ahead, 1)
    rows = lax.broadcasted_iota(I32, (PACKED, COUNT), 0)
    return (rows == slot).astype(F32).astype(BF)


def unpack_matrix(shifts, ahead):
    taken, slot = from_other_side(shifts, ahead, 0)
    columns = lax.broadcasted_iota(I32, (COUNT, PACKED), 1)
    return taken, (columns == slot).astype(F32).astype(BF)


def select_other(taken, spread, packed, own):
    return jnp.where(taken, dot(spread, packed, NN), own.astype(F32))


def pack_kernel(ahead, windows, chosen, sent, shifts, x_ref, cot_ref, *refs):
    part = WLAT * WLON
    grid = x_ref.shape[1]
    count = len(chosen)
    tile_refs, send_refs = refs[:count], refs[count:]
    chooser = pack_matrix(shifts, ahead)
    parts = [[[None] * LEV for _ in range(count)] for _ in range(2)]
    for level in range(LEV):
        slot, _, _ = level_slots(windows, shifts[level, 0], 0)
        slot = jnp.concatenate([slot[w * part : (w + 1) * part] for w in chosen], axis=0)
        cells = lax.broadcasted_iota(I32, (count * part, grid), 1)
        mover = (cells == slot).astype(F32).astype(BF)
        for field, ref in enumerate((x_ref, cot_ref)):
            moved = dot(mover, ref[level], NN)
            for w in range(count):
                parts[field][w][level] = moved[w * part : (w + 1) * part]
    for field in range(2):
        whole = [jnp.concatenate(p, axis=0).astype(BF) for p in parts[field]]
        for tile_ref, tile in zip(tile_refs, whole):
            tile_ref[field] = tile
        for send_ref, tile in zip(send_refs, whole[:sent]):
            send_ref[field] = dot(chooser, tile, NN).astype(BF)


def pack_last_kernel(ahead, shifts, last_ref, halo_ref, tile_ref, send_ref):
    lower = from_next_row(shifts, 0)
    chooser = pack_matrix(shifts, ahead)
    for field in range(2):
        tile = jnp.where(lower, halo_ref[field].astype(F32), last_ref[field].astype(F32))
        tile_ref[field] = tile.astype(BF)
        send_ref[field] = dot(chooser, tile.astype(BF), NN).astype(BF)


def standardize(values_full):
    center = values_full - jnp.mean(values_full, axis=1, keepdims=True)
    variance = jnp.mean(center * center, axis=1, keepdims=True)
    inv_scale = lax.rsqrt(variance + NORM_EPS)
    return center * inv_scale, inv_scale


def bars(shifts, ids, first_row, grid_rows, bar_q, bar_k):
    level, row, _ = place(1)
    wrapped = jnp.where(row < by_level(level, [shifts[n, 0] for n in range(LEV)]), WLAT, 0)
    at = first_row + row + wrapped
    at = jnp.where(at >= grid_rows, at - grid_rows, at)
    top = sum((ids[n] == ids[0]).astype(I32) for n in range(WLAT - 1))
    bottom = sum((ids[grid_rows - 1 - n] == ids[grid_rows - 1]).astype(I32) for n in range(WLAT - 1))
    kind = jnp.where(at < top, 1, jnp.where(at >= grid_rows - bottom, 2, 0))
    features = lax.broadcasted_iota(I32, (32, COUNT), 0)
    same = (features == kind).astype(F32)
    bar_q[...] = jnp.zeros_like(bar_q)
    bar_q[:, :COUNT] = (same * -BARRED).astype(BF)
    bar_k[...] = jnp.zeros_like(bar_k)
    bar_k[:, :COUNT] = jnp.where(features < 3, 1.0 - same, 0.0).astype(BF)


def attend(size, bar_q, bar_k, q_s, k_s, v_s, g_s, buffers, ctx_ref, gp_ref):
    scale = 1.0 / math.sqrt(size)
    heads = HEADS
    part = heads * size

    def rows_of(h):
        return pl.ds(pl.multiple_of(h * size, size), size)

    def products(h, buffer):
        score_b, grad_b = buffer[:2]
        rows = rows_of(h)
        q_high, q_low = split_bf16(q_s[rows])
        k_high, k_low = split_bf16(k_s[rows])
        q_all = jnp.concatenate([q_high, q_low, q_high, bar_q[...]], axis=0)
        k_all = jnp.concatenate([k_high, k_high, k_low, bar_k[...]], axis=0)
        score_b[...] = dot(k_all.T[:COUNT], q_all, NN)
        grad_b[...] = dot(v_s[rows].T[:COUNT], g_s[rows], NN)

    def soften(buffer):
        score_b, grad_b, weight_b, high_b, low_b = buffer
        for start in range(0, LANES, 128):
            lanes = slice(start, start + 128)
            scores = score_b[:, lanes]
            expo = jnp.exp2(scores - jnp.max(scores, axis=0, keepdims=True))
            weights = expo * (1.0 / jnp.sum(expo, axis=0, keepdims=True))
            weight_b[:, lanes] = weights.astype(BF)
            grad_w = grad_b[:, lanes]
            grad_sc = weights * (grad_w - jnp.sum(weights * grad_w, axis=0, keepdims=True))
            high_b[:, lanes], low_b[:, lanes] = split_bf16(grad_sc)

    def results(h, buffer):
        weight_b, high_b, low_b = buffer[2:]
        rows = rows_of(h)
        q_high, q_low = split_bf16(q_s[rows])
        k_high, k_low = split_bf16(k_s[rows])
        rounded, high, low = weight_b[...], high_b[...], low_b[...]
        ctx_ref[rows] = dot(v_s[rows][:, :COUNT], rounded, NN)[:, :COUNT].astype(BF)
        k_pair = jnp.concatenate([k_high[:, :COUNT], k_low[:, :COUNT]], axis=0)
        q_pair = jnp.concatenate([q_high, q_low], axis=0)
        gq = dot(k_pair, high, NN)
        gq = gq[:size] + gq[size:] + dot(k_high[:, :COUNT], low, NN)
        gk = dot(q_pair, high, NT)
        gk = gk[:size] + gk[size:] + dot(q_high, low, NT)
        gv = dot(g_s[rows], rounded, NT)
        base = pl.multiple_of(h * size, size)
        gp_ref[pl.ds(base, size)] = (gq[:, :COUNT] * scale).astype(BF)
        gp_ref[pl.ds(part + base, size)] = (gk * math.log(2.0)).astype(BF)
        gp_ref[pl.ds(2 * part + base, size)] = gv.astype(BF)

    even, odd = buffers[:5], buffers[5:]
    products(0, even)

    def pair(p, carry):
        h = 2 * p
        products(h + 1, odd)
        soften(even)
        results(jnp.maximum(h - 1, 0), odd)
        products(jnp.minimum(h + 2, heads - 1), even)
        soften(odd)
        results(h, even)
        return carry

    lax.fori_loop(0, heads // 2, pair, 0)
    results(heads - 1, odd)


def project(w_ref, wp_ref, norm_s, cot_s, q_s, k_s, v_s, g_s):
    norm = norm_s[...]
    width = norm.shape[1]
    factor = math.log2(math.e) / math.sqrt(width // HEADS)
    q_s[...] = dot(w_ref[:width], norm, NT) * factor
    k_s[...] = dot(w_ref[width : 2 * width], norm, NT)
    v_s[...] = dot(w_ref[2 * width :], norm, NT).astype(BF)
    g_s[...] = dot(wp_ref[...], cot_s[...], NT).astype(BF)


def head_scratch(width):
    return [
        pltpu.VMEM((LANES, width), BF),
        pltpu.VMEM((LANES, width), BF),
        pltpu.VMEM((32, LANES), BF),
        pltpu.VMEM((32, LANES), BF),
        pltpu.VMEM((width, LANES), F32),
        pltpu.VMEM((width, LANES), F32),
        pltpu.VMEM((width, LANES), BF),
        pltpu.VMEM((width, LANES), BF),
    ] + [
        pltpu.VMEM((COUNT, LANES), kind) for _ in range(2) for kind in (F32, F32, BF, BF, BF)
    ]


def window_kernel(
    ahead, window, shifts, ids, spot, own_ref, got_ref, w_ref, wp_ref,
    tile_ref, norm_ref, ctx_ref, gp_ref,
    norm_s, cot_s, bar_q, bar_k, q_s, k_s, v_s, g_s, *buffers,
):
    width = own_ref.shape[-1]
    taken, spread = unpack_matrix(shifts, ahead)
    x = select_other(taken, spread, got_ref[0], own_ref[0])
    cot = select_other(taken, spread, got_ref[1], own_ref[1]).astype(BF)
    tile_ref[0] = x.astype(BF)
    tile_ref[1] = cot
    normed = standardize(x)[0].astype(BF)
    norm_ref[...] = normed
    norm_s[:COUNT] = normed
    norm_s[COUNT:] = jnp.zeros((LANES - COUNT, width), BF)
    cot_s[:COUNT] = cot
    cot_s[COUNT:] = jnp.zeros((LANES - COUNT, width), BF)
    bars(shifts, ids, spot[0] + window * WLAT, ids.shape[0], bar_q, bar_k)
    project(w_ref, wp_ref, norm_s, cot_s, q_s, k_s, v_s, g_s)
    attend(width // HEADS, bar_q, bar_k, q_s, k_s, v_s, g_s, buffers, ctx_ref, gp_ref)


def close_kernel(ahead, shifts, tile_ref, ctx_ref, gp_ref, w_ref, wp_ref, out_ref, send_ref):
    update = dot(ctx_ref[...], wp_ref[...], TN).astype(BF)
    grad_normed = dot(gp_ref[...], w_ref[...], TN)
    standard, inv_scale = standardize(tile_ref[0].astype(F32))
    grad = inv_scale * (
        grad_normed
        - jnp.mean(grad_normed, axis=1, keepdims=True)
        - standard * jnp.mean(grad_normed * standard, axis=1, keepdims=True)
    )
    grad = grad.astype(BF)
    chooser = pack_matrix(shifts, ahead)
    for field, value in enumerate((update, grad)):
        out_ref[field] = value
        send_ref[field] = dot(chooser, value, NN).astype(BF)


def weight_kernel(windows, kept, spot, *refs):
    norms, tiles, ctxs, gps = (refs[n * windows : (n + 1) * windows] for n in range(4))
    out_ref = refs[-1]
    part = ctxs[0].shape[0]

    def total(left, right):
        return functools.reduce(jnp.add, (dot(a, b, TT) for a, b in zip(left, right)))

    side = spot[1] if kept else 1 - spot[1]

    @pl.when(side == 0)
    def _():
        out_ref[...] = total([n[...] for n in norms], [g[: 2 * part] for g in gps])

    @pl.when(side == 1)
    def _():
        out_ref[:, :part] = total([n[...] for n in norms], [g[2 * part :] for g in gps])
        out_ref[:, part:] = total([t[1] for t in tiles], [c[...] for c in ctxs])


def halve_kernel(bit, spot, mine_ref, got_ref, keep_ref, send_ref):
    rows = keep_ref.shape[0]
    for side, ref in ((spot[bit], keep_ref), (1 - spot[bit], send_ref)):
        at = pl.ds(pl.multiple_of(side * rows, rows), rows)
        ref[...] = mine_ref[at] + got_ref[at]


def spread_kernel(spot, mine_ref, got_ref, *out_refs):
    rows = out_refs[0].shape[0]
    for d, ref in enumerate(out_refs):
        at = pl.ds(pl.multiple_of((spot[4] ^ d) * rows, rows), rows)
        ref[...] = mine_ref[at] + got_ref[at]


def gather_sum_kernel(*refs):
    refs[-1][...] = functools.reduce(jnp.add, (r[...] for r in refs[:-1])).astype(BF)


def arrange_kernel(spot, *refs):
    for d, ref in enumerate(refs[:-1]):
        refs[-1][spot[4] ^ d] = ref[...]


def join_kernel(bit, spot, mine_ref, got_ref, out_ref):
    count = mine_ref.shape[0]
    for side, ref in ((spot[bit], mine_ref), (1 - spot[bit], got_ref)):
        for n in range(count):
            out_ref[side * count + n] = ref[n]


def gradient_kernel(factor, spot, mine_ref, got_ref, qkv_ref, proj_ref):
    width = proj_ref.shape[0]
    count, rows = mine_ref.shape[:2]

    def write(pair_ref, rest_ref):
        for n in range(count):
            here = slice(n * rows, (n + 1) * rows)
            rest = rest_ref[n].astype(F32) * factor
            qkv_ref[here, : 2 * width] = pair_ref[n].astype(F32) * factor
            qkv_ref[here, 2 * width :] = rest[:, :width]
            proj_ref[:, here] = rest[:, width:].T

    first = spot[1] == 0

    @pl.when(first)
    def _():
        write(mine_ref, got_ref)

    @pl.when(jnp.logical_not(first))
    def _():
        write(got_ref, mine_ref)


def turn_kernel(w_ref, out_ref):
    out_ref[...] = w_ref[...].T


def last_back_kernel(ahead, shifts, own_ref, got_ref, out_ref):
    taken, spread = unpack_matrix(shifts, ahead)
    for field in range(2):
        out_ref[field] = select_other(taken, spread, got_ref[field], own_ref[field]).astype(BF)


def finish_kernel(ahead, windows, shifts, x_ref, cot_ref, above_ref, final_ref, *refs):
    owns, gots = refs[: windows - 1], refs[windows - 1 : 2 * windows - 2]
    outs = refs[2 * windows - 2 :]
    part = WLAT * WLON
    grid = x_ref.shape[1]
    taken, spread = unpack_matrix(shifts, ahead)
    movers = []
    for level in range(LEV):
        cut = shifts[level, 0]
        slot, first, row = level_slots(windows, cut, 1)
        slot = jnp.where(jnp.logical_and(first, row >= cut), -1, slot)
        cells = lax.broadcasted_iota(I32, (grid, (windows + 1) * part), 0)
        movers.append((cells == slot).astype(F32).astype(BF))
    for field, ref in enumerate((x_ref, cot_ref)):
        tiles = [
            select_other(taken, spread, gots[w][field], owns[w][field]) for w in range(windows - 1)
        ]
        tiles += [final_ref[field].astype(F32), above_ref[field].astype(F32)]
        for level in range(LEV):
            here = slice(level * part, (level + 1) * part)
            source = jnp.concatenate([t[here] for t in tiles], axis=0).astype(BF)
            value = ref[level].astype(F32) + dot(movers[level], source, NN)
            outs[field][level] = value.astype(BF)


def route(pairs_of, lat, lon):
    return [
        (a * lon + o, pairs_of(a, o)[0] * lon + pairs_of(a, o)[1])
        for a in range(lat)
        for o in range(lon)
    ]


def across_core(a, o):
    return a ^ 1, o


def step_one(a, o):
    return (a, o ^ 1) if a % 2 else (a ^ 2, o)


def step_two(a, o):
    return (a ^ 2, o) if a % 2 else (a, o ^ 1)


def all_sum(weights, spot, beside, earlier):
    lat, lon = lax.axis_size("lat"), lax.axis_size("lon")
    reach = lon // 2

    def swap(value, pairs_of):
        return lax.ppermute(value, ("lat", "lon"), route(pairs_of, lat, lon))

    def along(d):
        return lambda a, o: (a, o ^ (2 * d))

    sent = weights(False, earlier)
    got = swap(sent, across_core)
    held = weights(True, (sent,))
    after = beside(held)
    for bit, pairs_of in ((2, step_one), (3, step_two)):
        rows, width = held.shape[0] // 2, held.shape[1]
        held, sent = call(
            functools.partial(halve_kernel, bit),
            (spot, held, got),
            [shape_of(F32, rows, width)] * 2,
            scalars=1,
            after=after,
        )
        got = swap(sent, pairs_of)
        after = beside(held)
    rows = held.shape[0] // reach
    pieces = call(
        spread_kernel, (spot, held, got), [shape_of(F32, rows, width)] * reach, scalars=1, after=after
    )
    gots = [swap(pieces[d], along(d)) for d in range(1, reach)]
    after = beside(pieces[0])
    sums = call(gather_sum_kernel, (pieces[0], *gots), [shape_of(BF, rows, width)], after=after)[0]
    gots = [swap(sums, along(d)) for d in range(1, reach)]
    after = beside(sums)
    part = call(
        arrange_kernel, (spot, sums, *gots), [shape_of(BF, reach, rows, width)], scalars=1, after=after
    )[0]
    held = part.reshape(1, reach * rows, width)
    for bit, pairs_of in ((3, step_two), (2, step_one)):
        got = swap(held, pairs_of)
        after = beside(held)
        held = call(
            functools.partial(join_kernel, bit),
            (spot, held, got),
            [shape_of(BF, 2 * held.shape[0], *held.shape[1:])],
            scalars=1,
            after=after,
        )[0]
    return held, swap(held, across_core)


def ring(value, axis, step):
    count = lax.axis_size(axis)
    return lax.ppermute(value, axis, [(i, (i + step) % count) for i in range(count)])


def body(ahead, tokens, cotangent, w_qkv, w_proj, shifts, region_ids):
    levels, lat_rows, lon_cols, width = tokens.shape

    def by_column(grid_field):
        return grid_field.transpose(0, 2, 1, 3).reshape(levels, lon_cols * lat_rows, width)

    tokens, cotangent = by_column(tokens), by_column(cotangent)
    windows = lat_rows // WLAT
    my_lat, my_lon = lax.axis_index("lat"), lax.axis_index("lon")
    core, high, low = my_lat & 1, my_lat >> 1, my_lon & 1
    spot = jnp.stack(
        [
            my_lat * lat_rows,
            core,
            jnp.where(core == 1, low, high),
            jnp.where(core == 1, high, low),
            my_lon >> 1,
        ]
    ).astype(I32)
    out_step = -1 if ahead else 1
    pair = shape_of(BF, 2, COUNT, width)
    packed = shape_of(BF, 2, PACKED, width)

    def packs(chosen, sent, after):
        made = call(
            functools.partial(pack_kernel, ahead, windows, chosen, sent),
            (shifts, tokens, cotangent),
            [pair] * len(chosen) + [packed] * sent,
            scalars=1,
            after=after,
        )
        return made[: len(chosen)], made[len(chosen) :]

    def send_ahead(windows_sent, sends):
        for w, send in zip(windows_sent, sends):
            gots[w] = ring(send, "lon", out_step)

    gots, tiles = {}, {}
    (tiles[0], halo, last), sends = packs((0, windows, windows - 1), 1, ())
    send_ahead((0,), sends)
    below = ring(halo, "lat", -1)
    w_t = call(turn_kernel, (w_qkv,), [shape_of(BF, 3 * width, width)], after=(last,))[0]
    tiles[windows - 1], send = call(
        functools.partial(pack_last_kernel, ahead),
        (shifts, last, below),
        [pair, packed],
        scalars=1,
        after=(w_t,),
    )
    send_ahead((windows - 1,), (send,))
    middle = tuple(range(1, windows - 1))
    made, sends = packs(middle, len(middle), (send,))
    tiles.update(zip(middle, made))
    send_ahead(middle, sends)
    firsts, closed = {}, {}

    def window(w, after):
        firsts[w] = call(
            functools.partial(window_kernel, ahead, w),
            (shifts, region_ids, spot, tiles[w], gots[w], w_t, w_proj),
            [
                pair,
                shape_of(BF, COUNT, width),
                shape_of(BF, width, COUNT),
                shape_of(BF, 3 * width, COUNT),
            ],
            head_scratch(width),
            scalars=3,
            after=after,
        )
        return (firsts[w][1],)

    def close(w, after):
        tile, _, context, grads = firsts[w]
        out, send = call(
            functools.partial(close_kernel, ahead),
            (shifts, tile, context, grads, w_t, w_proj),
            [pair, packed],
            scalars=1,
            after=after,
        )
        closed[w] = out, ring(send, "lon", -out_step)
        return (send,)

    order = [0, windows - 1, *middle]
    after = (sends[0],)
    for n, w in enumerate(order):
        if n >= 2:
            after = (*after, closed[order[n - 2]][1])
        if n == windows - 1:
            final = call(
                functools.partial(last_back_kernel, ahead),
                (shifts, *closed[windows - 1]),
                [pair],
                scalars=1,
                after=after,
            )[0]
            above = ring(final, "lat", 1)
            after = (*after, final)
        after = close(w, window(w, after))

    operands = [[firsts[w][n] for w in range(windows)] for n in (1, 0, 2, 3)]
    operands = [a for group in operands for a in group]

    def weights(kept, after):
        return call(
            functools.partial(weight_kernel, windows, kept),
            (spot, *operands),
            [shape_of(F32, width, 2 * width)],
            scalars=1,
            after=after,
        )[0]

    stage, results = [], []

    def beside(value):
        stage.append(value)
        if len(stage) == 1:
            return (above, closed[order[-1]][1])
        if len(stage) == 2:
            results.extend(
                call(
                    functools.partial(finish_kernel, ahead, windows),
                    (
                        shifts, tokens, cotangent, above, final,
                        *[closed[w][0] for w in range(windows - 1)],
                        *[closed[w][1] for w in range(windows - 1)],
                    ),
                    [shape_of(BF, *tokens.shape)] * 2,
                    scalars=1,
                    after=(value,),
                )
            )
            return (results[0],)
        return ()

    summed = all_sum(weights, spot, beside, (*after, closed[order[-2]][1]))
    mixed, grad_tokens = (
        r.reshape(levels, lon_cols, lat_rows, width).transpose(0, 2, 1, 3) for r in results
    )
    total_tokens = levels * lat_rows * lax.axis_size("lat") * lon_cols * lax.axis_size("lon")
    gradients = call(
        functools.partial(gradient_kernel, 1.0 / math.sqrt(total_tokens)),
        (spot, *summed),
        [shape_of(F32, width, 3 * width), shape_of(F32, width, width)],
        scalars=1,
    )
    return (mixed, grad_tokens, *gradients)


def local(tokens, cotangent, w_qkv, w_proj, shifts, region_ids):
    return lax.cond(
        jnp.sum(shifts[:, 1]) <= ENTRIES,
        functools.partial(body, True),
        functools.partial(body, False),
        tokens, cotangent, w_qkv, w_proj, shifts, region_ids,
    )


def solution(mesh):
    return jax.shard_map(
        local,
        mesh=mesh,
        in_specs=(P(None, "lat", "lon", None), P(None, "lat", "lon", None), P(), P(), P(), P()),
        out_specs=(P(None, "lat", "lon", None), P(None, "lat", "lon", None), P(), P()),
        check_vma=False,
    )
```

```python
import functools
import math

import jax
import jax.numpy as jnp
from jax import lax
from jax.experimental import pallas as pl
from jax.experimental.pallas import tpu as pltpu
from jax.sharding import PartitionSpec as P

HEADS = 16
WLAT = 6
WLON = 12
LEV = 4
COUNT = LEV * WLAT * WLON
LANES = 384
ENTRIES = LEV * WLON // 2
PACKED = ENTRIES * WLAT
NORM_EPS = 1e-05
BARRED = 2.0**100
BF = jnp.bfloat16
F32 = jnp.float32
I32 = jnp.int32

NN = (((1,), (0,)), ((), ()))
NT = (((1,), (1,)), ((), ()))
TN = (((0,), (0,)), ((), ()))
TT = (((0,), (1,)), ((), ()))

SMEM = pl.BlockSpec(memory_space=pltpu.SMEM)
VMEM = pl.BlockSpec(memory_space=pltpu.VMEM)
ANY = pl.BlockSpec(memory_space=pl.ANY)


def dot(a, b, dims):
    return lax.dot_general(a, b, dims, preferred_element_type=F32)


def split_bf16(value):
    high = value.astype(BF)
    low = (value - high.astype(F32)).astype(BF)
    return high, low


def call(kernel, ins, outs, scratch=(), scalars=0, after=()):

    def ordered(*refs):
        kernel(*refs[: len(ins)], *refs[len(ins) + len(after) :])

    return pl.pallas_call(
        ordered,
        in_specs=[SMEM] * scalars + [VMEM] * (len(ins) - scalars) + [ANY] * len(after),
        out_specs=[VMEM] * len(outs),
        out_shape=list(outs),
        scratch_shapes=list(scratch),
        compiler_params=pltpu.CompilerParams(vmem_limit_bytes=24 * 1024 * 1024),
        cost_estimate=pl.CostEstimate(
            flops=1_000_000, bytes_accessed=10_000, transcendentals=0
        ),
    )(*ins, *after)


def shape_of(dtype, *dims):
    return jax.ShapeDtypeStruct(dims, dtype)


def place(axis):
    dims = (COUNT, 1) if axis == 0 else (1, COUNT)
    token = lax.broadcasted_iota(I32, dims, axis)
    level = sum((token >= n * WLAT * WLON).astype(I32) for n in range(1, LEV))
    column, row = column_and_row(token - level * (WLAT * WLON))
    return level, row, column


def column_and_row(rest):
    column = sum((rest >= n * WLAT).astype(I32) for n in range(1, WLON))
    return column, rest - column * WLAT


def level_slots(windows, cut, axis):
    part = WLAT * WLON
    size = (windows + 1) * part
    dims = (size, 1) if axis == 0 else (1, size)
    token = lax.broadcasted_iota(I32, dims, axis)
    window = sum((token >= n * part).astype(I32) for n in range(1, windows + 1))
    column, row = column_and_row(token - window * part)
    at = window * WLAT + row + jnp.where(row < cut, WLAT, 0)
    slot = jnp.where(at < windows * WLAT, column * (windows * WLAT) + at, -1)
    first = window == windows
    return jnp.where(first, column * (windows * WLAT) + row, slot), first, row


def by_level(level, values):
    result = jnp.full(level.shape, values[0], I32)
    for n in range(1, LEV):
        result = jnp.where(level == n, values[n], result)
    return result


def from_next_row(shifts, axis):
    level, row, _ = place(axis)
    return row < by_level(level, [shifts[n, 0] for n in range(LEV)])


def from_other_side(shifts, ahead, axis):
    level, row, column = place(axis)
    cut = [shifts[n, 1] for n in range(LEV)]
    counts = cut if ahead else [WLON - c for c in cut]
    starts = [0] * LEV if ahead else cut
    offsets = [0]
    for n in range(LEV - 1):
        offsets.append(offsets[-1] + counts[n])
    at = by_level(level, cut)
    taken = (column < at) if ahead else (column >= at)
    entry = by_level(level, [o - s for o, s in zip(offsets, starts)]) + column
    return taken, jnp.where(taken, entry * WLAT + row, -1)


def pack_matrix(shifts, ahead):
    _, slot = from_other_side(shifts, ahead, 1)
    rows = lax.broadcasted_iota(I32, (PACKED, COUNT), 0)
    return (rows == slot).astype(F32).astype(BF)


def unpack_matrix(shifts, ahead):
    taken, slot = from_other_side(shifts, ahead, 0)
    columns = lax.broadcasted_iota(I32, (COUNT, PACKED), 1)
    return taken, (columns == slot).astype(F32).astype(BF)


def select_other(taken, spread, packed, own):
    return jnp.where(taken, dot(spread, packed, NN), own.astype(F32))


def pack_kernel(ahead, windows, chosen, sent, shifts, x_ref, cot_ref, *refs):
    part = WLAT * WLON
    grid = x_ref.shape[1]
    count = len(chosen)
    tile_refs, send_refs = refs[:count], refs[count:]
    chooser = pack_matrix(shifts, ahead)
    parts = [[[None] * LEV for _ in range(count)] for _ in range(2)]
    for level in range(LEV):
        slot, _, _ = level_slots(windows, shifts[level, 0], 0)
        slot = jnp.concatenate([slot[w * part : (w + 1) * part] for w in chosen], axis=0)
        cells = lax.broadcasted_iota(I32, (count * part, grid), 1)
        mover = (cells == slot).astype(F32).astype(BF)
        for field, ref in enumerate((x_ref, cot_ref)):
            moved = dot(mover, ref[level], NN)
            for w in range(count):
                parts[field][w][level] = moved[w * part : (w + 1) * part]
    for field in range(2):
        whole = [jnp.concatenate(p, axis=0).astype(BF) for p in parts[field]]
        for tile_ref, tile in zip(tile_refs, whole):
            tile_ref[field] = tile
        for send_ref, tile in zip(send_refs, whole[:sent]):
            send_ref[field] = dot(chooser, tile, NN).astype(BF)


def pack_last_kernel(ahead, shifts, last_ref, halo_ref, tile_ref, send_ref):
    lower = from_next_row(shifts, 0)
    chooser = pack_matrix(shifts, ahead)
    for field in range(2):
        tile = jnp.where(lower, halo_ref[field].astype(F32), last_ref[field].astype(F32))
        tile_ref[field] = tile.astype(BF)
        send_ref[field] = dot(chooser, tile.astype(BF), NN).astype(BF)


def standardize(values_full):
    center = values_full - jnp.mean(values_full, axis=1, keepdims=True)
    variance = jnp.mean(center * center, axis=1, keepdims=True)
    inv_scale = lax.rsqrt(variance + NORM_EPS)
    return center * inv_scale, inv_scale


def bars(shifts, ids, first_row, grid_rows, bar_q, bar_k):
    level, row, _ = place(1)
    wrapped = jnp.where(row < by_level(level, [shifts[n, 0] for n in range(LEV)]), WLAT, 0)
    at = first_row + row + wrapped
    at = jnp.where(at >= grid_rows, at - grid_rows, at)
    top = sum((ids[n] == ids[0]).astype(I32) for n in range(WLAT - 1))
    bottom = sum((ids[grid_rows - 1 - n] == ids[grid_rows - 1]).astype(I32) for n in range(WLAT - 1))
    kind = jnp.where(at < top, 1, jnp.where(at >= grid_rows - bottom, 2, 0))
    features = lax.broadcasted_iota(I32, (32, COUNT), 0)
    same = (features == kind).astype(F32)
    bar_q[...] = jnp.zeros_like(bar_q)
    bar_q[:, :COUNT] = (same * -BARRED).astype(BF)
    bar_k[...] = jnp.zeros_like(bar_k)
    bar_k[:, :COUNT] = jnp.where(features < 3, 1.0 - same, 0.0).astype(BF)


def attend(size, bar_q, bar_k, q_s, k_s, v_s, g_s, buffers, ctx_ref, gp_ref):
    scale = 1.0 / math.sqrt(size)
    heads = HEADS
    part = heads * size

    def rows_of(h):
        return pl.ds(pl.multiple_of(h * size, size), size)

    def products(h, buffer):
        score_b, grad_b = buffer[:2]
        rows = rows_of(h)
        q_high, q_low = split_bf16(q_s[rows])
        k_high, k_low = split_bf16(k_s[rows])
        q_all = jnp.concatenate([q_high, q_low, q_high, bar_q[...]], axis=0)
        k_all = jnp.concatenate([k_high, k_high, k_low, bar_k[...]], axis=0)
        score_b[...] = dot(k_all.T[:COUNT], q_all, NN)
        grad_b[...] = dot(v_s[rows].T[:COUNT], g_s[rows], NN)

    def soften(buffer):
        score_b, grad_b, weight_b, high_b, low_b = buffer
        for start in range(0, LANES, 128):
            lanes = slice(start, start + 128)
            scores = score_b[:, lanes]
            expo = jnp.exp2(scores - jnp.max(scores, axis=0, keepdims=True))
            weights = expo * (1.0 / jnp.sum(expo, axis=0, keepdims=True))
            weight_b[:, lanes] = weights.astype(BF)
            grad_w = grad_b[:, lanes]
            grad_sc = weights * (grad_w - jnp.sum(weights * grad_w, axis=0, keepdims=True))
            high_b[:, lanes], low_b[:, lanes] = split_bf16(grad_sc)

    def results(h, buffer):
        weight_b, high_b, low_b = buffer[2:]
        rows = rows_of(h)
        q_high, q_low = split_bf16(q_s[rows])
        k_high, k_low = split_bf16(k_s[rows])
        rounded, high, low = weight_b[...], high_b[...], low_b[...]
        ctx_ref[rows] = dot(v_s[rows][:, :COUNT], rounded, NN)[:, :COUNT].astype(BF)
        k_pair = jnp.concatenate([k_high[:, :COUNT], k_low[:, :COUNT]], axis=0)
        q_pair = jnp.concatenate([q_high, q_low], axis=0)
        gq = dot(k_pair, high, NN)
        gq = gq[:size] + gq[size:] + dot(k_high[:, :COUNT], low, NN)
        gk = dot(q_pair, high, NT)
        gk = gk[:size] + gk[size:] + dot(q_high, low, NT)
        gv = dot(g_s[rows], rounded, NT)
        base = pl.multiple_of(h * size, size)
        gp_ref[pl.ds(base, size)] = (gq[:, :COUNT] * scale).astype(BF)
        gp_ref[pl.ds(part + base, size)] = (gk * math.log(2.0)).astype(BF)
        gp_ref[pl.ds(2 * part + base, size)] = gv.astype(BF)

    even, odd = buffers[:5], buffers[5:]
    products(0, even)

    def pair(p, carry):
        h = 2 * p
        products(h + 1, odd)
        soften(even)
        results(jnp.maximum(h - 1, 0), odd)
        products(jnp.minimum(h + 2, heads - 1), even)
        soften(odd)
        results(h, even)
        return carry

    lax.fori_loop(0, heads // 2, pair, 0)
    results(heads - 1, odd)


def project(w_ref, wp_ref, norm_s, cot_s, q_s, k_s, v_s, g_s):
    norm = norm_s[...]
    width = norm.shape[1]
    factor = math.log2(math.e) / math.sqrt(width // HEADS)
    q_s[...] = dot(w_ref[:width], norm, NT) * factor
    k_s[...] = dot(w_ref[width : 2 * width], norm, NT)
    v_s[...] = dot(w_ref[2 * width :], norm, NT).astype(BF)
    g_s[...] = dot(wp_ref[...], cot_s[...], NT).astype(BF)


def head_scratch(width):
    return [
        pltpu.VMEM((LANES, width), BF),
        pltpu.VMEM((LANES, width), BF),
        pltpu.VMEM((32, LANES), BF),
        pltpu.VMEM((32, LANES), BF),
        pltpu.VMEM((width, LANES), F32),
        pltpu.VMEM((width, LANES), F32),
        pltpu.VMEM((width, LANES), BF),
        pltpu.VMEM((width, LANES), BF),
    ] + [
        pltpu.VMEM((COUNT, LANES), kind) for _ in range(2) for kind in (F32, F32, BF, BF, BF)
    ]


def window_kernel(
    ahead, window, shifts, ids, spot, own_ref, got_ref, w_ref, wp_ref,
    tile_ref, norm_ref, ctx_ref, gp_ref,
    norm_s, cot_s, bar_q, bar_k, q_s, k_s, v_s, g_s, *buffers,
):
    width = own_ref.shape[-1]
    taken, spread = unpack_matrix(shifts, ahead)
    x = select_other(taken, spread, got_ref[0], own_ref[0])
    cot = select_other(taken, spread, got_ref[1], own_ref[1]).astype(BF)
    tile_ref[0] = x.astype(BF)
    tile_ref[1] = cot
    normed = standardize(x)[0].astype(BF)
    norm_ref[...] = normed
    norm_s[:COUNT] = normed
    norm_s[COUNT:] = jnp.zeros((LANES - COUNT, width), BF)
    cot_s[:COUNT] = cot
    cot_s[COUNT:] = jnp.zeros((LANES - COUNT, width), BF)
    bars(shifts, ids, spot[0] + window * WLAT, ids.shape[0], bar_q, bar_k)
    project(w_ref, wp_ref, norm_s, cot_s, q_s, k_s, v_s, g_s)
    attend(width // HEADS, bar_q, bar_k, q_s, k_s, v_s, g_s, buffers, ctx_ref, gp_ref)


def close_kernel(ahead, shifts, tile_ref, ctx_ref, gp_ref, w_ref, wp_ref, out_ref, send_ref):
    update = dot(ctx_ref[...], wp_ref[...], TN).astype(BF)
    grad_normed = dot(gp_ref[...], w_ref[...], TN)
    standard, inv_scale = standardize(tile_ref[0].astype(F32))
    grad = inv_scale * (
        grad_normed
        - jnp.mean(grad_normed, axis=1, keepdims=True)
        - standard * jnp.mean(grad_normed * standard, axis=1, keepdims=True)
    )
    grad = grad.astype(BF)
    chooser = pack_matrix(shifts, ahead)
    for field, value in enumerate((update, grad)):
        out_ref[field] = value
        send_ref[field] = dot(chooser, value, NN).astype(BF)


def weight_kernel(windows, kept, spot, *refs):
    norms, tiles, ctxs, gps = (refs[n * windows : (n + 1) * windows] for n in range(4))
    out_ref = refs[-1]
    part = ctxs[0].shape[0]

    def total(left, right):
        return functools.reduce(jnp.add, (dot(a, b, TT) for a, b in zip(left, right)))

    side = spot[1] if kept else 1 - spot[1]

    @pl.when(side == 0)
    def _():
        out_ref[...] = total([n[...] for n in norms], [g[: 2 * part] for g in gps])

    @pl.when(side == 1)
    def _():
        out_ref[:, :part] = total([n[...] for n in norms], [g[2 * part :] for g in gps])
        out_ref[:, part:] = total([t[1] for t in tiles], [c[...] for c in ctxs])


def halve_kernel(bit, spot, mine_ref, got_ref, keep_ref, send_ref):
    rows = keep_ref.shape[0]
    for side, ref in ((spot[bit], keep_ref), (1 - spot[bit], send_ref)):
        at = pl.ds(pl.multiple_of(side * rows, rows), rows)
        ref[...] = mine_ref[at] + got_ref[at]


def spread_kernel(spot, mine_ref, got_ref, *out_refs):
    rows = out_refs[0].shape[0]
    for d, ref in enumerate(out_refs):
        at = pl.ds(pl.multiple_of((spot[4] ^ d) * rows, rows), rows)
        ref[...] = mine_ref[at] + got_ref[at]


def gather_sum_kernel(*refs):
    refs[-1][...] = functools.reduce(jnp.add, (r[...] for r in refs[:-1])).astype(BF)


def arrange_kernel(spot, *refs):
    for d, ref in enumerate(refs[:-1]):
        refs[-1][spot[4] ^ d] = ref[...]


def join_kernel(bit, spot, mine_ref, got_ref, out_ref):
    count = mine_ref.shape[0]
    for side, ref in ((spot[bit], mine_ref), (1 - spot[bit], got_ref)):
        for n in range(count):
            out_ref[side * count + n] = ref[n]


def gradient_kernel(factor, spot, mine_ref, got_ref, qkv_ref, proj_ref):
    width = proj_ref.shape[0]
    count, rows = mine_ref.shape[:2]

    def write(pair_ref, rest_ref):
        for n in range(count):
            here = slice(n * rows, (n + 1) * rows)
            rest = rest_ref[n].astype(F32) * factor
            qkv_ref[here, : 2 * width] = pair_ref[n].astype(F32) * factor
            qkv_ref[here, 2 * width :] = rest[:, :width]
            proj_ref[:, here] = rest[:, width:].T

    first = spot[1] == 0

    @pl.when(first)
    def _():
        write(mine_ref, got_ref)

    @pl.when(jnp.logical_not(first))
    def _():
        write(got_ref, mine_ref)


def turn_kernel(w_ref, out_ref):
    out_ref[...] = w_ref[...].T


def last_back_kernel(ahead, shifts, own_ref, got_ref, out_ref):
    taken, spread = unpack_matrix(shifts, ahead)
    for field in range(2):
        out_ref[field] = select_other(taken, spread, got_ref[field], own_ref[field]).astype(BF)


def finish_kernel(ahead, windows, shifts, x_ref, cot_ref, above_ref, final_ref, *refs):
    owns, gots = refs[: windows - 1], refs[windows - 1 : 2 * windows - 2]
    outs = refs[2 * windows - 2 :]
    part = WLAT * WLON
    grid = x_ref.shape[1]
    taken, spread = unpack_matrix(shifts, ahead)
    movers = []
    for level in range(LEV):
        cut = shifts[level, 0]
        slot, first, row = level_slots(windows, cut, 1)
        slot = jnp.where(jnp.logical_and(first, row >= cut), -1, slot)
        cells = lax.broadcasted_iota(I32, (grid, (windows + 1) * part), 0)
        movers.append((cells == slot).astype(F32).astype(BF))
    for field, ref in enumerate((x_ref, cot_ref)):
        tiles = [
            select_other(taken, spread, gots[w][field], owns[w][field]) for w in range(windows - 1)
        ]
        tiles += [final_ref[field].astype(F32), above_ref[field].astype(F32)]
        for level in range(LEV):
            here = slice(level * part, (level + 1) * part)
            source = jnp.concatenate([t[here] for t in tiles], axis=0).astype(BF)
            value = ref[level].astype(F32) + dot(movers[level], source, NN)
            outs[field][level] = value.astype(BF)


def route(pairs_of, lat, lon):
    return [
        (a * lon + o, pairs_of(a, o)[0] * lon + pairs_of(a, o)[1])
        for a in range(lat)
        for o in range(lon)
    ]


def across_core(a, o):
    return a ^ 1, o


def step_one(a, o):
    return (a, o ^ 1) if a % 2 else (a ^ 2, o)


def step_two(a, o):
    return (a ^ 2, o) if a % 2 else (a, o ^ 1)


def all_sum(weights, spot, beside, earlier):
    lat, lon = lax.axis_size("lat"), lax.axis_size("lon")
    reach = lon // 2

    def swap(value, pairs_of):
        return lax.ppermute(value, ("lat", "lon"), route(pairs_of, lat, lon))

    def along(d):
        return lambda a, o: (a, o ^ (2 * d))

    sent = weights(False, earlier)
    got = swap(sent, across_core)
    held = weights(True, (sent,))
    after = beside(held)
    for bit, pairs_of in ((2, step_one), (3, step_two)):
        rows, width = held.shape[0] // 2, held.shape[1]
        held, sent = call(
            functools.partial(halve_kernel, bit),
            (spot, held, got),
            [shape_of(F32, rows, width)] * 2,
            scalars=1,
            after=after,
        )
        got = swap(sent, pairs_of)
        after = beside(held)
    rows = held.shape[0] // reach
    pieces = call(
        spread_kernel, (spot, held, got), [shape_of(F32, rows, width)] * reach, scalars=1, after=after
    )
    gots = [swap(pieces[d], along(d)) for d in range(1, reach)]
    after = beside(pieces[0])
    sums = call(gather_sum_kernel, (pieces[0], *gots), [shape_of(BF, rows, width)], after=after)[0]
    gots = [swap(sums, along(d)) for d in range(1, reach)]
    after = beside(sums)
    part = call(
        arrange_kernel, (spot, sums, *gots), [shape_of(BF, reach, rows, width)], scalars=1, after=after
    )[0]
    held = part.reshape(1, reach * rows, width)
    for bit, pairs_of in ((3, step_two), (2, step_one)):
        got = swap(held, pairs_of)
        after = beside(held)
        held = call(
            functools.partial(join_kernel, bit),
            (spot, held, got),
            [shape_of(BF, 2 * held.shape[0], *held.shape[1:])],
            scalars=1,
            after=after,
        )[0]
    return held, swap(held, across_core)


def ring(value, axis, step):
    count = lax.axis_size(axis)
    return lax.ppermute(value, axis, [(i, (i + step) % count) for i in range(count)])


def body(ahead, tokens, cotangent, w_qkv, w_proj, shifts, region_ids):
    levels, lat_rows, lon_cols, width = tokens.shape

    def by_column(grid_field):
        return grid_field.transpose(0, 2, 1, 3).reshape(levels, lon_cols * lat_rows, width)

    tokens, cotangent = by_column(tokens), by_column(cotangent)
    windows = lat_rows // WLAT
    my_lat, my_lon = lax.axis_index("lat"), lax.axis_index("lon")
    core, high, low = my_lat & 1, my_lat >> 1, my_lon & 1
    spot = jnp.stack(
        [
            my_lat * lat_rows,
            core,
            jnp.where(core == 1, low, high),
            jnp.where(core == 1, high, low),
            my_lon >> 1,
        ]
    ).astype(I32)
    out_step = -1 if ahead else 1
    pair = shape_of(BF, 2, COUNT, width)
    packed = shape_of(BF, 2, PACKED, width)

    def packs(chosen, sent, after):
        made = call(
            functools.partial(pack_kernel, ahead, windows, chosen, sent),
            (shifts, tokens, cotangent),
            [pair] * len(chosen) + [packed] * sent,
            scalars=1,
            after=after,
        )
        return made[: len(chosen)], made[len(chosen) :]

    def send_ahead(windows_sent, sends):
        for w, send in zip(windows_sent, sends):
            gots[w] = ring(send, "lon", out_step)

    gots, tiles = {}, {}
    (tiles[0], halo, last), sends = packs((0, windows, windows - 1), 1, ())
    send_ahead((0,), sends)
    below = ring(halo, "lat", -1)
    w_t = call(turn_kernel, (w_qkv,), [shape_of(BF, 3 * width, width)], after=(last,))[0]
    tiles[windows - 1], send = call(
        functools.partial(pack_last_kernel, ahead),
        (shifts, last, below),
        [pair, packed],
        scalars=1,
        after=(w_t,),
    )
    send_ahead((windows - 1,), (send,))
    middle = tuple(range(1, windows - 1))
    made, sends = packs(middle, len(middle), (send,))
    tiles.update(zip(middle, made))
    send_ahead(middle, sends)
    firsts, closed = {}, {}

    def window(w, after):
        firsts[w] = call(
            functools.partial(window_kernel, ahead, w),
            (shifts, region_ids, spot, tiles[w], gots[w], w_t, w_proj),
            [
                pair,
                shape_of(BF, COUNT, width),
                shape_of(BF, width, COUNT),
                shape_of(BF, 3 * width, COUNT),
            ],
            head_scratch(width),
            scalars=3,
            after=after,
        )
        return (firsts[w][1],)

    def close(w, after):
        tile, _, context, grads = firsts[w]
        out, send = call(
            functools.partial(close_kernel, ahead),
            (shifts, tile, context, grads, w_t, w_proj),
            [pair, packed],
            scalars=1,
            after=after,
        )
        closed[w] = out, ring(send, "lon", -out_step)
        return (send,)

    order = [0, windows - 1, *middle]
    after = (sends[0],)
    for n, w in enumerate(order):
        if n >= 2:
            after = (*after, closed[order[n - 2]][1])
        if n == windows - 1:
            final = call(
                functools.partial(last_back_kernel, ahead),
                (shifts, *closed[windows - 1]),
                [pair],
                scalars=1,
                after=after,
            )[0]
            above = ring(final, "lat", 1)
            after = (*after, final)
        after = window(w, after)
        if n < windows - 1:
            after = close(w, after)

    operands = [[firsts[w][n] for w in range(windows)] for n in (1, 0, 2, 3)]
    operands = [a for group in operands for a in group]

    def weights(kept, after):
        return call(
            functools.partial(weight_kernel, windows, kept),
            (spot, *operands),
            [shape_of(F32, width, 2 * width)],
            scalars=1,
            after=after,
        )[0]

    stage, results = [], []

    def beside(value):
        stage.append(value)
        if len(stage) == 1:
            return close(order[-1], (value,))
        if len(stage) == 2:
            return (above, closed[order[-1]][1])
        if len(stage) == 3:
            results.extend(
                call(
                    functools.partial(finish_kernel, ahead, windows),
                    (
                        shifts, tokens, cotangent, above, final,
                        *[closed[w][0] for w in range(windows - 1)],
                        *[closed[w][1] for w in range(windows - 1)],
                    ),
                    [shape_of(BF, *tokens.shape)] * 2,
                    scalars=1,
                    after=(value,),
                )
            )
            return (results[0],)
        return ()

    summed = all_sum(weights, spot, beside, (*after, closed[order[-2]][1]))
    mixed, grad_tokens = (
        r.reshape(levels, lon_cols, lat_rows, width).transpose(0, 2, 1, 3) for r in results
    )
    total_tokens = levels * lat_rows * lax.axis_size("lat") * lon_cols * lax.axis_size("lon")
    gradients = call(
        functools.partial(gradient_kernel, 1.0 / math.sqrt(total_tokens)),
        (spot, *summed),
        [shape_of(F32, width, 3 * width), shape_of(F32, width, width)],
        scalars=1,
    )
    return (mixed, grad_tokens, *gradients)


def local(tokens, cotangent, w_qkv, w_proj, shifts, region_ids):
    return lax.cond(
        jnp.sum(shifts[:, 1]) <= ENTRIES,
        functools.partial(body, True),
        functools.partial(body, False),
        tokens, cotangent, w_qkv, w_proj, shifts, region_ids,
    )


def solution(mesh):
    return jax.shard_map(
        local,
        mesh=mesh,
        in_specs=(P(None, "lat", "lon", None), P(None, "lat", "lon", None), P(), P(), P(), P()),
        out_specs=(P(None, "lat", "lon", None), P(None, "lat", "lon", None), P(), P()),
        check_vma=False,
    )
```

```python
import functools
import math

import jax
import jax.numpy as jnp
from jax import lax
from jax.experimental import pallas as pl
from jax.experimental.pallas import tpu as pltpu
from jax.sharding import PartitionSpec as P

HEADS = 16
WLAT = 6
WLON = 12
LEV = 4
COUNT = LEV * WLAT * WLON
LANES = 384
ENTRIES = LEV * WLON // 2
PACKED = ENTRIES * WLAT
NORM_EPS = 1e-05
BARRED = 2.0**100
BF = jnp.bfloat16
F32 = jnp.float32
I32 = jnp.int32

NN = (((1,), (0,)), ((), ()))
NT = (((1,), (1,)), ((), ()))
TN = (((0,), (0,)), ((), ()))
TT = (((0,), (1,)), ((), ()))

SMEM = pl.BlockSpec(memory_space=pltpu.SMEM)
VMEM = pl.BlockSpec(memory_space=pltpu.VMEM)
ANY = pl.BlockSpec(memory_space=pl.ANY)


def dot(a, b, dims):
    return lax.dot_general(a, b, dims, preferred_element_type=F32)


def split_bf16(value):
    high = value.astype(BF)
    low = (value - high.astype(F32)).astype(BF)
    return high, low


def call(kernel, ins, outs, scratch=(), scalars=0, after=()):

    def ordered(*refs):
        kernel(*refs[: len(ins)], *refs[len(ins) + len(after) :])

    return pl.pallas_call(
        ordered,
        in_specs=[SMEM] * scalars + [VMEM] * (len(ins) - scalars) + [ANY] * len(after),
        out_specs=[VMEM] * len(outs),
        out_shape=list(outs),
        scratch_shapes=list(scratch),
        compiler_params=pltpu.CompilerParams(vmem_limit_bytes=24 * 1024 * 1024),
        cost_estimate=pl.CostEstimate(
            flops=1_000_000, bytes_accessed=10_000, transcendentals=0
        ),
    )(*ins, *after)


def shape_of(dtype, *dims):
    return jax.ShapeDtypeStruct(dims, dtype)


def place(axis):
    dims = (COUNT, 1) if axis == 0 else (1, COUNT)
    token = lax.broadcasted_iota(I32, dims, axis)
    level = sum((token >= n * WLAT * WLON).astype(I32) for n in range(1, LEV))
    column, row = column_and_row(token - level * (WLAT * WLON))
    return level, row, column


def column_and_row(rest):
    column = sum((rest >= n * WLAT).astype(I32) for n in range(1, WLON))
    return column, rest - column * WLAT


def level_slots(windows, cut, axis):
    part = WLAT * WLON
    size = (windows + 1) * part
    dims = (size, 1) if axis == 0 else (1, size)
    token = lax.broadcasted_iota(I32, dims, axis)
    window = sum((token >= n * part).astype(I32) for n in range(1, windows + 1))
    column, row = column_and_row(token - window * part)
    at = window * WLAT + row + jnp.where(row < cut, WLAT, 0)
    slot = jnp.where(at < windows * WLAT, column * (windows * WLAT) + at, -1)
    first = window == windows
    return jnp.where(first, column * (windows * WLAT) + row, slot), first, row


def by_level(level, values):
    result = jnp.full(level.shape, values[0], I32)
    for n in range(1, LEV):
        result = jnp.where(level == n, values[n], result)
    return result


def from_next_row(shifts, axis):
    level, row, _ = place(axis)
    return row < by_level(level, [shifts[n, 0] for n in range(LEV)])


def from_other_side(shifts, ahead, axis):
    level, row, column = place(axis)
    cut = [shifts[n, 1] for n in range(LEV)]
    counts = cut if ahead else [WLON - c for c in cut]
    starts = [0] * LEV if ahead else cut
    offsets = [0]
    for n in range(LEV - 1):
        offsets.append(offsets[-1] + counts[n])
    at = by_level(level, cut)
    taken = (column < at) if ahead else (column >= at)
    entry = by_level(level, [o - s for o, s in zip(offsets, starts)]) + column
    return taken, jnp.where(taken, entry * WLAT + row, -1)


def pack_matrix(shifts, ahead):
    _, slot = from_other_side(shifts, ahead, 1)
    rows = lax.broadcasted_iota(I32, (PACKED, COUNT), 0)
    return (rows == slot).astype(F32).astype(BF)


def unpack_matrix(shifts, ahead):
    taken, slot = from_other_side(shifts, ahead, 0)
    columns = lax.broadcasted_iota(I32, (COUNT, PACKED), 1)
    return taken, (columns == slot).astype(F32).astype(BF)


def select_other(taken, spread, packed, own):
    return jnp.where(taken, dot(spread, packed, NN), own.astype(F32))


def pack_kernel(ahead, windows, chosen, sent, shifts, x_ref, cot_ref, *refs):
    part = WLAT * WLON
    grid = x_ref.shape[1]
    count = len(chosen)
    tile_refs, send_refs = refs[:count], refs[count:]
    chooser = pack_matrix(shifts, ahead)
    parts = [[[None] * LEV for _ in range(count)] for _ in range(2)]
    for level in range(LEV):
        slot, _, _ = level_slots(windows, shifts[level, 0], 0)
        slot = jnp.concatenate([slot[w * part : (w + 1) * part] for w in chosen], axis=0)
        cells = lax.broadcasted_iota(I32, (count * part, grid), 1)
        mover = (cells == slot).astype(F32).astype(BF)
        for field, ref in enumerate((x_ref, cot_ref)):
            moved = dot(mover, ref[level], NN)
            for w in range(count):
                parts[field][w][level] = moved[w * part : (w + 1) * part]
    for field in range(2):
        whole = [jnp.concatenate(p, axis=0).astype(BF) for p in parts[field]]
        for tile_ref, tile in zip(tile_refs, whole):
            tile_ref[field] = tile
        for send_ref, tile in zip(send_refs, whole[:sent]):
            send_ref[field] = dot(chooser, tile, NN).astype(BF)


def pack_last_kernel(ahead, shifts, last_ref, halo_ref, tile_ref, send_ref):
    lower = from_next_row(shifts, 0)
    chooser = pack_matrix(shifts, ahead)
    for field in range(2):
        tile = jnp.where(lower, halo_ref[field].astype(F32), last_ref[field].astype(F32))
        tile_ref[field] = tile.astype(BF)
        send_ref[field] = dot(chooser, tile.astype(BF), NN).astype(BF)


def standardize(values_full):
    center = values_full - jnp.mean(values_full, axis=1, keepdims=True)
    variance = jnp.mean(center * center, axis=1, keepdims=True)
    inv_scale = lax.rsqrt(variance + NORM_EPS)
    return center * inv_scale, inv_scale


def bars(shifts, ids, first_row, grid_rows, bar_q, bar_k):
    level, row, _ = place(1)
    wrapped = jnp.where(row < by_level(level, [shifts[n, 0] for n in range(LEV)]), WLAT, 0)
    at = first_row + row + wrapped
    at = jnp.where(at >= grid_rows, at - grid_rows, at)
    top = sum((ids[n] == ids[0]).astype(I32) for n in range(WLAT - 1))
    bottom = sum((ids[grid_rows - 1 - n] == ids[grid_rows - 1]).astype(I32) for n in range(WLAT - 1))
    kind = jnp.where(at < top, 1, jnp.where(at >= grid_rows - bottom, 2, 0))
    features = lax.broadcasted_iota(I32, (32, COUNT), 0)
    same = (features == kind).astype(F32)
    bar_q[...] = jnp.zeros_like(bar_q)
    bar_q[:, :COUNT] = (same * -BARRED).astype(BF)
    bar_k[...] = jnp.zeros_like(bar_k)
    bar_k[:, :COUNT] = jnp.where(features < 3, 1.0 - same, 0.0).astype(BF)


def attend(size, bar_q, bar_k, q_s, k_s, v_s, g_s, buffers, ctx_ref, gp_ref):
    scale = 1.0 / math.sqrt(size)
    heads = HEADS
    part = heads * size

    def rows_of(h):
        return pl.ds(pl.multiple_of(h * size, size), size)

    def products(h, buffer):
        score_b, grad_b = buffer[:2]
        rows = rows_of(h)
        q_high, q_low = split_bf16(q_s[rows])
        k_high, k_low = split_bf16(k_s[rows])
        q_all = jnp.concatenate([q_high, q_low, q_high, bar_q[...]], axis=0)
        k_all = jnp.concatenate([k_high, k_high, k_low, bar_k[...]], axis=0)
        score_b[...] = dot(k_all.T[:COUNT], q_all, NN)
        grad_b[...] = dot(v_s[rows].T[:COUNT], g_s[rows], NN)

    def soften(buffer):
        score_b, grad_b, weight_b, high_b, low_b = buffer
        for start in range(0, LANES, 128):
            lanes = slice(start, start + 128)
            scores = score_b[:, lanes]
            expo = jnp.exp2(scores - jnp.max(scores, axis=0, keepdims=True))
            weights = expo * (1.0 / jnp.sum(expo, axis=0, keepdims=True))
            weight_b[:, lanes] = weights.astype(BF)
            grad_w = grad_b[:, lanes]
            grad_sc = weights * (grad_w - jnp.sum(weights * grad_w, axis=0, keepdims=True))
            high_b[:, lanes], low_b[:, lanes] = split_bf16(grad_sc)

    def results(h, buffer):
        weight_b, high_b, low_b = buffer[2:]
        rows = rows_of(h)
        q_high, q_low = split_bf16(q_s[rows])
        k_high, k_low = split_bf16(k_s[rows])
        rounded, high, low = weight_b[...], high_b[...], low_b[...]
        ctx_ref[rows] = dot(v_s[rows][:, :COUNT], rounded, NN)[:, :COUNT].astype(BF)
        k_pair = jnp.concatenate([k_high[:, :COUNT], k_low[:, :COUNT]], axis=0)
        q_pair = jnp.concatenate([q_high, q_low], axis=0)
        gq = dot(k_pair, high, NN)
        gq = gq[:size] + gq[size:] + dot(k_high[:, :COUNT], low, NN)
        gk = dot(q_pair, high, NT)
        gk = gk[:size] + gk[size:] + dot(q_high, low, NT)
        gv = dot(g_s[rows], rounded, NT)
        base = pl.multiple_of(h * size, size)
        gp_ref[pl.ds(base, size)] = (gq[:, :COUNT] * scale).astype(BF)
        gp_ref[pl.ds(part + base, size)] = (gk * math.log(2.0)).astype(BF)
        gp_ref[pl.ds(2 * part + base, size)] = gv.astype(BF)

    even, odd = buffers[:5], buffers[5:]
    products(0, even)

    def pair(p, carry):
        h = 2 * p
        products(h + 1, odd)
        soften(even)
        results(jnp.maximum(h - 1, 0), odd)
        products(jnp.minimum(h + 2, heads - 1), even)
        soften(odd)
        results(h, even)
        return carry

    lax.fori_loop(0, heads // 2, pair, 0)
    results(heads - 1, odd)


def project(w_ref, wp_ref, norm_s, cot_s, q_s, k_s, v_s, g_s):
    norm = norm_s[...]
    width = norm.shape[1]
    factor = math.log2(math.e) / math.sqrt(width // HEADS)
    q_s[...] = dot(w_ref[:width], norm, NT) * factor
    k_s[...] = dot(w_ref[width : 2 * width], norm, NT)
    v_s[...] = dot(w_ref[2 * width :], norm, NT).astype(BF)
    g_s[...] = dot(wp_ref[...], cot_s[...], NT).astype(BF)


def head_scratch(width):
    return [
        pltpu.VMEM((LANES, width), BF),
        pltpu.VMEM((LANES, width), BF),
        pltpu.VMEM((32, LANES), BF),
        pltpu.VMEM((32, LANES), BF),
        pltpu.VMEM((width, LANES), F32),
        pltpu.VMEM((width, LANES), F32),
        pltpu.VMEM((width, LANES), BF),
        pltpu.VMEM((width, LANES), BF),
    ] + [
        pltpu.VMEM((COUNT, LANES), kind) for _ in range(2) for kind in (F32, F32, BF, BF, BF)
    ]


def window_kernel(
    ahead, window, shifts, ids, spot, own_ref, got_ref, w_ref, wp_ref,
    tile_ref, norm_ref, ctx_ref, gp_ref,
    norm_s, cot_s, bar_q, bar_k, q_s, k_s, v_s, g_s, *buffers,
):
    width = own_ref.shape[-1]
    taken, spread = unpack_matrix(shifts, ahead)
    x = select_other(taken, spread, got_ref[0], own_ref[0])
    cot = select_other(taken, spread, got_ref[1], own_ref[1]).astype(BF)
    tile_ref[0] = x.astype(BF)
    tile_ref[1] = cot
    normed = standardize(x)[0].astype(BF)
    norm_ref[...] = normed
    norm_s[:COUNT] = normed
    norm_s[COUNT:] = jnp.zeros((LANES - COUNT, width), BF)
    cot_s[:COUNT] = cot
    cot_s[COUNT:] = jnp.zeros((LANES - COUNT, width), BF)
    bars(shifts, ids, spot[0] + window * WLAT, ids.shape[0], bar_q, bar_k)
    project(w_ref, wp_ref, norm_s, cot_s, q_s, k_s, v_s, g_s)
    attend(width // HEADS, bar_q, bar_k, q_s, k_s, v_s, g_s, buffers, ctx_ref, gp_ref)


def close_kernel(ahead, shifts, tile_ref, ctx_ref, gp_ref, w_ref, wp_ref, out_ref, send_ref):
    update = dot(ctx_ref[...], wp_ref[...], TN).astype(BF)
    grad_normed = dot(gp_ref[...], w_ref[...], TN)
    standard, inv_scale = standardize(tile_ref[0].astype(F32))
    grad = inv_scale * (
        grad_normed
        - jnp.mean(grad_normed, axis=1, keepdims=True)
        - standard * jnp.mean(grad_normed * standard, axis=1, keepdims=True)
    )
    grad = grad.astype(BF)
    chooser = pack_matrix(shifts, ahead)
    for field, value in enumerate((update, grad)):
        out_ref[field] = value
        send_ref[field] = dot(chooser, value, NN).astype(BF)


def weight_kernel(windows, kept, spot, *refs):
    norms, tiles, ctxs, gps = (refs[n * windows : (n + 1) * windows] for n in range(4))
    out_ref = refs[-1]
    part = ctxs[0].shape[0]

    def total(left, right):
        return functools.reduce(jnp.add, (dot(a, b, TT) for a, b in zip(left, right)))

    side = spot[1] if kept else 1 - spot[1]

    @pl.when(side == 0)
    def _():
        out_ref[...] = total([n[...] for n in norms], [g[: 2 * part] for g in gps])

    @pl.when(side == 1)
    def _():
        out_ref[:, :part] = total([n[...] for n in norms], [g[2 * part :] for g in gps])
        out_ref[:, part:] = total([t[1] for t in tiles], [c[...] for c in ctxs])


def halve_kernel(bit, spot, mine_ref, got_ref, keep_ref, send_ref):
    rows = keep_ref.shape[0]
    for side, ref in ((spot[bit], keep_ref), (1 - spot[bit], send_ref)):
        at = pl.ds(pl.multiple_of(side * rows, rows), rows)
        ref[...] = mine_ref[at] + got_ref[at]


def spread_kernel(spot, mine_ref, got_ref, *out_refs):
    rows = out_refs[0].shape[0]
    for d, ref in enumerate(out_refs):
        at = pl.ds(pl.multiple_of((spot[4] ^ d) * rows, rows), rows)
        ref[...] = mine_ref[at] + got_ref[at]


def gather_sum_kernel(*refs):
    refs[-1][...] = functools.reduce(jnp.add, (r[...] for r in refs[:-1])).astype(BF)


def arrange_kernel(spot, *refs):
    for d, ref in enumerate(refs[:-1]):
        refs[-1][spot[4] ^ d] = ref[...]


def join_kernel(bit, spot, mine_ref, got_ref, out_ref):
    count = mine_ref.shape[0]
    for side, ref in ((spot[bit], mine_ref), (1 - spot[bit], got_ref)):
        for n in range(count):
            out_ref[side * count + n] = ref[n]


def gradient_kernel(factor, spot, mine_ref, got_ref, qkv_ref, proj_ref):
    width = proj_ref.shape[0]
    count, rows = mine_ref.shape[:2]

    def write(pair_ref, rest_ref):
        for n in range(count):
            here = slice(n * rows, (n + 1) * rows)
            rest = rest_ref[n].astype(F32) * factor
            qkv_ref[here, : 2 * width] = pair_ref[n].astype(F32) * factor
            qkv_ref[here, 2 * width :] = rest[:, :width]
            proj_ref[:, here] = rest[:, width:].T

    first = spot[1] == 0

    @pl.when(first)
    def _():
        write(mine_ref, got_ref)

    @pl.when(jnp.logical_not(first))
    def _():
        write(got_ref, mine_ref)


def turn_kernel(w_ref, out_ref):
    out_ref[...] = w_ref[...].T


def last_back_kernel(ahead, shifts, own_ref, got_ref, out_ref):
    taken, spread = unpack_matrix(shifts, ahead)
    for field in range(2):
        out_ref[field] = select_other(taken, spread, got_ref[field], own_ref[field]).astype(BF)


def finish_kernel(ahead, windows, shifts, x_ref, cot_ref, above_ref, final_ref, *refs):
    owns, gots = refs[: windows - 1], refs[windows - 1 : 2 * windows - 2]
    outs = refs[2 * windows - 2 :]
    part = WLAT * WLON
    grid = x_ref.shape[1]
    taken, spread = unpack_matrix(shifts, ahead)
    movers = []
    for level in range(LEV):
        cut = shifts[level, 0]
        slot, first, row = level_slots(windows, cut, 1)
        slot = jnp.where(jnp.logical_and(first, row >= cut), -1, slot)
        cells = lax.broadcasted_iota(I32, (grid, (windows + 1) * part), 0)
        movers.append((cells == slot).astype(F32).astype(BF))
    for field, ref in enumerate((x_ref, cot_ref)):
        tiles = [
            select_other(taken, spread, gots[w][field], owns[w][field]) for w in range(windows - 1)
        ]
        tiles += [final_ref[field].astype(F32), above_ref[field].astype(F32)]
        for level in range(LEV):
            here = slice(level * part, (level + 1) * part)
            source = jnp.concatenate([t[here] for t in tiles], axis=0).astype(BF)
            value = ref[level].astype(F32) + dot(movers[level], source, NN)
            outs[field][level] = value.astype(BF)


def route(pairs_of, lat, lon):
    return [
        (a * lon + o, pairs_of(a, o)[0] * lon + pairs_of(a, o)[1])
        for a in range(lat)
        for o in range(lon)
    ]


def across_core(a, o):
    return a ^ 1, o


def step_one(a, o):
    return (a, o ^ 1) if a % 2 else (a ^ 2, o)


def step_two(a, o):
    return (a ^ 2, o) if a % 2 else (a, o ^ 1)


def all_sum(weights, spot, beside, earlier):
    lat, lon = lax.axis_size("lat"), lax.axis_size("lon")
    reach = lon // 2

    def swap(value, pairs_of):
        return lax.ppermute(value, ("lat", "lon"), route(pairs_of, lat, lon))

    def along(d):
        return lambda a, o: (a, o ^ (2 * d))

    sent = weights(False, earlier)
    got = swap(sent, across_core)
    held = weights(True, (sent,))
    after = beside(held)
    for bit, pairs_of in ((2, step_one), (3, step_two)):
        rows, width = held.shape[0] // 2, held.shape[1]
        held, sent = call(
            functools.partial(halve_kernel, bit),
            (spot, held, got),
            [shape_of(F32, rows, width)] * 2,
            scalars=1,
            after=after,
        )
        got = swap(sent, pairs_of)
        after = beside(held)
    rows = held.shape[0] // reach
    pieces = call(
        spread_kernel, (spot, held, got), [shape_of(F32, rows, width)] * reach, scalars=1, after=after
    )
    gots = [swap(pieces[d], along(d)) for d in range(1, reach)]
    after = beside(pieces[0])
    sums = call(gather_sum_kernel, (pieces[0], *gots), [shape_of(BF, rows, width)], after=after)[0]
    gots = [swap(sums, along(d)) for d in range(1, reach)]
    after = beside(sums)
    part = call(
        arrange_kernel, (spot, sums, *gots), [shape_of(BF, reach, rows, width)], scalars=1, after=after
    )[0]
    held = part.reshape(1, reach * rows, width)
    for bit, pairs_of in ((3, step_two), (2, step_one)):
        got = swap(held, pairs_of)
        after = beside(held)
        held = call(
            functools.partial(join_kernel, bit),
            (spot, held, got),
            [shape_of(BF, 2 * held.shape[0], *held.shape[1:])],
            scalars=1,
            after=after,
        )[0]
    return held, swap(held, across_core)


def ring(value, axis, step):
    count = lax.axis_size(axis)
    return lax.ppermute(value, axis, [(i, (i + step) % count) for i in range(count)])


def body(ahead, tokens, cotangent, w_qkv, w_proj, shifts, region_ids):
    levels, lat_rows, lon_cols, width = tokens.shape

    def by_column(grid_field):
        return grid_field.transpose(0, 2, 1, 3).reshape(levels, lon_cols * lat_rows, width)

    tokens, cotangent = by_column(tokens), by_column(cotangent)
    windows = lat_rows // WLAT
    my_lat, my_lon = lax.axis_index("lat"), lax.axis_index("lon")
    core, high, low = my_lat & 1, my_lat >> 1, my_lon & 1
    spot = jnp.stack(
        [
            my_lat * lat_rows,
            core,
            jnp.where(core == 1, low, high),
            jnp.where(core == 1, high, low),
            my_lon >> 1,
        ]
    ).astype(I32)
    out_step = -1 if ahead else 1
    pair = shape_of(BF, 2, COUNT, width)
    packed = shape_of(BF, 2, PACKED, width)

    def packs(chosen, sent, after):
        made = call(
            functools.partial(pack_kernel, ahead, windows, chosen, sent),
            (shifts, tokens, cotangent),
            [pair] * len(chosen) + [packed] * sent,
            scalars=1,
            after=after,
        )
        return made[: len(chosen)], made[len(chosen) :]

    def send_ahead(windows_sent, sends):
        for w, send in zip(windows_sent, sends):
            gots[w] = ring(send, "lon", out_step)

    gots, tiles = {}, {}
    (tiles[0], halo, last), sends = packs((0, windows, windows - 1), 1, ())
    send_ahead((0,), sends)
    below = ring(halo, "lat", -1)
    w_t = call(turn_kernel, (w_qkv,), [shape_of(BF, 3 * width, width)], after=(last,))[0]
    tiles[windows - 1], send = call(
        functools.partial(pack_last_kernel, ahead),
        (shifts, last, below),
        [pair, packed],
        scalars=1,
        after=(w_t,),
    )
    send_ahead((windows - 1,), (send,))
    middle = tuple(range(1, windows - 1))
    made, sends = packs(middle, len(middle), (send,))
    tiles.update(zip(middle, made))
    send_ahead(middle, sends)
    firsts, closed = {}, {}

    def window(w, after):
        firsts[w] = call(
            functools.partial(window_kernel, ahead, w),
            (shifts, region_ids, spot, tiles[w], gots[w], w_t, w_proj),
            [
                pair,
                shape_of(BF, COUNT, width),
                shape_of(BF, width, COUNT),
                shape_of(BF, 3 * width, COUNT),
            ],
            head_scratch(width),
            scalars=3,
            after=after,
        )
        return (firsts[w][1],)

    def close(w, after):
        tile, _, context, grads = firsts[w]
        out, send = call(
            functools.partial(close_kernel, ahead),
            (shifts, tile, context, grads, w_t, w_proj),
            [pair, packed],
            scalars=1,
            after=after,
        )
        closed[w] = out, ring(send, "lon", -out_step)
        return (send,)

    order = [0, windows - 1, *middle]
    after = (sends[0],)
    for n, w in enumerate(order):
        if n >= 2:
            after = (*after, closed[order[n - 2]][1])
        if n == windows - 2:
            after = (*after, gots[order[-1]])
        if n == windows - 1:
            final = call(
                functools.partial(last_back_kernel, ahead),
                (shifts, *closed[windows - 1]),
                [pair],
                scalars=1,
                after=after,
            )[0]
            above = ring(final, "lat", 1)
            after = (*after, final)
        after = window(w, after)
        if n < windows - 1:
            after = close(w, after)

    operands = [[firsts[w][n] for w in range(windows)] for n in (1, 0, 2, 3)]
    operands = [a for group in operands for a in group]

    def weights(kept, after):
        return call(
            functools.partial(weight_kernel, windows, kept),
            (spot, *operands),
            [shape_of(F32, width, 2 * width)],
            scalars=1,
            after=after,
        )[0]

    stage, results = [], []

    def beside(value):
        stage.append(value)
        if len(stage) == 1:
            return close(order[-1], (value,))
        if len(stage) == 4:
            return (closed[order[-1]][1],)
        if len(stage) == 5:
            results.extend(
                call(
                    functools.partial(finish_kernel, ahead, windows),
                    (
                        shifts, tokens, cotangent, above, final,
                        *[closed[w][0] for w in range(windows - 1)],
                        *[closed[w][1] for w in range(windows - 1)],
                    ),
                    [shape_of(BF, *tokens.shape)] * 2,
                    scalars=1,
                    after=(value,),
                )
            )
            return (results[0],)
        return ()

    summed = all_sum(weights, spot, beside, (*after, above, closed[order[-2]][1]))
    mixed, grad_tokens = (
        r.reshape(levels, lon_cols, lat_rows, width).transpose(0, 2, 1, 3) for r in results
    )
    total_tokens = levels * lat_rows * lax.axis_size("lat") * lon_cols * lax.axis_size("lon")
    gradients = call(
        functools.partial(gradient_kernel, 1.0 / math.sqrt(total_tokens)),
        (spot, *summed),
        [shape_of(F32, width, 3 * width), shape_of(F32, width, width)],
        scalars=1,
    )
    return (mixed, grad_tokens, *gradients)


def local(tokens, cotangent, w_qkv, w_proj, shifts, region_ids):
    return lax.cond(
        jnp.sum(shifts[:, 1]) <= ENTRIES,
        functools.partial(body, True),
        functools.partial(body, False),
        tokens, cotangent, w_qkv, w_proj, shifts, region_ids,
    )


def solution(mesh):
    return jax.shard_map(
        local,
        mesh=mesh,
        in_specs=(P(None, "lat", "lon", None), P(None, "lat", "lon", None), P(), P(), P(), P()),
        out_specs=(P(None, "lat", "lon", None), P(None, "lat", "lon", None), P(), P()),
        check_vma=False,
    )
```

```python
import functools
import math

import jax
import jax.numpy as jnp
from jax import lax
from jax.experimental import pallas as pl
from jax.experimental.pallas import tpu as pltpu
from jax.sharding import PartitionSpec as P

HEADS = 16
WLAT = 6
WLON = 12
LEV = 4
COUNT = LEV * WLAT * WLON
LANES = 384
MAIN = 256
REST = COUNT - MAIN
ENTRIES = LEV * WLON // 2
PACKED = ENTRIES * WLAT
NORM_EPS = 1e-05
BARRED = 2.0**100
BF = jnp.bfloat16
F32 = jnp.float32
I32 = jnp.int32

NN = (((1,), (0,)), ((), ()))
NT = (((1,), (1,)), ((), ()))
TN = (((0,), (0,)), ((), ()))
TT = (((0,), (1,)), ((), ()))

SMEM = pl.BlockSpec(memory_space=pltpu.SMEM)
VMEM = pl.BlockSpec(memory_space=pltpu.VMEM)
ANY = pl.BlockSpec(memory_space=pl.ANY)


def dot(a, b, dims):
    return lax.dot_general(a, b, dims, preferred_element_type=F32)


def split_bf16(value):
    high = value.astype(BF)
    low = (value - high.astype(F32)).astype(BF)
    return high, low


def call(kernel, ins, outs, scratch=(), scalars=0, after=()):

    def ordered(*refs):
        kernel(*refs[: len(ins)], *refs[len(ins) + len(after) :])

    return pl.pallas_call(
        ordered,
        in_specs=[SMEM] * scalars + [VMEM] * (len(ins) - scalars) + [ANY] * len(after),
        out_specs=[VMEM] * len(outs),
        out_shape=list(outs),
        scratch_shapes=list(scratch),
        compiler_params=pltpu.CompilerParams(vmem_limit_bytes=24 * 1024 * 1024),
        cost_estimate=pl.CostEstimate(
            flops=1_000_000, bytes_accessed=10_000, transcendentals=0
        ),
    )(*ins, *after)


def shape_of(dtype, *dims):
    return jax.ShapeDtypeStruct(dims, dtype)


def place(axis):
    dims = (COUNT, 1) if axis == 0 else (1, COUNT)
    token = lax.broadcasted_iota(I32, dims, axis)
    level = sum((token >= n * WLAT * WLON).astype(I32) for n in range(1, LEV))
    column, row = column_and_row(token - level * (WLAT * WLON))
    return level, row, column


def column_and_row(rest):
    column = sum((rest >= n * WLAT).astype(I32) for n in range(1, WLON))
    return column, rest - column * WLAT


def level_slots(windows, cut, axis):
    part = WLAT * WLON
    size = (windows + 1) * part
    dims = (size, 1) if axis == 0 else (1, size)
    token = lax.broadcasted_iota(I32, dims, axis)
    window = sum((token >= n * part).astype(I32) for n in range(1, windows + 1))
    column, row = column_and_row(token - window * part)
    at = window * WLAT + row + jnp.where(row < cut, WLAT, 0)
    slot = jnp.where(at < windows * WLAT, column * (windows * WLAT) + at, -1)
    first = window == windows
    return jnp.where(first, column * (windows * WLAT) + row, slot), first, row


def by_level(level, values):
    result = jnp.full(level.shape, values[0], I32)
    for n in range(1, LEV):
        result = jnp.where(level == n, values[n], result)
    return result


def from_next_row(shifts, axis):
    level, row, _ = place(axis)
    return row < by_level(level, [shifts[n, 0] for n in range(LEV)])


def from_other_side(shifts, ahead, axis):
    level, row, column = place(axis)
    cut = [shifts[n, 1] for n in range(LEV)]
    counts = cut if ahead else [WLON - c for c in cut]
    starts = [0] * LEV if ahead else cut
    offsets = [0]
    for n in range(LEV - 1):
        offsets.append(offsets[-1] + counts[n])
    at = by_level(level, cut)
    taken = (column < at) if ahead else (column >= at)
    entry = by_level(level, [o - s for o, s in zip(offsets, starts)]) + column
    return taken, jnp.where(taken, entry * WLAT + row, -1)


def pack_matrix(shifts, ahead):
    _, slot = from_other_side(shifts, ahead, 1)
    rows = lax.broadcasted_iota(I32, (PACKED, COUNT), 0)
    return (rows == slot).astype(F32).astype(BF)


def unpack_matrix(shifts, ahead):
    taken, slot = from_other_side(shifts, ahead, 0)
    columns = lax.broadcasted_iota(I32, (COUNT, PACKED), 1)
    return taken, (columns == slot).astype(F32).astype(BF)


def select_other(taken, spread, packed, own):
    return jnp.where(taken, dot(spread, packed, NN), own.astype(F32))


def pack_kernel(ahead, windows, chosen, sent, shifts, x_ref, cot_ref, *refs):
    part = WLAT * WLON
    grid = x_ref.shape[1]
    count = len(chosen)
    tile_refs, send_refs = refs[:count], refs[count:]
    chooser = pack_matrix(shifts, ahead)
    parts = [[[None] * LEV for _ in range(count)] for _ in range(2)]
    for level in range(LEV):
        slot, _, _ = level_slots(windows, shifts[level, 0], 0)
        slot = jnp.concatenate([slot[w * part : (w + 1) * part] for w in chosen], axis=0)
        cells = lax.broadcasted_iota(I32, (count * part, grid), 1)
        mover = (cells == slot).astype(F32).astype(BF)
        for field, ref in enumerate((x_ref, cot_ref)):
            moved = dot(mover, ref[level], NN)
            for w in range(count):
                parts[field][w][level] = moved[w * part : (w + 1) * part]
    for field in range(2):
        whole = [jnp.concatenate(p, axis=0).astype(BF) for p in parts[field]]
        for tile_ref, tile in zip(tile_refs, whole):
            tile_ref[field] = tile
        for send_ref, tile in zip(send_refs, whole[:sent]):
            send_ref[field] = dot(chooser, tile, NN).astype(BF)


def pack_last_kernel(ahead, shifts, last_ref, halo_ref, tile_ref, send_ref):
    lower = from_next_row(shifts, 0)
    chooser = pack_matrix(shifts, ahead)
    for field in range(2):
        tile = jnp.where(lower, halo_ref[field].astype(F32), last_ref[field].astype(F32))
        tile_ref[field] = tile.astype(BF)
        send_ref[field] = dot(chooser, tile.astype(BF), NN).astype(BF)


def standardize(values_full):
    center = values_full - jnp.mean(values_full, axis=1, keepdims=True)
    variance = jnp.mean(center * center, axis=1, keepdims=True)
    inv_scale = lax.rsqrt(variance + NORM_EPS)
    return center * inv_scale, inv_scale


def bars(shifts, ids, first_row, grid_rows, bar_q, bar_k):
    level, row, _ = place(1)
    wrapped = jnp.where(row < by_level(level, [shifts[n, 0] for n in range(LEV)]), WLAT, 0)
    at = first_row + row + wrapped
    at = jnp.where(at >= grid_rows, at - grid_rows, at)
    top = sum((ids[n] == ids[0]).astype(I32) for n in range(WLAT - 1))
    bottom = sum((ids[grid_rows - 1 - n] == ids[grid_rows - 1]).astype(I32) for n in range(WLAT - 1))
    kind = jnp.where(at < top, 1, jnp.where(at >= grid_rows - bottom, 2, 0))
    features = lax.broadcasted_iota(I32, (32, COUNT), 0)
    same = (features == kind).astype(F32)
    bar_q[...] = jnp.zeros_like(bar_q)
    bar_q[:, :COUNT] = (same * -BARRED).astype(BF)
    bar_k[...] = jnp.zeros_like(bar_k)
    bar_k[:, :COUNT] = jnp.where(features < 3, 1.0 - same, 0.0).astype(BF)


def attend(size, bar_q, bar_k, q_s, k_s, v_s, g_s, q_rest, g_rest, buffers, ctx_ref, gp_ref):
    scale = 1.0 / math.sqrt(size)
    part = HEADS * size
    even, odd, both = buffers[:6], buffers[6:12], buffers[12:]

    def rows_of(h, count=1):
        return pl.ds(pl.multiple_of(h * size, size), count * size)

    def stacked(query, bar):
        high, low = split_bf16(query)
        return jnp.concatenate([high, low, high, bar], axis=0)

    def products(h, buffer):
        score_b, grad_b, key_b = buffer[0], buffer[1], buffer[5]
        rows = rows_of(h)
        high, low = split_bf16(k_s[rows])
        key_b[...] = jnp.concatenate([high, high, low, bar_k[...]], axis=0).T[:COUNT]
        score_b[...] = dot(key_b[...], stacked(q_s[rows, :MAIN], bar_q[:, :MAIN]), NN)
        grad_b[...] = dot(v_s[rows].T[:COUNT], g_s[rows, :MAIN], NN)

    def products_both(h):
        keys = jnp.concatenate([even[5][...], odd[5][...]], axis=1)
        bar = bar_q[:, MAIN:]
        rolled = pltpu.roll(bar.astype(F32), REST, 1).astype(BF)
        queries = [stacked(q_rest[rows_of(h)], bar), stacked(q_rest[rows_of(h + 1)], rolled)]
        both[0][...] = dot(keys, jnp.concatenate(queries, axis=0), NN)
        rows = rows_of(h, 2)
        both[1][...] = dot(v_s[rows].T[:COUNT], g_rest[rows], NN)

    def soften(buffer):
        score_b, grad_b, weight_b, high_b, low_b = buffer[:5]
        for start in range(0, score_b.shape[1], 128):
            lanes = slice(start, start + 128)
            scores = score_b[:, lanes]
            expo = jnp.exp2(scores - jnp.max(scores, axis=0, keepdims=True))
            weights = expo * (1.0 / jnp.sum(expo, axis=0, keepdims=True))
            weight_b[:, lanes] = weights.astype(BF)
            grad_w = grad_b[:, lanes]
            grad_sc = weights * (grad_w - jnp.sum(weights * grad_w, axis=0, keepdims=True))
            high_b[:, lanes], low_b[:, lanes] = split_bf16(grad_sc)

    def results(h, buffer, roll):
        rows = rows_of(h)
        value = v_s[rows][:, :COUNT]
        k_high, k_low = split_bf16(k_s[rows][:, :COUNT])
        k_pair = jnp.concatenate([k_high, k_low], axis=0)
        base = pl.multiple_of(h * size, size)
        gk = gv = 0.0
        pieces = (
            (buffer[2:5], q_s[rows, :MAIN], g_s[rows, :MAIN], 0, slice(0, MAIN)),
            (both[2:5], q_rest[rows], g_rest[rows], roll, slice(MAIN, COUNT)),
        )
        for (weight_b, high_b, low_b), query, grad_ctx, turn, lanes in pieces:
            rounded, high, low = weight_b[...], high_b[...], low_b[...]
            q_high, q_low = split_bf16(query)
            context = dot(value, rounded, NN)
            gq = dot(k_pair, high, NN)
            gq = (gq[:size] + gq[size:] + dot(k_high, low, NN)) * scale
            if turn:
                context, gq = (pltpu.roll(a, 128 - turn, 1) for a in (context, gq))
            width = lanes.stop - lanes.start
            ctx_ref[rows, lanes] = context[:, :width].astype(BF)
            gp_ref[pl.ds(base, size), lanes] = gq[:, :width].astype(BF)
            pair = dot(jnp.concatenate([q_high, q_low], axis=0), high, NT)
            gk = gk + pair[:size] + pair[size:] + dot(q_high, low, NT)
            gv = gv + dot(grad_ctx, rounded, NT)
        gp_ref[pl.ds(part + base, size)] = (gk * math.log(2.0)).astype(BF)
        gp_ref[pl.ds(2 * part + base, size)] = gv.astype(BF)

    products(0, even)
    products(1, odd)
    products_both(0)

    def pair(p, carry):
        h = 2 * p
        after = jnp.minimum(h + 2, HEADS - 2)
        soften(even)
        results(jnp.maximum(h - 1, 1), odd, REST)
        soften(odd)
        products(after, even)
        soften(both)
        products(after + 1, odd)
        results(h, even, 0)
        products_both(after)
        return carry

    lax.fori_loop(0, HEADS // 2, pair, 0)
    results(HEADS - 1, odd, REST)


def project(w_ref, wp_ref, norm_s, cot_s, q_s, k_s, v_s, g_s, q_rest, g_rest):
    norm = norm_s[...]
    width = norm.shape[1]
    factor = math.log2(math.e) / math.sqrt(width // HEADS)
    q_s[...] = dot(w_ref[:width], norm, NT) * factor
    k_s[...] = dot(w_ref[width : 2 * width], norm, NT)
    v_s[...] = dot(w_ref[2 * width :], norm, NT).astype(BF)
    g_s[...] = dot(wp_ref[...], cot_s[...], NT).astype(BF)
    odd = (lax.broadcasted_iota(I32, (width, 128), 0) // (width // HEADS)) % 2 == 1
    for source, rest in ((q_s, q_rest), (g_s, g_rest)):
        value = source[:, MAIN:].astype(F32)
        rest[...] = jnp.where(odd, pltpu.roll(value, REST, 1), value).astype(rest.dtype)


def head_scratch(width):
    return [
        pltpu.VMEM((LANES, width), BF),
        pltpu.VMEM((LANES, width), BF),
        pltpu.VMEM((32, LANES), BF),
        pltpu.VMEM((32, LANES), BF),
        pltpu.VMEM((width, LANES), F32),
        pltpu.VMEM((width, LANES), F32),
        pltpu.VMEM((width, LANES), BF),
        pltpu.VMEM((width, LANES), BF),
        pltpu.VMEM((width, 128), F32),
        pltpu.VMEM((width, 128), BF),
    ] + [
        pltpu.VMEM((COUNT, lanes), kind)
        for size in (MAIN, MAIN, 128)
        for kind, lanes in ((F32, size), (F32, size), (BF, size), (BF, size), (BF, size), (BF, 128))
    ]


def window_kernel(
    ahead, window, shifts, ids, spot, own_ref, got_ref, w_ref, wp_ref,
    tile_ref, norm_ref, ctx_ref, gp_ref,
    norm_s, cot_s, bar_q, bar_k, q_s, k_s, v_s, g_s, q_rest, g_rest, *buffers,
):
    width = own_ref.shape[-1]
    taken, spread = unpack_matrix(shifts, ahead)
    x = select_other(taken, spread, got_ref[0], own_ref[0])
    cot = select_other(taken, spread, got_ref[1], own_ref[1]).astype(BF)
    tile_ref[0] = x.astype(BF)
    tile_ref[1] = cot
    normed = standardize(x)[0].astype(BF)
    norm_ref[...] = normed
    norm_s[:COUNT] = normed
    norm_s[COUNT:] = jnp.zeros((LANES - COUNT, width), BF)
    cot_s[:COUNT] = cot
    cot_s[COUNT:] = jnp.zeros((LANES - COUNT, width), BF)
    bars(shifts, ids, spot[0] + window * WLAT, ids.shape[0], bar_q, bar_k)
    rests = q_rest, g_rest
    project(w_ref, wp_ref, norm_s, cot_s, q_s, k_s, v_s, g_s, *rests)
    attend(
        width // HEADS, bar_q, bar_k, q_s, k_s, v_s, g_s, *rests, buffers, ctx_ref, gp_ref
    )


def close_kernel(ahead, shifts, tile_ref, ctx_ref, gp_ref, w_ref, wp_ref, out_ref, send_ref):
    update = dot(ctx_ref[...], wp_ref[...], TN).astype(BF)
    grad_normed = dot(gp_ref[...], w_ref[...], TN)
    standard, inv_scale = standardize(tile_ref[0].astype(F32))
    grad = inv_scale * (
        grad_normed
        - jnp.mean(grad_normed, axis=1, keepdims=True)
        - standard * jnp.mean(grad_normed * standard, axis=1, keepdims=True)
    )
    grad = grad.astype(BF)
    chooser = pack_matrix(shifts, ahead)
    for field, value in enumerate((update, grad)):
        out_ref[field] = value
        send_ref[field] = dot(chooser, value, NN).astype(BF)


def weight_kernel(windows, kept, spot, *refs):
    norms, tiles, ctxs, gps = (refs[n * windows : (n + 1) * windows] for n in range(4))
    out_ref = refs[-1]
    part = ctxs[0].shape[0]

    def total(left, right):
        return functools.reduce(jnp.add, (dot(a, b, TT) for a, b in zip(left, right)))

    side = spot[1] if kept else 1 - spot[1]

    @pl.when(side == 0)
    def _():
        out_ref[...] = total([n[...] for n in norms], [g[: 2 * part] for g in gps])

    @pl.when(side == 1)
    def _():
        out_ref[:, :part] = total([n[...] for n in norms], [g[2 * part :] for g in gps])
        out_ref[:, part:] = total([t[1] for t in tiles], [c[...] for c in ctxs])


def halve_kernel(bit, spot, mine_ref, got_ref, keep_ref, send_ref):
    rows = keep_ref.shape[0]
    for side, ref in ((spot[bit], keep_ref), (1 - spot[bit], send_ref)):
        at = pl.ds(pl.multiple_of(side * rows, rows), rows)
        ref[...] = mine_ref[at] + got_ref[at]


def spread_kernel(spot, mine_ref, got_ref, *out_refs):
    rows = out_refs[0].shape[0]
    for d, ref in enumerate(out_refs):
        at = pl.ds(pl.multiple_of((spot[4] ^ d) * rows, rows), rows)
        ref[...] = mine_ref[at] + got_ref[at]


def gather_sum_kernel(*refs):
    refs[-1][...] = functools.reduce(jnp.add, (r[...] for r in refs[:-1])).astype(BF)


def arrange_kernel(spot, *refs):
    for d, ref in enumerate(refs[:-1]):
        refs[-1][spot[4] ^ d] = ref[...]


def join_kernel(bit, spot, mine_ref, got_ref, out_ref):
    count = mine_ref.shape[0]
    for side, ref in ((spot[bit], mine_ref), (1 - spot[bit], got_ref)):
        for n in range(count):
            out_ref[side * count + n] = ref[n]


def gradient_kernel(factor, spot, mine_ref, got_ref, qkv_ref, proj_ref):
    width = proj_ref.shape[0]
    count, rows = mine_ref.shape[:2]

    def write(pair_ref, rest_ref):
        for n in range(count):
            here = slice(n * rows, (n + 1) * rows)
            rest = rest_ref[n].astype(F32) * factor
            qkv_ref[here, : 2 * width] = pair_ref[n].astype(F32) * factor
            qkv_ref[here, 2 * width :] = rest[:, :width]
            proj_ref[:, here] = rest[:, width:].T

    first = spot[1] == 0

    @pl.when(first)
    def _():
        write(mine_ref, got_ref)

    @pl.when(jnp.logical_not(first))
    def _():
        write(got_ref, mine_ref)


def turn_kernel(w_ref, out_ref):
    out_ref[...] = w_ref[...].T


def last_back_kernel(ahead, shifts, own_ref, got_ref, out_ref):
    taken, spread = unpack_matrix(shifts, ahead)
    for field in range(2):
        out_ref[field] = select_other(taken, spread, got_ref[field], own_ref[field]).astype(BF)


def finish_kernel(ahead, windows, shifts, x_ref, cot_ref, above_ref, final_ref, *refs):
    owns, gots = refs[: windows - 1], refs[windows - 1 : 2 * windows - 2]
    outs = refs[2 * windows - 2 :]
    part = WLAT * WLON
    grid = x_ref.shape[1]
    taken, spread = unpack_matrix(shifts, ahead)
    movers = []
    for level in range(LEV):
        cut = shifts[level, 0]
        slot, first, row = level_slots(windows, cut, 1)
        slot = jnp.where(jnp.logical_and(first, row >= cut), -1, slot)
        cells = lax.broadcasted_iota(I32, (grid, (windows + 1) * part), 0)
        movers.append((cells == slot).astype(F32).astype(BF))
    for field, ref in enumerate((x_ref, cot_ref)):
        tiles = [
            select_other(taken, spread, gots[w][field], owns[w][field]) for w in range(windows - 1)
        ]
        tiles += [final_ref[field].astype(F32), above_ref[field].astype(F32)]
        for level in range(LEV):
            here = slice(level * part, (level + 1) * part)
            source = jnp.concatenate([t[here] for t in tiles], axis=0).astype(BF)
            value = ref[level].astype(F32) + dot(movers[level], source, NN)
            outs[field][level] = value.astype(BF)


def route(pairs_of, lat, lon):
    return [
        (a * lon + o, pairs_of(a, o)[0] * lon + pairs_of(a, o)[1])
        for a in range(lat)
        for o in range(lon)
    ]


def across_core(a, o):
    return a ^ 1, o


def step_one(a, o):
    return (a, o ^ 1) if a % 2 else (a ^ 2, o)


def step_two(a, o):
    return (a ^ 2, o) if a % 2 else (a, o ^ 1)


def all_sum(weights, spot, beside, earlier):
    lat, lon = lax.axis_size("lat"), lax.axis_size("lon")
    reach = lon // 2

    def swap(value, pairs_of):
        return lax.ppermute(value, ("lat", "lon"), route(pairs_of, lat, lon))

    def along(d):
        return lambda a, o: (a, o ^ (2 * d))

    sent = weights(False, earlier)
    got = swap(sent, across_core)
    held = weights(True, (sent,))
    after = beside(held)
    for bit, pairs_of in ((2, step_one), (3, step_two)):
        rows, width = held.shape[0] // 2, held.shape[1]
        held, sent = call(
            functools.partial(halve_kernel, bit),
            (spot, held, got),
            [shape_of(F32, rows, width)] * 2,
            scalars=1,
            after=after,
        )
        got = swap(sent, pairs_of)
        after = beside(held)
    rows = held.shape[0] // reach
    pieces = call(
        spread_kernel, (spot, held, got), [shape_of(F32, rows, width)] * reach, scalars=1, after=after
    )
    gots = [swap(pieces[d], along(d)) for d in range(1, reach)]
    after = beside(pieces[0])
    sums = call(gather_sum_kernel, (pieces[0], *gots), [shape_of(BF, rows, width)], after=after)[0]
    gots = [swap(sums, along(d)) for d in range(1, reach)]
    after = beside(sums)
    part = call(
        arrange_kernel, (spot, sums, *gots), [shape_of(BF, reach, rows, width)], scalars=1, after=after
    )[0]
    held = part.reshape(1, reach * rows, width)
    for bit, pairs_of in ((3, step_two), (2, step_one)):
        got = swap(held, pairs_of)
        after = beside(held)
        held = call(
            functools.partial(join_kernel, bit),
            (spot, held, got),
            [shape_of(BF, 2 * held.shape[0], *held.shape[1:])],
            scalars=1,
            after=after,
        )[0]
    return held, swap(held, across_core)


def ring(value, axis, step):
    count = lax.axis_size(axis)
    return lax.ppermute(value, axis, [(i, (i + step) % count) for i in range(count)])


def body(ahead, tokens, cotangent, w_qkv, w_proj, shifts, region_ids):
    levels, lat_rows, lon_cols, width = tokens.shape

    def by_column(grid_field):
        return grid_field.transpose(0, 2, 1, 3).reshape(levels, lon_cols * lat_rows, width)

    tokens, cotangent = by_column(tokens), by_column(cotangent)
    windows = lat_rows // WLAT
    my_lat, my_lon = lax.axis_index("lat"), lax.axis_index("lon")
    core, high, low = my_lat & 1, my_lat >> 1, my_lon & 1
    spot = jnp.stack(
        [
            my_lat * lat_rows,
            core,
            jnp.where(core == 1, low, high),
            jnp.where(core == 1, high, low),
            my_lon >> 1,
        ]
    ).astype(I32)
    out_step = -1 if ahead else 1
    pair = shape_of(BF, 2, COUNT, width)
    packed = shape_of(BF, 2, PACKED, width)

    def packs(chosen, sent, after):
        made = call(
            functools.partial(pack_kernel, ahead, windows, chosen, sent),
            (shifts, tokens, cotangent),
            [pair] * len(chosen) + [packed] * sent,
            scalars=1,
            after=after,
        )
        return made[: len(chosen)], made[len(chosen) :]

    def send_ahead(windows_sent, sends):
        for w, send in zip(windows_sent, sends):
            gots[w] = ring(send, "lon", out_step)

    gots, tiles = {}, {}
    (tiles[0], halo, last), sends = packs((0, windows, windows - 1), 1, ())
    send_ahead((0,), sends)
    below = ring(halo, "lat", -1)
    w_t = call(turn_kernel, (w_qkv,), [shape_of(BF, 3 * width, width)], after=(last,))[0]
    tiles[windows - 1], send = call(
        functools.partial(pack_last_kernel, ahead),
        (shifts, last, below),
        [pair, packed],
        scalars=1,
        after=(w_t,),
    )
    send_ahead((windows - 1,), (send,))
    middle = tuple(range(1, windows - 1))
    made, sends = packs(middle, len(middle), (send,))
    tiles.update(zip(middle, made))
    send_ahead(middle, sends)
    firsts, closed = {}, {}

    def window(w, after):
        firsts[w] = call(
            functools.partial(window_kernel, ahead, w),
            (shifts, region_ids, spot, tiles[w], gots[w], w_t, w_proj),
            [
                pair,
                shape_of(BF, COUNT, width),
                shape_of(BF, width, COUNT),
                shape_of(BF, 3 * width, COUNT),
            ],
            head_scratch(width),
            scalars=3,
            after=after,
        )
        return (firsts[w][1],)

    def close(w, after):
        tile, _, context, grads = firsts[w]
        out, send = call(
            functools.partial(close_kernel, ahead),
            (shifts, tile, context, grads, w_t, w_proj),
            [pair, packed],
            scalars=1,
            after=after,
        )
        closed[w] = out, ring(send, "lon", -out_step)
        return (send,)

    order = [0, windows - 1, *middle]
    after = (sends[0],)
    for n, w in enumerate(order):
        if n >= 2:
            after = (*after, closed[order[n - 2]][1])
        if n == windows - 2:
            after = (*after, gots[order[-1]])
        if n == windows - 1:
            final = call(
                functools.partial(last_back_kernel, ahead),
                (shifts, *closed[windows - 1]),
                [pair],
                scalars=1,
                after=after,
            )[0]
            above = ring(final, "lat", 1)
            after = (*after, final)
        after = window(w, after)
        if n < windows - 1:
            after = close(w, after)

    operands = [[firsts[w][n] for w in range(windows)] for n in (1, 0, 2, 3)]
    operands = [a for group in operands for a in group]

    def weights(kept, after):
        return call(
            functools.partial(weight_kernel, windows, kept),
            (spot, *operands),
            [shape_of(F32, width, 2 * width)],
            scalars=1,
            after=after,
        )[0]

    stage, results = [], []

    def beside(value):
        stage.append(value)
        if len(stage) == 1:
            return close(order[-1], (value,))
        if len(stage) == 4:
            return (closed[order[-1]][1],)
        if len(stage) == 5:
            results.extend(
                call(
                    functools.partial(finish_kernel, ahead, windows),
                    (
                        shifts, tokens, cotangent, above, final,
                        *[closed[w][0] for w in range(windows - 1)],
                        *[closed[w][1] for w in range(windows - 1)],
                    ),
                    [shape_of(BF, *tokens.shape)] * 2,
                    scalars=1,
                    after=(value,),
                )
            )
            return (results[0],)
        return ()

    summed = all_sum(weights, spot, beside, (*after, above, closed[order[-2]][1]))
    mixed, grad_tokens = (
        r.reshape(levels, lon_cols, lat_rows, width).transpose(0, 2, 1, 3) for r in results
    )
    total_tokens = levels * lat_rows * lax.axis_size("lat") * lon_cols * lax.axis_size("lon")
    gradients = call(
        functools.partial(gradient_kernel, 1.0 / math.sqrt(total_tokens)),
        (spot, *summed),
        [shape_of(F32, width, 3 * width), shape_of(F32, width, width)],
        scalars=1,
    )
    return (mixed, grad_tokens, *gradients)


def local(tokens, cotangent, w_qkv, w_proj, shifts, region_ids):
    return lax.cond(
        jnp.sum(shifts[:, 1]) <= ENTRIES,
        functools.partial(body, True),
        functools.partial(body, False),
        tokens, cotangent, w_qkv, w_proj, shifts, region_ids,
    )


def solution(mesh):
    return jax.shard_map(
        local,
        mesh=mesh,
        in_specs=(P(None, "lat", "lon", None), P(None, "lat", "lon", None), P(), P(), P(), P()),
        out_specs=(P(None, "lat", "lon", None), P(None, "lat", "lon", None), P(), P()),
        check_vma=False,
    )
```

```python
import functools
import math

import jax
import jax.numpy as jnp
from jax import lax
from jax.experimental import pallas as pl
from jax.experimental.pallas import tpu as pltpu
from jax.sharding import PartitionSpec as P

HEADS = 16
WLAT = 6
WLON = 12
LEV = 4
COUNT = LEV * WLAT * WLON
LANES = 384
MAIN = 256
REST = COUNT - MAIN
ENTRIES = LEV * WLON // 2
PACKED = ENTRIES * WLAT
NORM_EPS = 1e-05
BARRED = 2.0**100
BF = jnp.bfloat16
F32 = jnp.float32
I32 = jnp.int32

NN = (((1,), (0,)), ((), ()))
NT = (((1,), (1,)), ((), ()))
TN = (((0,), (0,)), ((), ()))
TT = (((0,), (1,)), ((), ()))

SMEM = pl.BlockSpec(memory_space=pltpu.SMEM)
VMEM = pl.BlockSpec(memory_space=pltpu.VMEM)
ANY = pl.BlockSpec(memory_space=pl.ANY)


def dot(a, b, dims):
    return lax.dot_general(a, b, dims, preferred_element_type=F32)


def split_bf16(value):
    high = value.astype(BF)
    low = (value - high.astype(F32)).astype(BF)
    return high, low


def call(kernel, ins, outs, scratch=(), scalars=0, after=()):

    def ordered(*refs):
        kernel(*refs[: len(ins)], *refs[len(ins) + len(after) :])

    return pl.pallas_call(
        ordered,
        in_specs=[SMEM] * scalars + [VMEM] * (len(ins) - scalars) + [ANY] * len(after),
        out_specs=[VMEM] * len(outs),
        out_shape=list(outs),
        scratch_shapes=list(scratch),
        compiler_params=pltpu.CompilerParams(vmem_limit_bytes=24 * 1024 * 1024),
        cost_estimate=pl.CostEstimate(
            flops=1_000_000, bytes_accessed=10_000, transcendentals=0
        ),
    )(*ins, *after)


def shape_of(dtype, *dims):
    return jax.ShapeDtypeStruct(dims, dtype)


def place(axis):
    dims = (COUNT, 1) if axis == 0 else (1, COUNT)
    token = lax.broadcasted_iota(I32, dims, axis)
    level = sum((token >= n * WLAT * WLON).astype(I32) for n in range(1, LEV))
    column, row = column_and_row(token - level * (WLAT * WLON))
    return level, row, column


def column_and_row(rest):
    column = sum((rest >= n * WLAT).astype(I32) for n in range(1, WLON))
    return column, rest - column * WLAT


def level_slots(windows, cut, axis):
    part = WLAT * WLON
    size = (windows + 1) * part
    dims = (size, 1) if axis == 0 else (1, size)
    token = lax.broadcasted_iota(I32, dims, axis)
    window = sum((token >= n * part).astype(I32) for n in range(1, windows + 1))
    column, row = column_and_row(token - window * part)
    at = window * WLAT + row + jnp.where(row < cut, WLAT, 0)
    slot = jnp.where(at < windows * WLAT, column * (windows * WLAT) + at, -1)
    first = window == windows
    return jnp.where(first, column * (windows * WLAT) + row, slot), first, row


def by_level(level, values):
    result = jnp.full(level.shape, values[0], I32)
    for n in range(1, LEV):
        result = jnp.where(level == n, values[n], result)
    return result


def from_next_row(shifts, axis):
    level, row, _ = place(axis)
    return row < by_level(level, [shifts[n, 0] for n in range(LEV)])


def from_other_side(shifts, ahead, axis):
    level, row, column = place(axis)
    cut = [shifts[n, 1] for n in range(LEV)]
    counts = cut if ahead else [WLON - c for c in cut]
    starts = [0] * LEV if ahead else cut
    offsets = [0]
    for n in range(LEV - 1):
        offsets.append(offsets[-1] + counts[n])
    at = by_level(level, cut)
    taken = (column < at) if ahead else (column >= at)
    entry = by_level(level, [o - s for o, s in zip(offsets, starts)]) + column
    return taken, jnp.where(taken, entry * WLAT + row, -1)


def pack_matrix(shifts, ahead):
    _, slot = from_other_side(shifts, ahead, 1)
    rows = lax.broadcasted_iota(I32, (PACKED, COUNT), 0)
    return (rows == slot).astype(F32).astype(BF)


def unpack_matrix(shifts, ahead):
    taken, slot = from_other_side(shifts, ahead, 0)
    columns = lax.broadcasted_iota(I32, (COUNT, PACKED), 1)
    return taken, (columns == slot).astype(F32).astype(BF)


def select_other(taken, spread, packed, own):
    return jnp.where(taken, dot(spread, packed, NN), own.astype(F32))


def pack_kernel(ahead, windows, chosen, sent, shifts, x_ref, cot_ref, *refs):
    part = WLAT * WLON
    grid = x_ref.shape[1]
    count = len(chosen)
    tile_refs, send_refs = refs[:count], refs[count:]
    chooser = pack_matrix(shifts, ahead)
    parts = [[[None] * LEV for _ in range(count)] for _ in range(2)]
    for level in range(LEV):
        slot, _, _ = level_slots(windows, shifts[level, 0], 0)
        slot = jnp.concatenate([slot[w * part : (w + 1) * part] for w in chosen], axis=0)
        cells = lax.broadcasted_iota(I32, (count * part, grid), 1)
        mover = (cells == slot).astype(F32).astype(BF)
        for field, ref in enumerate((x_ref, cot_ref)):
            moved = dot(mover, ref[level], NN)
            for w in range(count):
                parts[field][w][level] = moved[w * part : (w + 1) * part]
    for field in range(2):
        whole = [jnp.concatenate(p, axis=0).astype(BF) for p in parts[field]]
        for tile_ref, tile in zip(tile_refs, whole):
            tile_ref[field] = tile
        for send_ref, tile in zip(send_refs, whole):
            send_ref[field] = dot(chooser, tile, NN).astype(BF)


def pack_last_kernel(ahead, shifts, last_ref, halo_ref, *refs):
    count = len(refs) // 2 - 1
    others, (tile_ref, send_ref, *passed) = refs[:count], refs[count:]
    lower = from_next_row(shifts, 0)
    chooser = pack_matrix(shifts, ahead)
    for field in range(2):
        tile = jnp.where(lower, halo_ref[field].astype(F32), last_ref[field].astype(F32))
        tile_ref[field] = tile.astype(BF)
        send_ref[field] = dot(chooser, tile.astype(BF), NN).astype(BF)
    for ref, other in zip(passed, others):
        ref[...] = other[...]


def standardize(values_full):
    center = values_full - jnp.mean(values_full, axis=1, keepdims=True)
    variance = jnp.mean(center * center, axis=1, keepdims=True)
    inv_scale = lax.rsqrt(variance + NORM_EPS)
    return center * inv_scale, inv_scale


def bars(shifts, ids, first_row, grid_rows, bar_q, bar_k):
    level, row, _ = place(1)
    wrapped = jnp.where(row < by_level(level, [shifts[n, 0] for n in range(LEV)]), WLAT, 0)
    at = first_row + row + wrapped
    at = jnp.where(at >= grid_rows, at - grid_rows, at)
    top = sum((ids[n] == ids[0]).astype(I32) for n in range(WLAT - 1))
    bottom = sum((ids[grid_rows - 1 - n] == ids[grid_rows - 1]).astype(I32) for n in range(WLAT - 1))
    kind = jnp.where(at < top, 1, jnp.where(at >= grid_rows - bottom, 2, 0))
    features = lax.broadcasted_iota(I32, (32, COUNT), 0)
    same = (features == kind).astype(F32)
    bar_q[...] = jnp.zeros_like(bar_q)
    bar_q[:, :COUNT] = (same * -BARRED).astype(BF)
    bar_k[...] = jnp.zeros_like(bar_k)
    bar_k[:, :COUNT] = jnp.where(features < 3, 1.0 - same, 0.0).astype(BF)


def attend(size, bar_q, bar_k, q_s, k_s, v_s, g_s, q_rest, g_rest, buffers, ctx_ref, gp_ref):
    scale = 1.0 / math.sqrt(size)
    part = HEADS * size
    even, odd, both = buffers[:6], buffers[6:12], buffers[12:]

    def rows_of(h, count=1):
        return pl.ds(pl.multiple_of(h * size, size), count * size)

    def stacked(query, bar):
        high, low = split_bf16(query)
        return jnp.concatenate([high, low, high, bar], axis=0)

    def products(h, buffer):
        score_b, grad_b, key_b = buffer[0], buffer[1], buffer[5]
        rows = rows_of(h)
        high, low = split_bf16(k_s[rows])
        key_b[...] = jnp.concatenate([high, high, low, bar_k[...]], axis=0).T[:COUNT]
        score_b[...] = dot(key_b[...], stacked(q_s[rows, :MAIN], bar_q[:, :MAIN]), NN)
        grad_b[...] = dot(v_s[rows].T[:COUNT], g_s[rows, :MAIN], NN)

    def products_both(h):
        keys = jnp.concatenate([even[5][...], odd[5][...]], axis=1)
        bar = bar_q[:, MAIN:]
        rolled = pltpu.roll(bar.astype(F32), REST, 1).astype(BF)
        queries = [stacked(q_rest[rows_of(h)], bar), stacked(q_rest[rows_of(h + 1)], rolled)]
        both[0][...] = dot(keys, jnp.concatenate(queries, axis=0), NN)
        rows = rows_of(h, 2)
        both[1][...] = dot(v_s[rows].T[:COUNT], g_rest[rows], NN)

    def soften(buffer):
        score_b, grad_b, weight_b, high_b, low_b = buffer[:5]
        for start in range(0, score_b.shape[1], 128):
            lanes = slice(start, start + 128)
            scores = score_b[:, lanes]
            expo = jnp.exp2(scores - jnp.max(scores, axis=0, keepdims=True))
            weights = expo * (1.0 / jnp.sum(expo, axis=0, keepdims=True))
            weight_b[:, lanes] = weights.astype(BF)
            grad_w = grad_b[:, lanes]
            grad_sc = weights * (grad_w - jnp.sum(weights * grad_w, axis=0, keepdims=True))
            high_b[:, lanes], low_b[:, lanes] = split_bf16(grad_sc)

    def results(h, buffer, roll):
        rows = rows_of(h)
        value = v_s[rows][:, :COUNT]
        k_high, k_low = split_bf16(k_s[rows][:, :COUNT])
        k_pair = jnp.concatenate([k_high, k_low], axis=0)
        base = pl.multiple_of(h * size, size)
        gk = gv = 0.0
        pieces = (
            (buffer[2:5], q_s[rows, :MAIN], g_s[rows, :MAIN], 0, slice(0, MAIN)),
            (both[2:5], q_rest[rows], g_rest[rows], roll, slice(MAIN, COUNT)),
        )
        for (weight_b, high_b, low_b), query, grad_ctx, turn, lanes in pieces:
            rounded, high, low = weight_b[...], high_b[...], low_b[...]
            q_high, q_low = split_bf16(query)
            context = dot(value, rounded, NN)
            gq = dot(k_pair, high, NN)
            gq = (gq[:size] + gq[size:] + dot(k_high, low, NN)) * scale
            if turn:
                context, gq = (pltpu.roll(a, 128 - turn, 1) for a in (context, gq))
            width = lanes.stop - lanes.start
            ctx_ref[rows, lanes] = context[:, :width].astype(BF)
            gp_ref[pl.ds(base, size), lanes] = gq[:, :width].astype(BF)
            pair = dot(jnp.concatenate([q_high, q_low], axis=0), high, NT)
            gk = gk + pair[:size] + pair[size:] + dot(q_high, low, NT)
            gv = gv + dot(grad_ctx, rounded, NT)
        gp_ref[pl.ds(part + base, size)] = (gk * math.log(2.0)).astype(BF)
        gp_ref[pl.ds(2 * part + base, size)] = gv.astype(BF)

    products(0, even)
    products(1, odd)
    products_both(0)

    def pair(p, carry):
        h = 2 * p
        after = jnp.minimum(h + 2, HEADS - 2)
        soften(even)
        results(jnp.maximum(h - 1, 1), odd, REST)
        soften(odd)
        products(after, even)
        soften(both)
        products(after + 1, odd)
        results(h, even, 0)
        products_both(after)
        return carry

    lax.fori_loop(0, HEADS // 2, pair, 0)
    results(HEADS - 1, odd, REST)


def project(w_ref, wp_ref, norm_s, cot_s, q_s, k_s, v_s, g_s, q_rest, g_rest):
    norm = norm_s[...]
    width = norm.shape[1]
    factor = math.log2(math.e) / math.sqrt(width // HEADS)
    q_s[...] = dot(w_ref[:width], norm, NT) * factor
    k_s[...] = dot(w_ref[width : 2 * width], norm, NT)
    v_s[...] = dot(w_ref[2 * width :], norm, NT).astype(BF)
    g_s[...] = dot(wp_ref[...], cot_s[...], NT).astype(BF)
    odd = (lax.broadcasted_iota(I32, (width, 128), 0) // (width // HEADS)) % 2 == 1
    for source, rest in ((q_s, q_rest), (g_s, g_rest)):
        value = source[:, MAIN:].astype(F32)
        rest[...] = jnp.where(odd, pltpu.roll(value, REST, 1), value).astype(rest.dtype)


def head_scratch(width):
    return [
        pltpu.VMEM((LANES, width), BF),
        pltpu.VMEM((LANES, width), BF),
        pltpu.VMEM((32, LANES), BF),
        pltpu.VMEM((32, LANES), BF),
        pltpu.VMEM((width, LANES), F32),
        pltpu.VMEM((width, LANES), F32),
        pltpu.VMEM((width, LANES), BF),
        pltpu.VMEM((width, LANES), BF),
        pltpu.VMEM((width, 128), F32),
        pltpu.VMEM((width, 128), BF),
    ] + [
        pltpu.VMEM((COUNT, lanes), kind)
        for size in (MAIN, MAIN, 128)
        for kind, lanes in ((F32, size), (F32, size), (BF, size), (BF, size), (BF, size), (BF, 128))
    ]


def window_kernel(
    ahead, window, shifts, ids, spot, own_ref, got_ref, w_ref, wp_ref,
    tile_ref, norm_ref, ctx_ref, gp_ref,
    norm_s, cot_s, bar_q, bar_k, q_s, k_s, v_s, g_s, q_rest, g_rest, *buffers,
):
    width = own_ref.shape[-1]
    taken, spread = unpack_matrix(shifts, ahead)
    x = select_other(taken, spread, got_ref[0], own_ref[0])
    cot = select_other(taken, spread, got_ref[1], own_ref[1]).astype(BF)
    tile_ref[0] = x.astype(BF)
    tile_ref[1] = cot
    normed = standardize(x)[0].astype(BF)
    norm_ref[...] = normed
    norm_s[:COUNT] = normed
    norm_s[COUNT:] = jnp.zeros((LANES - COUNT, width), BF)
    cot_s[:COUNT] = cot
    cot_s[COUNT:] = jnp.zeros((LANES - COUNT, width), BF)
    bars(shifts, ids, spot[0] + window * WLAT, ids.shape[0], bar_q, bar_k)
    rests = q_rest, g_rest
    project(w_ref, wp_ref, norm_s, cot_s, q_s, k_s, v_s, g_s, *rests)
    attend(
        width // HEADS, bar_q, bar_k, q_s, k_s, v_s, g_s, *rests, buffers, ctx_ref, gp_ref
    )


def close_kernel(ahead, shifts, tile_ref, ctx_ref, gp_ref, w_ref, wp_ref, out_ref, send_ref):
    update = dot(ctx_ref[...], wp_ref[...], TN).astype(BF)
    grad_normed = dot(gp_ref[...], w_ref[...], TN)
    standard, inv_scale = standardize(tile_ref[0].astype(F32))
    grad = inv_scale * (
        grad_normed
        - jnp.mean(grad_normed, axis=1, keepdims=True)
        - standard * jnp.mean(grad_normed * standard, axis=1, keepdims=True)
    )
    grad = grad.astype(BF)
    chooser = pack_matrix(shifts, ahead)
    for field, value in enumerate((update, grad)):
        out_ref[field] = value
        send_ref[field] = dot(chooser, value, NN).astype(BF)


def weight_kernel(windows, kept, spot, *refs):
    norms, tiles, ctxs, gps = (refs[n * windows : (n + 1) * windows] for n in range(4))
    out_ref = refs[-1]
    part = ctxs[0].shape[0]

    def total(left, right):
        return functools.reduce(jnp.add, (dot(a, b, TT) for a, b in zip(left, right)))

    side = spot[1] if kept else 1 - spot[1]

    @pl.when(side == 0)
    def _():
        out_ref[...] = total([n[...] for n in norms], [g[: 2 * part] for g in gps])

    @pl.when(side == 1)
    def _():
        out_ref[:, :part] = total([n[...] for n in norms], [g[2 * part :] for g in gps])
        out_ref[:, part:] = total([t[1] for t in tiles], [c[...] for c in ctxs])


def halve_kernel(bit, spot, mine_ref, got_ref, keep_ref, send_ref):
    rows = keep_ref.shape[0]
    for side, ref in ((spot[bit], keep_ref), (1 - spot[bit], send_ref)):
        at = pl.ds(pl.multiple_of(side * rows, rows), rows)
        ref[...] = mine_ref[at] + got_ref[at]


def spread_kernel(spot, mine_ref, got_ref, last_ref, *out_refs):
    *out_refs, passed_ref = out_refs
    passed_ref[...] = last_ref[...]
    rows = out_refs[0].shape[0]
    for d, ref in enumerate(out_refs):
        at = pl.ds(pl.multiple_of((spot[4] ^ d) * rows, rows), rows)
        ref[...] = mine_ref[at] + got_ref[at]


def gather_sum_kernel(*refs):
    refs[-1][...] = functools.reduce(jnp.add, (r[...] for r in refs[:-1])).astype(BF)


def arrange_kernel(spot, *refs):
    for d, ref in enumerate(refs[:-1]):
        refs[-1][spot[4] ^ d] = ref[...]


def join_kernel(bit, spot, mine_ref, got_ref, out_ref):
    count = mine_ref.shape[0]
    for side, ref in ((spot[bit], mine_ref), (1 - spot[bit], got_ref)):
        for n in range(count):
            out_ref[side * count + n] = ref[n]


def gradient_kernel(factor, spot, mine_ref, got_ref, qkv_ref, proj_ref):
    width = proj_ref.shape[0]
    count, rows = mine_ref.shape[:2]

    def write(pair_ref, rest_ref):
        for n in range(count):
            here = slice(n * rows, (n + 1) * rows)
            rest = rest_ref[n].astype(F32) * factor
            qkv_ref[here, : 2 * width] = pair_ref[n].astype(F32) * factor
            qkv_ref[here, 2 * width :] = rest[:, :width]
            proj_ref[:, here] = rest[:, width:].T

    first = spot[1] == 0

    @pl.when(first)
    def _():
        write(mine_ref, got_ref)

    @pl.when(jnp.logical_not(first))
    def _():
        write(got_ref, mine_ref)


def turn_kernel(w_ref, out_ref):
    out_ref[...] = w_ref[...].T


def last_back_kernel(ahead, shifts, own_ref, got_ref, out_ref):
    taken, spread = unpack_matrix(shifts, ahead)
    for field in range(2):
        out_ref[field] = select_other(taken, spread, got_ref[field], own_ref[field]).astype(BF)


def finish_kernel(ahead, windows, shifts, x_ref, cot_ref, above_ref, final_ref, *refs):
    owns, gots = refs[: windows - 1], refs[windows - 1 : 2 * windows - 2]
    outs = refs[2 * windows - 2 :]
    part = WLAT * WLON
    grid = x_ref.shape[1]
    taken, spread = unpack_matrix(shifts, ahead)
    movers = []
    for level in range(LEV):
        cut = shifts[level, 0]
        slot, first, row = level_slots(windows, cut, 1)
        slot = jnp.where(jnp.logical_and(first, row >= cut), -1, slot)
        cells = lax.broadcasted_iota(I32, (grid, (windows + 1) * part), 0)
        movers.append((cells == slot).astype(F32).astype(BF))
    for field, ref in enumerate((x_ref, cot_ref)):
        tiles = [
            select_other(taken, spread, gots[w][field], owns[w][field]) for w in range(windows - 1)
        ]
        tiles += [final_ref[field].astype(F32), above_ref[field].astype(F32)]
        for level in range(LEV):
            here = slice(level * part, (level + 1) * part)
            source = jnp.concatenate([t[here] for t in tiles], axis=0).astype(BF)
            value = ref[level].astype(F32) + dot(movers[level], source, NN)
            outs[field][level] = value.astype(BF)


def route(pairs_of, lat, lon):
    return [
        (a * lon + o, pairs_of(a, o)[0] * lon + pairs_of(a, o)[1])
        for a in range(lat)
        for o in range(lon)
    ]


def across_core(a, o):
    return a ^ 1, o


def step_one(a, o):
    return (a, o ^ 1) if a % 2 else (a ^ 2, o)


def step_two(a, o):
    return (a ^ 2, o) if a % 2 else (a, o ^ 1)


def all_sum(weights, spot, beside, earlier, held_back):
    lat, lon = lax.axis_size("lat"), lax.axis_size("lon")
    reach = lon // 2

    def swap(value, pairs_of):
        return lax.ppermute(value, ("lat", "lon"), route(pairs_of, lat, lon))

    def along(d):
        return lambda a, o: (a, o ^ (2 * d))

    sent = weights(False, earlier)
    got = swap(sent, across_core)
    held = weights(True, (sent,))
    after = beside(held)
    for bit, pairs_of in ((2, step_one), (3, step_two)):
        rows, width = held.shape[0] // 2, held.shape[1]
        held, sent = call(
            functools.partial(halve_kernel, bit),
            (spot, held, got),
            [shape_of(F32, rows, width)] * 2,
            scalars=1,
            after=after,
        )
        got = swap(sent, pairs_of)
        after = beside(held)
    rows = held.shape[0] // reach
    *pieces, passed = call(
        spread_kernel,
        (spot, held, got, held_back[0]),
        [shape_of(F32, rows, width)] * reach + [shape_of(BF, *held_back[0].shape)],
        scalars=1,
        after=after,
    )
    held_back.append(passed)
    gots = [swap(pieces[d], along(d)) for d in range(1, reach)]
    after = beside(pieces[0])
    sums = call(gather_sum_kernel, (pieces[0], *gots), [shape_of(BF, rows, width)], after=after)[0]
    gots = [swap(sums, along(d)) for d in range(1, reach)]
    after = beside(sums)
    part = call(
        arrange_kernel, (spot, sums, *gots), [shape_of(BF, reach, rows, width)], scalars=1, after=after
    )[0]
    held = part.reshape(1, reach * rows, width)
    for bit, pairs_of in ((3, step_two), (2, step_one)):
        got = swap(held, pairs_of)
        after = beside(held)
        held = call(
            functools.partial(join_kernel, bit),
            (spot, held, got),
            [shape_of(BF, 2 * held.shape[0], *held.shape[1:])],
            scalars=1,
            after=after,
        )[0]
    return held, swap(held, across_core)


def ring(value, axis, step):
    count = lax.axis_size(axis)
    return lax.ppermute(value, axis, [(i, (i + step) % count) for i in range(count)])


def body(ahead, tokens, cotangent, w_qkv, w_proj, shifts, region_ids):
    levels, lat_rows, lon_cols, width = tokens.shape

    def by_column(grid_field):
        return grid_field.transpose(0, 2, 1, 3).reshape(levels, lon_cols * lat_rows, width)

    tokens, cotangent = by_column(tokens), by_column(cotangent)
    windows = lat_rows // WLAT
    my_lat, my_lon = lax.axis_index("lat"), lax.axis_index("lon")
    core, high, low = my_lat & 1, my_lat >> 1, my_lon & 1
    spot = jnp.stack(
        [
            my_lat * lat_rows,
            core,
            jnp.where(core == 1, low, high),
            jnp.where(core == 1, high, low),
            my_lon >> 1,
        ]
    ).astype(I32)
    out_step = -1 if ahead else 1
    pair = shape_of(BF, 2, COUNT, width)
    packed = shape_of(BF, 2, PACKED, width)

    def packs(chosen, sent, after):
        made = call(
            functools.partial(pack_kernel, ahead, windows, chosen, sent),
            (shifts, tokens, cotangent),
            [pair] * len(chosen) + [packed] * sent,
            scalars=1,
            after=after,
        )
        return made[: len(chosen)], made[len(chosen) :]

    def send_ahead(windows_sent, sends):
        for w, send in zip(windows_sent, sends):
            gots[w] = ring(send, "lon", out_step)

    gots, tiles = {}, {}
    (tiles[0], halo), sends = packs((0, windows), 1, ())
    send_ahead((0,), sends)
    below = ring(halo, "lat", -1)
    w_t = call(turn_kernel, (w_qkv,), [shape_of(BF, 3 * width, width)], after=(halo,))[0]
    middle = tuple(range(1, windows - 1))
    made, sends = packs((*middle, windows - 1), len(middle), (w_t,))
    *made, last = made
    tiles.update(zip(middle, made))
    tiles[windows - 1], *sends = call(
        functools.partial(pack_last_kernel, ahead),
        (shifts, last, below, *sends),
        [pair, packed] + [packed] * len(middle),
        scalars=1,
    )
    send_ahead((windows - 1, *middle), sends)
    firsts, closed, held_back = {}, {}, []

    def window(w, after):
        firsts[w] = call(
            functools.partial(window_kernel, ahead, w),
            (shifts, region_ids, spot, tiles[w], gots[w], w_t, w_proj),
            [
                pair,
                shape_of(BF, COUNT, width),
                shape_of(BF, width, COUNT),
                shape_of(BF, 3 * width, COUNT),
            ],
            head_scratch(width),
            scalars=3,
            after=after,
        )
        return (firsts[w][1],)

    def close(w, after):
        tile, _, context, grads = firsts[w]
        out, send = call(
            functools.partial(close_kernel, ahead),
            (shifts, tile, context, grads, w_t, w_proj),
            [pair, packed],
            scalars=1,
            after=after,
        )
        if w == order[-1]:
            closed[w] = out, None
            held_back.append(send)
        else:
            closed[w] = out, ring(send, "lon", -out_step)
        return (send,)

    order = [0, windows - 1, *middle]
    after = (sends[0],)
    for n, w in enumerate(order):
        if n >= 2:
            after = (*after, closed[order[n - 2]][1])
        if n == windows - 2:
            after = (*after, gots[order[-1]])
        if n == windows - 1:
            final = call(
                functools.partial(last_back_kernel, ahead),
                (shifts, *closed[windows - 1]),
                [pair],
                scalars=1,
                after=after,
            )[0]
            above = ring(final, "lat", 1)
            after = (*after, final)
        after = window(w, after)
        if n < windows - 1:
            after = close(w, after)

    operands = [[firsts[w][n] for w in range(windows)] for n in (1, 0, 2, 3)]
    operands = [a for group in operands for a in group]

    def weights(kept, after):
        return call(
            functools.partial(weight_kernel, windows, kept),
            (spot, *operands),
            [shape_of(F32, width, 2 * width)],
            scalars=1,
            after=after,
        )[0]

    stage, results = [], []

    def beside(value):
        stage.append(value)
        if len(stage) == 1:
            return close(order[-1], (value,))
        if len(stage) == 4:
            closed[order[-1]] = closed[order[-1]][0], ring(held_back[1], "lon", -out_step)
        if len(stage) == 5:
            return (closed[order[-1]][1],)
        if len(stage) == 7:
            results.extend(
                call(
                    functools.partial(finish_kernel, ahead, windows),
                    (
                        shifts, tokens, cotangent, above, final,
                        *[closed[w][0] for w in range(windows - 1)],
                        *[closed[w][1] for w in range(windows - 1)],
                    ),
                    [shape_of(BF, *tokens.shape)] * 2,
                    scalars=1,
                    after=(value,),
                )
            )
            return (results[0],)
        return ()

    summed = all_sum(weights, spot, beside, (*after, above, closed[order[-2]][1]), held_back)
    mixed, grad_tokens = (
        r.reshape(levels, lon_cols, lat_rows, width).transpose(0, 2, 1, 3) for r in results
    )
    total_tokens = levels * lat_rows * lax.axis_size("lat") * lon_cols * lax.axis_size("lon")
    gradients = call(
        functools.partial(gradient_kernel, 1.0 / math.sqrt(total_tokens)),
        (spot, *summed),
        [shape_of(F32, width, 3 * width), shape_of(F32, width, width)],
        scalars=1,
    )
    return (mixed, grad_tokens, *gradients)


def local(tokens, cotangent, w_qkv, w_proj, shifts, region_ids):
    return lax.cond(
        jnp.sum(shifts[:, 1]) <= ENTRIES,
        functools.partial(body, True),
        functools.partial(body, False),
        tokens, cotangent, w_qkv, w_proj, shifts, region_ids,
    )


def solution(mesh):
    return jax.shard_map(
        local,
        mesh=mesh,
        in_specs=(P(None, "lat", "lon", None), P(None, "lat", "lon", None), P(), P(), P(), P()),
        out_specs=(P(None, "lat", "lon", None), P(None, "lat", "lon", None), P(), P()),
        check_vma=False,
    )
```

```python
import functools
import math

import jax
import jax.numpy as jnp
from jax import lax
from jax.experimental import pallas as pl
from jax.experimental.pallas import tpu as pltpu
from jax.sharding import PartitionSpec as P

HEADS = 16
WLAT = 6
WLON = 12
LEV = 4
COUNT = LEV * WLAT * WLON
LANES = 384
MAIN = 256
REST = COUNT - MAIN
ENTRIES = LEV * WLON // 2
PACKED = ENTRIES * WLAT
NORM_EPS = 1e-05
BARRED = 2.0**100
BF = jnp.bfloat16
F32 = jnp.float32
I32 = jnp.int32

NN = (((1,), (0,)), ((), ()))
NT = (((1,), (1,)), ((), ()))
TN = (((0,), (0,)), ((), ()))
TT = (((0,), (1,)), ((), ()))

SMEM = pl.BlockSpec(memory_space=pltpu.SMEM)
VMEM = pl.BlockSpec(memory_space=pltpu.VMEM)
ANY = pl.BlockSpec(memory_space=pl.ANY)


def dot(a, b, dims):
    return lax.dot_general(a, b, dims, preferred_element_type=F32)


def split_bf16(value):
    high = value.astype(BF)
    low = (value - high.astype(F32)).astype(BF)
    return high, low


def call(kernel, ins, outs, scratch=(), scalars=0, after=()):

    def ordered(*refs):
        kernel(*refs[: len(ins)], *refs[len(ins) + len(after) :])

    return pl.pallas_call(
        ordered,
        in_specs=[SMEM] * scalars + [VMEM] * (len(ins) - scalars) + [ANY] * len(after),
        out_specs=[VMEM] * len(outs),
        out_shape=list(outs),
        scratch_shapes=list(scratch),
        compiler_params=pltpu.CompilerParams(vmem_limit_bytes=24 * 1024 * 1024),
        cost_estimate=pl.CostEstimate(
            flops=1_000_000, bytes_accessed=10_000, transcendentals=0
        ),
    )(*ins, *after)


def shape_of(dtype, *dims):
    return jax.ShapeDtypeStruct(dims, dtype)


def place(axis):
    dims = (COUNT, 1) if axis == 0 else (1, COUNT)
    token = lax.broadcasted_iota(I32, dims, axis)
    level = sum((token >= n * WLAT * WLON).astype(I32) for n in range(1, LEV))
    column, row = column_and_row(token - level * (WLAT * WLON))
    return level, row, column


def column_and_row(rest):
    column = sum((rest >= n * WLAT).astype(I32) for n in range(1, WLON))
    return column, rest - column * WLAT


def level_slots(windows, cut, axis):
    part = WLAT * WLON
    size = (windows + 1) * part
    dims = (size, 1) if axis == 0 else (1, size)
    token = lax.broadcasted_iota(I32, dims, axis)
    window = sum((token >= n * part).astype(I32) for n in range(1, windows + 1))
    column, row = column_and_row(token - window * part)
    at = window * WLAT + row + jnp.where(row < cut, WLAT, 0)
    slot = jnp.where(at < windows * WLAT, column * (windows * WLAT) + at, -1)
    first = window == windows
    return jnp.where(first, column * (windows * WLAT) + row, slot), first, row


def by_level(level, values):
    result = jnp.full(level.shape, values[0], I32)
    for n in range(1, LEV):
        result = jnp.where(level == n, values[n], result)
    return result


def from_next_row(shifts, axis):
    level, row, _ = place(axis)
    return row < by_level(level, [shifts[n, 0] for n in range(LEV)])


def from_other_side(shifts, ahead, axis):
    level, row, column = place(axis)
    cut = [shifts[n, 1] for n in range(LEV)]
    counts = cut if ahead else [WLON - c for c in cut]
    starts = [0] * LEV if ahead else cut
    offsets = [0]
    for n in range(LEV - 1):
        offsets.append(offsets[-1] + counts[n])
    at = by_level(level, cut)
    taken = (column < at) if ahead else (column >= at)
    entry = by_level(level, [o - s for o, s in zip(offsets, starts)]) + column
    return taken, jnp.where(taken, entry * WLAT + row, -1)


def pack_matrix(shifts, ahead):
    _, slot = from_other_side(shifts, ahead, 1)
    rows = lax.broadcasted_iota(I32, (PACKED, COUNT), 0)
    return (rows == slot).astype(F32).astype(BF)


def unpack_matrix(shifts, ahead):
    taken, slot = from_other_side(shifts, ahead, 0)
    columns = lax.broadcasted_iota(I32, (COUNT, PACKED), 1)
    return taken, (columns == slot).astype(F32).astype(BF)


def select_other(taken, spread, packed, own):
    return jnp.where(taken, dot(spread, packed, NN), own.astype(F32))


def pack_kernel(ahead, windows, chosen, sent, shifts, x_ref, cot_ref, *refs):
    part = WLAT * WLON
    grid = x_ref.shape[1]
    count = len(chosen)
    tile_refs, send_refs = refs[:count], refs[count:]
    chooser = pack_matrix(shifts, ahead)
    parts = [[[None] * LEV for _ in range(count)] for _ in range(2)]
    for level in range(LEV):
        slot, _, _ = level_slots(windows, shifts[level, 0], 0)
        slot = jnp.concatenate([slot[w * part : (w + 1) * part] for w in chosen], axis=0)
        cells = lax.broadcasted_iota(I32, (count * part, grid), 1)
        mover = (cells == slot).astype(F32).astype(BF)
        for field, ref in enumerate((x_ref, cot_ref)):
            moved = dot(mover, ref[level], NN)
            for w in range(count):
                parts[field][w][level] = moved[w * part : (w + 1) * part]
    for field in range(2):
        whole = [jnp.concatenate(p, axis=0).astype(BF) for p in parts[field]]
        for tile_ref, tile in zip(tile_refs, whole):
            tile_ref[field] = tile
        for send_ref, tile in zip(send_refs, whole):
            send_ref[field] = dot(chooser, tile, NN).astype(BF)


def pack_last_kernel(ahead, shifts, last_ref, halo_ref, *refs):
    count = len(refs) // 2 - 1
    others, (tile_ref, send_ref, *passed) = refs[:count], refs[count:]
    lower = from_next_row(shifts, 0)
    chooser = pack_matrix(shifts, ahead)
    for field in range(2):
        tile = jnp.where(lower, halo_ref[field].astype(F32), last_ref[field].astype(F32))
        tile_ref[field] = tile.astype(BF)
        send_ref[field] = dot(chooser, tile.astype(BF), NN).astype(BF)
    for ref, other in zip(passed, others):
        ref[...] = other[...]


def standardize(values_full):
    center = values_full - jnp.mean(values_full, axis=1, keepdims=True)
    variance = jnp.mean(center * center, axis=1, keepdims=True)
    inv_scale = lax.rsqrt(variance + NORM_EPS)
    return center * inv_scale, inv_scale


def bars(shifts, ids, first_row, grid_rows, bar_q, bar_k):
    level, row, _ = place(1)
    wrapped = jnp.where(row < by_level(level, [shifts[n, 0] for n in range(LEV)]), WLAT, 0)
    at = first_row + row + wrapped
    at = jnp.where(at >= grid_rows, at - grid_rows, at)
    top = sum((ids[n] == ids[0]).astype(I32) for n in range(WLAT - 1))
    bottom = sum((ids[grid_rows - 1 - n] == ids[grid_rows - 1]).astype(I32) for n in range(WLAT - 1))
    kind = jnp.where(at < top, 1, jnp.where(at >= grid_rows - bottom, 2, 0))
    features = lax.broadcasted_iota(I32, (32, COUNT), 0)
    same = (features == kind).astype(F32)
    bar_q[...] = jnp.zeros_like(bar_q)
    bar_q[:, :COUNT] = (same * -BARRED).astype(BF)
    bar_k[...] = jnp.zeros_like(bar_k)
    bar_k[:, :COUNT] = jnp.where(features < 3, 1.0 - same, 0.0).astype(BF)


def attend(size, bar_q, bar_k, q_s, k_s, v_s, g_s, q_rest, g_rest, buffers, ctx_ref, gp_ref):
    scale = 1.0 / math.sqrt(size)
    part = HEADS * size
    even, odd, both = buffers[:6], buffers[6:12], buffers[12:]

    def rows_of(h, count=1):
        return pl.ds(pl.multiple_of(h * size, size), count * size)

    def stacked(query, bar):
        high, low = split_bf16(query)
        return jnp.concatenate([high, low, high, bar], axis=0)

    def products(h, buffer):
        score_b, grad_b, key_b = buffer[0], buffer[1], buffer[5]
        rows = rows_of(h)
        high, low = split_bf16(k_s[rows])
        key_b[...] = jnp.concatenate([high, high, low, bar_k[...]], axis=0).T[:COUNT]
        score_b[...] = dot(key_b[...], stacked(q_s[rows, :MAIN], bar_q[:, :MAIN]), NN)
        grad_b[...] = dot(v_s[rows].T[:COUNT], g_s[rows, :MAIN], NN)

    def products_both(h):
        keys = jnp.concatenate([even[5][...], odd[5][...]], axis=1)
        bar = bar_q[:, MAIN:]
        rolled = pltpu.roll(bar.astype(F32), REST, 1).astype(BF)
        queries = [stacked(q_rest[rows_of(h)], bar), stacked(q_rest[rows_of(h + 1)], rolled)]
        both[0][...] = dot(keys, jnp.concatenate(queries, axis=0), NN)
        rows = rows_of(h, 2)
        both[1][...] = dot(v_s[rows].T[:COUNT], g_rest[rows], NN)

    def soften(buffer):
        score_b, grad_b, weight_b, high_b, low_b = buffer[:5]
        for start in range(0, score_b.shape[1], 128):
            lanes = slice(start, start + 128)
            scores = score_b[:, lanes]
            expo = jnp.exp2(scores - jnp.max(scores, axis=0, keepdims=True))
            weights = expo * (1.0 / jnp.sum(expo, axis=0, keepdims=True))
            weight_b[:, lanes] = weights.astype(BF)
            grad_w = grad_b[:, lanes]
            grad_sc = weights * (grad_w - jnp.sum(weights * grad_w, axis=0, keepdims=True))
            high_b[:, lanes], low_b[:, lanes] = split_bf16(grad_sc)

    def results(h, buffer, roll):
        rows = rows_of(h)
        value = v_s[rows][:, :COUNT]
        k_high, k_low = split_bf16(k_s[rows][:, :COUNT])
        k_pair = jnp.concatenate([k_high, k_low], axis=0)
        base = pl.multiple_of(h * size, size)
        gk = gv = 0.0
        pieces = (
            (buffer[2:5], q_s[rows, :MAIN], g_s[rows, :MAIN], 0, slice(0, MAIN)),
            (both[2:5], q_rest[rows], g_rest[rows], roll, slice(MAIN, COUNT)),
        )
        for (weight_b, high_b, low_b), query, grad_ctx, turn, lanes in pieces:
            rounded, high, low = weight_b[...], high_b[...], low_b[...]
            q_high, q_low = split_bf16(query)
            context = dot(value, rounded, NN)
            gq = dot(k_pair, high, NN)
            gq = (gq[:size] + gq[size:] + dot(k_high, low, NN)) * scale
            if turn:
                context, gq = (pltpu.roll(a, 128 - turn, 1) for a in (context, gq))
            width = lanes.stop - lanes.start
            ctx_ref[rows, lanes] = context[:, :width].astype(BF)
            gp_ref[pl.ds(base, size), lanes] = gq[:, :width].astype(BF)
            pair = dot(jnp.concatenate([q_high, q_low], axis=0), high, NT)
            gk = gk + pair[:size] + pair[size:] + dot(q_high, low, NT)
            gv = gv + dot(grad_ctx, rounded, NT)
        gp_ref[pl.ds(part + base, size)] = (gk * math.log(2.0)).astype(BF)
        gp_ref[pl.ds(2 * part + base, size)] = gv.astype(BF)

    products(0, even)
    products(1, odd)
    products_both(0)

    def pair(p, carry):
        h = 2 * p
        after = jnp.minimum(h + 2, HEADS - 2)
        soften(even)
        results(jnp.maximum(h - 1, 1), odd, REST)
        soften(odd)
        products(after, even)
        soften(both)
        products(after + 1, odd)
        results(h, even, 0)
        products_both(after)
        return carry

    lax.fori_loop(0, HEADS // 2, pair, 0)
    results(HEADS - 1, odd, REST)


def project(w_ref, wp_ref, norm_s, cot_s, q_s, k_s, v_s, g_s, q_rest, g_rest):
    norm = norm_s[...]
    width = norm.shape[1]
    factor = math.log2(math.e) / math.sqrt(width // HEADS)
    q_s[...] = dot(w_ref[:width], norm, NT) * factor
    k_s[...] = dot(w_ref[width : 2 * width], norm, NT)
    v_s[...] = dot(w_ref[2 * width :], norm, NT).astype(BF)
    g_s[...] = dot(wp_ref[...], cot_s[...], NT).astype(BF)
    odd = (lax.broadcasted_iota(I32, (width, 128), 0) // (width // HEADS)) % 2 == 1
    for source, rest in ((q_s, q_rest), (g_s, g_rest)):
        value = source[:, MAIN:].astype(F32)
        rest[...] = jnp.where(odd, pltpu.roll(value, REST, 1), value).astype(rest.dtype)


def head_scratch(width):
    return [
        pltpu.VMEM((LANES, width), BF),
        pltpu.VMEM((LANES, width), BF),
        pltpu.VMEM((32, LANES), BF),
        pltpu.VMEM((32, LANES), BF),
        pltpu.VMEM((width, LANES), F32),
        pltpu.VMEM((width, LANES), F32),
        pltpu.VMEM((width, LANES), BF),
        pltpu.VMEM((width, LANES), BF),
        pltpu.VMEM((width, 128), F32),
        pltpu.VMEM((width, 128), BF),
    ] + [
        pltpu.VMEM((COUNT, lanes), kind)
        for size in (MAIN, MAIN, 128)
        for kind, lanes in ((F32, size), (F32, size), (BF, size), (BF, size), (BF, size), (BF, 128))
    ]


def window_kernel(
    ahead, window, shifts, ids, spot, own_ref, got_ref, w_ref, wp_ref,
    tile_ref, norm_ref, ctx_ref, gp_ref,
    norm_s, cot_s, bar_q, bar_k, q_s, k_s, v_s, g_s, q_rest, g_rest, *buffers,
):
    width = own_ref.shape[-1]
    taken, spread = unpack_matrix(shifts, ahead)
    x = select_other(taken, spread, got_ref[0], own_ref[0])
    cot = select_other(taken, spread, got_ref[1], own_ref[1]).astype(BF)
    tile_ref[0] = x.astype(BF)
    tile_ref[1] = cot
    normed = standardize(x)[0].astype(BF)
    norm_ref[...] = normed
    norm_s[:COUNT] = normed
    norm_s[COUNT:] = jnp.zeros((LANES - COUNT, width), BF)
    cot_s[:COUNT] = cot
    cot_s[COUNT:] = jnp.zeros((LANES - COUNT, width), BF)
    bars(shifts, ids, spot[0] + window * WLAT, ids.shape[0], bar_q, bar_k)
    rests = q_rest, g_rest
    project(w_ref, wp_ref, norm_s, cot_s, q_s, k_s, v_s, g_s, *rests)
    attend(
        width // HEADS, bar_q, bar_k, q_s, k_s, v_s, g_s, *rests, buffers, ctx_ref, gp_ref
    )


def close_kernel(ahead, shifts, tile_ref, ctx_ref, gp_ref, w_ref, wp_ref, out_ref, send_ref):
    update = dot(ctx_ref[...], wp_ref[...], TN).astype(BF)
    grad_normed = dot(gp_ref[...], w_ref[...], TN)
    standard, inv_scale = standardize(tile_ref[0].astype(F32))
    grad = inv_scale * (
        grad_normed
        - jnp.mean(grad_normed, axis=1, keepdims=True)
        - standard * jnp.mean(grad_normed * standard, axis=1, keepdims=True)
    )
    grad = grad.astype(BF)
    chooser = pack_matrix(shifts, ahead)
    for field, value in enumerate((update, grad)):
        out_ref[field] = value
        send_ref[field] = dot(chooser, value, NN).astype(BF)


def weight_kernel(windows, chunk, kept, spot, *refs):
    norms, tiles, ctxs, gps = (refs[n * windows : (n + 1) * windows] for n in range(4))
    out_ref = refs[-1]
    width = norms[0].shape[-1]

    def of_columns(start):
        rows = slice(start * width, (start + 1) * width)
        terms = [dot(n[...], g[rows], TT) for n, g in zip(norms, gps)]
        out_ref[...] = functools.reduce(jnp.add, terms)

    side = spot[1] if kept else 1 - spot[1]

    @pl.when(side == 0)
    def _():
        of_columns(chunk)

    @pl.when(side == 1)
    def _():
        if chunk == 0:
            of_columns(2)
        else:
            terms = [dot(t[1], c[...], TT) for t, c in zip(tiles, ctxs)]
            out_ref[...] = functools.reduce(jnp.add, terms)


def halve_kernel(bit, spot, mine_ref, got_ref, keep_ref, send_ref):
    rows = keep_ref.shape[0]
    for side, ref in ((spot[bit], keep_ref), (1 - spot[bit], send_ref)):
        at = pl.ds(pl.multiple_of(side * rows, rows), rows)
        ref[...] = mine_ref[at] + got_ref[at]


def spread_kernel(spot, mine_ref, got_ref, *out_refs):
    rows = out_refs[0].shape[0]
    for d, ref in enumerate(out_refs):
        at = pl.ds(pl.multiple_of((spot[4] ^ d) * rows, rows), rows)
        ref[...] = mine_ref[at] + got_ref[at]


def gather_sum_kernel(*refs):
    refs[-1][...] = functools.reduce(jnp.add, (r[...] for r in refs[:-1])).astype(BF)


def arrange_kernel(spot, *refs):
    for d, ref in enumerate(refs[:-1]):
        refs[-1][spot[4] ^ d] = ref[...]


def join_kernel(bit, spot, mine_ref, got_ref, out_ref):
    count = mine_ref.shape[0]
    for side, ref in ((spot[bit], mine_ref), (1 - spot[bit], got_ref)):
        for n in range(count):
            out_ref[side * count + n] = ref[n]


def gradient_kernel(factor, spot, mine_a, got_a, mine_b, got_b, qkv_ref, proj_ref):
    width = proj_ref.shape[0]
    count, rows = mine_a.shape[:2]

    def write(query_ref, key_ref, value_ref, proj_part):
        for n in range(count):
            here = slice(n * rows, (n + 1) * rows)
            for at, ref in enumerate((query_ref, key_ref, value_ref)):
                qkv_ref[here, at * width : (at + 1) * width] = ref[n].astype(F32) * factor
            proj_ref[:, here] = (proj_part[n].astype(F32) * factor).T

    first = spot[1] == 0

    @pl.when(first)
    def _():
        write(mine_a, mine_b, got_a, got_b)

    @pl.when(jnp.logical_not(first))
    def _():
        write(got_a, got_b, mine_a, mine_b)


def turn_kernel(w_ref, out_ref):
    out_ref[...] = w_ref[...].T


def last_back_kernel(ahead, shifts, own_ref, got_ref, out_ref):
    taken, spread = unpack_matrix(shifts, ahead)
    for field in range(2):
        out_ref[field] = select_other(taken, spread, got_ref[field], own_ref[field]).astype(BF)


def finish_kernel(ahead, windows, shifts, x_ref, cot_ref, above_ref, final_ref, *refs):
    owns, gots = refs[: windows - 1], refs[windows - 1 : 2 * windows - 2]
    outs = refs[2 * windows - 2 :]
    part = WLAT * WLON
    grid = x_ref.shape[1]
    taken, spread = unpack_matrix(shifts, ahead)
    movers = []
    for level in range(LEV):
        cut = shifts[level, 0]
        slot, first, row = level_slots(windows, cut, 1)
        slot = jnp.where(jnp.logical_and(first, row >= cut), -1, slot)
        cells = lax.broadcasted_iota(I32, (grid, (windows + 1) * part), 0)
        movers.append((cells == slot).astype(F32).astype(BF))
    for field, ref in enumerate((x_ref, cot_ref)):
        tiles = [
            select_other(taken, spread, gots[w][field], owns[w][field]) for w in range(windows - 1)
        ]
        tiles += [final_ref[field].astype(F32), above_ref[field].astype(F32)]
        for level in range(LEV):
            here = slice(level * part, (level + 1) * part)
            source = jnp.concatenate([t[here] for t in tiles], axis=0).astype(BF)
            value = ref[level].astype(F32) + dot(movers[level], source, NN)
            outs[field][level] = value.astype(BF)


def route(pairs_of, lat, lon):
    return [
        (a * lon + o, pairs_of(a, o)[0] * lon + pairs_of(a, o)[1])
        for a in range(lat)
        for o in range(lon)
    ]


def across_core(a, o):
    return a ^ 1, o


def step_one(a, o):
    return (a, o ^ 1) if a % 2 else (a ^ 2, o)


def step_two(a, o):
    return (a ^ 2, o) if a % 2 else (a, o ^ 1)


def sum_chain(weights, spot, after):
    lat, lon = lax.axis_size("lat"), lax.axis_size("lon")
    reach = lon // 2

    def swap(value, pairs_of):
        return lax.ppermute(value, ("lat", "lon"), route(pairs_of, lat, lon))

    def along(d):
        return lambda a, o: (a, o ^ (2 * d))

    sent = weights(False, after)
    got = swap(sent, across_core)
    held = weights(True, (sent,))
    after = yield held
    for bit, pairs_of in ((2, step_one), (3, step_two)):
        rows, width = held.shape[0] // 2, held.shape[1]
        held, sent = call(
            functools.partial(halve_kernel, bit),
            (spot, held, got),
            [shape_of(F32, rows, width)] * 2,
            scalars=1,
            after=after,
        )
        got = swap(sent, pairs_of)
        after = yield held
    rows = held.shape[0] // reach
    pieces = call(
        spread_kernel, (spot, held, got), [shape_of(F32, rows, width)] * reach, scalars=1, after=after
    )
    gots = [swap(pieces[d], along(d)) for d in range(1, reach)]
    after = yield pieces[0]
    sums = call(gather_sum_kernel, (pieces[0], *gots), [shape_of(BF, rows, width)], after=after)[0]
    gots = [swap(sums, along(d)) for d in range(1, reach)]
    after = yield sums
    part = call(
        arrange_kernel, (spot, sums, *gots), [shape_of(BF, reach, rows, width)], scalars=1, after=after
    )[0]
    held = part.reshape(1, reach * rows, width)
    for bit, pairs_of in ((3, step_two), (2, step_one)):
        got = swap(held, pairs_of)
        after = yield held
        held = call(
            functools.partial(join_kernel, bit),
            (spot, held, got),
            [shape_of(BF, 2 * held.shape[0], *held.shape[1:])],
            scalars=1,
            after=after,
        )[0]
    return held, swap(held, across_core)


def ring(value, axis, step):
    count = lax.axis_size(axis)
    return lax.ppermute(value, axis, [(i, (i + step) % count) for i in range(count)])


def body(ahead, tokens, cotangent, w_qkv, w_proj, shifts, region_ids):
    levels, lat_rows, lon_cols, width = tokens.shape

    def by_column(grid_field):
        return grid_field.transpose(0, 2, 1, 3).reshape(levels, lon_cols * lat_rows, width)

    tokens, cotangent = by_column(tokens), by_column(cotangent)
    windows = lat_rows // WLAT
    my_lat, my_lon = lax.axis_index("lat"), lax.axis_index("lon")
    core, high, low = my_lat & 1, my_lat >> 1, my_lon & 1
    spot = jnp.stack(
        [
            my_lat * lat_rows,
            core,
            jnp.where(core == 1, low, high),
            jnp.where(core == 1, high, low),
            my_lon >> 1,
        ]
    ).astype(I32)
    out_step = -1 if ahead else 1
    pair = shape_of(BF, 2, COUNT, width)
    packed = shape_of(BF, 2, PACKED, width)

    def packs(chosen, sent, after):
        made = call(
            functools.partial(pack_kernel, ahead, windows, chosen, sent),
            (shifts, tokens, cotangent),
            [pair] * len(chosen) + [packed] * sent,
            scalars=1,
            after=after,
        )
        return made[: len(chosen)], made[len(chosen) :]

    def send_ahead(windows_sent, sends):
        for w, send in zip(windows_sent, sends):
            gots[w] = ring(send, "lon", out_step)

    gots, tiles = {}, {}
    (tiles[0], halo), sends = packs((0, windows), 1, ())
    send_ahead((0,), sends)
    below = ring(halo, "lat", -1)
    w_t = call(turn_kernel, (w_qkv,), [shape_of(BF, 3 * width, width)], after=(halo,))[0]
    middle = tuple(range(1, windows - 1))
    made, sends = packs((*middle, windows - 1), len(middle), (w_t,))
    *made, last = made
    tiles.update(zip(middle, made))
    tiles[windows - 1], *sends = call(
        functools.partial(pack_last_kernel, ahead),
        (shifts, last, below, *sends),
        [pair, packed] + [packed] * len(middle),
        scalars=1,
    )
    send_ahead((windows - 1, *middle), sends)
    firsts, closed = {}, {}

    def window(w, after):
        firsts[w] = call(
            functools.partial(window_kernel, ahead, w),
            (shifts, region_ids, spot, tiles[w], gots[w], w_t, w_proj),
            [
                pair,
                shape_of(BF, COUNT, width),
                shape_of(BF, width, COUNT),
                shape_of(BF, 3 * width, COUNT),
            ],
            head_scratch(width),
            scalars=3,
            after=after,
        )
        return (firsts[w][1],)

    def close(w, after):
        tile, _, context, grads = firsts[w]
        out, send = call(
            functools.partial(close_kernel, ahead),
            (shifts, tile, context, grads, w_t, w_proj),
            [pair, packed],
            scalars=1,
            after=after,
        )
        closed[w] = out, ring(send, "lon", -out_step)
        return (send,)

    order = [0, windows - 1, *middle]
    after = (sends[0],)
    for n, w in enumerate(order):
        if n >= 2:
            after = (*after, closed[order[n - 2]][1])
        if n == windows - 2:
            after = (*after, gots[order[-1]])
        if n == windows - 1:
            final = call(
                functools.partial(last_back_kernel, ahead),
                (shifts, *closed[windows - 1]),
                [pair],
                scalars=1,
                after=after,
            )[0]
            above = ring(final, "lat", 1)
            after = (*after, final)
        after = close(w, window(w, after))

    operands = [[firsts[w][n] for w in range(windows)] for n in (1, 0, 2, 3)]
    operands = [a for group in operands for a in group]

    def weights(chunk, kept, after):
        return call(
            functools.partial(weight_kernel, windows, chunk, kept),
            (spot, *operands),
            [shape_of(F32, width, width)],
            scalars=1,
            after=after,
        )[0]

    def finish(after):
        return call(
            functools.partial(finish_kernel, ahead, windows),
            (
                shifts, tokens, cotangent, above, final,
                *[closed[w][0] for w in range(windows - 1)],
                *[closed[w][1] for w in range(windows - 1)],
            ),
            [shape_of(BF, *tokens.shape)] * 2,
            scalars=1,
            after=after,
        )

    summed, results = [None, None], None
    chains = [None, None]
    chains[0] = sum_chain(
        functools.partial(weights, 0), spot, (*after, above, closed[order[-2]][1])
    )
    token = next(chains[0])
    token = chains[0].send((token,))
    chains[1] = sum_chain(functools.partial(weights, 1), spot, (token,))
    token = next(chains[1])
    turn, step = 0, 0
    while None in summed:
        extra = ()
        if step == 1:
            extra = (closed[order[-1]][1],)
        if step == 6:
            results = finish((token,))
            extra = (results[0],)
        try:
            token = chains[turn].send((token, *extra))
        except StopIteration as stop:
            summed[turn] = stop.value
            token = stop.value[0]
        turn = 1 - turn if summed[1 - turn] is None else turn
        step += 1
    mixed, grad_tokens = (
        r.reshape(levels, lon_cols, lat_rows, width).transpose(0, 2, 1, 3) for r in results
    )
    total_tokens = levels * lat_rows * lax.axis_size("lat") * lon_cols * lax.axis_size("lon")
    gradients = call(
        functools.partial(gradient_kernel, 1.0 / math.sqrt(total_tokens)),
        (spot, *summed[0], *summed[1]),
        [shape_of(F32, width, 3 * width), shape_of(F32, width, width)],
        scalars=1,
    )
    return (mixed, grad_tokens, *gradients)


def local(tokens, cotangent, w_qkv, w_proj, shifts, region_ids):
    return lax.cond(
        jnp.sum(shifts[:, 1]) <= ENTRIES,
        functools.partial(body, True),
        functools.partial(body, False),
        tokens, cotangent, w_qkv, w_proj, shifts, region_ids,
    )


def solution(mesh):
    return jax.shard_map(
        local,
        mesh=mesh,
        in_specs=(P(None, "lat", "lon", None), P(None, "lat", "lon", None), P(), P(), P(), P()),
        out_specs=(P(None, "lat", "lon", None), P(None, "lat", "lon", None), P(), P()),
        check_vma=False,
    )
```

```python
import functools
import math

import jax
import jax.numpy as jnp
from jax import lax
from jax.experimental import pallas as pl
from jax.experimental.pallas import tpu as pltpu
from jax.sharding import PartitionSpec as P

HEADS = 16
WLAT = 6
WLON = 12
LEV = 4
COUNT = LEV * WLAT * WLON
LANES = 384
MAIN = 256
REST = COUNT - MAIN
ENTRIES = LEV * WLON // 2
PACKED = ENTRIES * WLAT
NORM_EPS = 1e-05
BARRED = 2.0**100
BF = jnp.bfloat16
F32 = jnp.float32
I32 = jnp.int32

NN = (((1,), (0,)), ((), ()))
NT = (((1,), (1,)), ((), ()))
TN = (((0,), (0,)), ((), ()))
TT = (((0,), (1,)), ((), ()))

SMEM = pl.BlockSpec(memory_space=pltpu.SMEM)
VMEM = pl.BlockSpec(memory_space=pltpu.VMEM)
ANY = pl.BlockSpec(memory_space=pl.ANY)


def dot(a, b, dims):
    return lax.dot_general(a, b, dims, preferred_element_type=F32)


def split_bf16(value):
    high = value.astype(BF)
    low = (value - high.astype(F32)).astype(BF)
    return high, low


def call(kernel, ins, outs, scratch=(), scalars=0, after=()):

    def ordered(*refs):
        kernel(*refs[: len(ins)], *refs[len(ins) + len(after) :])

    return pl.pallas_call(
        ordered,
        in_specs=[SMEM] * scalars + [VMEM] * (len(ins) - scalars) + [ANY] * len(after),
        out_specs=[VMEM] * len(outs),
        out_shape=list(outs),
        scratch_shapes=list(scratch),
        compiler_params=pltpu.CompilerParams(vmem_limit_bytes=24 * 1024 * 1024),
        cost_estimate=pl.CostEstimate(
            flops=1_000_000, bytes_accessed=10_000, transcendentals=0
        ),
    )(*ins, *after)


def shape_of(dtype, *dims):
    return jax.ShapeDtypeStruct(dims, dtype)


def place(axis):
    dims = (COUNT, 1) if axis == 0 else (1, COUNT)
    token = lax.broadcasted_iota(I32, dims, axis)
    level = sum((token >= n * WLAT * WLON).astype(I32) for n in range(1, LEV))
    column, row = column_and_row(token - level * (WLAT * WLON))
    return level, row, column


def column_and_row(rest):
    column = sum((rest >= n * WLAT).astype(I32) for n in range(1, WLON))
    return column, rest - column * WLAT


def level_slots(windows, cut, axis):
    part = WLAT * WLON
    size = (windows + 1) * part
    dims = (size, 1) if axis == 0 else (1, size)
    token = lax.broadcasted_iota(I32, dims, axis)
    window = sum((token >= n * part).astype(I32) for n in range(1, windows + 1))
    column, row = column_and_row(token - window * part)
    at = window * WLAT + row + jnp.where(row < cut, WLAT, 0)
    slot = jnp.where(at < windows * WLAT, column * (windows * WLAT) + at, -1)
    first = window == windows
    return jnp.where(first, column * (windows * WLAT) + row, slot), first, row


def by_level(level, values):
    result = jnp.full(level.shape, values[0], I32)
    for n in range(1, LEV):
        result = jnp.where(level == n, values[n], result)
    return result


def from_next_row(shifts, axis):
    level, row, _ = place(axis)
    return row < by_level(level, [shifts[n, 0] for n in range(LEV)])


def from_other_side(shifts, ahead, axis):
    level, row, column = place(axis)
    cut = [shifts[n, 1] for n in range(LEV)]
    counts = cut if ahead else [WLON - c for c in cut]
    starts = [0] * LEV if ahead else cut
    offsets = [0]
    for n in range(LEV - 1):
        offsets.append(offsets[-1] + counts[n])
    at = by_level(level, cut)
    taken = (column < at) if ahead else (column >= at)
    entry = by_level(level, [o - s for o, s in zip(offsets, starts)]) + column
    return taken, jnp.where(taken, entry * WLAT + row, -1)


def pack_matrix(shifts, ahead):
    _, slot = from_other_side(shifts, ahead, 1)
    rows = lax.broadcasted_iota(I32, (PACKED, COUNT), 0)
    return (rows == slot).astype(F32).astype(BF)


def unpack_matrix(shifts, ahead):
    taken, slot = from_other_side(shifts, ahead, 0)
    columns = lax.broadcasted_iota(I32, (COUNT, PACKED), 1)
    return taken, (columns == slot).astype(F32).astype(BF)


def select_other(taken, spread, packed, own):
    return jnp.where(taken, dot(spread, packed, NN), own.astype(F32))


def pack_kernel(ahead, windows, chosen, sent, shifts, x_ref, cot_ref, *refs):
    part = WLAT * WLON
    grid = x_ref.shape[1]
    count = len(chosen)
    tile_refs, send_refs = refs[:count], refs[count:]
    chooser = pack_matrix(shifts, ahead)
    parts = [[[None] * LEV for _ in range(count)] for _ in range(2)]
    for level in range(LEV):
        slot, _, _ = level_slots(windows, shifts[level, 0], 0)
        slot = jnp.concatenate([slot[w * part : (w + 1) * part] for w in chosen], axis=0)
        cells = lax.broadcasted_iota(I32, (count * part, grid), 1)
        mover = (cells == slot).astype(F32).astype(BF)
        for field, ref in enumerate((x_ref, cot_ref)):
            moved = dot(mover, ref[level], NN)
            for w in range(count):
                parts[field][w][level] = moved[w * part : (w + 1) * part]
    for field in range(2):
        whole = [jnp.concatenate(p, axis=0).astype(BF) for p in parts[field]]
        for tile_ref, tile in zip(tile_refs, whole):
            tile_ref[field] = tile
        for send_ref, tile in zip(send_refs, whole):
            send_ref[field] = dot(chooser, tile, NN).astype(BF)


def pack_last_kernel(ahead, shifts, last_ref, halo_ref, *refs):
    count = len(refs) // 2 - 1
    others, (tile_ref, send_ref, *passed) = refs[:count], refs[count:]
    lower = from_next_row(shifts, 0)
    chooser = pack_matrix(shifts, ahead)
    for field in range(2):
        tile = jnp.where(lower, halo_ref[field].astype(F32), last_ref[field].astype(F32))
        tile_ref[field] = tile.astype(BF)
        send_ref[field] = dot(chooser, tile.astype(BF), NN).astype(BF)
    for ref, other in zip(passed, others):
        ref[...] = other[...]


def standardize(values_full):
    center = values_full - jnp.mean(values_full, axis=1, keepdims=True)
    variance = jnp.mean(center * center, axis=1, keepdims=True)
    inv_scale = lax.rsqrt(variance + NORM_EPS)
    return center * inv_scale, inv_scale


def bars(shifts, ids, first_row, grid_rows, bar_q, bar_k):
    level, row, _ = place(1)
    wrapped = jnp.where(row < by_level(level, [shifts[n, 0] for n in range(LEV)]), WLAT, 0)
    at = first_row + row + wrapped
    at = jnp.where(at >= grid_rows, at - grid_rows, at)
    top = sum((ids[n] == ids[0]).astype(I32) for n in range(WLAT - 1))
    bottom = sum((ids[grid_rows - 1 - n] == ids[grid_rows - 1]).astype(I32) for n in range(WLAT - 1))
    kind = jnp.where(at < top, 1, jnp.where(at >= grid_rows - bottom, 2, 0))
    features = lax.broadcasted_iota(I32, (32, COUNT), 0)
    same = (features == kind).astype(F32)
    bar_q[...] = jnp.zeros_like(bar_q)
    bar_q[:, :COUNT] = (same * -BARRED).astype(BF)
    bar_k[...] = jnp.zeros_like(bar_k)
    bar_k[:, :COUNT] = jnp.where(features < 3, 1.0 - same, 0.0).astype(BF)


def attend(size, bar_q, bar_k, q_s, k_s, v_s, g_s, q_rest, g_rest, buffers, ctx_ref, gp_ref):
    scale = 1.0 / math.sqrt(size)
    part = HEADS * size
    even, odd, both = buffers[:6], buffers[6:12], buffers[12:]

    def rows_of(h, count=1):
        return pl.ds(pl.multiple_of(h * size, size), count * size)

    def stacked(query, bar):
        high, low = split_bf16(query)
        return jnp.concatenate([high, low, high, bar], axis=0)

    def products(h, buffer):
        score_b, grad_b, key_b = buffer[0], buffer[1], buffer[5]
        rows = rows_of(h)
        high, low = split_bf16(k_s[rows])
        key_b[...] = jnp.concatenate([high, high, low, bar_k[...]], axis=0).T[:COUNT]
        score_b[...] = dot(key_b[...], stacked(q_s[rows, :MAIN], bar_q[:, :MAIN]), NN)
        grad_b[...] = dot(v_s[rows].T[:COUNT], g_s[rows, :MAIN], NN)

    def products_both(h):
        keys = jnp.concatenate([even[5][...], odd[5][...]], axis=1)
        bar = bar_q[:, MAIN:]
        rolled = pltpu.roll(bar.astype(F32), REST, 1).astype(BF)
        queries = [stacked(q_rest[rows_of(h)], bar), stacked(q_rest[rows_of(h + 1)], rolled)]
        both[0][...] = dot(keys, jnp.concatenate(queries, axis=0), NN)
        rows = rows_of(h, 2)
        both[1][...] = dot(v_s[rows].T[:COUNT], g_rest[rows], NN)

    def soften(buffer):
        score_b, grad_b, weight_b, high_b, low_b = buffer[:5]
        for start in range(0, score_b.shape[1], 128):
            lanes = slice(start, start + 128)
            scores = score_b[:, lanes]
            expo = jnp.exp2(scores - jnp.max(scores, axis=0, keepdims=True))
            weights = expo * (1.0 / jnp.sum(expo, axis=0, keepdims=True))
            weight_b[:, lanes] = weights.astype(BF)
            grad_w = grad_b[:, lanes]
            grad_sc = weights * (grad_w - jnp.sum(weights * grad_w, axis=0, keepdims=True))
            high_b[:, lanes], low_b[:, lanes] = split_bf16(grad_sc)

    def results(h, buffer, roll):
        rows = rows_of(h)
        value = v_s[rows][:, :COUNT]
        k_high, k_low = split_bf16(k_s[rows][:, :COUNT])
        k_pair = jnp.concatenate([k_high, k_low], axis=0)
        base = pl.multiple_of(h * size, size)
        gk = gv = 0.0
        pieces = (
            (buffer[2:5], q_s[rows, :MAIN], g_s[rows, :MAIN], 0, slice(0, MAIN)),
            (both[2:5], q_rest[rows], g_rest[rows], roll, slice(MAIN, COUNT)),
        )
        for (weight_b, high_b, low_b), query, grad_ctx, turn, lanes in pieces:
            rounded, high, low = weight_b[...], high_b[...], low_b[...]
            q_high, q_low = split_bf16(query)
            context = dot(value, rounded, NN)
            gq = dot(k_pair, high, NN)
            gq = (gq[:size] + gq[size:] + dot(k_high, low, NN)) * scale
            if turn:
                context, gq = (pltpu.roll(a, 128 - turn, 1) for a in (context, gq))
            width = lanes.stop - lanes.start
            ctx_ref[rows, lanes] = context[:, :width].astype(BF)
            gp_ref[pl.ds(base, size), lanes] = gq[:, :width].astype(BF)
            pair = dot(jnp.concatenate([q_high, q_low], axis=0), high, NT)
            gk = gk + pair[:size] + pair[size:] + dot(q_high, low, NT)
            gv = gv + dot(grad_ctx, rounded, NT)
        gp_ref[pl.ds(part + base, size)] = (gk * math.log(2.0)).astype(BF)
        gp_ref[pl.ds(2 * part + base, size)] = gv.astype(BF)

    products(0, even)
    products(1, odd)
    products_both(0)

    def pair(p, carry):
        h = 2 * p
        after = jnp.minimum(h + 2, HEADS - 2)
        soften(even)
        results(jnp.maximum(h - 1, 1), odd, REST)
        soften(odd)
        products(after, even)
        soften(both)
        products(after + 1, odd)
        results(h, even, 0)
        products_both(after)
        return carry

    lax.fori_loop(0, HEADS // 2, pair, 0)
    results(HEADS - 1, odd, REST)


def project(w_ref, wp_ref, norm_s, cot_s, q_s, k_s, v_s, g_s, q_rest, g_rest):
    norm = norm_s[...]
    width = norm.shape[1]
    factor = math.log2(math.e) / math.sqrt(width // HEADS)
    q_s[...] = dot(w_ref[:width], norm, NT) * factor
    k_s[...] = dot(w_ref[width : 2 * width], norm, NT)
    v_s[...] = dot(w_ref[2 * width :], norm, NT).astype(BF)
    g_s[...] = dot(wp_ref[...], cot_s[...], NT).astype(BF)
    odd = (lax.broadcasted_iota(I32, (width, 128), 0) // (width // HEADS)) % 2 == 1
    for source, rest in ((q_s, q_rest), (g_s, g_rest)):
        value = source[:, MAIN:].astype(F32)
        rest[...] = jnp.where(odd, pltpu.roll(value, REST, 1), value).astype(rest.dtype)


def head_scratch(width):
    return [
        pltpu.VMEM((LANES, width), BF),
        pltpu.VMEM((LANES, width), BF),
        pltpu.VMEM((32, LANES), BF),
        pltpu.VMEM((32, LANES), BF),
        pltpu.VMEM((width, LANES), F32),
        pltpu.VMEM((width, LANES), F32),
        pltpu.VMEM((width, LANES), BF),
        pltpu.VMEM((width, LANES), BF),
        pltpu.VMEM((width, 128), F32),
        pltpu.VMEM((width, 128), BF),
    ] + [
        pltpu.VMEM((COUNT, lanes), kind)
        for size in (MAIN, MAIN, 128)
        for kind, lanes in ((F32, size), (F32, size), (BF, size), (BF, size), (BF, size), (BF, 128))
    ]


def window_kernel(
    ahead, window, shifts, ids, spot, own_ref, got_ref, w_ref, wp_ref,
    tile_ref, norm_ref, ctx_ref, gp_ref,
    norm_s, cot_s, bar_q, bar_k, q_s, k_s, v_s, g_s, q_rest, g_rest, *buffers,
):
    width = own_ref.shape[-1]
    taken, spread = unpack_matrix(shifts, ahead)
    x = select_other(taken, spread, got_ref[0], own_ref[0])
    cot = select_other(taken, spread, got_ref[1], own_ref[1]).astype(BF)
    tile_ref[0] = x.astype(BF)
    tile_ref[1] = cot
    normed = standardize(x)[0].astype(BF)
    norm_ref[...] = normed
    norm_s[:COUNT] = normed
    norm_s[COUNT:] = jnp.zeros((LANES - COUNT, width), BF)
    cot_s[:COUNT] = cot
    cot_s[COUNT:] = jnp.zeros((LANES - COUNT, width), BF)
    bars(shifts, ids, spot[0] + window * WLAT, ids.shape[0], bar_q, bar_k)
    rests = q_rest, g_rest
    project(w_ref, wp_ref, norm_s, cot_s, q_s, k_s, v_s, g_s, *rests)
    attend(
        width // HEADS, bar_q, bar_k, q_s, k_s, v_s, g_s, *rests, buffers, ctx_ref, gp_ref
    )


def close_kernel(ahead, shifts, tile_ref, ctx_ref, gp_ref, w_ref, wp_ref, out_ref, send_ref):
    update = dot(ctx_ref[...], wp_ref[...], TN).astype(BF)
    grad_normed = dot(gp_ref[...], w_ref[...], TN)
    standard, inv_scale = standardize(tile_ref[0].astype(F32))
    grad = inv_scale * (
        grad_normed
        - jnp.mean(grad_normed, axis=1, keepdims=True)
        - standard * jnp.mean(grad_normed * standard, axis=1, keepdims=True)
    )
    grad = grad.astype(BF)
    chooser = pack_matrix(shifts, ahead)
    for field, value in enumerate((update, grad)):
        out_ref[field] = value
        send_ref[field] = dot(chooser, value, NN).astype(BF)


def weight_kernel(windows, kept, spot, *refs):
    norms, tiles, ctxs, gps = (refs[n * windows : (n + 1) * windows] for n in range(4))
    out_ref = refs[-1]
    part = ctxs[0].shape[0]

    def total(left, right, dims=TT):
        return functools.reduce(jnp.add, (dot(a, b, dims) for a, b in zip(left, right)))

    side = spot[1] if kept else 1 - spot[1]

    @pl.when(side == 0)
    def _():
        out_ref[...] = total([n[...] for n in norms], [g[: 2 * part] for g in gps])

    @pl.when(side == 1)
    def _():
        out_ref[:, :part] = total([n[...] for n in norms], [g[2 * part :] for g in gps])
        out_ref[:, part:] = total([c[...] for c in ctxs], [t[1] for t in tiles], NN)


def halve_kernel(bit, spot, mine_ref, got_ref, keep_ref, send_ref):
    rows = keep_ref.shape[0]
    for side, ref in ((spot[bit], keep_ref), (1 - spot[bit], send_ref)):
        at = pl.ds(pl.multiple_of(side * rows, rows), rows)
        ref[...] = mine_ref[at] + got_ref[at]


def spread_kernel(spot, mine_ref, got_ref, *out_refs):
    rows = out_refs[0].shape[0]
    for d, ref in enumerate(out_refs):
        at = pl.ds(pl.multiple_of((spot[4] ^ d) * rows, rows), rows)
        ref[...] = mine_ref[at] + got_ref[at]


def gather_sum_kernel(*refs):
    refs[-1][...] = functools.reduce(jnp.add, (r[...] for r in refs[:-1])).astype(BF)


def arrange_kernel(spot, *refs):
    for d, ref in enumerate(refs[:-1]):
        refs[-1][spot[4] ^ d] = ref[...]


def join_kernel(bit, spot, mine_ref, got_ref, out_ref):
    count = mine_ref.shape[0]
    for side, ref in ((spot[bit], mine_ref), (1 - spot[bit], got_ref)):
        for n in range(count):
            out_ref[side * count + n] = ref[n]


def gradient_kernel(factor, spot, mine_ref, got_ref, qkv_ref, proj_ref):
    width = proj_ref.shape[1]

    def write(pair_ref, rest_ref):
        rest = rest_ref[...].astype(F32) * factor
        qkv_ref[:, : 2 * width] = pair_ref[...].astype(F32) * factor
        qkv_ref[:, 2 * width :] = rest[:, :width]
        proj_ref[...] = rest[:, width:]

    first = spot[1] == 0

    @pl.when(first)
    def _():
        write(mine_ref, got_ref)

    @pl.when(jnp.logical_not(first))
    def _():
        write(got_ref, mine_ref)


def write_gradients(factor, spot, mine, got):
    count, rows, columns = mine.shape
    width = columns // 2
    piece = pl.BlockSpec((None, rows, columns), lambda n: (n, 0, 0))
    return pl.pallas_call(
        functools.partial(gradient_kernel, factor),
        grid=(count,),
        in_specs=[SMEM, piece, piece],
        out_specs=[
            pl.BlockSpec((rows, 3 * width), lambda n: (n, 0)),
            pl.BlockSpec((rows, width), lambda n: (n, 0)),
        ],
        out_shape=[
            shape_of(F32, count * rows, 3 * width),
            shape_of(F32, count * rows, width),
        ],
        compiler_params=pltpu.CompilerParams(vmem_limit_bytes=24 * 1024 * 1024),
    )(spot, mine, got)


def turn_kernel(w_ref, out_ref):
    out_ref[...] = w_ref[...].T


def last_back_kernel(ahead, shifts, own_ref, got_ref, out_ref):
    taken, spread = unpack_matrix(shifts, ahead)
    for field in range(2):
        out_ref[field] = select_other(taken, spread, got_ref[field], own_ref[field]).astype(BF)


def finish_kernel(ahead, windows, shifts, x_ref, cot_ref, above_ref, final_ref, *refs):
    owns, gots = refs[: windows - 1], refs[windows - 1 : 2 * windows - 2]
    outs = refs[2 * windows - 2 :]
    part = WLAT * WLON
    grid = x_ref.shape[1]
    taken, spread = unpack_matrix(shifts, ahead)
    movers = []
    for level in range(LEV):
        cut = shifts[level, 0]
        slot, first, row = level_slots(windows, cut, 1)
        slot = jnp.where(jnp.logical_and(first, row >= cut), -1, slot)
        cells = lax.broadcasted_iota(I32, (grid, (windows + 1) * part), 0)
        movers.append((cells == slot).astype(F32).astype(BF))
    for field, ref in enumerate((x_ref, cot_ref)):
        tiles = [
            select_other(taken, spread, gots[w][field], owns[w][field]) for w in range(windows - 1)
        ]
        tiles += [final_ref[field].astype(F32), above_ref[field].astype(F32)]
        for level in range(LEV):
            here = slice(level * part, (level + 1) * part)
            source = jnp.concatenate([t[here] for t in tiles], axis=0).astype(BF)
            value = ref[level].astype(F32) + dot(movers[level], source, NN)
            outs[field][level] = value.astype(BF)


def route(pairs_of, lat, lon):
    return [
        (a * lon + o, pairs_of(a, o)[0] * lon + pairs_of(a, o)[1])
        for a in range(lat)
        for o in range(lon)
    ]


def across_core(a, o):
    return a ^ 1, o


def step_one(a, o):
    return (a, o ^ 1) if a % 2 else (a ^ 2, o)


def step_two(a, o):
    return (a ^ 2, o) if a % 2 else (a, o ^ 1)


def all_sum(weights, spot, beside, earlier):
    lat, lon = lax.axis_size("lat"), lax.axis_size("lon")
    reach = lon // 2

    def swap(value, pairs_of):
        return lax.ppermute(value, ("lat", "lon"), route(pairs_of, lat, lon))

    def along(d):
        return lambda a, o: (a, o ^ (2 * d))

    sent = weights(False, earlier)
    got = swap(sent, across_core)
    held = weights(True, (sent,))
    after = beside(held)
    for bit, pairs_of in ((2, step_one), (3, step_two)):
        rows, width = held.shape[0] // 2, held.shape[1]
        held, sent = call(
            functools.partial(halve_kernel, bit),
            (spot, held, got),
            [shape_of(F32, rows, width)] * 2,
            scalars=1,
            after=after,
        )
        got = swap(sent, pairs_of)
        after = beside(held)
    rows = held.shape[0] // reach
    pieces = call(
        spread_kernel, (spot, held, got), [shape_of(F32, rows, width)] * reach, scalars=1, after=after
    )
    gots = [swap(pieces[d], along(d)) for d in range(1, reach)]
    after = beside(pieces[0])
    sums = call(gather_sum_kernel, (pieces[0], *gots), [shape_of(BF, rows, width)], after=after)[0]
    gots = [swap(sums, along(d)) for d in range(1, reach)]
    after = beside(sums)
    part = call(
        arrange_kernel, (spot, sums, *gots), [shape_of(BF, reach, rows, width)], scalars=1, after=after
    )[0]
    held = part.reshape(1, reach * rows, width)
    for bit, pairs_of in ((3, step_two), (2, step_one)):
        got = swap(held, pairs_of)
        after = beside(held)
        held = call(
            functools.partial(join_kernel, bit),
            (spot, held, got),
            [shape_of(BF, 2 * held.shape[0], *held.shape[1:])],
            scalars=1,
            after=after,
        )[0]
    return held, swap(held, across_core)


def ring(value, axis, step):
    count = lax.axis_size(axis)
    return lax.ppermute(value, axis, [(i, (i + step) % count) for i in range(count)])


def body(ahead, tokens, cotangent, w_qkv, w_proj, shifts, region_ids):
    levels, lat_rows, lon_cols, width = tokens.shape

    def by_column(grid_field):
        return grid_field.transpose(0, 2, 1, 3).reshape(levels, lon_cols * lat_rows, width)

    tokens, cotangent = by_column(tokens), by_column(cotangent)
    windows = lat_rows // WLAT
    my_lat, my_lon = lax.axis_index("lat"), lax.axis_index("lon")
    core, high, low = my_lat & 1, my_lat >> 1, my_lon & 1
    spot = jnp.stack(
        [
            my_lat * lat_rows,
            core,
            jnp.where(core == 1, low, high),
            jnp.where(core == 1, high, low),
            my_lon >> 1,
        ]
    ).astype(I32)
    out_step = -1 if ahead else 1
    pair = shape_of(BF, 2, COUNT, width)
    packed = shape_of(BF, 2, PACKED, width)

    def packs(chosen, sent, after):
        made = call(
            functools.partial(pack_kernel, ahead, windows, chosen, sent),
            (shifts, tokens, cotangent),
            [pair] * len(chosen) + [packed] * sent,
            scalars=1,
            after=after,
        )
        return made[: len(chosen)], made[len(chosen) :]

    def send_ahead(windows_sent, sends):
        for w, send in zip(windows_sent, sends):
            gots[w] = ring(send, "lon", out_step)

    gots, tiles = {}, {}
    (tiles[0], halo), sends = packs((0, windows), 1, ())
    send_ahead((0,), sends)
    below = ring(halo, "lat", -1)
    w_t = call(turn_kernel, (w_qkv,), [shape_of(BF, 3 * width, width)], after=(halo,))[0]
    middle = tuple(range(1, windows - 1))
    made, sends = packs((*middle, windows - 1), len(middle), (w_t,))
    *made, last = made
    tiles.update(zip(middle, made))
    tiles[windows - 1], *sends = call(
        functools.partial(pack_last_kernel, ahead),
        (shifts, last, below, *sends),
        [pair, packed] + [packed] * len(middle),
        scalars=1,
    )
    send_ahead((windows - 1, *middle), sends)
    firsts, closed = {}, {}

    def window(w, after):
        firsts[w] = call(
            functools.partial(window_kernel, ahead, w),
            (shifts, region_ids, spot, tiles[w], gots[w], w_t, w_proj),
            [
                pair,
                shape_of(BF, COUNT, width),
                shape_of(BF, width, COUNT),
                shape_of(BF, 3 * width, COUNT),
            ],
            head_scratch(width),
            scalars=3,
            after=after,
        )
        return (firsts[w][1],)

    def close(w, after):
        tile, _, context, grads = firsts[w]
        out, send = call(
            functools.partial(close_kernel, ahead),
            (shifts, tile, context, grads, w_t, w_proj),
            [pair, packed],
            scalars=1,
            after=after,
        )
        closed[w] = out, ring(send, "lon", -out_step)
        return (send,)

    order = [0, windows - 1, *middle]
    after = (sends[0],)
    for n, w in enumerate(order):
        if n >= 2:
            after = (*after, closed[order[n - 2]][1])
        if n == windows - 2:
            after = (*after, gots[order[-1]])
        if n == windows - 1:
            final = call(
                functools.partial(last_back_kernel, ahead),
                (shifts, *closed[windows - 1]),
                [pair],
                scalars=1,
                after=after,
            )[0]
            above = ring(final, "lat", 1)
            after = (*after, final)
        after = close(w, window(w, after))

    operands = [[firsts[w][n] for w in range(windows)] for n in (1, 0, 2, 3)]
    operands = [a for group in operands for a in group]

    def weights(kept, after):
        return call(
            functools.partial(weight_kernel, windows, kept),
            (spot, *operands),
            [shape_of(F32, width, 2 * width)],
            scalars=1,
            after=after,
        )[0]

    stage, results = [], []

    def beside(value):
        stage.append(value)
        if len(stage) == 1:
            return (closed[order[-1]][1],)
        if len(stage) == 3:
            results.extend(
                call(
                    functools.partial(finish_kernel, ahead, windows),
                    (
                        shifts, tokens, cotangent, above, final,
                        *[closed[w][0] for w in range(windows - 1)],
                        *[closed[w][1] for w in range(windows - 1)],
                    ),
                    [shape_of(BF, *tokens.shape)] * 2,
                    scalars=1,
                    after=(value,),
                )
            )
            return (results[0],)
        return ()

    summed = all_sum(weights, spot, beside, (*after, above, closed[order[-2]][1]))
    mixed, grad_tokens = (
        r.reshape(levels, lon_cols, lat_rows, width).transpose(0, 2, 1, 3) for r in results
    )
    total_tokens = levels * lat_rows * lax.axis_size("lat") * lon_cols * lax.axis_size("lon")
    gradients = write_gradients(1.0 / math.sqrt(total_tokens), spot, *summed)
    return (mixed, grad_tokens, *gradients)


def local(tokens, cotangent, w_qkv, w_proj, shifts, region_ids):
    return lax.cond(
        jnp.sum(shifts[:, 1]) <= ENTRIES,
        functools.partial(body, True),
        functools.partial(body, False),
        tokens, cotangent, w_qkv, w_proj, shifts, region_ids,
    )


def solution(mesh):
    return jax.shard_map(
        local,
        mesh=mesh,
        in_specs=(P(None, "lat", "lon", None), P(None, "lat", "lon", None), P(), P(), P(), P()),
        out_specs=(P(None, "lat", "lon", None), P(None, "lat", "lon", None), P(), P()),
        check_vma=False,
    )
```

```python
import functools
import math

import jax
import jax.numpy as jnp
from jax import lax
from jax.experimental import pallas as pl
from jax.experimental.pallas import tpu as pltpu
from jax.sharding import PartitionSpec as P

HEADS = 16
WLAT = 6
WLON = 12
LEV = 4
COUNT = LEV * WLAT * WLON
LANES = 384
MAIN = 256
REST = COUNT - MAIN
ENTRIES = LEV * WLON // 2
PACKED = ENTRIES * WLAT
NORM_EPS = 1e-05
BARRED = 2.0**100
BF = jnp.bfloat16
F32 = jnp.float32
I32 = jnp.int32

NN = (((1,), (0,)), ((), ()))
NT = (((1,), (1,)), ((), ()))
TN = (((0,), (0,)), ((), ()))
TT = (((0,), (1,)), ((), ()))

SMEM = pl.BlockSpec(memory_space=pltpu.SMEM)
VMEM = pl.BlockSpec(memory_space=pltpu.VMEM)
ANY = pl.BlockSpec(memory_space=pl.ANY)


def dot(a, b, dims):
    return lax.dot_general(a, b, dims, preferred_element_type=F32)


def split_bf16(value):
    high = value.astype(BF)
    low = (value - high.astype(F32)).astype(BF)
    return high, low


def call(kernel, ins, outs, scratch=(), scalars=0, after=()):

    def ordered(*refs):
        kernel(*refs[: len(ins)], *refs[len(ins) + len(after) :])

    return pl.pallas_call(
        ordered,
        in_specs=[SMEM] * scalars + [VMEM] * (len(ins) - scalars) + [ANY] * len(after),
        out_specs=[VMEM] * len(outs),
        out_shape=list(outs),
        scratch_shapes=list(scratch),
        compiler_params=pltpu.CompilerParams(vmem_limit_bytes=24 * 1024 * 1024),
        cost_estimate=pl.CostEstimate(
            flops=1_000_000, bytes_accessed=10_000, transcendentals=0
        ),
    )(*ins, *after)


def shape_of(dtype, *dims):
    return jax.ShapeDtypeStruct(dims, dtype)


def place(axis):
    dims = (COUNT, 1) if axis == 0 else (1, COUNT)
    token = lax.broadcasted_iota(I32, dims, axis)
    level = sum((token >= n * WLAT * WLON).astype(I32) for n in range(1, LEV))
    column, row = column_and_row(token - level * (WLAT * WLON))
    return level, row, column


def column_and_row(rest):
    column = sum((rest >= n * WLAT).astype(I32) for n in range(1, WLON))
    return column, rest - column * WLAT


def level_slots(windows, cut, axis):
    part = WLAT * WLON
    size = (windows + 1) * part
    dims = (size, 1) if axis == 0 else (1, size)
    token = lax.broadcasted_iota(I32, dims, axis)
    window = sum((token >= n * part).astype(I32) for n in range(1, windows + 1))
    column, row = column_and_row(token - window * part)
    at = window * WLAT + row + jnp.where(row < cut, WLAT, 0)
    slot = jnp.where(at < windows * WLAT, column * (windows * WLAT) + at, -1)
    first = window == windows
    return jnp.where(first, column * (windows * WLAT) + row, slot), first, row


def by_level(level, values):
    result = jnp.full(level.shape, values[0], I32)
    for n in range(1, LEV):
        result = jnp.where(level == n, values[n], result)
    return result


def from_next_row(shifts, axis):
    level, row, _ = place(axis)
    return row < by_level(level, [shifts[n, 0] for n in range(LEV)])


def from_other_side(shifts, ahead, axis):
    level, row, column = place(axis)
    cut = [shifts[n, 1] for n in range(LEV)]
    counts = cut if ahead else [WLON - c for c in cut]
    starts = [0] * LEV if ahead else cut
    offsets = [0]
    for n in range(LEV - 1):
        offsets.append(offsets[-1] + counts[n])
    at = by_level(level, cut)
    taken = (column < at) if ahead else (column >= at)
    entry = by_level(level, [o - s for o, s in zip(offsets, starts)]) + column
    return taken, jnp.where(taken, entry * WLAT + row, -1)


def pack_matrix(shifts, ahead):
    _, slot = from_other_side(shifts, ahead, 1)
    rows = lax.broadcasted_iota(I32, (PACKED, COUNT), 0)
    return (rows == slot).astype(F32).astype(BF)


def unpack_matrix(shifts, ahead):
    taken, slot = from_other_side(shifts, ahead, 0)
    columns = lax.broadcasted_iota(I32, (COUNT, PACKED), 1)
    return taken, (columns == slot).astype(F32).astype(BF)


def select_other(taken, spread, packed, own):
    return jnp.where(taken, dot(spread, packed, NN), own.astype(F32))


def pack_kernel(ahead, windows, chosen, sent, shifts, x_ref, cot_ref, *refs):
    part = WLAT * WLON
    grid = x_ref.shape[1]
    count = len(chosen)
    tile_refs, send_refs = refs[:count], refs[count:]
    chooser = pack_matrix(shifts, ahead)
    parts = [[[None] * LEV for _ in range(count)] for _ in range(2)]
    for level in range(LEV):
        slot, _, _ = level_slots(windows, shifts[level, 0], 0)
        slot = jnp.concatenate([slot[w * part : (w + 1) * part] for w in chosen], axis=0)
        cells = lax.broadcasted_iota(I32, (count * part, grid), 1)
        mover = (cells == slot).astype(F32).astype(BF)
        for field, ref in enumerate((x_ref, cot_ref)):
            moved = dot(mover, ref[level], NN)
            for w in range(count):
                parts[field][w][level] = moved[w * part : (w + 1) * part]
    for field in range(2):
        whole = [jnp.concatenate(p, axis=0).astype(BF) for p in parts[field]]
        for tile_ref, tile in zip(tile_refs, whole):
            tile_ref[field] = tile
        for send_ref, tile in zip(send_refs, whole):
            send_ref[field] = dot(chooser, tile, NN).astype(BF)


def pack_last_kernel(ahead, shifts, last_ref, halo_ref, *refs):
    count = len(refs) // 2 - 1
    others, (tile_ref, send_ref, *passed) = refs[:count], refs[count:]
    lower = from_next_row(shifts, 0)
    chooser = pack_matrix(shifts, ahead)
    for field in range(2):
        tile = jnp.where(lower, halo_ref[field].astype(F32), last_ref[field].astype(F32))
        tile_ref[field] = tile.astype(BF)
        send_ref[field] = dot(chooser, tile.astype(BF), NN).astype(BF)
    for ref, other in zip(passed, others):
        ref[...] = other[...]


def standardize(values_full):
    center = values_full - jnp.mean(values_full, axis=1, keepdims=True)
    variance = jnp.mean(center * center, axis=1, keepdims=True)
    inv_scale = lax.rsqrt(variance + NORM_EPS)
    return center * inv_scale, inv_scale


def bars(shifts, ids, first_row, grid_rows, bar_q, bar_k):
    level, row, _ = place(1)
    wrapped = jnp.where(row < by_level(level, [shifts[n, 0] for n in range(LEV)]), WLAT, 0)
    at = first_row + row + wrapped
    at = jnp.where(at >= grid_rows, at - grid_rows, at)
    top = sum((ids[n] == ids[0]).astype(I32) for n in range(WLAT - 1))
    bottom = sum((ids[grid_rows - 1 - n] == ids[grid_rows - 1]).astype(I32) for n in range(WLAT - 1))
    kind = jnp.where(at < top, 1, jnp.where(at >= grid_rows - bottom, 2, 0))
    features = lax.broadcasted_iota(I32, (32, COUNT), 0)
    same = (features == kind).astype(F32)
    bar_q[...] = jnp.zeros_like(bar_q)
    bar_q[:, :COUNT] = (same * -BARRED).astype(BF)
    bar_k[...] = jnp.zeros_like(bar_k)
    bar_k[:, :COUNT] = jnp.where(features < 3, 1.0 - same, 0.0).astype(BF)


def attend(size, bar_q, bar_k, q_s, k_s, v_s, g_s, q_rest, g_rest, buffers, ctx_ref, gp_ref):
    scale = 1.0 / math.sqrt(size)
    part = HEADS * size
    even, odd, both = buffers[:6], buffers[6:12], buffers[12:]

    def rows_of(h, count=1):
        return pl.ds(pl.multiple_of(h * size, size), count * size)

    def stacked(query, bar):
        high, low = split_bf16(query)
        return jnp.concatenate([high, low, high, bar], axis=0)

    def products(h, buffer):
        score_b, grad_b, key_b = buffer[0], buffer[1], buffer[5]
        rows = rows_of(h)
        high, low = split_bf16(k_s[rows])
        key_b[...] = jnp.concatenate([high, high, low, bar_k[...]], axis=0).T[:COUNT]
        score_b[...] = dot(key_b[...], stacked(q_s[rows, :MAIN], bar_q[:, :MAIN]), NN)
        grad_b[...] = dot(v_s[rows].T[:COUNT], g_s[rows, :MAIN], NN)

    def products_both(h):
        keys = jnp.concatenate([even[5][...], odd[5][...]], axis=1)
        bar = bar_q[:, MAIN:]
        rolled = pltpu.roll(bar.astype(F32), REST, 1).astype(BF)
        queries = [stacked(q_rest[rows_of(h)], bar), stacked(q_rest[rows_of(h + 1)], rolled)]
        both[0][...] = dot(keys, jnp.concatenate(queries, axis=0), NN)
        rows = rows_of(h, 2)
        both[1][...] = dot(v_s[rows].T[:COUNT], g_rest[rows], NN)

    def soften(buffer):
        score_b, grad_b, weight_b, high_b, low_b = buffer[:5]
        for start in range(0, score_b.shape[1], 128):
            lanes = slice(start, start + 128)
            scores = score_b[:, lanes]
            expo = jnp.exp2(scores - jnp.max(scores, axis=0, keepdims=True))
            weights = expo * (1.0 / jnp.sum(expo, axis=0, keepdims=True))
            weight_b[:, lanes] = weights.astype(BF)
            grad_w = grad_b[:, lanes]
            grad_sc = weights * (grad_w - jnp.sum(weights * grad_w, axis=0, keepdims=True))
            high_b[:, lanes], low_b[:, lanes] = split_bf16(grad_sc)

    def results(h, buffer, roll):
        rows = rows_of(h)
        value = v_s[rows][:, :COUNT]
        k_high, k_low = split_bf16(k_s[rows][:, :COUNT])
        k_pair = jnp.concatenate([k_high, k_low], axis=0)
        base = pl.multiple_of(h * size, size)
        gk = gv = 0.0
        pieces = (
            (buffer[2:5], q_s[rows, :MAIN], g_s[rows, :MAIN], 0, slice(0, MAIN)),
            (both[2:5], q_rest[rows], g_rest[rows], roll, slice(MAIN, COUNT)),
        )
        for (weight_b, high_b, low_b), query, grad_ctx, turn, lanes in pieces:
            rounded, high, low = weight_b[...], high_b[...], low_b[...]
            q_high, q_low = split_bf16(query)
            context = dot(value, rounded, NN)
            gq = dot(k_pair, high, NN)
            gq = (gq[:size] + gq[size:] + dot(k_high, low, NN)) * scale
            if turn:
                context, gq = (pltpu.roll(a, 128 - turn, 1) for a in (context, gq))
            width = lanes.stop - lanes.start
            ctx_ref[rows, lanes] = context[:, :width].astype(BF)
            gp_ref[pl.ds(base, size), lanes] = gq[:, :width].astype(BF)
            pair = dot(jnp.concatenate([q_high, q_low], axis=0), high, NT)
            gk = gk + pair[:size] + pair[size:] + dot(q_high, low, NT)
            gv = gv + dot(grad_ctx, rounded, NT)
        gp_ref[pl.ds(part + base, size)] = (gk * math.log(2.0)).astype(BF)
        gp_ref[pl.ds(2 * part + base, size)] = gv.astype(BF)

    products(0, even)
    products(1, odd)
    products_both(0)

    def pair(p, carry):
        h = 2 * p
        after = jnp.minimum(h + 2, HEADS - 2)
        soften(even)
        results(jnp.maximum(h - 1, 1), odd, REST)
        soften(odd)
        products(after, even)
        soften(both)
        products(after + 1, odd)
        results(h, even, 0)
        products_both(after)
        return carry

    lax.fori_loop(0, HEADS // 2, pair, 0)
    results(HEADS - 1, odd, REST)


def project(w_ref, wp_ref, norm_s, cot_s, q_s, k_s, v_s, g_s, q_rest, g_rest):
    norm = norm_s[...]
    width = norm.shape[1]
    factor = math.log2(math.e) / math.sqrt(width // HEADS)
    q_s[...] = dot(w_ref[:width], norm, NT) * factor
    k_s[...] = dot(w_ref[width : 2 * width], norm, NT)
    v_s[...] = dot(w_ref[2 * width :], norm, NT).astype(BF)
    g_s[...] = dot(wp_ref[...], cot_s[...], NT).astype(BF)
    odd = (lax.broadcasted_iota(I32, (width, 128), 0) // (width // HEADS)) % 2 == 1
    for source, rest in ((q_s, q_rest), (g_s, g_rest)):
        value = source[:, MAIN:].astype(F32)
        rest[...] = jnp.where(odd, pltpu.roll(value, REST, 1), value).astype(rest.dtype)


def head_scratch(width):
    return [
        pltpu.VMEM((LANES, width), BF),
        pltpu.VMEM((LANES, width), BF),
        pltpu.VMEM((32, LANES), BF),
        pltpu.VMEM((32, LANES), BF),
        pltpu.VMEM((width, LANES), F32),
        pltpu.VMEM((width, LANES), F32),
        pltpu.VMEM((width, LANES), BF),
        pltpu.VMEM((width, LANES), BF),
        pltpu.VMEM((width, 128), F32),
        pltpu.VMEM((width, 128), BF),
    ] + [
        pltpu.VMEM((COUNT, lanes), kind)
        for size in (MAIN, MAIN, 128)
        for kind, lanes in ((F32, size), (F32, size), (BF, size), (BF, size), (BF, size), (BF, 128))
    ]


def window_kernel(
    ahead, window, shifts, ids, spot, own_ref, got_ref, w_ref, wp_ref,
    tile_ref, norm_ref, ctx_ref, gp_ref,
    norm_s, cot_s, bar_q, bar_k, q_s, k_s, v_s, g_s, q_rest, g_rest, *buffers,
):
    width = own_ref.shape[-1]
    taken, spread = unpack_matrix(shifts, ahead)
    x = select_other(taken, spread, got_ref[0], own_ref[0])
    cot = select_other(taken, spread, got_ref[1], own_ref[1]).astype(BF)
    tile_ref[0] = x.astype(BF)
    tile_ref[1] = cot
    normed = standardize(x)[0].astype(BF)
    norm_ref[...] = normed
    norm_s[:COUNT] = normed
    norm_s[COUNT:] = jnp.zeros((LANES - COUNT, width), BF)
    cot_s[:COUNT] = cot
    cot_s[COUNT:] = jnp.zeros((LANES - COUNT, width), BF)
    bars(shifts, ids, spot[0] + window * WLAT, ids.shape[0], bar_q, bar_k)
    rests = q_rest, g_rest
    project(w_ref, wp_ref, norm_s, cot_s, q_s, k_s, v_s, g_s, *rests)
    attend(
        width // HEADS, bar_q, bar_k, q_s, k_s, v_s, g_s, *rests, buffers, ctx_ref, gp_ref
    )


def close_kernel(ahead, shifts, tile_ref, ctx_ref, gp_ref, w_ref, wp_ref, out_ref, send_ref):
    update = dot(ctx_ref[...], wp_ref[...], TN).astype(BF)
    grad_normed = dot(gp_ref[...], w_ref[...], TN)
    standard, inv_scale = standardize(tile_ref[0].astype(F32))
    grad = inv_scale * (
        grad_normed
        - jnp.mean(grad_normed, axis=1, keepdims=True)
        - standard * jnp.mean(grad_normed * standard, axis=1, keepdims=True)
    )
    grad = grad.astype(BF)
    chooser = pack_matrix(shifts, ahead)
    for field, value in enumerate((update, grad)):
        out_ref[field] = value
        send_ref[field] = dot(chooser, value, NN).astype(BF)


def weight_kernel(windows, kept, spot, *refs):
    norms, tiles, ctxs, gps = (refs[n * windows : (n + 1) * windows] for n in range(4))
    out_ref = refs[-1]
    part = ctxs[0].shape[0]

    def total(left, right, dims=TT):
        return functools.reduce(jnp.add, (dot(a, b, dims) for a, b in zip(left, right)))

    side = spot[1] if kept else 1 - spot[1]

    @pl.when(side == 0)
    def _():
        out_ref[...] = total([n[...] for n in norms], [g[: 2 * part] for g in gps])

    @pl.when(side == 1)
    def _():
        out_ref[:, :part] = total([n[...] for n in norms], [g[2 * part :] for g in gps])
        out_ref[:, part:] = total([c[...] for c in ctxs], [t[1] for t in tiles], NN)


def halve_kernel(bit, spot, mine_ref, got_ref, keep_ref, send_ref):
    rows = keep_ref.shape[0]
    for side, ref in ((spot[bit], keep_ref), (1 - spot[bit], send_ref)):
        at = pl.ds(pl.multiple_of(side * rows, rows), rows)
        ref[...] = mine_ref[at] + got_ref[at]


def spread_kernel(spot, mine_ref, got_ref, *out_refs):
    rows = out_refs[0].shape[0]
    for d, ref in enumerate(out_refs):
        at = pl.ds(pl.multiple_of((spot[4] ^ d) * rows, rows), rows)
        ref[...] = mine_ref[at] + got_ref[at]


def gather_sum_kernel(*refs):
    refs[-1][...] = functools.reduce(jnp.add, (r[...] for r in refs[:-1])).astype(BF)


def arrange_kernel(spot, *refs):
    for d, ref in enumerate(refs[:-1]):
        refs[-1][spot[4] ^ d] = ref[...]


def join_kernel(bit, spot, mine_ref, got_ref, out_ref):
    count = mine_ref.shape[0]
    for side, ref in ((spot[bit], mine_ref), (1 - spot[bit], got_ref)):
        for n in range(count):
            out_ref[side * count + n] = ref[n]


def gradient_kernel(factor, spot, mine_ref, got_ref, qkv_ref, proj_ref):
    width = proj_ref.shape[1]

    def write(pair_ref, rest_ref):
        rest = rest_ref[...].astype(F32) * factor
        qkv_ref[:, : 2 * width] = pair_ref[...].astype(F32) * factor
        qkv_ref[:, 2 * width :] = rest[:, :width]
        proj_ref[...] = rest[:, width:]

    first = spot[1] == 0

    @pl.when(first)
    def _():
        write(mine_ref, got_ref)

    @pl.when(jnp.logical_not(first))
    def _():
        write(got_ref, mine_ref)


def write_gradients(factor, spot, mine, got):
    count, rows, columns = mine.shape
    width = columns // 2
    piece = pl.BlockSpec((None, rows, columns), lambda n: (n, 0, 0))
    return pl.pallas_call(
        functools.partial(gradient_kernel, factor),
        grid=(count,),
        in_specs=[SMEM, piece, piece],
        out_specs=[
            pl.BlockSpec((rows, 3 * width), lambda n: (n, 0)),
            pl.BlockSpec((rows, width), lambda n: (n, 0)),
        ],
        out_shape=[
            shape_of(F32, count * rows, 3 * width),
            shape_of(F32, count * rows, width),
        ],
        compiler_params=pltpu.CompilerParams(vmem_limit_bytes=24 * 1024 * 1024),
    )(spot, mine, got)


def turn_kernel(w_ref, out_ref):
    out_ref[...] = w_ref[...].T


def last_back_kernel(ahead, shifts, own_ref, got_ref, out_ref):
    taken, spread = unpack_matrix(shifts, ahead)
    for field in range(2):
        out_ref[field] = select_other(taken, spread, got_ref[field], own_ref[field]).astype(BF)


def finish_kernel(ahead, windows, shifts, x_ref, cot_ref, above_ref, final_ref, *refs):
    owns, gots = refs[: windows - 1], refs[windows - 1 : 2 * windows - 2]
    outs = refs[2 * windows - 2 :]
    part = WLAT * WLON
    grid = x_ref.shape[1]
    taken, spread = unpack_matrix(shifts, ahead)
    movers = []
    for level in range(LEV):
        cut = shifts[level, 0]
        slot, first, row = level_slots(windows, cut, 1)
        slot = jnp.where(jnp.logical_and(first, row >= cut), -1, slot)
        cells = lax.broadcasted_iota(I32, (grid, (windows + 1) * part), 0)
        movers.append((cells == slot).astype(F32).astype(BF))
    for field, ref in enumerate((x_ref, cot_ref)):
        tiles = [
            select_other(taken, spread, gots[w][field], owns[w][field]) for w in range(windows - 1)
        ]
        tiles += [final_ref[field].astype(F32), above_ref[field].astype(F32)]
        for level in range(LEV):
            here = slice(level * part, (level + 1) * part)
            source = jnp.concatenate([t[here] for t in tiles], axis=0).astype(BF)
            value = ref[level].astype(F32) + dot(movers[level], source, NN)
            outs[field][level] = value.astype(BF)


def route(pairs_of, lat, lon):
    return [
        (a * lon + o, pairs_of(a, o)[0] * lon + pairs_of(a, o)[1])
        for a in range(lat)
        for o in range(lon)
    ]


def across_core(a, o):
    return a ^ 1, o


def step_one(a, o):
    return (a, o ^ 1) if a % 2 else (a ^ 2, o)


def step_two(a, o):
    return (a ^ 2, o) if a % 2 else (a, o ^ 1)


def all_sum(weights, spot, beside, earlier):
    lat, lon = lax.axis_size("lat"), lax.axis_size("lon")
    reach = lon // 2

    def swap(value, pairs_of):
        return lax.ppermute(value, ("lat", "lon"), route(pairs_of, lat, lon))

    def along(d):
        return lambda a, o: (a, o ^ (2 * d))

    sent = weights(False, earlier)
    got = swap(sent, across_core)
    held = weights(True, (sent,))
    after = beside(held)
    for bit, pairs_of in ((2, step_one), (3, step_two)):
        rows, width = held.shape[0] // 2, held.shape[1]
        held, sent = call(
            functools.partial(halve_kernel, bit),
            (spot, held, got),
            [shape_of(F32, rows, width)] * 2,
            scalars=1,
            after=after,
        )
        got = swap(sent, pairs_of)
        after = beside(held)
    rows = held.shape[0] // reach
    pieces = call(
        spread_kernel, (spot, held, got), [shape_of(F32, rows, width)] * reach, scalars=1, after=after
    )
    gots = [swap(pieces[d], along(d)) for d in range(1, reach)]
    after = beside(pieces[0])
    sums = call(gather_sum_kernel, (pieces[0], *gots), [shape_of(BF, rows, width)], after=after)[0]
    gots = [swap(sums, along(d)) for d in range(1, reach)]
    after = beside(sums)
    part = call(
        arrange_kernel, (spot, sums, *gots), [shape_of(BF, reach, rows, width)], scalars=1, after=after
    )[0]
    held = part.reshape(1, reach * rows, width)
    for bit, pairs_of in ((3, step_two), (2, step_one)):
        got = swap(held, pairs_of)
        after = beside(held)
        held = call(
            functools.partial(join_kernel, bit),
            (spot, held, got),
            [shape_of(BF, 2 * held.shape[0], *held.shape[1:])],
            scalars=1,
            after=after,
        )[0]
    return held, swap(held, across_core)


def ring(value, axis, step):
    count = lax.axis_size(axis)
    return lax.ppermute(value, axis, [(i, (i + step) % count) for i in range(count)])


def body(ahead, tokens, cotangent, w_qkv, w_proj, shifts, region_ids):
    levels, lat_rows, lon_cols, width = tokens.shape

    def by_column(grid_field):
        return grid_field.transpose(0, 2, 1, 3).reshape(levels, lon_cols * lat_rows, width)

    tokens, cotangent = by_column(tokens), by_column(cotangent)
    windows = lat_rows // WLAT
    my_lat, my_lon = lax.axis_index("lat"), lax.axis_index("lon")
    core, high, low = my_lat & 1, my_lat >> 1, my_lon & 1
    spot = jnp.stack(
        [
            my_lat * lat_rows,
            core,
            jnp.where(core == 1, low, high),
            jnp.where(core == 1, high, low),
            my_lon >> 1,
        ]
    ).astype(I32)
    out_step = -1 if ahead else 1
    pair = shape_of(BF, 2, COUNT, width)
    packed = shape_of(BF, 2, PACKED, width)

    def packs(chosen, sent, after):
        made = call(
            functools.partial(pack_kernel, ahead, windows, chosen, sent),
            (shifts, tokens, cotangent),
            [pair] * len(chosen) + [packed] * sent,
            scalars=1,
            after=after,
        )
        return made[: len(chosen)], made[len(chosen) :]

    def send_ahead(windows_sent, sends):
        for w, send in zip(windows_sent, sends):
            gots[w] = ring(send, "lon", out_step)

    gots, tiles = {}, {}
    (tiles[0], halo), sends = packs((0, windows), 1, ())
    send_ahead((0,), sends)
    below = ring(halo, "lat", -1)
    w_t = call(turn_kernel, (w_qkv,), [shape_of(BF, 3 * width, width)], after=(halo,))[0]
    middle = tuple(range(1, windows - 1))
    made, sends = packs((*middle, windows - 1), len(middle), (w_t,))
    *made, last = made
    tiles.update(zip(middle, made))
    tiles[windows - 1], *sends = call(
        functools.partial(pack_last_kernel, ahead),
        (shifts, last, below, *sends),
        [pair, packed] + [packed] * len(middle),
        scalars=1,
    )
    send_ahead((windows - 1, *middle), sends)
    firsts, closed = {}, {}

    def window(w, after):
        firsts[w] = call(
            functools.partial(window_kernel, ahead, w),
            (shifts, region_ids, spot, tiles[w], gots[w], w_t, w_proj),
            [
                pair,
                shape_of(BF, COUNT, width),
                shape_of(BF, width, COUNT),
                shape_of(BF, 3 * width, COUNT),
            ],
            head_scratch(width),
            scalars=3,
            after=after,
        )
        return (firsts[w][1],)

    def close(w, after):
        tile, _, context, grads = firsts[w]
        out, send = call(
            functools.partial(close_kernel, ahead),
            (shifts, tile, context, grads, w_t, w_proj),
            [pair, packed],
            scalars=1,
            after=after,
        )
        closed[w] = out, ring(send, "lon", -out_step)
        return (send,)

    order = [0, windows - 1, *middle]
    after = (sends[0],)
    for n, w in enumerate(order):
        if n >= 2:
            after = (*after, closed[order[n - 2]][1])
        if n == windows - 2:
            after = (*after, gots[order[-1]])
        if n == windows - 1:
            final = call(
                functools.partial(last_back_kernel, ahead),
                (shifts, *closed[windows - 1]),
                [pair],
                scalars=1,
                after=after,
            )[0]
            above = ring(final, "lat", 1)
            after = (*after, final)
        after = window(w, after)
        if n < windows - 1:
            after = close(w, after)

    operands = [[firsts[w][n] for w in range(windows)] for n in (1, 0, 2, 3)]
    operands = [a for group in operands for a in group]

    def weights(kept, after):
        return call(
            functools.partial(weight_kernel, windows, kept),
            (spot, *operands),
            [shape_of(F32, width, 2 * width)],
            scalars=1,
            after=after,
        )[0]

    stage, results = [], []

    def beside(value):
        stage.append(value)
        if len(stage) == 1:
            return close(order[-1], (value,))
        if len(stage) == 2:
            return (closed[order[-1]][1],)
        if len(stage) == 3:
            results.extend(
                call(
                    functools.partial(finish_kernel, ahead, windows),
                    (
                        shifts, tokens, cotangent, above, final,
                        *[closed[w][0] for w in range(windows - 1)],
                        *[closed[w][1] for w in range(windows - 1)],
                    ),
                    [shape_of(BF, *tokens.shape)] * 2,
                    scalars=1,
                    after=(value,),
                )
            )
            return (results[0],)
        return ()

    summed = all_sum(weights, spot, beside, (*after, above, closed[order[-2]][1]))
    mixed, grad_tokens = (
        r.reshape(levels, lon_cols, lat_rows, width).transpose(0, 2, 1, 3) for r in results
    )
    total_tokens = levels * lat_rows * lax.axis_size("lat") * lon_cols * lax.axis_size("lon")
    gradients = write_gradients(1.0 / math.sqrt(total_tokens), spot, *summed)
    return (mixed, grad_tokens, *gradients)


def local(tokens, cotangent, w_qkv, w_proj, shifts, region_ids):
    return lax.cond(
        jnp.sum(shifts[:, 1]) <= ENTRIES,
        functools.partial(body, True),
        functools.partial(body, False),
        tokens, cotangent, w_qkv, w_proj, shifts, region_ids,
    )


def solution(mesh):
    return jax.shard_map(
        local,
        mesh=mesh,
        in_specs=(P(None, "lat", "lon", None), P(None, "lat", "lon", None), P(), P(), P(), P()),
        out_specs=(P(None, "lat", "lon", None), P(None, "lat", "lon", None), P(), P()),
        check_vma=False,
    )
```

```python
import functools
import math

import jax
import jax.numpy as jnp
from jax import lax
from jax.experimental import pallas as pl
from jax.experimental.pallas import tpu as pltpu
from jax.sharding import PartitionSpec as P

HEADS = 16
WLAT = 6
WLON = 12
LEV = 4
COUNT = LEV * WLAT * WLON
LANES = 384
MAIN = 256
REST = COUNT - MAIN
ENTRIES = LEV * WLON // 2
PACKED = ENTRIES * WLAT
NORM_EPS = 1e-05
BARRED = 2.0**100
BF = jnp.bfloat16
F32 = jnp.float32
I32 = jnp.int32

NN = (((1,), (0,)), ((), ()))
NT = (((1,), (1,)), ((), ()))
TN = (((0,), (0,)), ((), ()))
TT = (((0,), (1,)), ((), ()))

SMEM = pl.BlockSpec(memory_space=pltpu.SMEM)
VMEM = pl.BlockSpec(memory_space=pltpu.VMEM)
ANY = pl.BlockSpec(memory_space=pl.ANY)


def dot(a, b, dims):
    return lax.dot_general(a, b, dims, preferred_element_type=F32)


def split_bf16(value):
    high = value.astype(BF)
    low = (value - high.astype(F32)).astype(BF)
    return high, low


def call(kernel, ins, outs, scratch=(), scalars=0, after=()):

    def ordered(*refs):
        kernel(*refs[: len(ins)], *refs[len(ins) + len(after) :])

    return pl.pallas_call(
        ordered,
        in_specs=[SMEM] * scalars + [VMEM] * (len(ins) - scalars) + [ANY] * len(after),
        out_specs=[VMEM] * len(outs),
        out_shape=list(outs),
        scratch_shapes=list(scratch),
        compiler_params=pltpu.CompilerParams(vmem_limit_bytes=24 * 1024 * 1024),
        cost_estimate=pl.CostEstimate(
            flops=1_000_000, bytes_accessed=10_000, transcendentals=0
        ),
    )(*ins, *after)


def shape_of(dtype, *dims):
    return jax.ShapeDtypeStruct(dims, dtype)


def place(axis):
    dims = (COUNT, 1) if axis == 0 else (1, COUNT)
    token = lax.broadcasted_iota(I32, dims, axis)
    level = sum((token >= n * WLAT * WLON).astype(I32) for n in range(1, LEV))
    column, row = column_and_row(token - level * (WLAT * WLON))
    return level, row, column


def column_and_row(rest):
    column = sum((rest >= n * WLAT).astype(I32) for n in range(1, WLON))
    return column, rest - column * WLAT


def level_slots(windows, cut, axis):
    part = WLAT * WLON
    size = (windows + 1) * part
    dims = (size, 1) if axis == 0 else (1, size)
    token = lax.broadcasted_iota(I32, dims, axis)
    window = sum((token >= n * part).astype(I32) for n in range(1, windows + 1))
    column, row = column_and_row(token - window * part)
    at = window * WLAT + row + jnp.where(row < cut, WLAT, 0)
    slot = jnp.where(at < windows * WLAT, column * (windows * WLAT) + at, -1)
    first = window == windows
    return jnp.where(first, column * (windows * WLAT) + row, slot), first, row


def by_level(level, values):
    result = jnp.full(level.shape, values[0], I32)
    for n in range(1, LEV):
        result = jnp.where(level == n, values[n], result)
    return result


def from_next_row(shifts, axis):
    level, row, _ = place(axis)
    return row < by_level(level, [shifts[n, 0] for n in range(LEV)])


def from_other_side(shifts, ahead, axis):
    level, row, column = place(axis)
    cut = [shifts[n, 1] for n in range(LEV)]
    counts = cut if ahead else [WLON - c for c in cut]
    starts = [0] * LEV if ahead else cut
    offsets = [0]
    for n in range(LEV - 1):
        offsets.append(offsets[-1] + counts[n])
    at = by_level(level, cut)
    taken = (column < at) if ahead else (column >= at)
    entry = by_level(level, [o - s for o, s in zip(offsets, starts)]) + column
    return taken, jnp.where(taken, entry * WLAT + row, -1)


def pack_matrix(shifts, ahead):
    _, slot = from_other_side(shifts, ahead, 1)
    rows = lax.broadcasted_iota(I32, (PACKED, COUNT), 0)
    return (rows == slot).astype(F32).astype(BF)


def unpack_matrix(shifts, ahead):
    taken, slot = from_other_side(shifts, ahead, 0)
    columns = lax.broadcasted_iota(I32, (COUNT, PACKED), 1)
    return taken, (columns == slot).astype(F32).astype(BF)


def select_other(taken, spread, packed, own):
    return jnp.where(taken, dot(spread, packed, NN), own.astype(F32))


def pack_kernel(ahead, windows, chosen, sent, shifts, x_ref, cot_ref, *refs):
    part = WLAT * WLON
    grid = x_ref.shape[1]
    count = len(chosen)
    tile_refs, send_refs = refs[:count], refs[count:]
    chooser = pack_matrix(shifts, ahead)
    parts = [[[None] * LEV for _ in range(count)] for _ in range(2)]
    for level in range(LEV):
        slot, _, _ = level_slots(windows, shifts[level, 0], 0)
        slot = jnp.concatenate([slot[w * part : (w + 1) * part] for w in chosen], axis=0)
        cells = lax.broadcasted_iota(I32, (count * part, grid), 1)
        mover = (cells == slot).astype(F32).astype(BF)
        for field, ref in enumerate((x_ref, cot_ref)):
            moved = dot(mover, ref[level], NN)
            for w in range(count):
                parts[field][w][level] = moved[w * part : (w + 1) * part]
    for field in range(2):
        whole = [jnp.concatenate(p, axis=0).astype(BF) for p in parts[field]]
        for tile_ref, tile in zip(tile_refs, whole):
            tile_ref[field] = tile
        for send_ref, tile in zip(send_refs, whole):
            send_ref[field] = dot(chooser, tile, NN).astype(BF)


def pack_last_kernel(ahead, shifts, last_ref, halo_ref, *refs):
    count = len(refs) // 2 - 1
    others, (tile_ref, send_ref, *passed) = refs[:count], refs[count:]
    lower = from_next_row(shifts, 0)
    chooser = pack_matrix(shifts, ahead)
    for field in range(2):
        tile = jnp.where(lower, halo_ref[field].astype(F32), last_ref[field].astype(F32))
        tile_ref[field] = tile.astype(BF)
        send_ref[field] = dot(chooser, tile.astype(BF), NN).astype(BF)
    for ref, other in zip(passed, others):
        ref[...] = other[...]


def standardize(values_full):
    center = values_full - jnp.mean(values_full, axis=1, keepdims=True)
    variance = jnp.mean(center * center, axis=1, keepdims=True)
    inv_scale = lax.rsqrt(variance + NORM_EPS)
    return center * inv_scale, inv_scale


def bars(shifts, ids, first_row, grid_rows, bar_q, bar_k):
    level, row, _ = place(1)
    wrapped = jnp.where(row < by_level(level, [shifts[n, 0] for n in range(LEV)]), WLAT, 0)
    at = first_row + row + wrapped
    at = jnp.where(at >= grid_rows, at - grid_rows, at)
    top = sum((ids[n] == ids[0]).astype(I32) for n in range(WLAT - 1))
    bottom = sum((ids[grid_rows - 1 - n] == ids[grid_rows - 1]).astype(I32) for n in range(WLAT - 1))
    kind = jnp.where(at < top, 1, jnp.where(at >= grid_rows - bottom, 2, 0))
    features = lax.broadcasted_iota(I32, (32, COUNT), 0)
    same = (features == kind).astype(F32)
    bar_q[...] = jnp.zeros_like(bar_q)
    bar_q[:, :COUNT] = (same * -BARRED).astype(BF)
    bar_k[...] = jnp.zeros_like(bar_k)
    bar_k[:, :COUNT] = jnp.where(features < 3, 1.0 - same, 0.0).astype(BF)


def attend(size, bar_q, bar_k, q_s, k_s, v_s, g_s, q_rest, g_rest, buffers, ctx_ref, gp_ref):
    scale = 1.0 / math.sqrt(size)
    part = HEADS * size
    even, odd, both = buffers[:6], buffers[6:12], buffers[12:]

    def rows_of(h, count=1):
        return pl.ds(pl.multiple_of(h * size, size), count * size)

    def stacked(query, bar):
        high, low = split_bf16(query)
        return jnp.concatenate([high, low, high, bar], axis=0)

    def products(h, buffer):
        score_b, grad_b, key_b = buffer[0], buffer[1], buffer[5]
        rows = rows_of(h)
        high, low = split_bf16(k_s[rows])
        key_b[...] = jnp.concatenate([high, high, low, bar_k[...]], axis=0).T[:COUNT]
        score_b[...] = dot(key_b[...], stacked(q_s[rows, :MAIN], bar_q[:, :MAIN]), NN)
        grad_b[...] = dot(v_s[rows].T[:COUNT], g_s[rows, :MAIN], NN)

    def products_both(h):
        keys = jnp.concatenate([even[5][...], odd[5][...]], axis=1)
        bar = bar_q[:, MAIN:]
        rolled = pltpu.roll(bar.astype(F32), REST, 1).astype(BF)
        queries = [stacked(q_rest[rows_of(h)], bar), stacked(q_rest[rows_of(h + 1)], rolled)]
        both[0][...] = dot(keys, jnp.concatenate(queries, axis=0), NN)
        rows = rows_of(h, 2)
        both[1][...] = dot(v_s[rows].T[:COUNT], g_rest[rows], NN)

    def soften(buffer):
        score_b, grad_b, weight_b, high_b, low_b = buffer[:5]
        for start in range(0, score_b.shape[1], 128):
            lanes = slice(start, start + 128)
            scores = score_b[:, lanes]
            expo = jnp.exp2(scores - jnp.max(scores, axis=0, keepdims=True))
            weights = expo * (1.0 / jnp.sum(expo, axis=0, keepdims=True))
            weight_b[:, lanes] = weights.astype(BF)
            grad_w = grad_b[:, lanes]
            grad_sc = weights * (grad_w - jnp.sum(weights * grad_w, axis=0, keepdims=True))
            high_b[:, lanes], low_b[:, lanes] = split_bf16(grad_sc)

    def results(h, buffer, roll):
        rows = rows_of(h)
        value = v_s[rows][:, :COUNT]
        k_high, k_low = split_bf16(k_s[rows][:, :COUNT])
        k_pair = jnp.concatenate([k_high, k_low], axis=0)
        base = pl.multiple_of(h * size, size)
        gk = gv = 0.0
        pieces = (
            (buffer[2:5], q_s[rows, :MAIN], g_s[rows, :MAIN], 0, slice(0, MAIN)),
            (both[2:5], q_rest[rows], g_rest[rows], roll, slice(MAIN, COUNT)),
        )
        for (weight_b, high_b, low_b), query, grad_ctx, turn, lanes in pieces:
            rounded, high, low = weight_b[...], high_b[...], low_b[...]
            q_high, q_low = split_bf16(query)
            context = dot(value, rounded, NN)
            gq = dot(k_pair, high, NN)
            gq = (gq[:size] + gq[size:] + dot(k_high, low, NN)) * scale
            if turn:
                context, gq = (pltpu.roll(a, 128 - turn, 1) for a in (context, gq))
            width = lanes.stop - lanes.start
            ctx_ref[rows, lanes] = context[:, :width].astype(BF)
            gp_ref[pl.ds(base, size), lanes] = gq[:, :width].astype(BF)
            pair = dot(jnp.concatenate([q_high, q_low], axis=0), high, NT)
            gk = gk + pair[:size] + pair[size:] + dot(q_high, low, NT)
            gv = gv + dot(grad_ctx, rounded, NT)
        gp_ref[pl.ds(part + base, size)] = (gk * math.log(2.0)).astype(BF)
        gp_ref[pl.ds(2 * part + base, size)] = gv.astype(BF)

    products(0, even)
    products(1, odd)
    products_both(0)

    def pair(p, carry):
        h = 2 * p
        after = jnp.minimum(h + 2, HEADS - 2)
        soften(even)
        results(jnp.maximum(h - 1, 1), odd, REST)
        soften(odd)
        products(after, even)
        soften(both)
        products(after + 1, odd)
        results(h, even, 0)
        products_both(after)
        return carry

    lax.fori_loop(0, HEADS // 2, pair, 0)
    results(HEADS - 1, odd, REST)


def project(w_ref, wp_ref, norm_s, cot_s, q_s, k_s, v_s, g_s, q_rest, g_rest):
    norm = norm_s[...]
    width = norm.shape[1]
    factor = math.log2(math.e) / math.sqrt(width // HEADS)
    q_s[...] = dot(w_ref[:width], norm, NT) * factor
    k_s[...] = dot(w_ref[width : 2 * width], norm, NT)
    v_s[...] = dot(w_ref[2 * width :], norm, NT).astype(BF)
    g_s[...] = dot(wp_ref[...], cot_s[...], NT).astype(BF)
    odd = (lax.broadcasted_iota(I32, (width, 128), 0) // (width // HEADS)) % 2 == 1
    for source, rest in ((q_s, q_rest), (g_s, g_rest)):
        value = source[:, MAIN:].astype(F32)
        rest[...] = jnp.where(odd, pltpu.roll(value, REST, 1), value).astype(rest.dtype)


def head_scratch(width):
    return [
        pltpu.VMEM((LANES, width), BF),
        pltpu.VMEM((LANES, width), BF),
        pltpu.VMEM((32, LANES), BF),
        pltpu.VMEM((32, LANES), BF),
        pltpu.VMEM((width, LANES), F32),
        pltpu.VMEM((width, LANES), F32),
        pltpu.VMEM((width, LANES), BF),
        pltpu.VMEM((width, LANES), BF),
        pltpu.VMEM((width, 128), F32),
        pltpu.VMEM((width, 128), BF),
    ] + [
        pltpu.VMEM((COUNT, lanes), kind)
        for size in (MAIN, MAIN, 128)
        for kind, lanes in ((F32, size), (F32, size), (BF, size), (BF, size), (BF, size), (BF, 128))
    ]


def window_kernel(
    ahead, window, shifts, ids, spot, own_ref, got_ref, w_ref, wp_ref,
    tile_ref, norm_ref, ctx_ref, gp_ref,
    norm_s, cot_s, bar_q, bar_k, q_s, k_s, v_s, g_s, q_rest, g_rest, *buffers,
):
    width = own_ref.shape[-1]
    taken, spread = unpack_matrix(shifts, ahead)
    x = select_other(taken, spread, got_ref[0], own_ref[0])
    cot = select_other(taken, spread, got_ref[1], own_ref[1]).astype(BF)
    tile_ref[0] = x.astype(BF)
    tile_ref[1] = cot
    normed = standardize(x)[0].astype(BF)
    norm_ref[...] = normed
    norm_s[:COUNT] = normed
    norm_s[COUNT:] = jnp.zeros((LANES - COUNT, width), BF)
    cot_s[:COUNT] = cot
    cot_s[COUNT:] = jnp.zeros((LANES - COUNT, width), BF)
    bars(shifts, ids, spot[0] + window * WLAT, ids.shape[0], bar_q, bar_k)
    rests = q_rest, g_rest
    project(w_ref, wp_ref, norm_s, cot_s, q_s, k_s, v_s, g_s, *rests)
    attend(
        width // HEADS, bar_q, bar_k, q_s, k_s, v_s, g_s, *rests, buffers, ctx_ref, gp_ref
    )


def close_kernel(ahead, shifts, tile_ref, ctx_ref, gp_ref, w_ref, wp_ref, out_ref, send_ref):
    update = dot(ctx_ref[...], wp_ref[...], TN).astype(BF)
    grad_normed = dot(gp_ref[...], w_ref[...], TN)
    standard, inv_scale = standardize(tile_ref[0].astype(F32))
    grad = inv_scale * (
        grad_normed
        - jnp.mean(grad_normed, axis=1, keepdims=True)
        - standard * jnp.mean(grad_normed * standard, axis=1, keepdims=True)
    )
    grad = grad.astype(BF)
    chooser = pack_matrix(shifts, ahead)
    for field, value in enumerate((update, grad)):
        out_ref[field] = value
        send_ref[field] = dot(chooser, value, NN).astype(BF)


def weight_kernel(windows, kept, spot, *refs):
    norms, tiles, ctxs, gps = (refs[n * windows : (n + 1) * windows] for n in range(4))
    out_ref = refs[-1]
    part = ctxs[0].shape[0]

    def total(left, right, dims=TT):
        sides = (0, 1) if dims == TT else (1, 0)
        return dot(*(jnp.concatenate(a, axis=n) for a, n in zip((left, right), sides)), dims)

    side = spot[1] if kept else 1 - spot[1]

    @pl.when(side == 0)
    def _():
        out_ref[...] = total([n[...] for n in norms], [g[: 2 * part] for g in gps])

    @pl.when(side == 1)
    def _():
        out_ref[:, :part] = total([n[...] for n in norms], [g[2 * part :] for g in gps])
        out_ref[:, part:] = total([c[...] for c in ctxs], [t[1] for t in tiles], NN)


def halve_kernel(bit, spot, mine_ref, got_ref, keep_ref, send_ref):
    rows = keep_ref.shape[0]
    for side, ref in ((spot[bit], keep_ref), (1 - spot[bit], send_ref)):
        at = pl.ds(pl.multiple_of(side * rows, rows), rows)
        ref[...] = mine_ref[at] + got_ref[at]


def spread_kernel(spot, mine_ref, got_ref, *out_refs):
    rows = out_refs[0].shape[0]
    for d, ref in enumerate(out_refs):
        at = pl.ds(pl.multiple_of((spot[4] ^ d) * rows, rows), rows)
        ref[...] = mine_ref[at] + got_ref[at]


def gather_sum_kernel(*refs):
    refs[-1][...] = functools.reduce(jnp.add, (r[...] for r in refs[:-1])).astype(BF)


def arrange_kernel(spot, *refs):
    for d, ref in enumerate(refs[:-1]):
        refs[-1][spot[4] ^ d] = ref[...]


def join_kernel(bit, spot, mine_ref, got_ref, out_ref):
    count = mine_ref.shape[0]
    for side, ref in ((spot[bit], mine_ref), (1 - spot[bit], got_ref)):
        for n in range(count):
            out_ref[side * count + n] = ref[n]


def gradient_kernel(factor, spot, mine_ref, got_ref, qkv_ref, proj_ref):
    width = proj_ref.shape[1]

    def write(pair_ref, rest_ref):
        here = pl.program_id(0)
        rest = rest_ref[here].astype(F32) * factor
        qkv_ref[:, : 2 * width] = pair_ref[here].astype(F32) * factor
        qkv_ref[:, 2 * width :] = rest[:, :width]
        proj_ref[...] = rest[:, width:]

    first = spot[1] == 0

    @pl.when(first)
    def _():
        write(mine_ref, got_ref)

    @pl.when(jnp.logical_not(first))
    def _():
        write(got_ref, mine_ref)


def write_gradients(factor, spot, mine, got):
    count, rows, columns = mine.shape
    width = columns // 2
    return pl.pallas_call(
        functools.partial(gradient_kernel, factor),
        grid=(count,),
        in_specs=[SMEM, VMEM, VMEM],
        out_specs=[
            pl.BlockSpec((rows, 3 * width), lambda n: (n, 0)),
            pl.BlockSpec((rows, width), lambda n: (n, 0)),
        ],
        out_shape=[
            shape_of(F32, count * rows, 3 * width),
            shape_of(F32, count * rows, width),
        ],
        compiler_params=pltpu.CompilerParams(vmem_limit_bytes=24 * 1024 * 1024),
    )(spot, mine, got)


def turn_kernel(w_ref, out_ref):
    out_ref[...] = w_ref[...].T


def last_back_kernel(ahead, shifts, own_ref, got_ref, out_ref):
    taken, spread = unpack_matrix(shifts, ahead)
    for field in range(2):
        out_ref[field] = select_other(taken, spread, got_ref[field], own_ref[field]).astype(BF)


def finish_kernel(ahead, windows, shifts, x_ref, cot_ref, above_ref, final_ref, *refs):
    owns, gots = refs[: windows - 1], refs[windows - 1 : 2 * windows - 2]
    outs = refs[2 * windows - 2 :]
    part = WLAT * WLON
    grid = x_ref.shape[1]
    taken, spread = unpack_matrix(shifts, ahead)
    movers = []
    for level in range(LEV):
        cut = shifts[level, 0]
        slot, first, row = level_slots(windows, cut, 1)
        slot = jnp.where(jnp.logical_and(first, row >= cut), -1, slot)
        cells = lax.broadcasted_iota(I32, (grid, (windows + 1) * part), 0)
        movers.append((cells == slot).astype(F32).astype(BF))
    for field, ref in enumerate((x_ref, cot_ref)):
        tiles = [
            select_other(taken, spread, gots[w][field], owns[w][field]) for w in range(windows - 1)
        ]
        tiles += [final_ref[field].astype(F32), above_ref[field].astype(F32)]
        for level in range(LEV):
            here = slice(level * part, (level + 1) * part)
            source = jnp.concatenate([t[here] for t in tiles], axis=0).astype(BF)
            value = ref[level].astype(F32) + dot(movers[level], source, NN)
            outs[field][level] = value.astype(BF)


def route(pairs_of, lat, lon):
    return [
        (a * lon + o, pairs_of(a, o)[0] * lon + pairs_of(a, o)[1])
        for a in range(lat)
        for o in range(lon)
    ]


def across_core(a, o):
    return a ^ 1, o


def step_one(a, o):
    return (a, o ^ 1) if a % 2 else (a ^ 2, o)


def step_two(a, o):
    return (a ^ 2, o) if a % 2 else (a, o ^ 1)


def all_sum(weights, spot, beside, earlier):
    lat, lon = lax.axis_size("lat"), lax.axis_size("lon")
    reach = lon // 2

    def swap(value, pairs_of):
        return lax.ppermute(value, ("lat", "lon"), route(pairs_of, lat, lon))

    def along(d):
        return lambda a, o: (a, o ^ (2 * d))

    sent = weights(False, earlier)
    got = swap(sent, across_core)
    held = weights(True, (sent,))
    after = beside(held)
    for bit, pairs_of in ((2, step_one), (3, step_two)):
        rows, width = held.shape[0] // 2, held.shape[1]
        held, sent = call(
            functools.partial(halve_kernel, bit),
            (spot, held, got),
            [shape_of(F32, rows, width)] * 2,
            scalars=1,
            after=after,
        )
        got = swap(sent, pairs_of)
        after = beside(held)
    rows = held.shape[0] // reach
    pieces = call(
        spread_kernel, (spot, held, got), [shape_of(F32, rows, width)] * reach, scalars=1, after=after
    )
    gots = [swap(pieces[d], along(d)) for d in range(1, reach)]
    after = beside(pieces[0])
    sums = call(gather_sum_kernel, (pieces[0], *gots), [shape_of(BF, rows, width)], after=after)[0]
    gots = [swap(sums, along(d)) for d in range(1, reach)]
    after = beside(sums)
    part = call(
        arrange_kernel, (spot, sums, *gots), [shape_of(BF, reach, rows, width)], scalars=1, after=after
    )[0]
    held = part.reshape(1, reach * rows, width)
    for bit, pairs_of in ((3, step_two), (2, step_one)):
        got = swap(held, pairs_of)
        after = beside(held)
        held = call(
            functools.partial(join_kernel, bit),
            (spot, held, got),
            [shape_of(BF, 2 * held.shape[0], *held.shape[1:])],
            scalars=1,
            after=after,
        )[0]
    return held, swap(held, across_core)


def ring(value, axis, step):
    count = lax.axis_size(axis)
    return lax.ppermute(value, axis, [(i, (i + step) % count) for i in range(count)])


def body(ahead, tokens, cotangent, w_qkv, w_proj, shifts, region_ids):
    levels, lat_rows, lon_cols, width = tokens.shape

    def by_column(grid_field):
        return grid_field.transpose(0, 2, 1, 3).reshape(levels, lon_cols * lat_rows, width)

    tokens, cotangent = by_column(tokens), by_column(cotangent)
    windows = lat_rows // WLAT
    my_lat, my_lon = lax.axis_index("lat"), lax.axis_index("lon")
    core, high, low = my_lat & 1, my_lat >> 1, my_lon & 1
    spot = jnp.stack(
        [
            my_lat * lat_rows,
            core,
            jnp.where(core == 1, low, high),
            jnp.where(core == 1, high, low),
            my_lon >> 1,
        ]
    ).astype(I32)
    out_step = -1 if ahead else 1
    pair = shape_of(BF, 2, COUNT, width)
    packed = shape_of(BF, 2, PACKED, width)

    def packs(chosen, sent, after):
        made = call(
            functools.partial(pack_kernel, ahead, windows, chosen, sent),
            (shifts, tokens, cotangent),
            [pair] * len(chosen) + [packed] * sent,
            scalars=1,
            after=after,
        )
        return made[: len(chosen)], made[len(chosen) :]

    def send_ahead(windows_sent, sends):
        for w, send in zip(windows_sent, sends):
            gots[w] = ring(send, "lon", out_step)

    gots, tiles = {}, {}
    (tiles[0], halo), sends = packs((0, windows), 1, ())
    send_ahead((0,), sends)
    below = ring(halo, "lat", -1)
    w_t = call(turn_kernel, (w_qkv,), [shape_of(BF, 3 * width, width)], after=(halo,))[0]
    middle = tuple(range(1, windows - 1))
    made, sends = packs((*middle, windows - 1), len(middle), (w_t,))
    *made, last = made
    tiles.update(zip(middle, made))
    tiles[windows - 1], *sends = call(
        functools.partial(pack_last_kernel, ahead),
        (shifts, last, below, *sends),
        [pair, packed] + [packed] * len(middle),
        scalars=1,
    )
    send_ahead((windows - 1, *middle), sends)
    firsts, closed = {}, {}

    def window(w, after):
        firsts[w] = call(
            functools.partial(window_kernel, ahead, w),
            (shifts, region_ids, spot, tiles[w], gots[w], w_t, w_proj),
            [
                pair,
                shape_of(BF, COUNT, width),
                shape_of(BF, width, COUNT),
                shape_of(BF, 3 * width, COUNT),
            ],
            head_scratch(width),
            scalars=3,
            after=after,
        )
        return (firsts[w][1],)

    def close(w, after):
        tile, _, context, grads = firsts[w]
        out, send = call(
            functools.partial(close_kernel, ahead),
            (shifts, tile, context, grads, w_t, w_proj),
            [pair, packed],
            scalars=1,
            after=after,
        )
        closed[w] = out, ring(send, "lon", -out_step)
        return (send,)

    order = [0, windows - 1, *middle]
    after = (sends[0],)
    for n, w in enumerate(order):
        if n >= 2:
            after = (*after, closed[order[n - 2]][1])
        if n == windows - 2:
            after = (*after, gots[order[-1]])
        if n == windows - 1:
            final = call(
                functools.partial(last_back_kernel, ahead),
                (shifts, *closed[windows - 1]),
                [pair],
                scalars=1,
                after=after,
            )[0]
            above = ring(final, "lat", 1)
            after = (*after, final)
        after = window(w, after)
        if n < windows - 1:
            after = close(w, after)

    operands = [[firsts[w][n] for w in range(windows)] for n in (1, 0, 2, 3)]
    operands = [a for group in operands for a in group]

    def weights(kept, after):
        return call(
            functools.partial(weight_kernel, windows, kept),
            (spot, *operands),
            [shape_of(F32, width, 2 * width)],
            scalars=1,
            after=after,
        )[0]

    stage, results = [], []

    def beside(value):
        stage.append(value)
        if len(stage) == 1:
            return close(order[-1], (value,))
        if len(stage) == 2:
            return (closed[order[-1]][1],)
        if len(stage) == 3:
            results.extend(
                call(
                    functools.partial(finish_kernel, ahead, windows),
                    (
                        shifts, tokens, cotangent, above, final,
                        *[closed[w][0] for w in range(windows - 1)],
                        *[closed[w][1] for w in range(windows - 1)],
                    ),
                    [shape_of(BF, *tokens.shape)] * 2,
                    scalars=1,
                    after=(value,),
                )
            )
            return (results[0],)
        return ()

    summed = all_sum(weights, spot, beside, (*after, above, closed[order[-2]][1]))
    mixed, grad_tokens = (
        r.reshape(levels, lon_cols, lat_rows, width).transpose(0, 2, 1, 3) for r in results
    )
    total_tokens = levels * lat_rows * lax.axis_size("lat") * lon_cols * lax.axis_size("lon")
    gradients = write_gradients(1.0 / math.sqrt(total_tokens), spot, *summed)
    return (mixed, grad_tokens, *gradients)


def local(tokens, cotangent, w_qkv, w_proj, shifts, region_ids):
    return lax.cond(
        jnp.sum(shifts[:, 1]) <= ENTRIES,
        functools.partial(body, True),
        functools.partial(body, False),
        tokens, cotangent, w_qkv, w_proj, shifts, region_ids,
    )


def solution(mesh):
    return jax.shard_map(
        local,
        mesh=mesh,
        in_specs=(P(None, "lat", "lon", None), P(None, "lat", "lon", None), P(), P(), P(), P()),
        out_specs=(P(None, "lat", "lon", None), P(None, "lat", "lon", None), P(), P()),
        check_vma=False,
    )
```
